32 devices in a mesh: fsdp: 4 (over y, x), seq: 8 (over z, core).
Axes of the slice: x: 2, y: 2, z: 4, core: 2. Of those that a mesh axis runs over, the one named last changes fastest.
Arguments:
- tokens: bfloat16 [4096, 2048], P(('fsdp', 'seq')), may hold values from -6 to 6
- norm_gains: bfloat16 [4, 2048], replicated, may hold values from 0.25 to 1.75
- w_query: bfloat16 [2048, 2048], P('fsdp', 'seq'), may hold values from -0.125 to 0.125
- w_key: bfloat16 [2048, 2048], P('fsdp', 'seq'), may hold values from -0.125 to 0.125
- w_value: bfloat16 [2048, 2048], P('fsdp', 'seq'), may hold values from -0.125 to 0.125
- w_out: bfloat16 [2048, 2048], P('seq', 'fsdp'), may hold values from -1 to 1
- w_router: bfloat16 [2048, 32], replicated, may hold values from -0.0625 to 0.0625
- w_gate: bfloat16 [32, 2048, 1024], P('seq', 'fsdp'), may hold values from -0.125 to 0.125
- w_up: bfloat16 [32, 2048, 1024], P('seq', 'fsdp'), may hold values from -0.125 to 0.125
- w_down: bfloat16 [32, 1024, 2048], P('seq', None, 'fsdp'), may hold values from -0.5 to 0.5
- segment_ids: int32 [4096], P('fsdp'), may hold values from 0 to 4, as said below
- expert_ids: int32 [4096, 8], P(('fsdp', 'seq')), may hold values from 0 to 31, as said below
- expert_slots: int32 [4096, 8], P(('fsdp', 'seq')), may hold values from 0 to 40, as said below
- cotangent: bfloat16 [4096, 2048], P(('fsdp', 'seq')), may hold values from -6 to 6
Outputs:
- mixed: bfloat16 [4096, 2048], P(('fsdp', 'seq'))
- grad_tokens: float32 [4096, 2048], P(('fsdp', 'seq'))
- grad_gains: float32 [4, 2048], replicated
- grad_query: float32 [2048, 2048], P('fsdp', 'seq')
- grad_key: float32 [2048, 2048], P('fsdp', 'seq')
- grad_value: float32 [2048, 2048], P('fsdp', 'seq')
- grad_out: float32 [2048, 2048], P('seq', 'fsdp')
- grad_router: float32 [2048, 32], replicated
- grad_gate: float32 [32, 2048, 1024], P('seq', 'fsdp')
- grad_up: float32 [32, 2048, 1024], P('seq', 'fsdp')
- grad_down: float32 [32, 1024, 2048], P('seq', None, 'fsdp')
The draws below stay inside these ranges and needn't reach their ends.
Inputs may be any that keep to these rules, and one draw needn't show every extreme that they name: `segment_ids`: within each sequence of 1024 rows the numbers start at 0, never fall and end at 4 (five documents); document 1 starts in the first 128 rows of the sequence and ends in its last 128 rows. `expert_ids`: each row names 8 different experts; in each sequence one expert is named by more than 40 rows of every block of 128 rows. `expert_slots`: within each block of 128 rows (one device's tokens), a pair's slot is its rank, in the order of rows and then of the row's choices, among the block's pairs that name the same expert, or 40 where that rank is 40 or more (the pair is dropped).
All inputs are finite; a program needn't handle non-finite values.
Results may differ from the reference program's by a relative error of at most 0.02.
Values may be sent and summed in bfloat16 or wider, within the bound.
A program may use at most 256 MiB of HBM per device.

```python
import math
import jax
import jax.numpy as jnp
from jax import lax

D = 2048
HEADS = 16
HEAD_DIM = 128
FF = 1024
TOPK = 8
EXPERTS = 32
TOK_DEV = 128
SEQ_LEN = 1024
TOKENS = 4096
CAP = 40
N_SEQ = 8


def routing(key):
    block_count = TOKENS // TOK_DEV
    key_score, key_bias, key_hot, key_rank = jax.random.split(key, 4)
    scores = jax.random.randint(key_score, (TOKENS, EXPERTS), 0, 65536)
    expert_bias = jax.random.randint(key_bias, (EXPERTS,), 0, 32768)
    hot_expert = jax.random.randint(key_hot, (TOKENS // SEQ_LEN,), 0, EXPERTS)
    hot_rows = min(TOK_DEV, CAP + CAP // 2)
    ranks = jax.vmap(lambda single: jax.random.permutation(single, TOK_DEV))(jax.random.split(key_rank, block_count))
    is_hot = (ranks < hot_rows).reshape(TOKENS)
    hot_token = jnp.repeat(hot_expert, SEQ_LEN)
    expert_range = jnp.arange(EXPERTS, dtype=jnp.int32)
    boost = jnp.where(is_hot[:, None] & (expert_range[None, :] == hot_token[:, None]), 1048576, 0)
    combined = (scores + expert_bias[None, :] + boost) * EXPERTS + expert_range[None, :]
    unused, chosen = lax.top_k(combined, TOPK)
    chosen = chosen.astype(jnp.int32)
    picks = (chosen[:, :, None] == expert_range).astype(jnp.int32).reshape(block_count, TOK_DEV * TOPK, EXPERTS)
    before = jnp.cumsum(picks, axis=1) - picks
    slot_rank = jnp.sum(before * picks, axis=-1).reshape(TOKENS, TOPK)
    return (chosen, jnp.minimum(slot_rank, CAP).astype(jnp.int32))


def draw_expert_ids(key, part):
    chosen, slot_rank = routing(key)
    return chosen


def draw_expert_slots(key, part):
    chosen, slot_rank = routing(key)
    return slot_rank


def draw_segment_ids(key, part):
    key = jax.random.fold_in(key, 7)
    count = TOKENS // SEQ_LEN
    key_start, key_end, key_first, key_second = jax.random.split(key, 4)
    starts = jax.random.randint(key_start, (count,), 1, TOK_DEV)
    ends = jax.random.randint(key_end, (count,), SEQ_LEN - TOK_DEV, SEQ_LEN - TOK_DEV // 2)
    tail_rows = SEQ_LEN - 2 - ends
    half_tail = tail_rows // 2
    first_break = ends + 2 + jax.random.randint(key_first, (count,), 0, 65536) % half_tail
    second_break = ends + 2 + half_tail + jax.random.randint(key_second, (count,), 0, 65536) % (tail_rows - half_tail)
    positions = jnp.arange(SEQ_LEN, dtype=jnp.int32)[None, :]
    begins = (positions == starts[:, None]) | (positions == ends[:, None] + 1) | (positions == first_break[:, None]) | (positions == second_break[:, None])
    numbers = jnp.cumsum(begins.astype(jnp.int32), axis=1)
    return numbers.reshape(TOKENS).astype(jnp.int32)


def levels(rng, dims, cuts, low, high):
    factor_of, own = 1.0, jax.random.fold_in(rng, 6)
    for axis_at, shards_of in cuts:
        steps = jnp.exp(jax.random.uniform(jax.random.fold_in(own, axis_at), (shards_of,), jnp.float32, low / len(cuts), high / len(cuts)))
        factor_of = factor_of * jnp.repeat(steps, dims[axis_at] // shards_of).reshape([-1 if axis == axis_at else 1 for axis in range(len(dims))])
    return factor_of


def scatter_about(key, extent, spread, most, cuts=(), held_as=jnp.bfloat16):
    values = jax.random.normal(key, extent, jnp.float32) * spread
    if len(cuts) > 0:
        values = levels(key, extent, cuts, -0.22, 0.18) * values
    return jnp.clip(values, min=-most, max=most).astype(held_as)


def setup_inputs(seed: int = 0) -> dict:
    streams_of = jax.random.split(jax.random.key(seed), 15)
    tokens = scatter_about(streams_of[0], (TOKENS, D), 1.0, 6.0, ((0, 32),))
    norm_gains = jnp.clip(1.0 + 0.15 * jax.random.normal(streams_of[1], (4, D), jnp.float32), 0.25, 1.75).astype(jnp.bfloat16)
    w_query = scatter_about(streams_of[2], (D, D), D ** -0.5, 0.125, ((0, 4), (1, 8)))
    w_key = scatter_about(streams_of[3], (D, D), D ** -0.5, 0.125, ((0, 4), (1, 8)))
    w_value = scatter_about(streams_of[4], (D, D), D ** -0.5, 0.125, ((0, 4), (1, 8)))
    w_out = scatter_about(streams_of[5], (D, D), (D // 64) ** -0.5, 1.0, ((0, 8), (1, 4)))
    w_router = scatter_about(streams_of[6], (D, EXPERTS), (4 * D) ** -0.5, 0.0625)
    w_gate = scatter_about(streams_of[7], (EXPERTS, D, FF), D ** -0.5, 0.125, ((0, 8), (1, 4)))
    w_up = scatter_about(streams_of[8], (EXPERTS, D, FF), D ** -0.5, 0.125, ((0, 8), (1, 4)))
    w_down = scatter_about(streams_of[9], (EXPERTS, FF, D), (FF // 8) ** -0.5, 0.5, ((0, 8), (2, 4)))
    segment_ids = draw_segment_ids(jax.random.fold_in(streams_of[14], 71), 0)
    expert_ids = draw_expert_ids(jax.random.fold_in(streams_of[14], 71), 0)
    expert_slots = draw_expert_slots(jax.random.fold_in(streams_of[14], 71), 0)
    cotangent = scatter_about(streams_of[13], (TOKENS, D), 1.0, 6.0, ((0, 32),))
    return {"tokens": tokens, "norm_gains": norm_gains, "w_query": w_query, "w_key": w_key, "w_value": w_value, "w_out": w_out, "w_router": w_router, "w_gate": w_gate, "w_up": w_up, "w_down": w_down, "segment_ids": segment_ids, "expert_ids": expert_ids, "expert_slots": expert_slots, "cotangent": cotangent}


EPSILON = 1e-06
THETA = 10000.0
MASKED = -1e+30
HIGHEST = lax.Precision.HIGHEST

@jax.custom_vjp
def low(v):
    return lax.optimization_barrier(v.astype(jnp.bfloat16)).astype(jnp.float32)

@jax.custom_vjp
def low_back(v):
    return v

def low_keep(v):
    return (low(v), None)

def low_pass(kept, grad):
    return (grad,)

def back_keep(v):
    return (v, None)

def back_low(kept, grad):
    return (low(grad),)
low.defvjp(low_keep, low_pass)
low_back.defvjp(back_keep, back_low)

def matmul(left_side, right_side):
    return jnp.dot(left_side, right_side, precision=HIGHEST, preferred_element_type=jnp.float32)

def normalize(values_in):
    return values_in * lax.rsqrt(lax.optimization_barrier(jnp.mean(values_in * values_in, -1, keepdims=True)) + EPSILON)

def rope_tables(positions, head_size):
    half_dim = head_size // 2
    frequency = THETA ** (-jnp.arange(half_dim, dtype=jnp.float32) / half_dim)
    angles = positions.astype(jnp.float32)[:, None] * frequency[None, :]
    return (jnp.cos(angles), jnp.sin(angles))

def rotate(values_in, cosine_table, sine_table, head_size):
    row_count = values_in.shape[0]
    pieces = values_in.reshape(row_count, -1, head_size)
    half_dim = head_size // 2
    former = pieces[..., :half_dim]
    latter = pieces[..., half_dim:]
    cosine_wide = cosine_table[:, None, :]
    sine_wide = sine_table[:, None, :]
    turned = jnp.concatenate([former * cosine_wide - latter * sine_wide, latter * cosine_wide + former * sine_wide], -1)
    return turned.reshape(row_count, -1)

def sequence_layer(inputs, weights):
    gain_rows, w_query, w_key, w_value, w_out, w_router, w_gate, w_up, w_down = weights
    tokens_seq, segments, choices_seq, slots_seq = inputs
    length = tokens_seq.shape[0]
    cosine_table, sine_table = rope_tables(jnp.arange(length), HEAD_DIM)
    normed = low(normalize(tokens_seq) * gain_rows[0])
    query_raw = low_back(matmul(normed, w_query))
    key_raw = low_back(matmul(normed, w_key))
    query = low_back(low(rotate(normalize(query_raw) * gain_rows[2], cosine_table, sine_table, HEAD_DIM)))
    keys = low_back(low(rotate(normalize(key_raw) * gain_rows[3], cosine_table, sine_table, HEAD_DIM)))
    values = low_back(low(matmul(normed, w_value)))
    key_cube = keys.reshape(length, HEADS, HEAD_DIM)
    value_cube = values.reshape(length, HEADS, HEAD_DIM)
    block_rows = math.gcd(512, length)
    score_scale = HEAD_DIM ** (-0.5)

    def attend(block_pair):
        query_block, segment_block = block_pair
        scores = jnp.einsum('qhd,khd->hqk', query_block, key_cube, precision=HIGHEST) * score_scale
        visible = segment_block[:, None] == segments[None, :]
        scores = low_back(jnp.where(visible[None], scores, MASKED))
        weights_soft = jax.nn.softmax(scores, axis=-1)
        return jnp.einsum('hqk,khd->qhd', low(weights_soft), value_cube, precision=HIGHEST)
    mixed_heads = lax.map(jax.checkpoint(attend), (query.reshape(length // block_rows, block_rows, HEADS, HEAD_DIM), segments.reshape(length // block_rows, block_rows)))
    attended = low_back(low(mixed_heads.reshape(length, D)))
    residual = tokens_seq + low_back(matmul(attended, w_out))
    routed = low(normalize(residual) * gain_rows[1])
    logits = low_back(matmul(routed, w_router))
    picked = jnp.take_along_axis(logits, choices_seq, axis=1)
    gate_weights = jax.nn.softmax(picked, axis=-1)
    places = jnp.where(slots_seq < CAP, choices_seq * CAP + slots_seq, -1)
    onehot = jax.nn.one_hot(places, EXPERTS * CAP, dtype=jnp.float32).reshape(N_SEQ, TOK_DEV, TOPK, EXPERTS * CAP)
    sources = routed.reshape(N_SEQ, TOK_DEV, D)
    buffers = jnp.einsum('btkc,btd->bcd', onehot, sources, precision=HIGHEST)
    expert_rows = buffers.reshape(N_SEQ, EXPERTS, CAP, D).transpose(1, 0, 2, 3).reshape(EXPERTS, N_SEQ * CAP, D)
    expert_rows = low_back(expert_rows)
    gate_pre = low_back(jnp.einsum('erd,edf->erf', expert_rows, w_gate, precision=HIGHEST))
    up_pre = low_back(jnp.einsum('erd,edf->erf', expert_rows, w_up, precision=HIGHEST))
    hidden = low(jax.nn.silu(gate_pre) * up_pre)
    returned = low_back(low(jnp.einsum('erf,efd->erd', hidden, w_down, precision=HIGHEST)))
    back_blocks = returned.reshape(EXPERTS, N_SEQ, CAP, D).transpose(1, 0, 2, 3).reshape(N_SEQ, EXPERTS * CAP, D)
    picked_rows = jnp.einsum('btkc,bcd->btkd', onehot, back_blocks, precision=HIGHEST).reshape(length, TOPK, D)
    mixture = lax.optimization_barrier(jnp.sum(gate_weights[:, :, None] * picked_rows, axis=1))
    return residual + mixture

def reference(tokens, norm_gains, w_query, w_key, w_value, w_out, w_router, w_gate, w_up, w_down, segment_ids, expert_ids, expert_slots, cotangent):
    sequences = TOKENS // SEQ_LEN
    floats = tuple((item.astype(jnp.float32) for item in (tokens, norm_gains, w_query, w_key, w_value, w_out, w_router, w_gate, w_up, w_down)))

    def forward(token_values, *weights):

        def per_sequence(inputs):
            return sequence_layer(inputs, weights)
        stacked = lax.map(jax.checkpoint(per_sequence), (token_values.reshape(sequences, SEQ_LEN, D), segment_ids.reshape(sequences, SEQ_LEN), expert_ids.reshape(sequences, SEQ_LEN, TOPK), expert_slots.reshape(sequences, SEQ_LEN, TOPK)))
        return stacked.reshape(TOKENS, D)
    result, pullback = jax.vjp(forward, *floats)
    gradients = pullback(cotangent.astype(jnp.float32))
    return (result.astype(jnp.bfloat16), gradients[0], gradients[1], gradients[2], gradients[3], gradients[4], gradients[5], gradients[6], gradients[7], gradients[8], gradients[9])
```

```python
import math

import jax
import jax.numpy as jnp
from jax import lax
from jax.sharding import PartitionSpec as P

HEAD_DIM = 128
CAP = 40


EPSILON = 1e-06
THETA = 10000.0
MASKED = -1e30
HIGHEST = lax.Precision.HIGHEST


def rope_tables(positions, head_size):
    half_dim = head_size // 2
    frequency = THETA ** (-jnp.arange(half_dim, dtype=jnp.float32) / half_dim)
    angles = positions.astype(jnp.float32)[:, None] * frequency[None, :]
    return (jnp.cos(angles), jnp.sin(angles))


def rotate(values_in, cosine_table, sine_table, head_size):
    row_count = values_in.shape[0]
    pieces = values_in.reshape(row_count, -1, head_size)
    half_dim = head_size // 2
    former = pieces[..., :half_dim]
    latter = pieces[..., half_dim:]
    cosine_wide = cosine_table[:, None, :]
    sine_wide = sine_table[:, None, :]
    turned = jnp.concatenate(
        [former * cosine_wide - latter * sine_wide, latter * cosine_wide + former * sine_wide], -1
    )
    return turned.reshape(row_count, -1)


def inverse_rms(values_in):
    return lax.rsqrt(jnp.mean(values_in * values_in, -1, keepdims=True) + EPSILON)


def norm_back(grad_unit, unit_values, inverse):
    return inverse * (
        grad_unit - unit_values * jnp.mean(grad_unit * unit_values, -1, keepdims=True)
    )


def shards(
    tokens,
    norm_gains,
    w_query,
    w_key,
    w_value,
    w_out,
    w_router,
    w_gate,
    w_up,
    w_down,
    segment_ids,
    expert_ids,
    expert_slots,
    cotangent,
):
    half_type = jnp.bfloat16
    float_type = jnp.float32
    tok_rows = tokens.shape[0]
    model_width = tokens.shape[1]
    expert_total = w_router.shape[1]
    top_count = expert_ids.shape[1]
    head_size = HEAD_DIM
    local_width = w_query.shape[1]
    heads_local = local_width // head_size
    capacity = CAP
    seq_index = lax.axis_index("seq")
    column_start = seq_index * local_width
    experts_local = w_gate.shape[0]
    split = lax.axis_size("fsdp")
    groups = split // experts_local
    partners = None
    if groups > 1:
        partners = [
            [group * experts_local + member for member in range(experts_local)]
            for group in range(groups)
        ]

    def to_owner(weight, dim):
        spread = jnp.concatenate([weight] * groups, 0) if groups > 1 else weight
        return lax.all_to_all(spread, "fsdp", split_axis=0, concat_axis=dim, tiled=True)[0]

    def to_shards(grad, dim):
        parts = lax.all_to_all(
            grad.astype(half_type)[None], "fsdp", split_axis=dim, concat_axis=0, tiled=True
        ).astype(float_type)
        if groups > 1:
            parts = parts.reshape(groups, experts_local, *parts.shape[1:]).sum(0)
        return parts

    def exchange(rows):
        return lax.all_to_all(
            rows, "fsdp", split_axis=0, concat_axis=0, tiled=True, axis_index_groups=partners
        )

    qkv_cols = lax.all_gather(
        jnp.concatenate([w_query, w_key, w_value], 1), "fsdp", axis=0, tiled=True
    )
    out_rows = lax.all_gather(w_out, "fsdp", axis=1, tiled=True)
    gate_full = to_owner(w_gate, 1)
    up_full = to_owner(w_up, 1)
    down_full = to_owner(w_down, 2)
    places = jnp.where(
        expert_slots < capacity, expert_ids * capacity + expert_slots, -(10**6)
    )
    both_seq = lax.all_gather(
        jnp.concatenate([expert_ids, places], 1), "seq", axis=0, tiled=True
    )
    ids_seq = both_seq[:, :top_count]
    places_seq = both_seq[:, top_count:]
    cotangent_seq = lax.all_gather(cotangent, "seq", axis=0, tiled=True)
    gain_rows = norm_gains.astype(float_type)
    gain_cols = lax.dynamic_slice_in_dim(gain_rows, column_start, local_width, 1)
    inputs = tokens.astype(float_type)
    inverse_first = inverse_rms(inputs)
    unit_first = inputs * inverse_first
    normed = (unit_first * gain_rows[0]).astype(half_type)
    normed_seq = lax.all_gather(normed, "seq", axis=0, tiled=True)
    length = normed_seq.shape[0]
    raw = jnp.dot(normed_seq, qkv_cols, preferred_element_type=float_type)
    query_raw = raw[:, :local_width]
    key_raw = raw[:, local_width : 2 * local_width]
    value_heads = raw[:, 2 * local_width :].astype(half_type)
    square_sums = lax.psum(
        (jnp.sum(query_raw * query_raw, -1), jnp.sum(key_raw * key_raw, -1)), "seq"
    )
    inverse_query = lax.rsqrt(square_sums[0] / model_width + EPSILON)[:, None]
    inverse_key = lax.rsqrt(square_sums[1] / model_width + EPSILON)[:, None]
    positions = jnp.arange(length, dtype=jnp.int32)
    cosine_table, sine_table = rope_tables(positions, head_size)
    unit_query = query_raw * inverse_query
    unit_key = key_raw * inverse_key
    query_heads = rotate(unit_query * gain_cols[2], cosine_table, sine_table, head_size).astype(
        half_type
    )
    key_heads = rotate(unit_key * gain_cols[3], cosine_table, sine_table, head_size).astype(
        half_type
    )
    block_rows = math.gcd(512, length)
    blocks = length // block_rows
    score_scale = head_size ** (-0.5)
    query_cube = query_heads.reshape(blocks, block_rows, heads_local, head_size)
    key_cube = key_heads.reshape(length, heads_local, head_size)
    value_cube = value_heads.reshape(length, heads_local, head_size)
    segment_blocks = segment_ids.reshape(blocks, block_rows)

    def block_scores(query_block, segment_block):
        scores = (
            jnp.einsum("qhd,khd->hqk", query_block, key_cube, preferred_element_type=float_type)
            * score_scale
        )
        visible = segment_block[:, None] == segment_ids[None, :]
        return jnp.where(visible[None], scores, MASKED)

    def attend(block_pair):
        query_block, segment_block = block_pair
        scores = block_scores(query_block, segment_block)
        row_peak = jnp.max(scores, -1, keepdims=True)
        exp_scores = jnp.exp(scores - row_peak)
        exp_total = jnp.sum(exp_scores, -1, keepdims=True)
        weights_soft = (exp_scores / exp_total).astype(half_type)
        mixed_block = jnp.einsum(
            "hqk,khd->qhd", weights_soft, value_cube, preferred_element_type=float_type
        )
        return (mixed_block.astype(half_type), (row_peak + jnp.log(exp_total))[..., 0])

    mixed_heads, log_sums = lax.map(attend, (query_cube, segment_blocks))
    attended_heads = mixed_heads.reshape(length, local_width)
    projected = lax.psum_scatter(
        jnp.dot(attended_heads, out_rows, preferred_element_type=float_type).astype(half_type),
        "seq",
        scatter_dimension=0,
        tiled=True,
    ).astype(float_type)
    residual = inputs + projected
    inverse_second = inverse_rms(residual)
    unit_second = residual * inverse_second
    routed = (unit_second * gain_rows[1]).astype(half_type)
    routed_seq = lax.all_gather(routed, "seq", axis=0, tiled=True)
    seq_size = length // tok_rows
    slots = experts_local * capacity

    def gates_of(rows, ids):
        logits = jnp.dot(rows, w_router, preferred_element_type=float_type)
        chosen = (ids[:, :, None] == jnp.arange(expert_total, dtype=jnp.int32)).astype(float_type)
        picked = jnp.einsum("tke,te->tk", chosen, logits, precision=HIGHEST)
        return chosen, jax.nn.softmax(picked, axis=-1)

    chosen, gate_weights = gates_of(routed, expert_ids)
    gates_seq = gates_of(routed_seq, ids_seq)[1]
    mine = (places_seq - seq_index * slots).reshape(seq_size, tok_rows, top_count)
    hits = mine[:, :, :, None] == jnp.arange(slots, dtype=jnp.int32)
    onehot = jnp.any(hits, 2).astype(half_type)
    combine = jnp.sum(
        jnp.where(hits, gates_seq.reshape(seq_size, tok_rows, top_count)[..., None], 0.0), 2
    )

    def dispatch(rows):
        placed = jnp.einsum(
            "btc,btd->bcd",
            onehot,
            rows.reshape(seq_size, tok_rows, model_width),
            preferred_element_type=float_type,
        ).astype(half_type)
        placed = placed.reshape(seq_size, experts_local, capacity, model_width)
        return placed.transpose(1, 0, 2, 3)

    def undispatch(rows):
        rows = rows.reshape(experts_local, seq_size, capacity, model_width)
        return rows.transpose(1, 0, 2, 3).reshape(seq_size, slots, model_width)

    flat = experts_local * seq_size * capacity
    expert_rows = exchange(dispatch(routed_seq)).reshape(flat, model_width)
    upstream_slots = dispatch(cotangent_seq)
    upstream_rows = exchange(upstream_slots).reshape(flat, model_width)
    slot_gates = jnp.sum(combine, 1).reshape(seq_size, experts_local, capacity).transpose(1, 0, 2)
    row_gates = exchange(slot_gates).reshape(flat)
    gate_pre = jnp.dot(expert_rows, gate_full, preferred_element_type=float_type)
    up_pre = jnp.dot(expert_rows, up_full, preferred_element_type=float_type)
    gate_sigmoid = jax.nn.sigmoid(gate_pre)
    hidden = (gate_pre * gate_sigmoid * up_pre).astype(half_type)
    returned = jnp.dot(hidden, down_full, preferred_element_type=float_type).astype(half_type)
    slot_dots = jnp.sum(
        returned.astype(float_type) * upstream_rows.astype(float_type), -1
    ).reshape(experts_local, seq_size, capacity)
    slot_dots = exchange(slot_dots).transpose(1, 0, 2).reshape(seq_size, slots)
    gate_grad_part = jnp.sum(jnp.where(hits, slot_dots[:, None, None, :], 0.0), -1)
    gate_grad = lax.psum_scatter(
        gate_grad_part.reshape(length, top_count), "seq", scatter_dimension=0, tiled=True
    )
    incoming = undispatch(exchange(returned.reshape(experts_local, seq_size, capacity, model_width)))
    mixture_part = jnp.einsum(
        "btc,bcd->btd", combine.astype(half_type), incoming, preferred_element_type=float_type
    ).astype(half_type)
    mixture = lax.psum_scatter(
        mixture_part.reshape(length, model_width), "seq", scatter_dimension=0, tiled=True
    ).astype(float_type)
    output = (residual + mixture).astype(half_type)
    upstream = cotangent.astype(float_type)
    slot_grads = (row_gates[:, None] * upstream_rows.astype(float_type)).astype(half_type)
    hidden_grad = jnp.einsum(
        "rd,fd->rf", slot_grads, down_full, preferred_element_type=float_type
    )
    gate_pre_grad = (
        hidden_grad * up_pre * gate_sigmoid * (1.0 + gate_pre * (1.0 - gate_sigmoid))
    ).astype(half_type)
    up_pre_grad = (hidden_grad * gate_pre * gate_sigmoid).astype(half_type)
    rows_grad = jnp.einsum("rf,df->rd", gate_pre_grad, gate_full, preferred_element_type=float_type)
    rows_grad = (
        rows_grad
        + jnp.einsum("rf,df->rd", up_pre_grad, up_full, preferred_element_type=float_type)
    ).astype(half_type)
    sent_back = undispatch(
        exchange(rows_grad.reshape(experts_local, seq_size, capacity, model_width))
    )
    expert_part = jnp.einsum(
        "btc,bcd->btd", onehot, sent_back, preferred_element_type=float_type
    ).astype(half_type)
    routed_grad = lax.psum_scatter(
        expert_part.reshape(length, model_width), "seq", scatter_dimension=0, tiled=True
    ).astype(float_type)
    grad_down_full = jnp.einsum("rf,rd->fd", hidden, slot_grads, preferred_element_type=float_type)
    grad_gate_full = jnp.einsum(
        "rd,rf->df", expert_rows, gate_pre_grad, preferred_element_type=float_type
    )
    grad_up_full = jnp.einsum("rd,rf->df", expert_rows, up_pre_grad, preferred_element_type=float_type)
    mean_grad = jnp.sum(gate_weights * gate_grad, -1, keepdims=True)
    picked_grad = gate_weights * (gate_grad - mean_grad)
    logit_grad = jnp.einsum("tke,tk->te", chosen, picked_grad, precision=HIGHEST).astype(half_type)
    routed_grad = routed_grad + jnp.einsum(
        "te,de->td", logit_grad, w_router, preferred_element_type=float_type
    )
    grad_router_local = jnp.einsum(
        "td,te->ed", routed, logit_grad, preferred_element_type=float_type
    )
    gain_second_grad = jnp.sum(routed_grad * unit_second, axis=0)
    residual_grad = upstream + norm_back(routed_grad * gain_rows[1], unit_second, inverse_second)
    out_grad = residual_grad.astype(half_type)
    out_grad_seq = lax.all_gather(out_grad, "seq", axis=0, tiled=True)
    grad_out_local = jnp.einsum(
        "th,td->hd", attended_heads, out_grad_seq, preferred_element_type=float_type
    )
    attended_grad = jnp.einsum(
        "td,hd->th", out_grad_seq, out_rows, preferred_element_type=float_type
    ).astype(half_type)
    grad_cube = attended_grad.reshape(blocks, block_rows, heads_local, head_size)

    def attend_back(running, pieces):
        key_acc, value_acc = running
        query_block, segment_block, grad_block, log_block = pieces
        scores = block_scores(query_block, segment_block)
        soft_values = jnp.exp(scores - log_block[..., None])
        prob_grad = jnp.einsum(
            "qhd,khd->hqk", grad_block, value_cube, preferred_element_type=float_type
        )
        center = jnp.sum(soft_values * prob_grad, -1, keepdims=True)
        score_grad = (soft_values * (prob_grad - center)).astype(half_type)
        query_grad = (
            jnp.einsum("hqk,khd->qhd", score_grad, key_cube, preferred_element_type=float_type)
            * score_scale
        )
        key_acc = (
            key_acc
            + jnp.einsum("hqk,qhd->khd", score_grad, query_block, preferred_element_type=float_type)
            * score_scale
        )
        value_acc = value_acc + jnp.einsum(
            "hqk,qhd->khd",
            soft_values.astype(half_type),
            grad_block,
            preferred_element_type=float_type,
        )
        return ((key_acc, value_acc), query_grad.astype(half_type))

    empty_acc = jnp.zeros((length, heads_local, head_size), float_type)
    (key_acc, value_acc), query_grads = lax.scan(
        attend_back, (empty_acc, empty_acc), (query_cube, segment_blocks, grad_cube, log_sums)
    )
    query_back = query_grads.reshape(length, local_width)
    key_back = key_acc.reshape(length, local_width).astype(half_type)
    value_back = value_acc.reshape(length, local_width).astype(half_type)
    query_unit_grad = rotate(query_back.astype(float_type), cosine_table, -sine_table, head_size)
    key_unit_grad = rotate(key_back.astype(float_type), cosine_table, -sine_table, head_size)
    gain_query_grad = jnp.sum(query_unit_grad * unit_query, axis=0)
    gain_key_grad = jnp.sum(key_unit_grad * unit_key, axis=0)
    query_scaled = query_unit_grad * gain_cols[2]
    key_scaled = key_unit_grad * gain_cols[3]
    centers = lax.psum(
        (jnp.sum(query_scaled * unit_query, -1), jnp.sum(key_scaled * unit_key, -1)), "seq"
    )
    query_raw_grad = (
        inverse_query * (query_scaled - unit_query * (centers[0] / model_width)[:, None])
    ).astype(half_type)
    key_raw_grad = (
        inverse_key * (key_scaled - unit_key * (centers[1] / model_width)[:, None])
    ).astype(half_type)
    raw_grads = jnp.concatenate([query_raw_grad, key_raw_grad, value_back], 1)
    normed_part = jnp.einsum("th,dh->td", raw_grads, qkv_cols, preferred_element_type=float_type)
    grad_qkv_local = jnp.einsum("td,th->dh", normed_seq, raw_grads, preferred_element_type=float_type)
    normed_grad = lax.psum_scatter(
        normed_part.astype(jnp.bfloat16), "seq", scatter_dimension=0, tiled=True
    ).astype(jnp.float32)
    gain_first_grad = jnp.sum(normed_grad * unit_first, axis=0)
    input_grad = residual_grad + norm_back(normed_grad * gain_rows[0], unit_first, inverse_first)
    zero_row = jnp.zeros((model_width,), float_type)
    gain_query_full = lax.dynamic_update_slice_in_dim(zero_row, gain_query_grad, column_start, 0)
    gain_key_full = lax.dynamic_update_slice_in_dim(zero_row, gain_key_grad, column_start, 0)
    gain_grads = jnp.stack([gain_first_grad, gain_second_grad, gain_query_full, gain_key_full])
    router_grad = lax.psum(grad_router_local, ("fsdp", "seq")).T
    gain_sums = lax.psum(gain_grads, ("fsdp", "seq"))
    qkv_owned = lax.psum_scatter(
        grad_qkv_local.astype(half_type), "fsdp", scatter_dimension=0, tiled=True
    ).astype(float_type)
    out_owned = lax.psum_scatter(
        grad_out_local.astype(half_type), "fsdp", scatter_dimension=1, tiled=True
    ).astype(float_type)
    return (
        output,
        input_grad,
        gain_sums,
        qkv_owned[:, :local_width],
        qkv_owned[:, local_width : 2 * local_width],
        qkv_owned[:, 2 * local_width :],
        out_owned,
        router_grad,
        to_shards(grad_gate_full, 1),
        to_shards(grad_up_full, 1),
        to_shards(grad_down_full, 2),
    )


def solution(mesh):
    in_specs = (
        P(("fsdp", "seq"), None),
        P(),
        P("fsdp", "seq"),
        P("fsdp", "seq"),
        P("fsdp", "seq"),
        P("seq", "fsdp"),
        P(),
        P("seq", "fsdp", None),
        P("seq", "fsdp", None),
        P("seq", None, "fsdp"),
        P("fsdp"),
        P(("fsdp", "seq"), None),
        P(("fsdp", "seq"), None),
        P(("fsdp", "seq"), None),
    )
    out_specs = (
        P(("fsdp", "seq"), None),
        P(("fsdp", "seq"), None),
        P(),
        P("fsdp", "seq"),
        P("fsdp", "seq"),
        P("fsdp", "seq"),
        P("seq", "fsdp"),
        P(),
        P("seq", "fsdp", None),
        P("seq", "fsdp", None),
        P("seq", None, "fsdp"),
    )
    return jax.shard_map(shards, mesh=mesh, in_specs=in_specs, out_specs=out_specs, check_vma=False)
```

```python
import functools
import math

import jax
import jax.numpy as jnp
from jax import lax
from jax.experimental import pallas as pl
from jax.experimental.pallas import tpu as pltpu
from jax.sharding import PartitionSpec as P

HEAD_DIM = 128
CAP = 40


EPSILON = 1e-06
THETA = 10000.0
MASKED = -1e30
HIGHEST = lax.Precision.HIGHEST


def rope_tables(positions, head_size):
    half_dim = head_size // 2
    frequency = THETA ** (-jnp.arange(half_dim, dtype=jnp.float32) / half_dim)
    angles = positions.astype(jnp.float32)[:, None] * frequency[None, :]
    return (jnp.cos(angles), jnp.sin(angles))


def rotate(values_in, cosine_table, sine_table, head_size):
    row_count = values_in.shape[0]
    pieces = values_in.reshape(row_count, -1, head_size)
    half_dim = head_size // 2
    former = pieces[..., :half_dim]
    latter = pieces[..., half_dim:]
    cosine_wide = cosine_table[:, None, :]
    sine_wide = sine_table[:, None, :]
    turned = jnp.concatenate(
        [former * cosine_wide - latter * sine_wide, latter * cosine_wide + former * sine_wide], -1
    )
    return turned.reshape(row_count, -1)


def inverse_rms(values_in):
    return lax.rsqrt(jnp.mean(values_in * values_in, -1, keepdims=True) + EPSILON)


def norm_back(grad_unit, unit_values, inverse):
    return inverse * (
        grad_unit - unit_values * jnp.mean(grad_unit * unit_values, -1, keepdims=True)
    )


def greet_chain(chip, core, chips):
    barrier = pltpu.get_barrier_semaphore()

    def greet(target):
        pl.semaphore_signal(barrier, inc=1, device_id={"seq": target})

    greet(chip * 2 + 1 - core)

    @pl.when(chip < chips - 1)
    def _():
        greet(chip * 2 + 2 + core)

    @pl.when(chip > 0)
    def _():
        greet(chip * 2 - 2 + core)

    inner = jnp.where(chip < chips - 1, 1, 0) + jnp.where(chip > 0, 1, 0)
    pl.semaphore_wait(barrier, 1 + inner)


def gather_kernel(chips, x_ref, out_ref, local_sem, up_sem, down_sem, side_sem, chain_sem, cross_sem):
    me = lax.axis_index("seq")
    chip, core = me // 2, lax.rem(me, 2)
    rows = x_ref.shape[0]
    greet_chain(chip, core, chips)

    def block(source, source_core):
        start = pl.multiple_of((source * 2 + source_core) * rows, rows)
        return out_ref.at[pl.ds(start, rows)]

    def hop(source, ref, target, sends, arrivals):
        return pltpu.make_async_remote_copy(
            src_ref=ref,
            dst_ref=block(source, core),
            send_sem=sends.at[source],
            recv_sem=arrivals.at[source],
            device_id={"seq": target},
        )

    def upward(source, ref):
        return hop(source, ref, chip * 2 + 2 + core, up_sem, chain_sem)

    def downward(source, ref):
        return hop(source, ref, chip * 2 - 2 + core, down_sem, chain_sem)

    def sideways(source, ref):
        return hop(source, ref, chip * 2 + 1 - core, side_sem, cross_sem)

    own = pltpu.make_async_copy(x_ref, block(chip, core), local_sem)

    @pl.when(chip < chips - 1)
    def _():
        upward(chip, x_ref).start()

    @pl.when(chip > 0)
    def _():
        downward(chip, x_ref).start()

    sideways(chip, x_ref).start()
    own.start()
    for step in range(1, chips):
        below, above = chip - step, chip + step

        @pl.when(below >= 0)
        def _():
            landed = block(below, core)
            upward(below, landed).wait_recv()

            @pl.when(chip < chips - 1)
            def _():
                upward(below, landed).start()

            sideways(below, landed).start()

        @pl.when(above < chips)
        def _():
            landed = block(above, core)
            downward(above, landed).wait_recv()

            @pl.when(chip > 0)
            def _():
                downward(above, landed).start()

            sideways(above, landed).start()

    own.wait()
    for source in range(chips):
        sideways(source, block(source, core)).wait()

        @pl.when((chip < chips - 1) & (source <= chip))
        def _():
            upward(source, block(source, core)).wait_send()

        @pl.when((chip > 0) & (source >= chip))
        def _():
            downward(source, block(source, core)).wait_send()


def seq_gather(x, size, which):
    chips = size // 2
    rows, width = x.shape
    return pl.pallas_call(
        functools.partial(gather_kernel, chips),
        out_shape=jax.ShapeDtypeStruct((size * rows, width), x.dtype),
        in_specs=[pl.BlockSpec(memory_space=pl.ANY)],
        out_specs=pl.BlockSpec(memory_space=pl.ANY),
        scratch_shapes=[pltpu.SemaphoreType.DMA] + [pltpu.SemaphoreType.DMA((chips,))] * 5,
        compiler_params=pltpu.CompilerParams(collective_id=which, has_side_effects=True),
        cost_estimate=pl.CostEstimate(
            flops=0, bytes_accessed=40 * x.size * x.dtype.itemsize * chips, transcendentals=0
        ),
    )(x)


def reduce_kernel(
    chips,
    shared,
    turned,
    a_ref,
    b_ref,
    o_ref,
    side_out,
    side_in,
    chain_out,
    chain_in,
    total,
    side_send,
    side_recv,
    chain_send,
    chain_recv,
):
    me = lax.axis_index("seq")
    chip, core = me // 2, lax.rem(me, 2)
    rows, width = o_ref.shape
    step_cols = min(512, width)
    greet_chain(chip, core, chips)

    def product(block, store):
        left = a_ref[block]

        @pl.loop(0, width // step_cols)
        def _(index):
            cols = pl.ds(pl.multiple_of(index * step_cols, step_cols), step_cols)
            right_ref = b_ref if shared else b_ref.at[block]
            if turned:
                part = lax.dot_general(
                    left,
                    right_ref[cols, :],
                    (((1,), (1,)), ((), ())),
                    preferred_element_type=jnp.float32,
                )
            else:
                part = jnp.dot(left, right_ref[:, cols], preferred_element_type=jnp.float32)
            store(cols, part)

    def side_copy(dest):
        return pltpu.make_async_remote_copy(
            src_ref=side_out.at[dest],
            dst_ref=side_in.at[dest],
            send_sem=side_send.at[dest],
            recv_sem=side_recv.at[dest],
            device_id={"seq": chip * 2 + 1 - core},
        )

    def chain_copy(way, dest, target):
        return pltpu.make_async_remote_copy(
            src_ref=chain_out.at[dest],
            dst_ref=chain_in.at[way, dest],
            send_sem=chain_send.at[dest],
            recv_sem=chain_recv.at[way, dest],
            device_id={"seq": target},
        )

    def place(index):
        distance = chips - 1 - index // 2
        sign = 1 - 2 * lax.rem(index, 2)
        dest = chip + sign * distance
        inside = (dest >= 0) & (dest < chips)
        return dest, inside

    @pl.loop(0, 2 * chips - 1)
    def _(index):
        dest, inside = place(index)

        @pl.when(inside)
        def _():
            def store(cols, part):
                side_out[dest, :, cols] = part.astype(side_out.dtype)

            product(dest * 2 + 1 - core, store)
            side_copy(dest).start()

    @pl.loop(0, 2 * chips - 1)
    def _(index):
        dest, inside = place(index)

        @pl.when(inside)
        def _():
            def store(cols, part):
                total[:, cols] = part

            product(dest * 2 + core, store)
            side_copy(dest).wait_recv()
            total[...] += side_in[dest].astype(jnp.float32)

            @pl.when((dest >= chip) & (chip > 0))
            def _():
                chain_copy(0, dest, chip * 2 + 1 - core).wait_recv()
                total[...] += chain_in[0, dest].astype(jnp.float32)

            @pl.when((dest <= chip) & (chip < chips - 1))
            def _():
                chain_copy(1, dest, chip * 2 + 1 - core).wait_recv()
                total[...] += chain_in[1, dest].astype(jnp.float32)

            @pl.when(dest == chip)
            def _():
                o_ref[...] = total[...]

            @pl.when(dest != chip)
            def _():
                chain_out[dest] = total[...].astype(chain_out.dtype)

            @pl.when(dest > chip)
            def _():
                chain_copy(0, dest, chip * 2 + 2 + core).start()

            @pl.when(dest < chip)
            def _():
                chain_copy(1, dest, chip * 2 - 2 + core).start()

    @pl.loop(0, chips)
    def _(dest):
        side_copy(dest).wait_send()

        @pl.when(dest != chip)
        def _():
            chain_copy(0, dest, chip * 2 + 1 - core).wait_send()


def seq_reduce(a, b, width, turned, which):
    size, rows, depth = a.shape
    chips = size // 2
    half = jnp.bfloat16
    return pl.pallas_call(
        functools.partial(reduce_kernel, chips, b.ndim == 2, turned),
        out_shape=jax.ShapeDtypeStruct((rows, width), jnp.float32),
        in_specs=[pl.BlockSpec(memory_space=pltpu.VMEM)] * 2,
        out_specs=pl.BlockSpec(memory_space=pltpu.VMEM),
        scratch_shapes=[
            pltpu.VMEM((chips, rows, width), half),
            pltpu.VMEM((chips, rows, width), half),
            pltpu.VMEM((chips, rows, width), half),
            pltpu.VMEM((2, chips, rows, width), half),
            pltpu.VMEM((rows, width), jnp.float32),
            pltpu.SemaphoreType.DMA((chips,)),
            pltpu.SemaphoreType.DMA((chips,)),
            pltpu.SemaphoreType.DMA((chips,)),
            pltpu.SemaphoreType.DMA((2, chips)),
        ],
        compiler_params=pltpu.CompilerParams(
            collective_id=which, has_side_effects=True, vmem_limit_bytes=56 * 2**20
        ),
        cost_estimate=pl.CostEstimate(
            flops=2 * size * rows * depth * width,
            bytes_accessed=40 * rows * width * size,
            transcendentals=0,
        ),
    )(a, b)


def swap_kernel(size, summed, x_ref, o_ref, landing, send_sem, recv_sem):
    me = lax.axis_index("seq")
    barrier = pltpu.get_barrier_semaphore()
    for shift in range(1, size):
        pl.semaphore_signal(barrier, inc=1, device_id={"seq": lax.rem(me + shift, size)})
    pl.semaphore_wait(barrier, size - 1)

    def copy(shift):
        peer = lax.rem(me + shift, size)
        return pltpu.make_async_remote_copy(
            src_ref=x_ref if summed else x_ref.at[peer],
            dst_ref=landing.at[me],
            send_sem=send_sem.at[shift],
            recv_sem=recv_sem.at[shift],
            device_id={"seq": peer},
        )

    for shift in range(1, size):
        copy(shift).start()
    landing[me] = x_ref[...] if summed else x_ref[me]
    for shift in range(1, size):
        copy(shift).wait()
    if summed:
        o_ref[...] = jnp.sum(landing[...], 0)
    else:
        o_ref[...] = landing[...]


def seq_swap(x, size, summed, which):
    piece = x.shape if summed else x.shape[1:]
    return pl.pallas_call(
        functools.partial(swap_kernel, size, summed),
        out_shape=jax.ShapeDtypeStruct(x.shape, x.dtype),
        in_specs=[pl.BlockSpec(memory_space=pltpu.VMEM)],
        out_specs=pl.BlockSpec(memory_space=pltpu.VMEM),
        scratch_shapes=[
            pltpu.VMEM((size, *piece), x.dtype),
            pltpu.SemaphoreType.DMA((size,)),
            pltpu.SemaphoreType.DMA((size,)),
        ],
        compiler_params=pltpu.CompilerParams(collective_id=which, has_side_effects=True),
    )(x)


def seq_sum(pair, size, which):
    both = jnp.concatenate(pair).reshape(-1, 128)
    return seq_swap(both, size, True, which).reshape(2, -1)


def total_kernel(
    size, split, x_ref, o_ref, first, second, final, send_one, recv_one, send_two, recv_two, send_three, recv_three
):
    me, mine = lax.axis_index("seq"), lax.axis_index("fsdp")
    part = x_ref.shape[1] // size
    barrier = pltpu.get_barrier_semaphore()
    for shift in range(1, size):
        pl.semaphore_signal(barrier, inc=1, device_id={"seq": lax.rem(me + shift, size)})
    for shift in range(1, split):
        pl.semaphore_signal(barrier, inc=1, device_id={"fsdp": lax.rem(mine + shift, split)})
    pl.semaphore_wait(barrier, size + split - 2)

    def columns(index):
        return pl.ds(pl.multiple_of(index * part, part), part)

    def scatter(shift):
        peer = lax.rem(me + shift, size)
        return pltpu.make_async_remote_copy(
            src_ref=x_ref.at[:, columns(peer)],
            dst_ref=first.at[me],
            send_sem=send_one.at[shift],
            recv_sem=recv_one.at[shift],
            device_id={"seq": peer},
        )

    def share(shift):
        return pltpu.make_async_remote_copy(
            src_ref=second.at[mine],
            dst_ref=second.at[mine],
            send_sem=send_two.at[shift],
            recv_sem=recv_two.at[shift],
            device_id={"fsdp": lax.rem(mine + shift, split)},
        )

    def collect(shift):
        return pltpu.make_async_remote_copy(
            src_ref=final.at[me],
            dst_ref=final.at[me],
            send_sem=send_three.at[shift],
            recv_sem=recv_three.at[shift],
            device_id={"seq": lax.rem(me + shift, size)},
        )

    for shift in range(1, size):
        scatter(shift).start()
    first[me] = x_ref[:, columns(me)]
    for shift in range(1, size):
        scatter(shift).wait_recv()
    second[mine] = jnp.sum(first[...], 0)
    for shift in range(1, split):
        share(shift).start()
    for shift in range(1, split):
        share(shift).wait_recv()
    final[me] = jnp.sum(second[...], 0)
    for shift in range(1, size):
        collect(shift).start()
    for shift in range(1, size):
        scatter(shift).wait_send()
    for shift in range(1, split):
        share(shift).wait_send()
    for shift in range(1, size):
        collect(shift).wait()
    for index in range(size):
        o_ref[:, index * part : (index + 1) * part] = final[index]


def total_sum(x, size, split, which):
    rows, width = x.shape
    part = width // size
    kind = pltpu.SemaphoreType.DMA
    return pl.pallas_call(
        functools.partial(total_kernel, size, split),
        out_shape=jax.ShapeDtypeStruct(x.shape, x.dtype),
        in_specs=[pl.BlockSpec(memory_space=pltpu.VMEM)],
        out_specs=pl.BlockSpec(memory_space=pltpu.VMEM),
        scratch_shapes=[
            pltpu.VMEM((size, rows, part), x.dtype),
            pltpu.VMEM((split, rows, part), x.dtype),
            pltpu.VMEM((size, rows, part), x.dtype),
            kind((size,)),
            kind((size,)),
            kind((split,)),
            kind((split,)),
            kind((size,)),
            kind((size,)),
        ],
        compiler_params=pltpu.CompilerParams(collective_id=which, has_side_effects=True),
    )(x)


def shards(
    tokens,
    norm_gains,
    w_query,
    w_key,
    w_value,
    w_out,
    w_router,
    w_gate,
    w_up,
    w_down,
    segment_ids,
    expert_ids,
    expert_slots,
    cotangent,
):
    half_type = jnp.bfloat16
    float_type = jnp.float32
    tok_rows = tokens.shape[0]
    model_width = tokens.shape[1]
    expert_total = w_router.shape[1]
    top_count = expert_ids.shape[1]
    head_size = HEAD_DIM
    local_width = w_query.shape[1]
    heads_local = local_width // head_size
    capacity = CAP
    seq_index = lax.axis_index("seq")
    column_start = seq_index * local_width
    experts_local = w_gate.shape[0]
    seq_size = lax.axis_size("seq")
    split = lax.axis_size("fsdp")
    groups = split // experts_local
    shard_index = lax.axis_index("fsdp")
    member = lax.rem(shard_index, experts_local)

    def pick(stack, index):
        return lax.dynamic_index_in_dim(stack, index, 0, keepdims=False)

    def to_owner(weight, dim):
        pieces = []
        for shift in range(split):
            dest = lax.rem(shard_index + shift, split)
            piece = pick(weight, lax.rem(dest, experts_local))
            if shift:
                links = [(one, (one + shift) % split) for one in range(split)]
                piece = lax.ppermute(piece, "fsdp", links)
            pieces.append(piece)
        order = lax.rem(shard_index - jnp.arange(split) + split, split)
        whole = jnp.stack(pieces)[order]
        if dim == 0:
            return whole.reshape(-1, whole.shape[2])
        return whole.transpose(1, 0, 2).reshape(whole.shape[1], -1)

    def to_shards(grad, dim):
        part = grad.shape[dim] // split
        shape = [experts_local, *grad.shape]
        shape[dim + 1] = part
        owned = jnp.zeros(shape, float_type)
        for shift in range(split):
            dest = lax.rem(shard_index + shift, split)
            piece = lax.dynamic_slice_in_dim(grad, dest * part, part, dim).astype(half_type)
            if shift:
                links = [(one, (one + shift) % split) for one in range(split)]
                piece = lax.ppermute(piece, "fsdp", links)
            expert = lax.rem(shard_index - shift + split, experts_local)
            piece = piece.astype(float_type)
            if groups > 1:
                piece = piece + pick(owned, expert)
            owned = lax.dynamic_update_index_in_dim(owned, piece, expert, 0)
        return owned

    def exchange(pieces, back):
        moved = [pieces[0]]
        for shift in range(1, experts_local):
            turn = experts_local - shift if back else shift
            links = [
                (one, one - one % experts_local + (one + turn) % experts_local)
                for one in range(split)
            ]
            moved.append(lax.ppermute(pieces[shift], "fsdp", links))
        return moved

    qkv_cols = lax.all_gather(
        jnp.concatenate([w_query, w_key, w_value], 1), "fsdp", axis=0, tiled=True
    )
    out_rows = lax.all_gather(w_out, "fsdp", axis=1, tiled=True)
    gate_full = to_owner(w_gate, 0)
    up_full = to_owner(w_up, 0)
    down_full = to_owner(w_down, 1)
    turned_ids = lax.rem(expert_ids - member + experts_local, experts_local)
    turned_ids = turned_ids + expert_ids - lax.rem(expert_ids, experts_local)
    places = jnp.where(
        expert_slots < capacity, turned_ids * capacity + expert_slots, -(10**6)
    )
    both_seq = lax.all_gather(
        jnp.concatenate([expert_ids, places], 1), "seq", axis=0, tiled=True
    )
    ids_seq = both_seq[:, :top_count]
    places_seq = both_seq[:, top_count:]
    cotangent_seq = seq_gather(cotangent, seq_size, 0)
    gain_rows = norm_gains.astype(float_type)
    gain_cols = lax.dynamic_slice_in_dim(gain_rows, column_start, local_width, 1)
    inputs = tokens.astype(float_type)
    inverse_first = inverse_rms(inputs)
    unit_first = inputs * inverse_first
    normed = (unit_first * gain_rows[0]).astype(half_type)
    normed_seq = seq_gather(normed, seq_size, 0)
    length = normed_seq.shape[0]
    raw = jnp.dot(normed_seq, qkv_cols, preferred_element_type=float_type)
    query_raw = raw[:, :local_width]
    key_raw = raw[:, local_width : 2 * local_width]
    value_heads = raw[:, 2 * local_width :].astype(half_type)
    square_sums = seq_sum(
        (jnp.sum(query_raw * query_raw, -1), jnp.sum(key_raw * key_raw, -1)), seq_size, 1
    )
    inverse_query = lax.rsqrt(square_sums[0] / model_width + EPSILON)[:, None]
    inverse_key = lax.rsqrt(square_sums[1] / model_width + EPSILON)[:, None]
    positions = jnp.arange(length, dtype=jnp.int32)
    cosine_table, sine_table = rope_tables(positions, head_size)
    unit_query = query_raw * inverse_query
    unit_key = key_raw * inverse_key
    query_heads = rotate(unit_query * gain_cols[2], cosine_table, sine_table, head_size).astype(
        half_type
    )
    key_heads = rotate(unit_key * gain_cols[3], cosine_table, sine_table, head_size).astype(
        half_type
    )
    block_rows = math.gcd(512, length)
    blocks = length // block_rows
    score_scale = head_size ** (-0.5)
    query_cube = query_heads.reshape(blocks, block_rows, heads_local, head_size)
    key_cube = key_heads.reshape(length, heads_local, head_size)
    value_cube = value_heads.reshape(length, heads_local, head_size)
    segment_blocks = segment_ids.reshape(blocks, block_rows)

    def block_scores(query_block, segment_block):
        scores = (
            jnp.einsum("qhd,khd->hqk", query_block, key_cube, preferred_element_type=float_type)
            * score_scale
        )
        visible = segment_block[:, None] == segment_ids[None, :]
        return jnp.where(visible[None], scores, MASKED)

    def attend(block_pair):
        query_block, segment_block = block_pair
        scores = block_scores(query_block, segment_block)
        row_peak = jnp.max(scores, -1, keepdims=True)
        exp_scores = jnp.exp(scores - row_peak)
        exp_total = jnp.sum(exp_scores, -1, keepdims=True)
        weights_soft = (exp_scores / exp_total).astype(half_type)
        mixed_block = jnp.einsum(
            "hqk,khd->qhd", weights_soft, value_cube, preferred_element_type=float_type
        )
        return (mixed_block.astype(half_type), (row_peak + jnp.log(exp_total))[..., 0])

    mixed_heads, log_sums = lax.map(attend, (query_cube, segment_blocks))
    attended_heads = mixed_heads.reshape(length, local_width)
    attended_blocks = attended_heads.reshape(seq_size, tok_rows, local_width)
    projected = seq_reduce(attended_blocks, out_rows, model_width, False, 2)
    residual = inputs + projected
    inverse_second = inverse_rms(residual)
    unit_second = residual * inverse_second
    routed = (unit_second * gain_rows[1]).astype(half_type)
    routed_seq = seq_gather(routed, seq_size, 0)
    slots = experts_local * capacity

    def gates_of(rows, ids):
        logits = jnp.dot(rows, w_router, preferred_element_type=float_type)
        chosen = (ids[:, :, None] == jnp.arange(expert_total, dtype=jnp.int32)).astype(float_type)
        picked = jnp.einsum("tke,te->tk", chosen, logits, precision=HIGHEST)
        return chosen, jax.nn.softmax(picked, axis=-1)

    chosen, gate_weights = gates_of(routed, expert_ids)
    gates_seq = gates_of(routed_seq, ids_seq)[1]
    mine = (places_seq - seq_index * slots).reshape(seq_size, tok_rows, top_count)
    hits = mine[:, :, :, None] == jnp.arange(slots, dtype=jnp.int32)
    onehot = jnp.any(hits, 2).astype(half_type)
    combine = jnp.sum(
        jnp.where(hits, gates_seq.reshape(seq_size, tok_rows, top_count)[..., None], 0.0), 2
    )

    def dispatch(rows):
        cube = rows.reshape(seq_size, tok_rows, model_width)
        return [
            jnp.einsum(
                "btc,btd->bcd",
                onehot[:, :, index * capacity : (index + 1) * capacity],
                cube,
                preferred_element_type=float_type,
            )
            .astype(half_type)
            .reshape(seq_size * capacity, model_width)
            for index in range(experts_local)
        ]

    def undispatch(pieces):
        cubes = [piece.reshape(seq_size, capacity, model_width) for piece in pieces]
        return jnp.concatenate(cubes, 1)

    def parts_of(rows):
        depth = rows.shape[0] // experts_local
        return [rows[index * depth : (index + 1) * depth] for index in range(experts_local)]

    expert_rows = jnp.concatenate(exchange(dispatch(routed_seq), False))
    upstream_rows = jnp.concatenate(exchange(dispatch(cotangent_seq), False))
    slot_gates = jnp.sum(combine, 1).reshape(seq_size, experts_local, capacity).transpose(1, 0, 2)
    row_gates = jnp.concatenate(exchange(list(slot_gates.reshape(experts_local, -1)), False))
    gate_pre = jnp.dot(expert_rows, gate_full, preferred_element_type=float_type)
    up_pre = jnp.dot(expert_rows, up_full, preferred_element_type=float_type)
    gate_sigmoid = jax.nn.sigmoid(gate_pre)
    hidden = (gate_pre * gate_sigmoid * up_pre).astype(half_type)
    returned = jnp.dot(hidden, down_full, preferred_element_type=float_type).astype(half_type)
    row_dots = jnp.sum(returned.astype(float_type) * upstream_rows.astype(float_type), -1)
    slot_dots = jnp.stack(exchange(parts_of(row_dots), True))
    slot_dots = slot_dots.reshape(experts_local, seq_size, capacity).transpose(1, 0, 2)
    slot_dots = slot_dots.reshape(seq_size, 1, slots)
    padded = -(-slots // 128) * 128
    slot_dots = jnp.pad(slot_dots, ((0, 0), (0, 7), (0, padded - slots)))
    slot_dots = seq_swap(slot_dots, seq_size, False, 3)[:, 0, :slots].reshape(-1)
    at_place = places[:, :, None] == jnp.arange(expert_total * capacity, dtype=jnp.int32)
    gate_grad = jnp.sum(jnp.where(at_place, slot_dots, 0.0), -1)
    incoming = undispatch(exchange(parts_of(returned), True))
    mixture = seq_reduce(combine.astype(half_type), incoming, model_width, False, 4)
    output = (residual + mixture).astype(half_type)
    upstream = cotangent.astype(float_type)
    slot_grads = (row_gates[:, None] * upstream_rows.astype(float_type)).astype(half_type)
    hidden_grad = jnp.einsum(
        "rd,fd->rf", slot_grads, down_full, preferred_element_type=float_type
    )
    gate_pre_grad = (
        hidden_grad * up_pre * gate_sigmoid * (1.0 + gate_pre * (1.0 - gate_sigmoid))
    ).astype(half_type)
    up_pre_grad = (hidden_grad * gate_pre * gate_sigmoid).astype(half_type)
    rows_grad = jnp.einsum("rf,df->rd", gate_pre_grad, gate_full, preferred_element_type=float_type)
    rows_grad = (
        rows_grad
        + jnp.einsum("rf,df->rd", up_pre_grad, up_full, preferred_element_type=float_type)
    ).astype(half_type)
    sent_back = undispatch(exchange(parts_of(rows_grad), True))
    routed_grad = seq_reduce(onehot, sent_back, model_width, False, 4)
    grad_down_full = jnp.einsum("rf,rd->fd", hidden, slot_grads, preferred_element_type=float_type)
    grad_gate_full = jnp.einsum(
        "rd,rf->df", expert_rows, gate_pre_grad, preferred_element_type=float_type
    )
    grad_up_full = jnp.einsum("rd,rf->df", expert_rows, up_pre_grad, preferred_element_type=float_type)
    mean_grad = jnp.sum(gate_weights * gate_grad, -1, keepdims=True)
    picked_grad = gate_weights * (gate_grad - mean_grad)
    logit_grad = jnp.einsum("tke,tk->te", chosen, picked_grad, precision=HIGHEST).astype(half_type)
    routed_grad = routed_grad + jnp.einsum(
        "te,de->td", logit_grad, w_router, preferred_element_type=float_type
    )
    grad_router_local = jnp.einsum(
        "td,te->ed", routed, logit_grad, preferred_element_type=float_type
    )
    gain_second_grad = jnp.sum(routed_grad * unit_second, axis=0)
    residual_grad = upstream + norm_back(routed_grad * gain_rows[1], unit_second, inverse_second)
    out_grad = residual_grad.astype(half_type)
    out_grad_seq = seq_gather(out_grad, seq_size, 0)
    grad_out_local = jnp.einsum(
        "th,td->hd", attended_heads, out_grad_seq, preferred_element_type=float_type
    )
    attended_grad = jnp.einsum(
        "td,hd->th", out_grad_seq, out_rows, preferred_element_type=float_type
    ).astype(half_type)
    grad_cube = attended_grad.reshape(blocks, block_rows, heads_local, head_size)

    def attend_back(running, pieces):
        key_acc, value_acc = running
        query_block, segment_block, grad_block, log_block = pieces
        scores = block_scores(query_block, segment_block)
        soft_values = jnp.exp(scores - log_block[..., None])
        prob_grad = jnp.einsum(
            "qhd,khd->hqk", grad_block, value_cube, preferred_element_type=float_type
        )
        center = jnp.sum(soft_values * prob_grad, -1, keepdims=True)
        score_grad = (soft_values * (prob_grad - center)).astype(half_type)
        query_grad = (
            jnp.einsum("hqk,khd->qhd", score_grad, key_cube, preferred_element_type=float_type)
            * score_scale
        )
        key_acc = (
            key_acc
            + jnp.einsum("hqk,qhd->khd", score_grad, query_block, preferred_element_type=float_type)
            * score_scale
        )
        value_acc = value_acc + jnp.einsum(
            "hqk,qhd->khd",
            soft_values.astype(half_type),
            grad_block,
            preferred_element_type=float_type,
        )
        return ((key_acc, value_acc), query_grad.astype(half_type))

    empty_acc = jnp.zeros((length, heads_local, head_size), float_type)
    (key_acc, value_acc), query_grads = lax.scan(
        attend_back, (empty_acc, empty_acc), (query_cube, segment_blocks, grad_cube, log_sums)
    )
    query_back = query_grads.reshape(length, local_width)
    key_back = key_acc.reshape(length, local_width).astype(half_type)
    value_back = value_acc.reshape(length, local_width).astype(half_type)
    query_unit_grad = rotate(query_back.astype(float_type), cosine_table, -sine_table, head_size)
    key_unit_grad = rotate(key_back.astype(float_type), cosine_table, -sine_table, head_size)
    gain_query_grad = jnp.sum(query_unit_grad * unit_query, axis=0)
    gain_key_grad = jnp.sum(key_unit_grad * unit_key, axis=0)
    query_scaled = query_unit_grad * gain_cols[2]
    key_scaled = key_unit_grad * gain_cols[3]
    centers = seq_sum(
        (jnp.sum(query_scaled * unit_query, -1), jnp.sum(key_scaled * unit_key, -1)), seq_size, 1
    )
    query_raw_grad = (
        inverse_query * (query_scaled - unit_query * (centers[0] / model_width)[:, None])
    ).astype(half_type)
    key_raw_grad = (
        inverse_key * (key_scaled - unit_key * (centers[1] / model_width)[:, None])
    ).astype(half_type)
    raw_grads = jnp.concatenate([query_raw_grad, key_raw_grad, value_back], 1)
    raw_blocks = raw_grads.reshape(seq_size, tok_rows, 3 * local_width)
    normed_grad = seq_reduce(raw_blocks, qkv_cols, model_width, True, 5)
    grad_qkv_local = jnp.einsum("td,th->dh", normed_seq, raw_grads, preferred_element_type=float_type)
    gain_first_grad = jnp.sum(normed_grad * unit_first, axis=0)
    input_grad = residual_grad + norm_back(normed_grad * gain_rows[0], unit_first, inverse_first)
    zero_row = jnp.zeros((model_width,), float_type)
    gain_query_full = lax.dynamic_update_slice_in_dim(zero_row, gain_query_grad, column_start, 0)
    gain_key_full = lax.dynamic_update_slice_in_dim(zero_row, gain_key_grad, column_start, 0)
    gain_grads = jnp.stack([gain_first_grad, gain_second_grad, gain_query_full, gain_key_full])
    small = jnp.concatenate([gain_grads, jnp.zeros_like(gain_grads), grad_router_local])
    small = total_sum(small, seq_size, split, 6)
    gain_sums, router_grad = small[:4], small[8:].T
    qkv_owned = lax.psum_scatter(
        grad_qkv_local.astype(half_type), "fsdp", scatter_dimension=0, tiled=True
    ).astype(float_type)
    out_owned = lax.psum_scatter(
        grad_out_local.astype(half_type), "fsdp", scatter_dimension=1, tiled=True
    ).astype(float_type)
    return (
        output,
        input_grad,
        gain_sums,
        qkv_owned[:, :local_width],
        qkv_owned[:, local_width : 2 * local_width],
        qkv_owned[:, 2 * local_width :],
        out_owned,
        router_grad,
        to_shards(grad_gate_full, 0),
        to_shards(grad_up_full, 0),
        to_shards(grad_down_full, 1),
    )


def solution(mesh):
    in_specs = (
        P(("fsdp", "seq"), None),
        P(),
        P("fsdp", "seq"),
        P("fsdp", "seq"),
        P("fsdp", "seq"),
        P("seq", "fsdp"),
        P(),
        P("seq", "fsdp", None),
        P("seq", "fsdp", None),
        P("seq", None, "fsdp"),
        P("fsdp"),
        P(("fsdp", "seq"), None),
        P(("fsdp", "seq"), None),
        P(("fsdp", "seq"), None),
    )
    out_specs = (
        P(("fsdp", "seq"), None),
        P(("fsdp", "seq"), None),
        P(),
        P("fsdp", "seq"),
        P("fsdp", "seq"),
        P("fsdp", "seq"),
        P("seq", "fsdp"),
        P(),
        P("seq", "fsdp", None),
        P("seq", "fsdp", None),
        P("seq", None, "fsdp"),
    )
    return jax.shard_map(shards, mesh=mesh, in_specs=in_specs, out_specs=out_specs, check_vma=False)
```

```python
import functools
import math

import jax
import jax.numpy as jnp
from jax import lax
from jax.experimental import pallas as pl
from jax.experimental.pallas import tpu as pltpu
from jax.sharding import PartitionSpec as P

HEAD_DIM = 128
CAP = 40


EPSILON = 1e-06
THETA = 10000.0
MASKED = -1e30
HIGHEST = lax.Precision.HIGHEST


def rope_tables(positions, head_size):
    half_dim = head_size // 2
    frequency = THETA ** (-jnp.arange(half_dim, dtype=jnp.float32) / half_dim)
    angles = positions.astype(jnp.float32)[:, None] * frequency[None, :]
    return (jnp.cos(angles), jnp.sin(angles))


def rotate(values_in, cosine_table, sine_table, head_size):
    row_count = values_in.shape[0]
    pieces = values_in.reshape(row_count, -1, head_size)
    half_dim = head_size // 2
    former = pieces[..., :half_dim]
    latter = pieces[..., half_dim:]
    cosine_wide = cosine_table[:, None, :]
    sine_wide = sine_table[:, None, :]
    turned = jnp.concatenate(
        [former * cosine_wide - latter * sine_wide, latter * cosine_wide + former * sine_wide], -1
    )
    return turned.reshape(row_count, -1)


def inverse_rms(values_in):
    return lax.rsqrt(jnp.mean(values_in * values_in, -1, keepdims=True) + EPSILON)


def norm_back(grad_unit, unit_values, inverse):
    return inverse * (
        grad_unit - unit_values * jnp.mean(grad_unit * unit_values, -1, keepdims=True)
    )


def greet_chain(chip, core, chips):
    barrier = pltpu.get_barrier_semaphore()

    def greet(target):
        pl.semaphore_signal(barrier, inc=1, device_id={"seq": target})

    greet(chip * 2 + 1 - core)

    @pl.when(chip < chips - 1)
    def _():
        greet(chip * 2 + 2 + core)

    @pl.when(chip > 0)
    def _():
        greet(chip * 2 - 2 + core)

    inner = jnp.where(chip < chips - 1, 1, 0) + jnp.where(chip > 0, 1, 0)
    pl.semaphore_wait(barrier, 1 + inner)


class ChainGather:
    def __init__(self, chips, x_ref, out_ref, local_sem, sends, arrivals):
        self.chips, self.x_ref, self.out_ref = chips, x_ref, out_ref
        self.local_sem, self.sends, self.arrivals = local_sem, sends, arrivals
        me = lax.axis_index("seq")
        self.chip, self.core = me // 2, lax.rem(me, 2)
        self.rows = x_ref.shape[0]

    def block(self, source, core):
        start = pl.multiple_of((source * 2 + core) * self.rows, self.rows)
        return self.out_ref.at[pl.ds(start, self.rows)]

    def hop(self, source, ref, target, way, lane):
        return pltpu.make_async_remote_copy(
            src_ref=ref,
            dst_ref=self.block(source, self.core),
            send_sem=self.sends.at[way, source],
            recv_sem=self.arrivals.at[lane, source],
            device_id={"seq": target},
        )

    def upward(self, source, ref):
        return self.hop(source, ref, self.chip * 2 + 2 + self.core, 0, 0)

    def downward(self, source, ref):
        return self.hop(source, ref, self.chip * 2 - 2 + self.core, 1, 0)

    def sideways(self, source, ref):
        return self.hop(source, ref, self.chip * 2 + 1 - self.core, 2, 1)

    def own(self):
        return pltpu.make_async_copy(
            self.x_ref, self.block(self.chip, self.core), self.local_sem
        )

    def start(self):
        @pl.when(self.chip < self.chips - 1)
        def _():
            self.upward(self.chip, self.x_ref).start()

        @pl.when(self.chip > 0)
        def _():
            self.downward(self.chip, self.x_ref).start()

        self.sideways(self.chip, self.x_ref).start()
        self.own().start()

    def step(self, distance):
        below, above = self.chip - distance, self.chip + distance

        @pl.when(below >= 0)
        def _():
            landed = self.block(below, self.core)
            self.upward(below, landed).wait_recv()

            @pl.when(self.chip < self.chips - 1)
            def _():
                self.upward(below, landed).start()

            self.sideways(below, landed).start()

        @pl.when(above < self.chips)
        def _():
            landed = self.block(above, self.core)
            self.downward(above, landed).wait_recv()

            @pl.when(self.chip > 0)
            def _():
                self.downward(above, landed).start()

            self.sideways(above, landed).start()

    def steps(self):
        for distance in range(1, self.chips):
            self.step(distance)

    def landed(self):
        self.own().wait()
        for source in range(self.chips):
            self.sideways(source, self.block(source, self.core)).wait_recv()

    def sent(self):
        for source in range(self.chips):
            ref = self.block(source, self.core)
            self.sideways(source, ref).wait_send()

            @pl.when((self.chip < self.chips - 1) & (source <= self.chip))
            def _():
                self.upward(source, ref).wait_send()

            @pl.when((self.chip > 0) & (source >= self.chip))
            def _():
                self.downward(source, ref).wait_send()


class ChainReduce:
    def __init__(self, chips, rows, width, buffers):
        (
            self.side_out,
            self.side_in,
            self.chain_out,
            self.chain_in,
            self.total,
            self.side_send,
            self.side_recv,
            self.chain_send,
            self.chain_recv,
        ) = buffers
        self.chips = chips
        me = lax.axis_index("seq")
        self.chip, self.core = me // 2, lax.rem(me, 2)

    @staticmethod
    def scratch(chips, rows, width):
        half = jnp.bfloat16
        return [
            pltpu.VMEM((chips, rows, width), half),
            pltpu.VMEM((chips, rows, width), half),
            pltpu.VMEM((chips, rows, width), half),
            pltpu.VMEM((2, chips, rows, width), half),
            pltpu.VMEM((rows, width), jnp.float32),
            pltpu.SemaphoreType.DMA((chips,)),
            pltpu.SemaphoreType.DMA((chips,)),
            pltpu.SemaphoreType.DMA((chips,)),
            pltpu.SemaphoreType.DMA((2, chips)),
        ]

    def side_copy(self, dest):
        return pltpu.make_async_remote_copy(
            src_ref=self.side_out.at[dest],
            dst_ref=self.side_in.at[dest],
            send_sem=self.side_send.at[dest],
            recv_sem=self.side_recv.at[dest],
            device_id={"seq": self.chip * 2 + 1 - self.core},
        )

    def chain_copy(self, way, dest, target):
        return pltpu.make_async_remote_copy(
            src_ref=self.chain_out.at[dest],
            dst_ref=self.chain_in.at[way, dest],
            send_sem=self.chain_send.at[dest],
            recv_sem=self.chain_recv.at[way, dest],
            device_id={"seq": target},
        )

    def place(self, index):
        distance = self.chips - 1 - index // 2
        dest = self.chip + (1 - 2 * lax.rem(index, 2)) * distance
        return dest, (dest >= 0) & (dest < self.chips)

    def run(self, product):
        chips, chip, core, total = self.chips, self.chip, self.core, self.total
        sibling = chip * 2 + 1 - core

        @pl.loop(0, 2 * chips - 1)
        def _(index):
            dest, inside = self.place(index)

            @pl.when(inside)
            def _():
                def store(cols, part):
                    self.side_out[dest, :, cols] = part.astype(self.side_out.dtype)

                product(dest * 2 + 1 - core, store)
                self.side_copy(dest).start()

        @pl.loop(0, 2 * chips - 1)
        def _(index):
            dest, inside = self.place(index)

            @pl.when(inside)
            def _():
                def store(cols, part):
                    total[:, cols] = part

                product(dest * 2 + core, store)
                self.side_copy(dest).wait_recv()
                total[...] += self.side_in[dest].astype(jnp.float32)

                @pl.when((dest >= chip) & (chip > 0))
                def _():
                    self.chain_copy(0, dest, sibling).wait_recv()
                    total[...] += self.chain_in[0, dest].astype(jnp.float32)

                @pl.when((dest <= chip) & (chip < chips - 1))
                def _():
                    self.chain_copy(1, dest, sibling).wait_recv()
                    total[...] += self.chain_in[1, dest].astype(jnp.float32)

                @pl.when(dest != chip)
                def _():
                    self.chain_out[dest] = total[...].astype(self.chain_out.dtype)

                @pl.when(dest > chip)
                def _():
                    self.chain_copy(0, dest, chip * 2 + 2 + core).start()

                @pl.when(dest < chip)
                def _():
                    self.chain_copy(1, dest, chip * 2 - 2 + core).start()

    def sent(self):
        sibling = self.chip * 2 + 1 - self.core

        @pl.loop(0, self.chips)
        def _(dest):
            self.side_copy(dest).wait_send()

            @pl.when(dest != self.chip)
            def _():
                self.chain_copy(0, dest, sibling).wait_send()


def gather_kernel(chips, x_ref, out_ref, local_sem, sends, arrivals):
    gather = ChainGather(chips, x_ref, out_ref, local_sem, sends, arrivals)
    greet_chain(gather.chip, gather.core, chips)
    gather.start()
    gather.steps()
    gather.landed()
    gather.sent()


def seq_gather(x, size, which):
    chips = size // 2
    rows, width = x.shape
    return pl.pallas_call(
        functools.partial(gather_kernel, chips),
        out_shape=jax.ShapeDtypeStruct((size * rows, width), x.dtype),
        in_specs=[pl.BlockSpec(memory_space=pl.ANY)],
        out_specs=pl.BlockSpec(memory_space=pl.ANY),
        scratch_shapes=[
            pltpu.SemaphoreType.DMA,
            pltpu.SemaphoreType.DMA((3, chips)),
            pltpu.SemaphoreType.DMA((2, chips)),
        ],
        compiler_params=pltpu.CompilerParams(collective_id=which, has_side_effects=True),
        cost_estimate=pl.CostEstimate(
            flops=0, bytes_accessed=40 * x.size * x.dtype.itemsize * chips, transcendentals=0
        ),
    )(x)


def reduce_kernel(chips, shared, turned, a_ref, b_ref, o_ref, *buffers):
    rows, width = o_ref.shape
    step_cols = min(512, width)
    reduce = ChainReduce(chips, rows, width, buffers)
    greet_chain(reduce.chip, reduce.core, chips)

    def product(block, store):
        left = a_ref[block]

        @pl.loop(0, width // step_cols)
        def _(index):
            cols = pl.ds(pl.multiple_of(index * step_cols, step_cols), step_cols)
            right_ref = b_ref if shared else b_ref.at[block]
            if turned:
                part = lax.dot_general(
                    left,
                    right_ref[cols, :],
                    (((1,), (1,)), ((), ())),
                    preferred_element_type=jnp.float32,
                )
            else:
                part = jnp.dot(left, right_ref[:, cols], preferred_element_type=jnp.float32)
            store(cols, part)

    reduce.run(product)
    o_ref[...] = reduce.total[...]
    reduce.sent()


def seq_reduce(a, b, width, turned, which):
    size, rows, depth = a.shape
    chips = size // 2
    half = jnp.bfloat16
    return pl.pallas_call(
        functools.partial(reduce_kernel, chips, b.ndim == 2, turned),
        out_shape=jax.ShapeDtypeStruct((rows, width), jnp.float32),
        in_specs=[pl.BlockSpec(memory_space=pltpu.VMEM)] * 2,
        out_specs=pl.BlockSpec(memory_space=pltpu.VMEM),
        scratch_shapes=ChainReduce.scratch(chips, rows, width),
        compiler_params=pltpu.CompilerParams(
            collective_id=which, has_side_effects=True, vmem_limit_bytes=56 * 2**20
        ),
        cost_estimate=pl.CostEstimate(
            flops=2 * size * rows * depth * width,
            bytes_accessed=40 * rows * width * size,
            transcendentals=0,
        ),
    )(a, b)


def swap_kernel(size, summed, x_ref, o_ref, landing, send_sem, recv_sem):
    me = lax.axis_index("seq")
    barrier = pltpu.get_barrier_semaphore()
    for shift in range(1, size):
        pl.semaphore_signal(barrier, inc=1, device_id={"seq": lax.rem(me + shift, size)})
    pl.semaphore_wait(barrier, size - 1)

    def copy(shift):
        peer = lax.rem(me + shift, size)
        return pltpu.make_async_remote_copy(
            src_ref=x_ref if summed else x_ref.at[peer],
            dst_ref=landing.at[me],
            send_sem=send_sem.at[shift],
            recv_sem=recv_sem.at[shift],
            device_id={"seq": peer},
        )

    for shift in range(1, size):
        copy(shift).start()
    landing[me] = x_ref[...] if summed else x_ref[me]
    for shift in range(1, size):
        copy(shift).wait()
    if summed:
        o_ref[...] = jnp.sum(landing[...], 0)
    else:
        o_ref[...] = landing[...]


def seq_swap(x, size, summed, which):
    piece = x.shape if summed else x.shape[1:]
    return pl.pallas_call(
        functools.partial(swap_kernel, size, summed),
        out_shape=jax.ShapeDtypeStruct(x.shape, x.dtype),
        in_specs=[pl.BlockSpec(memory_space=pltpu.VMEM)],
        out_specs=pl.BlockSpec(memory_space=pltpu.VMEM),
        scratch_shapes=[
            pltpu.VMEM((size, *piece), x.dtype),
            pltpu.SemaphoreType.DMA((size,)),
            pltpu.SemaphoreType.DMA((size,)),
        ],
        compiler_params=pltpu.CompilerParams(collective_id=which, has_side_effects=True),
    )(x)


def seq_sum(pair, size, which):
    both = jnp.concatenate(pair).reshape(-1, 128)
    return seq_swap(both, size, True, which).reshape(2, -1)


def total_kernel(
    size, split, x_ref, o_ref, first, second, final, send_one, recv_one, send_two, recv_two, send_three, recv_three
):
    me, mine = lax.axis_index("seq"), lax.axis_index("fsdp")
    part = x_ref.shape[1] // size
    barrier = pltpu.get_barrier_semaphore()
    for shift in range(1, size):
        pl.semaphore_signal(barrier, inc=1, device_id={"seq": lax.rem(me + shift, size)})
    for shift in range(1, split):
        pl.semaphore_signal(barrier, inc=1, device_id={"fsdp": lax.rem(mine + shift, split)})
    pl.semaphore_wait(barrier, size + split - 2)

    def columns(index):
        return pl.ds(pl.multiple_of(index * part, part), part)

    def scatter(shift):
        peer = lax.rem(me + shift, size)
        return pltpu.make_async_remote_copy(
            src_ref=x_ref.at[:, columns(peer)],
            dst_ref=first.at[me],
            send_sem=send_one.at[shift],
            recv_sem=recv_one.at[shift],
            device_id={"seq": peer},
        )

    def share(shift):
        return pltpu.make_async_remote_copy(
            src_ref=second.at[mine],
            dst_ref=second.at[mine],
            send_sem=send_two.at[shift],
            recv_sem=recv_two.at[shift],
            device_id={"fsdp": lax.rem(mine + shift, split)},
        )

    def collect(shift):
        return pltpu.make_async_remote_copy(
            src_ref=final.at[me],
            dst_ref=final.at[me],
            send_sem=send_three.at[shift],
            recv_sem=recv_three.at[shift],
            device_id={"seq": lax.rem(me + shift, size)},
        )

    for shift in range(1, size):
        scatter(shift).start()
    first[me] = x_ref[:, columns(me)]
    for shift in range(1, size):
        scatter(shift).wait_recv()
    second[mine] = jnp.sum(first[...], 0)
    for shift in range(1, split):
        share(shift).start()
    for shift in range(1, split):
        share(shift).wait_recv()
    final[me] = jnp.sum(second[...], 0)
    for shift in range(1, size):
        collect(shift).start()
    for shift in range(1, size):
        scatter(shift).wait_send()
    for shift in range(1, split):
        share(shift).wait_send()
    for shift in range(1, size):
        collect(shift).wait()
    for index in range(size):
        o_ref[:, index * part : (index + 1) * part] = final[index]


def total_sum(x, size, split, which):
    rows, width = x.shape
    part = width // size
    kind = pltpu.SemaphoreType.DMA
    return pl.pallas_call(
        functools.partial(total_kernel, size, split),
        out_shape=jax.ShapeDtypeStruct(x.shape, x.dtype),
        in_specs=[pl.BlockSpec(memory_space=pltpu.VMEM)],
        out_specs=pl.BlockSpec(memory_space=pltpu.VMEM),
        scratch_shapes=[
            pltpu.VMEM((size, rows, part), x.dtype),
            pltpu.VMEM((split, rows, part), x.dtype),
            pltpu.VMEM((size, rows, part), x.dtype),
            kind((size,)),
            kind((size,)),
            kind((split,)),
            kind((split,)),
            kind((size,)),
            kind((size,)),
        ],
        compiler_params=pltpu.CompilerParams(collective_id=which, has_side_effects=True),
    )(x)

def greet_all(size, split):
    me, mine = lax.axis_index("seq"), lax.axis_index("fsdp")
    barrier = pltpu.get_barrier_semaphore()
    for shift in range(1, size):
        pl.semaphore_signal(barrier, inc=1, device_id={"seq": lax.rem(me + shift, size)})
    for shift in range(1, split):
        pl.semaphore_signal(barrier, inc=1, device_id={"fsdp": lax.rem(mine + shift, split)})
    pl.semaphore_wait(barrier, size + split - 2)


def turned_halves(head):
    return pltpu.roll(head, head.shape[-1] // 2, 1)


def row_sums(values, pick):
    return lax.dot_general(
        pick, values, (((1,), (1,)), ((), ())), precision=HIGHEST, preferred_element_type=jnp.float32
    )


def column_of(row_form, pick):
    return lax.dot_general(
        row_form, pick, (((0,), (0,)), ((), ())), precision=HIGHEST, preferred_element_type=jnp.float32
    )


def front_kernel(
    sizes,
    tokens_ref,
    gains_ref,
    gain_cols_ref,
    cos_ref,
    sin_ref,
    seg_col_ref,
    seg_row_ref,
    cotangent_ref,
    wq_ref,
    wk_ref,
    wv_ref,
    wo_ref,
    w_gate_ref,
    w_up_ref,
    w_down_ref,
    choice_ref,
    normed_out,
    qkv_out,
    rows_out,
    q_ref,
    k_ref,
    v_ref,
    unit_ref,
    sums_ref,
    log_ref,
    attended_ref,
    residual_ref,
    routed_out,
    cotangent_out,
    gate_full,
    up_full,
    down_full,
    choices,
    normed,
    qkv,
    rows_full,
    routed_own,
    raw,
    sums_own,
    sums_in,
    gather_local,
    gather_send,
    gather_recv,
    sums_send,
    sums_recv,
    choice_send,
    choice_recv,
    shard_local,
    shard_send,
    shard_recv,
    expert_local,
    expert_send,
    expert_recv,
    out_sem,
    *reduce_buffers,
):
    size, split, chips, experts_local = sizes
    f32, half = jnp.float32, jnp.bfloat16
    me, mine = lax.axis_index("seq"), lax.axis_index("fsdp")
    tok_rows, model_width = tokens_ref.shape
    length, local_width = q_ref.shape
    part = model_width // split
    head = HEAD_DIM
    heads = local_width // head

    inputs = tokens_ref[...].astype(f32)
    inverse = lax.rsqrt(jnp.mean(inputs * inputs, -1, keepdims=True) + EPSILON)
    own_rows = pl.ds(pl.multiple_of(me * tok_rows, tok_rows), tok_rows)
    routed_own[...] = (inputs * inverse * gains_ref[0:1, :]).astype(half)
    greet_all(size, split)

    def gather(index, x_ref, out_ref):
        return ChainGather(
            chips,
            x_ref,
            out_ref,
            gather_local.at[index],
            gather_send.at[index],
            gather_recv.at[index],
        )

    first = gather(0, routed_own, normed)
    first.start()

    def choice_copy(shift):
        return pltpu.make_async_remote_copy(
            src_ref=choice_ref,
            dst_ref=choices.at[me],
            send_sem=choice_send.at[shift],
            recv_sem=choice_recv.at[shift],
            device_id={"seq": lax.rem(me + shift, size)},
        )

    own_part = pl.ds(pl.multiple_of(mine * part, part), part)
    shard_pairs = (
        (wq_ref, qkv.at[0, own_part]),
        (wk_ref, qkv.at[1, own_part]),
        (wv_ref, qkv.at[2, own_part]),
        (wo_ref, rows_full.at[mine]),
    )

    def shard_copy(index, shift):
        source, target = shard_pairs[index]
        return pltpu.make_async_remote_copy(
            src_ref=source,
            dst_ref=target,
            send_sem=shard_send.at[index, shift],
            recv_sem=shard_recv.at[index, shift],
            device_id={"fsdp": lax.rem(mine + shift, split)},
        )

    def shard_own(index):
        source, target = shard_pairs[index]
        return pltpu.make_async_copy(source, target, shard_local.at[index])

    for index in range(4):
        for shift in range(1, split):
            shard_copy(index, shift).start()
        shard_own(index).start()

    def expert_pair(index, dest):
        expert = lax.rem(dest, experts_local)
        if index == 2:
            return w_down_ref.at[expert], down_full.at[:, own_part]
        source, target = ((w_gate_ref, gate_full), (w_up_ref, up_full))[index]
        return source.at[expert], target.at[own_part]

    def expert_copy(index, shift):
        dest = lax.rem(mine + shift, split)
        source, target = expert_pair(index, dest)
        return pltpu.make_async_remote_copy(
            src_ref=source,
            dst_ref=target,
            send_sem=expert_send.at[index, shift],
            recv_sem=expert_recv.at[index, shift],
            device_id={"fsdp": dest},
        )

    def expert_own(index):
        source, target = expert_pair(index, mine)
        return pltpu.make_async_copy(source, target, expert_local.at[index])

    first.steps()
    for index in range(4):
        shard_own(index).wait()
        for shift in range(1, split):
            shard_copy(index, shift).wait_recv()
    for index in range(3):
        for shift in range(1, split):
            expert_copy(index, shift).start()
        expert_own(index).start()
    first.landed()
    for shift in range(1, size):
        choice_copy(shift).start()
    choices[me] = choice_ref[...]
    second = gather(1, cotangent_ref, cotangent_out)
    second.start()
    keeps = [
        pltpu.make_async_copy(normed, normed_out, out_sem.at[0]),
        pltpu.make_async_copy(qkv, qkv_out, out_sem.at[1]),
        pltpu.make_async_copy(rows_full, rows_out, out_sem.at[2]),
    ]
    for keep in keeps:
        keep.start()

    block = min(512, length)
    lanes = lax.broadcasted_iota(jnp.int32, (8, local_width), 0)
    first_row, second_row = (lanes == 0).astype(f32), (lanes == 1).astype(f32)

    @pl.loop(0, length // block)
    def _(step):
        rows = pl.ds(pl.multiple_of(step * block, block), block)
        left = normed[rows, :]
        query = jnp.dot(left, qkv[0], preferred_element_type=f32)
        raw[0, rows, :] = query
        keys = jnp.dot(left, qkv[1], preferred_element_type=f32)
        raw[1, rows, :] = keys
        sums_own[:, rows] = row_sums(query * query, first_row) + row_sums(keys * keys, second_row)
        v_ref[rows, :] = jnp.dot(left, qkv[2], preferred_element_type=f32).astype(half)

    def sums_copy(shift):
        return pltpu.make_async_remote_copy(
            src_ref=sums_own,
            dst_ref=sums_in.at[me],
            send_sem=sums_send.at[shift],
            recv_sem=sums_recv.at[shift],
            device_id={"seq": lax.rem(me + shift, size)},
        )

    for shift in range(1, size):
        sums_copy(shift).start()
    sums_in[me] = sums_own[...]
    for shift in range(1, size):
        sums_copy(shift).wait()
    sums_ref[...] = jnp.sum(sums_in[...], 0)

    @pl.loop(0, length // block)
    def _(step):
        rows = pl.ds(pl.multiple_of(step * block, block), block)
        square_sums = sums_ref[:, rows]
        for index, pick, target in ((0, first_row, q_ref), (1, second_row, k_ref)):
            scale = lax.rsqrt(column_of(square_sums, pick) / model_width + EPSILON)
            unit = raw[index, rows, :] * scale
            unit_ref[index, rows, :] = unit
            scaled = unit * gain_cols_ref[2 + index : 3 + index, :]
            for number in range(heads):
                cols = slice(number * head, (number + 1) * head)
                piece = scaled[:, cols]
                target[rows, cols] = (
                    piece * cos_ref[rows, :] + turned_halves(piece) * sin_ref[rows, :]
                ).astype(half)

    second.step(1)

    wide = min(256, length)
    for number in range(heads):
        cols = slice(number * head, (number + 1) * head)

        @pl.loop(0, length // wide)
        def _(step):
            rows = pl.ds(pl.multiple_of(step * wide, wide), wide)
            scores = lax.dot_general(
                q_ref[rows, cols],
                k_ref[:, cols],
                (((1,), (1,)), ((), ())),
                preferred_element_type=f32,
            )
            scores = scores * (head**-0.5)
            scores = jnp.where(seg_col_ref[rows, :] == seg_row_ref[...], scores, MASKED)
            peak = jnp.max(scores, -1, keepdims=True)
            grown = jnp.exp(scores - peak)
            weight = jnp.sum(grown, -1, keepdims=True)
            probs = (grown * (1.0 / weight)).astype(half)
            attended_ref[rows, cols] = jnp.dot(
                probs, v_ref[:, cols], preferred_element_type=f32
            ).astype(half)
            log_ref[rows, cols] = jnp.broadcast_to(peak + jnp.log(weight), (wide, head))

        if number + 2 < chips:
            second.step(number + 2)

    for distance in range(heads + 2, chips):
        second.step(distance)

    reduce = ChainReduce(chips, tok_rows, model_width, reduce_buffers)

    def product(index, store):
        left = attended_ref[pl.ds(pl.multiple_of(index * tok_rows, tok_rows), tok_rows), :]
        for piece in range(split):
            cols = pl.ds(piece * part, part)
            store(cols, jnp.dot(left, rows_full[piece], preferred_element_type=f32))

    reduce.run(product)
    residual = tokens_ref[...].astype(f32) + reduce.total[...]
    residual_ref[...] = residual
    inverse = lax.rsqrt(jnp.mean(residual * residual, -1, keepdims=True) + EPSILON)
    first.sent()
    routed_own[...] = (residual * inverse * gains_ref[1:2, :]).astype(half)
    third = gather(2, routed_own, routed_out)
    third.start()
    third.steps()
    third.landed()

    second.landed()
    reduce.sent()
    second.sent()
    third.sent()
    for index in range(4):
        for shift in range(1, split):
            shard_copy(index, shift).wait_send()
    for shift in range(1, size):
        choice_copy(shift).wait()
    for keep in keeps:
        keep.wait()
    for index in range(3):
        expert_own(index).wait()
        for shift in range(1, split):
            expert_copy(index, shift).wait()


def front(
    sizes, tokens, gain_rows, gain_cols, cos, sin, segment_ids, cotangent, weights, choice, which
):
    size, split, chips, experts_local = sizes
    w_query, w_key, w_value, w_out, w_gate, w_up, w_down = weights
    tok_rows, model_width = tokens.shape
    length = size * tok_rows
    local_width = w_query.shape[1]
    hidden_width = w_gate.shape[2]
    f32, half = jnp.float32, jnp.bfloat16
    vmem = pl.BlockSpec(memory_space=pltpu.VMEM)
    anywhere = pl.BlockSpec(memory_space=pl.ANY)
    kind = pltpu.SemaphoreType.DMA
    shape = jax.ShapeDtypeStruct
    return pl.pallas_call(
        functools.partial(front_kernel, sizes),
        out_shape=(
            shape((length, model_width), half),
            shape((3, model_width, local_width), half),
            shape((split, *w_out.shape), half),
            shape((length, local_width), half),
            shape((length, local_width), half),
            shape((length, local_width), half),
            shape((2, length, local_width), f32),
            shape((8, length), f32),
            shape((length, local_width), f32),
            shape((length, local_width), half),
            shape((tok_rows, model_width), f32),
            shape((length, model_width), half),
            shape((length, model_width), half),
            shape((model_width, hidden_width), half),
            shape((model_width, hidden_width), half),
            shape((hidden_width, model_width), half),
            shape((size, *choice.shape), choice.dtype),
        ),
        in_specs=[vmem] * 7 + [anywhere] * 8 + [vmem],
        out_specs=tuple([anywhere] * 3 + [vmem] * 8 + [anywhere] * 5 + [vmem]),
        scratch_shapes=[
            pltpu.VMEM((length, model_width), half),
            pltpu.VMEM((3, model_width, local_width), half),
            pltpu.VMEM((split, *w_out.shape), half),
            pltpu.VMEM((tok_rows, model_width), half),
            pltpu.VMEM((2, length, local_width), f32),
            pltpu.VMEM((8, length), f32),
            pltpu.VMEM((size, 8, length), f32),
            kind((3,)),
            kind((3, 3, chips)),
            kind((3, 2, chips)),
            kind((size,)),
            kind((size,)),
            kind((size,)),
            kind((size,)),
            kind((4,)),
            kind((4, split)),
            kind((4, split)),
            kind((3,)),
            kind((3, split)),
            kind((3, split)),
            kind((3,)),
            *ChainReduce.scratch(chips, tok_rows, model_width),
        ],
        compiler_params=pltpu.CompilerParams(
            collective_id=which, has_side_effects=True, vmem_limit_bytes=58 * 2**20
        ),
        cost_estimate=pl.CostEstimate(
            flops=2 * length * model_width * local_width * 4,
            bytes_accessed=500 * 2**20,
            transcendentals=0,
        ),
    )(
        tokens,
        gain_rows,
        gain_cols,
        cos,
        sin,
        segment_ids.reshape(-1, 1),
        segment_ids.reshape(1, -1),
        cotangent,
        *weights,
        choice,
    )


def shards(
    tokens,
    norm_gains,
    w_query,
    w_key,
    w_value,
    w_out,
    w_router,
    w_gate,
    w_up,
    w_down,
    segment_ids,
    expert_ids,
    expert_slots,
    cotangent,
):
    half_type = jnp.bfloat16
    float_type = jnp.float32
    tok_rows = tokens.shape[0]
    model_width = tokens.shape[1]
    expert_total = w_router.shape[1]
    top_count = expert_ids.shape[1]
    head_size = HEAD_DIM
    local_width = w_query.shape[1]
    heads_local = local_width // head_size
    capacity = CAP
    seq_index = lax.axis_index("seq")
    column_start = seq_index * local_width
    experts_local = w_gate.shape[0]
    seq_size = lax.axis_size("seq")
    split = lax.axis_size("fsdp")
    groups = split // experts_local
    shard_index = lax.axis_index("fsdp")
    member = lax.rem(shard_index, experts_local)

    def pick(stack, index):
        return lax.dynamic_index_in_dim(stack, index, 0, keepdims=False)

    def to_shards(grad, dim):
        part = grad.shape[dim] // split
        shape = [experts_local, *grad.shape]
        shape[dim + 1] = part
        owned = jnp.zeros(shape, float_type)
        for shift in range(split):
            dest = lax.rem(shard_index + shift, split)
            piece = lax.dynamic_slice_in_dim(grad, dest * part, part, dim).astype(half_type)
            if shift:
                links = [(one, (one + shift) % split) for one in range(split)]
                piece = lax.ppermute(piece, "fsdp", links)
            expert = lax.rem(shard_index - shift + split, experts_local)
            piece = piece.astype(float_type)
            if groups > 1:
                piece = piece + pick(owned, expert)
            owned = lax.dynamic_update_index_in_dim(owned, piece, expert, 0)
        return owned

    def exchange(pieces, back):
        moved = [pieces[0]]
        for shift in range(1, experts_local):
            turn = experts_local - shift if back else shift
            links = [
                (one, one - one % experts_local + (one + turn) % experts_local)
                for one in range(split)
            ]
            moved.append(lax.ppermute(pieces[shift], "fsdp", links))
        return moved

    turned_ids = lax.rem(expert_ids - member + experts_local, experts_local)
    turned_ids = turned_ids + expert_ids - lax.rem(expert_ids, experts_local)
    places = jnp.where(
        expert_slots < capacity, turned_ids * capacity + expert_slots, -(10**6)
    )
    gain_rows = norm_gains.astype(float_type)
    gain_cols = lax.dynamic_slice_in_dim(gain_rows, column_start, local_width, 1)
    inputs = tokens.astype(float_type)
    inverse_first = inverse_rms(inputs)
    unit_first = inputs * inverse_first
    length = seq_size * tok_rows
    positions = jnp.arange(length, dtype=jnp.int32)
    cosine_table, sine_table = rope_tables(positions, head_size)
    cosine_wide = jnp.concatenate([cosine_table, cosine_table], 1)
    sine_wide = jnp.concatenate([-sine_table, sine_table], 1)
    (
        normed_seq,
        qkv_stack,
        out_stack,
        query_heads,
        key_heads,
        value_heads,
        unit_pair,
        square_sums,
        log_wide,
        attended_heads,
        residual,
        routed_seq,
        cotangent_seq,
        gate_full,
        up_full,
        down_full,
        choices,
    ) = front(
        (seq_size, split, seq_size // 2, experts_local),
        tokens,
        gain_rows,
        gain_cols,
        cosine_wide,
        sine_wide,
        segment_ids,
        cotangent,
        (w_query, w_key, w_value, w_out, w_gate, w_up, w_down),
        jnp.concatenate([expert_ids, places], 1).T,
        0,
    )
    both_seq = choices.transpose(0, 2, 1).reshape(length, 2 * top_count)
    ids_seq = both_seq[:, :top_count]
    places_seq = both_seq[:, top_count:]
    unit_query, unit_key = unit_pair[0], unit_pair[1]
    inverse_query = lax.rsqrt(square_sums[0] / model_width + EPSILON)[:, None]
    inverse_key = lax.rsqrt(square_sums[1] / model_width + EPSILON)[:, None]
    qkv_cols = jnp.concatenate([qkv_stack[0], qkv_stack[1], qkv_stack[2]], 1)
    out_rows = out_stack.transpose(1, 0, 2).reshape(local_width, model_width)
    block_rows = math.gcd(512, length)
    blocks = length // block_rows
    score_scale = head_size ** (-0.5)
    query_cube = query_heads.reshape(blocks, block_rows, heads_local, head_size)
    key_cube = key_heads.reshape(length, heads_local, head_size)
    value_cube = value_heads.reshape(length, heads_local, head_size)
    segment_blocks = segment_ids.reshape(blocks, block_rows)
    log_sums = log_wide.reshape(blocks, block_rows, heads_local, head_size)[..., 0]
    log_sums = log_sums.transpose(0, 2, 1)

    def block_scores(query_block, segment_block):
        scores = (
            jnp.einsum("qhd,khd->hqk", query_block, key_cube, preferred_element_type=float_type)
            * score_scale
        )
        visible = segment_block[:, None] == segment_ids[None, :]
        return jnp.where(visible[None], scores, MASKED)

    inverse_second = inverse_rms(residual)
    unit_second = residual * inverse_second
    routed = (unit_second * gain_rows[1]).astype(half_type)
    slots = experts_local * capacity

    def gates_of(rows, ids):
        logits = jnp.dot(rows, w_router, preferred_element_type=float_type)
        chosen = (ids[:, :, None] == jnp.arange(expert_total, dtype=jnp.int32)).astype(float_type)
        picked = jnp.einsum("tke,te->tk", chosen, logits, precision=HIGHEST)
        return chosen, jax.nn.softmax(picked, axis=-1)

    chosen, gate_weights = gates_of(routed, expert_ids)
    gates_seq = gates_of(routed_seq, ids_seq)[1]
    mine = (places_seq - seq_index * slots).reshape(seq_size, tok_rows, top_count)
    hits = mine[:, :, :, None] == jnp.arange(slots, dtype=jnp.int32)
    onehot = jnp.any(hits, 2).astype(half_type)
    combine = jnp.sum(
        jnp.where(hits, gates_seq.reshape(seq_size, tok_rows, top_count)[..., None], 0.0), 2
    )

    def dispatch(rows):
        cube = rows.reshape(seq_size, tok_rows, model_width)
        return [
            jnp.einsum(
                "btc,btd->bcd",
                onehot[:, :, index * capacity : (index + 1) * capacity],
                cube,
                preferred_element_type=float_type,
            )
            .astype(half_type)
            .reshape(seq_size * capacity, model_width)
            for index in range(experts_local)
        ]

    def undispatch(pieces):
        cubes = [piece.reshape(seq_size, capacity, model_width) for piece in pieces]
        return jnp.concatenate(cubes, 1)

    def parts_of(rows):
        depth = rows.shape[0] // experts_local
        return [rows[index * depth : (index + 1) * depth] for index in range(experts_local)]

    expert_rows = jnp.concatenate(exchange(dispatch(routed_seq), False))
    upstream_rows = jnp.concatenate(exchange(dispatch(cotangent_seq), False))
    slot_gates = jnp.sum(combine, 1).reshape(seq_size, experts_local, capacity).transpose(1, 0, 2)
    row_gates = jnp.concatenate(exchange(list(slot_gates.reshape(experts_local, -1)), False))
    gate_pre = jnp.dot(expert_rows, gate_full, preferred_element_type=float_type)
    up_pre = jnp.dot(expert_rows, up_full, preferred_element_type=float_type)
    gate_sigmoid = jax.nn.sigmoid(gate_pre)
    hidden = (gate_pre * gate_sigmoid * up_pre).astype(half_type)
    returned = jnp.dot(hidden, down_full, preferred_element_type=float_type).astype(half_type)
    row_dots = jnp.sum(returned.astype(float_type) * upstream_rows.astype(float_type), -1)
    slot_dots = jnp.stack(exchange(parts_of(row_dots), True))
    slot_dots = slot_dots.reshape(experts_local, seq_size, capacity).transpose(1, 0, 2)
    slot_dots = slot_dots.reshape(seq_size, 1, slots)
    padded = -(-slots // 128) * 128
    slot_dots = jnp.pad(slot_dots, ((0, 0), (0, 7), (0, padded - slots)))
    slot_dots = seq_swap(slot_dots, seq_size, False, 3)[:, 0, :slots].reshape(-1)
    at_place = places[:, :, None] == jnp.arange(expert_total * capacity, dtype=jnp.int32)
    gate_grad = jnp.sum(jnp.where(at_place, slot_dots, 0.0), -1)
    incoming = undispatch(exchange(parts_of(returned), True))
    mixture = seq_reduce(combine.astype(half_type), incoming, model_width, False, 4)
    output = (residual + mixture).astype(half_type)
    upstream = cotangent.astype(float_type)
    slot_grads = (row_gates[:, None] * upstream_rows.astype(float_type)).astype(half_type)
    hidden_grad = jnp.einsum(
        "rd,fd->rf", slot_grads, down_full, preferred_element_type=float_type
    )
    gate_pre_grad = (
        hidden_grad * up_pre * gate_sigmoid * (1.0 + gate_pre * (1.0 - gate_sigmoid))
    ).astype(half_type)
    up_pre_grad = (hidden_grad * gate_pre * gate_sigmoid).astype(half_type)
    rows_grad = jnp.einsum("rf,df->rd", gate_pre_grad, gate_full, preferred_element_type=float_type)
    rows_grad = (
        rows_grad
        + jnp.einsum("rf,df->rd", up_pre_grad, up_full, preferred_element_type=float_type)
    ).astype(half_type)
    sent_back = undispatch(exchange(parts_of(rows_grad), True))
    routed_grad = seq_reduce(onehot, sent_back, model_width, False, 4)
    grad_down_full = jnp.einsum("rf,rd->fd", hidden, slot_grads, preferred_element_type=float_type)
    grad_gate_full = jnp.einsum(
        "rd,rf->df", expert_rows, gate_pre_grad, preferred_element_type=float_type
    )
    grad_up_full = jnp.einsum("rd,rf->df", expert_rows, up_pre_grad, preferred_element_type=float_type)
    mean_grad = jnp.sum(gate_weights * gate_grad, -1, keepdims=True)
    picked_grad = gate_weights * (gate_grad - mean_grad)
    logit_grad = jnp.einsum("tke,tk->te", chosen, picked_grad, precision=HIGHEST).astype(half_type)
    routed_grad = routed_grad + jnp.einsum(
        "te,de->td", logit_grad, w_router, preferred_element_type=float_type
    )
    grad_router_local = jnp.einsum(
        "td,te->ed", routed, logit_grad, preferred_element_type=float_type
    )
    gain_second_grad = jnp.sum(routed_grad * unit_second, axis=0)
    residual_grad = upstream + norm_back(routed_grad * gain_rows[1], unit_second, inverse_second)
    out_grad = residual_grad.astype(half_type)
    out_grad_seq = seq_gather(out_grad, seq_size, 2)
    grad_out_local = jnp.einsum(
        "th,td->hd", attended_heads, out_grad_seq, preferred_element_type=float_type
    )
    attended_grad = jnp.einsum(
        "td,hd->th", out_grad_seq, out_rows, preferred_element_type=float_type
    ).astype(half_type)
    grad_cube = attended_grad.reshape(blocks, block_rows, heads_local, head_size)

    def attend_back(running, pieces):
        key_acc, value_acc = running
        query_block, segment_block, grad_block, log_block = pieces
        scores = block_scores(query_block, segment_block)
        soft_values = jnp.exp(scores - log_block[..., None])
        prob_grad = jnp.einsum(
            "qhd,khd->hqk", grad_block, value_cube, preferred_element_type=float_type
        )
        center = jnp.sum(soft_values * prob_grad, -1, keepdims=True)
        score_grad = (soft_values * (prob_grad - center)).astype(half_type)
        query_grad = (
            jnp.einsum("hqk,khd->qhd", score_grad, key_cube, preferred_element_type=float_type)
            * score_scale
        )
        key_acc = (
            key_acc
            + jnp.einsum("hqk,qhd->khd", score_grad, query_block, preferred_element_type=float_type)
            * score_scale
        )
        value_acc = value_acc + jnp.einsum(
            "hqk,qhd->khd",
            soft_values.astype(half_type),
            grad_block,
            preferred_element_type=float_type,
        )
        return ((key_acc, value_acc), query_grad.astype(half_type))

    empty_acc = jnp.zeros((length, heads_local, head_size), float_type)
    (key_acc, value_acc), query_grads = lax.scan(
        attend_back, (empty_acc, empty_acc), (query_cube, segment_blocks, grad_cube, log_sums)
    )
    query_back = query_grads.reshape(length, local_width)
    key_back = key_acc.reshape(length, local_width).astype(half_type)
    value_back = value_acc.reshape(length, local_width).astype(half_type)
    query_unit_grad = rotate(query_back.astype(float_type), cosine_table, -sine_table, head_size)
    key_unit_grad = rotate(key_back.astype(float_type), cosine_table, -sine_table, head_size)
    gain_query_grad = jnp.sum(query_unit_grad * unit_query, axis=0)
    gain_key_grad = jnp.sum(key_unit_grad * unit_key, axis=0)
    query_scaled = query_unit_grad * gain_cols[2]
    key_scaled = key_unit_grad * gain_cols[3]
    centers = seq_sum(
        (jnp.sum(query_scaled * unit_query, -1), jnp.sum(key_scaled * unit_key, -1)), seq_size, 1
    )
    query_raw_grad = (
        inverse_query * (query_scaled - unit_query * (centers[0] / model_width)[:, None])
    ).astype(half_type)
    key_raw_grad = (
        inverse_key * (key_scaled - unit_key * (centers[1] / model_width)[:, None])
    ).astype(half_type)
    raw_grads = jnp.concatenate([query_raw_grad, key_raw_grad, value_back], 1)
    raw_blocks = raw_grads.reshape(seq_size, tok_rows, 3 * local_width)
    normed_grad = seq_reduce(raw_blocks, qkv_cols, model_width, True, 5)
    grad_qkv_local = jnp.einsum("td,th->dh", normed_seq, raw_grads, preferred_element_type=float_type)
    gain_first_grad = jnp.sum(normed_grad * unit_first, axis=0)
    input_grad = residual_grad + norm_back(normed_grad * gain_rows[0], unit_first, inverse_first)
    zero_row = jnp.zeros((model_width,), float_type)
    gain_query_full = lax.dynamic_update_slice_in_dim(zero_row, gain_query_grad, column_start, 0)
    gain_key_full = lax.dynamic_update_slice_in_dim(zero_row, gain_key_grad, column_start, 0)
    gain_grads = jnp.stack([gain_first_grad, gain_second_grad, gain_query_full, gain_key_full])
    small = jnp.concatenate([gain_grads, jnp.zeros_like(gain_grads), grad_router_local])
    small = total_sum(small, seq_size, split, 6)
    gain_sums, router_grad = small[:4], small[8:].T
    qkv_owned = lax.psum_scatter(
        grad_qkv_local.astype(half_type), "fsdp", scatter_dimension=0, tiled=True
    ).astype(float_type)
    out_owned = lax.psum_scatter(
        grad_out_local.astype(half_type), "fsdp", scatter_dimension=1, tiled=True
    ).astype(float_type)
    return (
        output,
        input_grad,
        gain_sums,
        qkv_owned[:, :local_width],
        qkv_owned[:, local_width : 2 * local_width],
        qkv_owned[:, 2 * local_width :],
        out_owned,
        router_grad,
        to_shards(grad_gate_full, 0),
        to_shards(grad_up_full, 0),
        to_shards(grad_down_full, 1),
    )


def solution(mesh):
    in_specs = (
        P(("fsdp", "seq"), None),
        P(),
        P("fsdp", "seq"),
        P("fsdp", "seq"),
        P("fsdp", "seq"),
        P("seq", "fsdp"),
        P(),
        P("seq", "fsdp", None),
        P("seq", "fsdp", None),
        P("seq", None, "fsdp"),
        P("fsdp"),
        P(("fsdp", "seq"), None),
        P(("fsdp", "seq"), None),
        P(("fsdp", "seq"), None),
    )
    out_specs = (
        P(("fsdp", "seq"), None),
        P(("fsdp", "seq"), None),
        P(),
        P("fsdp", "seq"),
        P("fsdp", "seq"),
        P("fsdp", "seq"),
        P("seq", "fsdp"),
        P(),
        P("seq", "fsdp", None),
        P("seq", "fsdp", None),
        P("seq", None, "fsdp"),
    )
    return jax.shard_map(shards, mesh=mesh, in_specs=in_specs, out_specs=out_specs, check_vma=False)
```

```python
import functools
import math

import jax
import jax.numpy as jnp
from jax import lax
from jax.experimental import pallas as pl
from jax.experimental.pallas import tpu as pltpu
from jax.sharding import PartitionSpec as P

HEAD_DIM = 128
CAP = 40


EPSILON = 1e-06
THETA = 10000.0
MASKED = -1e30
HIGHEST = lax.Precision.HIGHEST


def rope_tables(positions, head_size):
    half_dim = head_size // 2
    frequency = THETA ** (-jnp.arange(half_dim, dtype=jnp.float32) / half_dim)
    angles = positions.astype(jnp.float32)[:, None] * frequency[None, :]
    return (jnp.cos(angles), jnp.sin(angles))


def rotate(values_in, cosine_table, sine_table, head_size):
    row_count = values_in.shape[0]
    pieces = values_in.reshape(row_count, -1, head_size)
    half_dim = head_size // 2
    former = pieces[..., :half_dim]
    latter = pieces[..., half_dim:]
    cosine_wide = cosine_table[:, None, :]
    sine_wide = sine_table[:, None, :]
    turned = jnp.concatenate(
        [former * cosine_wide - latter * sine_wide, latter * cosine_wide + former * sine_wide], -1
    )
    return turned.reshape(row_count, -1)


def inverse_rms(values_in):
    return lax.rsqrt(jnp.mean(values_in * values_in, -1, keepdims=True) + EPSILON)


def norm_back(grad_unit, unit_values, inverse):
    return inverse * (
        grad_unit - unit_values * jnp.mean(grad_unit * unit_values, -1, keepdims=True)
    )


def greet_chain(chip, core, chips):
    barrier = pltpu.get_barrier_semaphore()

    def greet(target):
        pl.semaphore_signal(barrier, inc=1, device_id={"seq": target})

    greet(chip * 2 + 1 - core)

    @pl.when(chip < chips - 1)
    def _():
        greet(chip * 2 + 2 + core)

    @pl.when(chip > 0)
    def _():
        greet(chip * 2 - 2 + core)

    inner = jnp.where(chip < chips - 1, 1, 0) + jnp.where(chip > 0, 1, 0)
    pl.semaphore_wait(barrier, 1 + inner)


class ChainGather:
    def __init__(self, chips, x_ref, out_ref, local_sem, sends, arrivals):
        self.chips, self.x_ref, self.out_ref = chips, x_ref, out_ref
        self.local_sem, self.sends, self.arrivals = local_sem, sends, arrivals
        me = lax.axis_index("seq")
        self.chip, self.core = me // 2, lax.rem(me, 2)
        self.rows = x_ref.shape[0]

    def block(self, source, core):
        start = pl.multiple_of((source * 2 + core) * self.rows, self.rows)
        return self.out_ref.at[pl.ds(start, self.rows)]

    def hop(self, source, ref, target, way, lane):
        return pltpu.make_async_remote_copy(
            src_ref=ref,
            dst_ref=self.block(source, self.core),
            send_sem=self.sends.at[way, source],
            recv_sem=self.arrivals.at[lane, source],
            device_id={"seq": target},
        )

    def upward(self, source, ref):
        return self.hop(source, ref, self.chip * 2 + 2 + self.core, 0, 0)

    def downward(self, source, ref):
        return self.hop(source, ref, self.chip * 2 - 2 + self.core, 1, 0)

    def sideways(self, source, ref):
        return self.hop(source, ref, self.chip * 2 + 1 - self.core, 2, 1)

    def own(self):
        return pltpu.make_async_copy(
            self.x_ref, self.block(self.chip, self.core), self.local_sem
        )

    def start(self):
        @pl.when(self.chip < self.chips - 1)
        def _():
            self.upward(self.chip, self.x_ref).start()

        @pl.when(self.chip > 0)
        def _():
            self.downward(self.chip, self.x_ref).start()

        self.sideways(self.chip, self.x_ref).start()
        self.own().start()

    def step(self, distance):
        below, above = self.chip - distance, self.chip + distance

        @pl.when(below >= 0)
        def _():
            landed = self.block(below, self.core)
            self.upward(below, landed).wait_recv()

            @pl.when(self.chip < self.chips - 1)
            def _():
                self.upward(below, landed).start()

            self.sideways(below, landed).start()

        @pl.when(above < self.chips)
        def _():
            landed = self.block(above, self.core)
            self.downward(above, landed).wait_recv()

            @pl.when(self.chip > 0)
            def _():
                self.downward(above, landed).start()

            self.sideways(above, landed).start()

    def steps(self):
        for distance in range(1, self.chips):
            self.step(distance)

    def landed(self):
        self.own().wait()
        for source in range(self.chips):
            self.sideways(source, self.block(source, self.core)).wait_recv()

    def sent(self):
        for source in range(self.chips):
            ref = self.block(source, self.core)
            self.sideways(source, ref).wait_send()

            @pl.when((self.chip < self.chips - 1) & (source <= self.chip))
            def _():
                self.upward(source, ref).wait_send()

            @pl.when((self.chip > 0) & (source >= self.chip))
            def _():
                self.downward(source, ref).wait_send()


class ChainReduce:
    def __init__(self, chips, total, buffers):
        self.total = total
        (
            self.side_out,
            self.side_in,
            self.chain_in,
            self.side_send,
            self.side_recv,
            self.chain_send,
            self.chain_recv,
        ) = buffers
        self.chips = chips
        me = lax.axis_index("seq")
        self.chip, self.core = me // 2, lax.rem(me, 2)

    @staticmethod
    def scratch(chips, rows, width):
        half = jnp.bfloat16
        return [
            pltpu.VMEM((chips, rows, width), half),
            pltpu.VMEM((chips, rows, width), half),
            pltpu.VMEM((chips + 1, rows, width), half),
            pltpu.SemaphoreType.DMA((chips,)),
            pltpu.SemaphoreType.DMA((chips,)),
            pltpu.SemaphoreType.DMA((chips,)),
            pltpu.SemaphoreType.DMA((2, chips)),
        ]

    def side_copy(self, dest):
        return pltpu.make_async_remote_copy(
            src_ref=self.side_out.at[dest],
            dst_ref=self.side_in.at[dest],
            send_sem=self.side_send.at[dest],
            recv_sem=self.side_recv.at[dest],
            device_id={"seq": self.chip * 2 + 1 - self.core},
        )

    def chain_copy(self, way, dest, target):
        return pltpu.make_async_remote_copy(
            src_ref=self.side_out.at[dest],
            dst_ref=self.chain_in.at[self.slot(way, dest, target // 2)],
            send_sem=self.chain_send.at[dest],
            recv_sem=self.chain_recv.at[way, dest],
            device_id={"seq": target},
        )

    def slot(self, way, dest, holder):
        return jnp.where(dest == holder, self.chips, dest) if way else dest

    def place(self, index):
        distance = self.chips - 1 - index // 2
        dest = self.chip + (1 - 2 * lax.rem(index, 2)) * distance
        return dest, (dest >= 0) & (dest < self.chips)

    def run(self, product):
        chips, chip, core, total = self.chips, self.chip, self.core, self.total
        sibling = chip * 2 + 1 - core

        @pl.loop(0, 2 * chips - 1)
        def _(index):
            dest, inside = self.place(index)

            @pl.when(inside)
            def _():
                def store(cols, part):
                    self.side_out[dest, :, cols] = part.astype(self.side_out.dtype)

                product(dest * 2 + 1 - core, store)
                self.side_copy(dest).start()

        @pl.loop(0, 2 * chips - 1)
        def _(index):
            dest, inside = self.place(index)

            @pl.when(inside)
            def _():
                def store(cols, part):
                    total[:, cols] = part

                product(dest * 2 + core, store)
                self.side_copy(dest).wait_recv()
                total[...] += self.side_in[dest].astype(jnp.float32)

                @pl.when((dest >= chip) & (chip > 0))
                def _():
                    self.chain_copy(0, dest, sibling).wait_recv()
                    total[...] += self.chain_in[dest].astype(jnp.float32)

                @pl.when((dest <= chip) & (chip < chips - 1))
                def _():
                    self.chain_copy(1, dest, sibling).wait_recv()
                    total[...] += self.chain_in[self.slot(1, dest, chip)].astype(jnp.float32)

                self.side_copy(dest).wait_send()

                @pl.when(dest != chip)
                def _():
                    self.side_out[dest] = total[...].astype(self.side_out.dtype)

                @pl.when(dest > chip)
                def _():
                    self.chain_copy(0, dest, chip * 2 + 2 + core).start()

                @pl.when(dest < chip)
                def _():
                    self.chain_copy(1, dest, chip * 2 - 2 + core).start()

    def sent(self):
        sibling = self.chip * 2 + 1 - self.core

        @pl.loop(0, self.chips)
        def _(dest):
            @pl.when(dest != self.chip)
            def _():
                self.chain_copy(0, dest, sibling).wait_send()


def gather_kernel(chips, x_ref, out_ref, local_sem, sends, arrivals):
    gather = ChainGather(chips, x_ref, out_ref, local_sem, sends, arrivals)
    greet_chain(gather.chip, gather.core, chips)
    gather.start()
    gather.steps()
    gather.landed()
    gather.sent()


def seq_gather(x, size, which):
    chips = size // 2
    rows, width = x.shape
    return pl.pallas_call(
        functools.partial(gather_kernel, chips),
        out_shape=jax.ShapeDtypeStruct((size * rows, width), x.dtype),
        in_specs=[pl.BlockSpec(memory_space=pl.ANY)],
        out_specs=pl.BlockSpec(memory_space=pl.ANY),
        scratch_shapes=[
            pltpu.SemaphoreType.DMA,
            pltpu.SemaphoreType.DMA((3, chips)),
            pltpu.SemaphoreType.DMA((2, chips)),
        ],
        compiler_params=pltpu.CompilerParams(collective_id=which, has_side_effects=True),
        cost_estimate=pl.CostEstimate(
            flops=0, bytes_accessed=40 * x.size * x.dtype.itemsize * chips, transcendentals=0
        ),
    )(x)


def reduce_kernel(chips, shared, turned, a_ref, b_ref, o_ref, *buffers):
    rows, width = o_ref.shape
    step_cols = min(512, width)
    reduce = ChainReduce(chips, o_ref, buffers)
    greet_chain(reduce.chip, reduce.core, chips)

    def product(block, store):
        left = a_ref[block]

        @pl.loop(0, width // step_cols)
        def _(index):
            cols = pl.ds(pl.multiple_of(index * step_cols, step_cols), step_cols)
            right_ref = b_ref if shared else b_ref.at[block]
            if turned:
                part = lax.dot_general(
                    left,
                    right_ref[cols, :],
                    (((1,), (1,)), ((), ())),
                    preferred_element_type=jnp.float32,
                )
            else:
                part = jnp.dot(left, right_ref[:, cols], preferred_element_type=jnp.float32)
            store(cols, part)

    reduce.run(product)
    reduce.sent()


def seq_reduce(a, b, width, turned, which):
    size, rows, depth = a.shape
    chips = size // 2
    half = jnp.bfloat16
    return pl.pallas_call(
        functools.partial(reduce_kernel, chips, b.ndim == 2, turned),
        out_shape=jax.ShapeDtypeStruct((rows, width), jnp.float32),
        in_specs=[pl.BlockSpec(memory_space=pltpu.VMEM)] * 2,
        out_specs=pl.BlockSpec(memory_space=pltpu.VMEM),
        scratch_shapes=ChainReduce.scratch(chips, rows, width),
        compiler_params=pltpu.CompilerParams(
            collective_id=which, has_side_effects=True, vmem_limit_bytes=56 * 2**20
        ),
        cost_estimate=pl.CostEstimate(
            flops=2 * size * rows * depth * width,
            bytes_accessed=40 * rows * width * size,
            transcendentals=0,
        ),
    )(a, b)


def swap_kernel(size, summed, x_ref, o_ref, landing, send_sem, recv_sem):
    me = lax.axis_index("seq")
    barrier = pltpu.get_barrier_semaphore()
    for shift in range(1, size):
        pl.semaphore_signal(barrier, inc=1, device_id={"seq": lax.rem(me + shift, size)})
    pl.semaphore_wait(barrier, size - 1)

    def copy(shift):
        peer = lax.rem(me + shift, size)
        return pltpu.make_async_remote_copy(
            src_ref=x_ref if summed else x_ref.at[peer],
            dst_ref=landing.at[me],
            send_sem=send_sem.at[shift],
            recv_sem=recv_sem.at[shift],
            device_id={"seq": peer},
        )

    for shift in range(1, size):
        copy(shift).start()
    landing[me] = x_ref[...] if summed else x_ref[me]
    for shift in range(1, size):
        copy(shift).wait()
    if summed:
        o_ref[...] = jnp.sum(landing[...], 0)
    else:
        o_ref[...] = landing[...]


def seq_swap(x, size, summed, which):
    piece = x.shape if summed else x.shape[1:]
    return pl.pallas_call(
        functools.partial(swap_kernel, size, summed),
        out_shape=jax.ShapeDtypeStruct(x.shape, x.dtype),
        in_specs=[pl.BlockSpec(memory_space=pltpu.VMEM)],
        out_specs=pl.BlockSpec(memory_space=pltpu.VMEM),
        scratch_shapes=[
            pltpu.VMEM((size, *piece), x.dtype),
            pltpu.SemaphoreType.DMA((size,)),
            pltpu.SemaphoreType.DMA((size,)),
        ],
        compiler_params=pltpu.CompilerParams(collective_id=which, has_side_effects=True),
    )(x)


def seq_sum(pair, size, which):
    both = jnp.concatenate(pair).reshape(-1, 128)
    return seq_swap(both, size, True, which).reshape(2, -1)


def total_kernel(
    size, split, x_ref, o_ref, first, second, final, send_one, recv_one, send_two, recv_two, send_three, recv_three
):
    me, mine = lax.axis_index("seq"), lax.axis_index("fsdp")
    part = x_ref.shape[1] // size
    barrier = pltpu.get_barrier_semaphore()
    for shift in range(1, size):
        pl.semaphore_signal(barrier, inc=1, device_id={"seq": lax.rem(me + shift, size)})
    for shift in range(1, split):
        pl.semaphore_signal(barrier, inc=1, device_id={"fsdp": lax.rem(mine + shift, split)})
    pl.semaphore_wait(barrier, size + split - 2)

    def columns(index):
        return pl.ds(pl.multiple_of(index * part, part), part)

    def scatter(shift):
        peer = lax.rem(me + shift, size)
        return pltpu.make_async_remote_copy(
            src_ref=x_ref.at[:, columns(peer)],
            dst_ref=first.at[me],
            send_sem=send_one.at[shift],
            recv_sem=recv_one.at[shift],
            device_id={"seq": peer},
        )

    def share(shift):
        return pltpu.make_async_remote_copy(
            src_ref=second.at[mine],
            dst_ref=second.at[mine],
            send_sem=send_two.at[shift],
            recv_sem=recv_two.at[shift],
            device_id={"fsdp": lax.rem(mine + shift, split)},
        )

    def collect(shift):
        return pltpu.make_async_remote_copy(
            src_ref=final.at[me],
            dst_ref=final.at[me],
            send_sem=send_three.at[shift],
            recv_sem=recv_three.at[shift],
            device_id={"seq": lax.rem(me + shift, size)},
        )

    for shift in range(1, size):
        scatter(shift).start()
    first[me] = x_ref[:, columns(me)]
    for shift in range(1, size):
        scatter(shift).wait_recv()
    second[mine] = jnp.sum(first[...], 0)
    for shift in range(1, split):
        share(shift).start()
    for shift in range(1, split):
        share(shift).wait_recv()
    final[me] = jnp.sum(second[...], 0)
    for shift in range(1, size):
        collect(shift).start()
    for shift in range(1, size):
        scatter(shift).wait_send()
    for shift in range(1, split):
        share(shift).wait_send()
    for shift in range(1, size):
        collect(shift).wait()
    for index in range(size):
        o_ref[:, index * part : (index + 1) * part] = final[index]


def total_sum(x, size, split, which):
    rows, width = x.shape
    part = width // size
    kind = pltpu.SemaphoreType.DMA
    return pl.pallas_call(
        functools.partial(total_kernel, size, split),
        out_shape=jax.ShapeDtypeStruct(x.shape, x.dtype),
        in_specs=[pl.BlockSpec(memory_space=pltpu.VMEM)],
        out_specs=pl.BlockSpec(memory_space=pltpu.VMEM),
        scratch_shapes=[
            pltpu.VMEM((size, rows, part), x.dtype),
            pltpu.VMEM((split, rows, part), x.dtype),
            pltpu.VMEM((size, rows, part), x.dtype),
            kind((size,)),
            kind((size,)),
            kind((split,)),
            kind((split,)),
            kind((size,)),
            kind((size,)),
        ],
        compiler_params=pltpu.CompilerParams(collective_id=which, has_side_effects=True),
    )(x)

def partner_of(index, move):
    turned, bit = index, 1
    while bit <= move:
        if move // bit % 2:
            turned = turned + bit - 2 * bit * lax.rem(index // bit, 2)
        bit *= 2
    return turned


def greet_all(size, split):
    me, mine = lax.axis_index("seq"), lax.axis_index("fsdp")
    barrier = pltpu.get_barrier_semaphore()
    for shift in range(1, size):
        pl.semaphore_signal(barrier, inc=1, device_id={"seq": lax.rem(me + shift, size)})
    for shift in range(1, split):
        pl.semaphore_signal(barrier, inc=1, device_id={"fsdp": lax.rem(mine + shift, split)})
    pl.semaphore_wait(barrier, size + split - 2)


def turned_halves(head):
    return pltpu.roll(head, head.shape[-1] // 2, 1)


def row_sums(values, pick):
    return lax.dot_general(
        pick, values, (((1,), (1,)), ((), ())), precision=HIGHEST, preferred_element_type=jnp.float32
    )


def column_of(row_form, pick):
    return lax.dot_general(
        row_form, pick, (((0,), (0,)), ((), ())), precision=HIGHEST, preferred_element_type=jnp.float32
    )


def front_kernel(
    sizes,
    tokens_ref,
    gains_ref,
    gain_cols_ref,
    cos_ref,
    sin_ref,
    seg_col_ref,
    seg_row_ref,
    cotangent_ref,
    wq_ref,
    wk_ref,
    wv_ref,
    wo_ref,
    w_gate_ref,
    w_up_ref,
    w_down_ref,
    choice_ref,
    normed_out,
    qkv_out,
    rows_out,
    q_ref,
    k_ref,
    v_ref,
    unit_ref,
    sums_ref,
    log_ref,
    attended_ref,
    residual_ref,
    routed_out,
    cotangent_rows,
    gate_full,
    up_full,
    down_full,
    choices,
    onehot_ref,
    normed,
    qkv,
    rows_full,
    routed_own,
    cotangent_all,
    placed,
    raw,
    sums_own,
    sums_in,
    gather_local,
    gather_send,
    gather_recv,
    sums_send,
    sums_recv,
    choice_send,
    choice_recv,
    placed_local,
    placed_send,
    placed_recv,
    shard_local,
    shard_send,
    shard_recv,
    expert_local,
    expert_send,
    expert_recv,
    out_sem,
    *reduce_buffers,
):
    size, split, chips, experts_local = sizes
    f32, half = jnp.float32, jnp.bfloat16
    me, mine = lax.axis_index("seq"), lax.axis_index("fsdp")
    tok_rows, model_width = tokens_ref.shape
    length, local_width = q_ref.shape
    part = model_width // split
    head = HEAD_DIM
    heads = local_width // head

    inputs = tokens_ref[...].astype(f32)
    inverse = lax.rsqrt(jnp.mean(inputs * inputs, -1, keepdims=True) + EPSILON)
    own_rows = pl.ds(pl.multiple_of(me * tok_rows, tok_rows), tok_rows)
    routed_own[...] = (inputs * inverse * gains_ref[0:1, :]).astype(half)
    greet_all(size, split)

    def gather(index, x_ref, out_ref):
        return ChainGather(
            chips,
            x_ref,
            out_ref,
            gather_local.at[index],
            gather_send.at[index],
            gather_recv.at[index],
        )

    first = gather(0, routed_own, normed)
    first.start()

    def choice_copy(shift):
        return pltpu.make_async_remote_copy(
            src_ref=choice_ref,
            dst_ref=choices.at[me],
            send_sem=choice_send.at[shift],
            recv_sem=choice_recv.at[shift],
            device_id={"seq": lax.rem(me + shift, size)},
        )

    own_part = pl.ds(pl.multiple_of(mine * part, part), part)
    shard_pairs = (
        (wq_ref, qkv.at[0, own_part]),
        (wk_ref, qkv.at[1, own_part]),
        (wv_ref, qkv.at[2, own_part]),
        (wo_ref, rows_full.at[mine]),
    )

    def shard_copy(index, shift):
        source, target = shard_pairs[index]
        return pltpu.make_async_remote_copy(
            src_ref=source,
            dst_ref=target,
            send_sem=shard_send.at[index, shift],
            recv_sem=shard_recv.at[index, shift],
            device_id={"fsdp": lax.rem(mine + shift, split)},
        )

    def shard_own(index):
        source, target = shard_pairs[index]
        return pltpu.make_async_copy(source, target, shard_local.at[index])

    for index in range(4):
        for shift in range(1, split):
            shard_copy(index, shift).start()
        shard_own(index).start()

    def expert_pair(index, dest):
        expert = lax.rem(dest, experts_local)
        if index == 2:
            return w_down_ref.at[expert], down_full.at[:, own_part]
        source, target = ((w_gate_ref, gate_full), (w_up_ref, up_full))[index]
        return source.at[expert], target.at[own_part]

    def expert_copy(index, shift):
        dest = lax.rem(mine + shift, split)
        source, target = expert_pair(index, dest)
        return pltpu.make_async_remote_copy(
            src_ref=source,
            dst_ref=target,
            send_sem=expert_send.at[index, shift],
            recv_sem=expert_recv.at[index, shift],
            device_id={"fsdp": dest},
        )

    def expert_own(index):
        source, target = expert_pair(index, mine)
        return pltpu.make_async_copy(source, target, expert_local.at[index])

    first.steps()
    for index in range(4):
        shard_own(index).wait()
        for shift in range(1, split):
            shard_copy(index, shift).wait_recv()
    for index in range(3):
        for shift in range(1, split):
            expert_copy(index, shift).start()
        expert_own(index).start()
    first.landed()
    for shift in range(1, size):
        choice_copy(shift).start()
    choices[me] = choice_ref[...]
    second = gather(1, cotangent_ref, cotangent_all)
    second.start()
    keeps = [
        pltpu.make_async_copy(normed, normed_out, out_sem.at[0]),
        pltpu.make_async_copy(qkv, qkv_out, out_sem.at[1]),
        pltpu.make_async_copy(rows_full, rows_out, out_sem.at[2]),
    ]
    for keep in keeps:
        keep.start()

    block = min(512, length)
    lanes = lax.broadcasted_iota(jnp.int32, (8, local_width), 0)
    first_row, second_row = (lanes == 0).astype(f32), (lanes == 1).astype(f32)

    @pl.loop(0, length // block)
    def _(step):
        rows = pl.ds(pl.multiple_of(step * block, block), block)
        left = normed[rows, :]
        query = jnp.dot(left, qkv[0], preferred_element_type=f32)
        raw[0, rows, :] = query
        keys = jnp.dot(left, qkv[1], preferred_element_type=f32)
        raw[1, rows, :] = keys
        sums_own[:, rows] = row_sums(query * query, first_row) + row_sums(keys * keys, second_row)
        v_ref[rows, :] = jnp.dot(left, qkv[2], preferred_element_type=f32).astype(half)

    def sums_copy(shift):
        return pltpu.make_async_remote_copy(
            src_ref=sums_own,
            dst_ref=sums_in.at[me],
            send_sem=sums_send.at[shift],
            recv_sem=sums_recv.at[shift],
            device_id={"seq": lax.rem(me + shift, size)},
        )

    for shift in range(1, size):
        sums_copy(shift).start()
    sums_in[me] = sums_own[...]
    for shift in range(1, size):
        sums_copy(shift).wait()
    sums_ref[...] = jnp.sum(sums_in[...], 0)

    @pl.loop(0, length // block)
    def _(step):
        rows = pl.ds(pl.multiple_of(step * block, block), block)
        square_sums = sums_ref[:, rows]
        for index, pick, target in ((0, first_row, q_ref), (1, second_row, k_ref)):
            scale = lax.rsqrt(column_of(square_sums, pick) / model_width + EPSILON)
            unit = raw[index, rows, :] * scale
            unit_ref[index, rows, :] = unit
            scaled = unit * gain_cols_ref[2 + index : 3 + index, :]
            for number in range(heads):
                cols = slice(number * head, (number + 1) * head)
                piece = scaled[:, cols]
                target[rows, cols] = (
                    piece * cos_ref[rows, :] + turned_halves(piece) * sin_ref[rows, :]
                ).astype(half)

    second.step(1)

    wide = min(256, length)
    for number in range(heads):
        cols = slice(number * head, (number + 1) * head)

        @pl.loop(0, length // wide)
        def _(step):
            rows = pl.ds(pl.multiple_of(step * wide, wide), wide)
            scores = lax.dot_general(
                q_ref[rows, cols],
                k_ref[:, cols],
                (((1,), (1,)), ((), ())),
                preferred_element_type=f32,
            )
            scores = scores * (head**-0.5)
            scores = jnp.where(seg_col_ref[rows, :] == seg_row_ref[...], scores, MASKED)
            peak = jnp.max(scores, -1, keepdims=True)
            grown = jnp.exp(scores - peak)
            weight = jnp.sum(grown, -1, keepdims=True)
            probs = (grown * (1.0 / weight)).astype(half)
            attended_ref[rows, cols] = jnp.dot(
                probs, v_ref[:, cols], preferred_element_type=f32
            ).astype(half)
            log_ref[rows, cols] = jnp.broadcast_to(peak + jnp.log(weight), (wide, head))

        if number + 2 < chips:
            second.step(number + 2)

    for distance in range(heads + 2, chips):
        second.step(distance)

    reduce = ChainReduce(chips, residual_ref, reduce_buffers)

    def product(index, store):
        left = attended_ref[pl.ds(pl.multiple_of(index * tok_rows, tok_rows), tok_rows), :]
        for piece in range(split):
            cols = pl.ds(piece * part, part)
            store(cols, jnp.dot(left, rows_full[piece], preferred_element_type=f32))

    reduce.run(product)
    residual = tokens_ref[...].astype(f32) + reduce.total[...]
    residual_ref[...] = residual
    inverse = lax.rsqrt(jnp.mean(residual * residual, -1, keepdims=True) + EPSILON)
    first.sent()
    routed_own[...] = (residual * inverse * gains_ref[1:2, :]).astype(half)
    third = gather(2, routed_own, routed_out)
    third.start()
    third.steps()
    third.landed()

    second.landed()
    for shift in range(1, size):
        choice_copy(shift).wait()
    double = 2 * CAP
    member = lax.rem(mine, experts_local)
    top_count = choice_ref.shape[0] // 2
    slot_row = lax.broadcasted_iota(jnp.int32, (double, tok_rows), 0)

    @pl.loop(0, size // 2)
    def _(pair):
        for move in range(experts_local):
            base = (me * experts_local + partner_of(member, move)) * CAP
            for side in range(2):
                want = jnp.where(slot_row // CAP == side, slot_row - side * CAP + base, -1)
                places = choices[pair * 2 + side]
                hit = want == places[top_count : top_count + 1, :]
                for choice in range(1, top_count):
                    hit = hit | (want == places[top_count + choice : top_count + choice + 1, :])
                cols = slice(side * tok_rows, (side + 1) * tok_rows)
                onehot_ref[pair, move * double : (move + 1) * double, cols] = jnp.where(
                    hit, 1.0, 0.0
                ).astype(half)
        start = pl.multiple_of(pair * 2 * tok_rows, 2 * tok_rows)
        made = jnp.dot(
            onehot_ref[pair], cotangent_all[pl.ds(start, 2 * tok_rows), :], preferred_element_type=f32
        ).astype(half)
        for move in range(experts_local):
            placed[move, pair] = made[move * double : (move + 1) * double]

    def placed_copy(move):
        return pltpu.make_async_remote_copy(
            src_ref=placed.at[move],
            dst_ref=cotangent_rows.at[move],
            send_sem=placed_send.at[move],
            recv_sem=placed_recv.at[move],
            device_id={"fsdp": partner_of(mine, move)},
        )

    for move in range(experts_local - 1, 0, -1):
        placed_copy(move).start()
    placed_own = pltpu.make_async_copy(placed.at[0], cotangent_rows.at[0], placed_local)
    placed_own.start()

    reduce.sent()
    second.sent()
    third.sent()
    for index in range(4):
        for shift in range(1, split):
            shard_copy(index, shift).wait_send()
    for keep in keeps:
        keep.wait()
    placed_own.wait()
    for move in range(1, experts_local):
        placed_copy(move).wait()
    for index in range(3):
        expert_own(index).wait()
        for shift in range(1, split):
            expert_copy(index, shift).wait()


def front(
    sizes, tokens, gain_rows, gain_cols, cos, sin, segment_ids, cotangent, weights, choice, which
):
    size, split, chips, experts_local = sizes
    w_query, w_key, w_value, w_out, w_gate, w_up, w_down = weights
    tok_rows, model_width = tokens.shape
    length = size * tok_rows
    local_width = w_query.shape[1]
    hidden_width = w_gate.shape[2]
    f32, half = jnp.float32, jnp.bfloat16
    vmem = pl.BlockSpec(memory_space=pltpu.VMEM)
    anywhere = pl.BlockSpec(memory_space=pl.ANY)
    kind = pltpu.SemaphoreType.DMA
    shape = jax.ShapeDtypeStruct
    return pl.pallas_call(
        functools.partial(front_kernel, sizes),
        out_shape=(
            shape((length, model_width), half),
            shape((3, model_width, local_width), half),
            shape((split, *w_out.shape), half),
            shape((length, local_width), half),
            shape((length, local_width), half),
            shape((length, local_width), half),
            shape((2, length, local_width), f32),
            shape((8, length), f32),
            shape((length, local_width), f32),
            shape((length, local_width), half),
            shape((tok_rows, model_width), f32),
            shape((length, model_width), half),
            shape((experts_local, size // 2, 2 * CAP, model_width), half),
            shape((model_width, hidden_width), half),
            shape((model_width, hidden_width), half),
            shape((hidden_width, model_width), half),
            shape((size, *choice.shape), choice.dtype),
            shape((size // 2, experts_local * 2 * CAP, 2 * tok_rows), half),
        ),
        in_specs=[vmem] * 7 + [anywhere] * 8 + [vmem],
        out_specs=tuple([anywhere] * 3 + [vmem] * 8 + [anywhere] * 5 + [vmem] * 2),
        scratch_shapes=[
            pltpu.VMEM((length, model_width), half),
            pltpu.VMEM((3, model_width, local_width), half),
            pltpu.VMEM((split, *w_out.shape), half),
            pltpu.VMEM((tok_rows, model_width), half),
            pltpu.VMEM((length, model_width), half),
            pltpu.VMEM((experts_local, size // 2, 2 * CAP, model_width), half),
            pltpu.VMEM((2, length, local_width), f32),
            pltpu.VMEM((8, length), f32),
            pltpu.VMEM((size, 8, length), f32),
            kind((3,)),
            kind((3, 3, chips)),
            kind((3, 2, chips)),
            kind((size,)),
            kind((size,)),
            kind((size,)),
            kind((size,)),
            kind,
            kind((experts_local,)),
            kind((experts_local,)),
            kind((4,)),
            kind((4, split)),
            kind((4, split)),
            kind((3,)),
            kind((3, split)),
            kind((3, split)),
            kind((3,)),
            *ChainReduce.scratch(chips, tok_rows, model_width),
        ],
        compiler_params=pltpu.CompilerParams(
            collective_id=which, has_side_effects=True, vmem_limit_bytes=58 * 2**20
        ),
        cost_estimate=pl.CostEstimate(
            flops=2 * length * model_width * local_width * 4,
            bytes_accessed=500 * 2**20,
            transcendentals=0,
        ),
    )(
        tokens,
        gain_rows,
        gain_cols,
        cos,
        sin,
        segment_ids.reshape(-1, 1),
        segment_ids.reshape(1, -1),
        cotangent,
        *weights,
        choice,
    )

def experts_kernel(
    sizes,
    routed_ref,
    choices_ref,
    onehot_ref,
    cotangent_rows_ref,
    router_ref,
    gains_ref,
    residual_ref,
    cotangent_ref,
    gate_ref,
    up_ref,
    down_ref,
    residual_grad_ref,
    out_grad_ref,
    gain_ref,
    router_grad_ref,
    combine_ref,
    hidden_out,
    grad_gate_ref,
    grad_up_ref,
    grad_down_ref,
    gate_full,
    up_full,
    down_full,
    upstream,
    pair_rows,
    outgoing,
    arrived,
    hidden,
    gate_grad,
    up_grad,
    back,
    gates,
    gates_out,
    gates_in,
    dots_out,
    dots_in,
    token_out,
    token_in,
    scales,
    load_sem,
    pair_sem,
    keep_sem,
    rows_send,
    rows_recv,
    gates_send,
    gates_recv,
    back_send,
    back_recv,
    dots_send,
    dots_recv,
    token_send,
    token_recv,
    *reduce_buffers,
):
    size, split, chips, experts_local = sizes
    f32, half = jnp.float32, jnp.bfloat16
    me, mine = lax.axis_index("seq"), lax.axis_index("fsdp")
    tok_rows, model_width = residual_ref.shape
    pairs = size // 2
    double = 2 * CAP
    wide = 2 * tok_rows
    hidden_width = gate_full.shape[1]
    rows_of = pairs * double
    part = model_width // split
    member = lax.rem(mine, experts_local)

    loads = [
        pltpu.make_async_copy(source, target, load_sem.at[index])
        for index, (source, target) in enumerate(
            (
                (gate_ref, gate_full),
                (up_ref, up_full),
                (down_ref, down_full),
                (cotangent_rows_ref, upstream),
            )
        )
    ]

    slots = pair_rows.shape[0]

    def pair_load(pair):
        slot = lax.rem(pair, slots)
        start = pl.multiple_of(pair * wide, wide)
        return pltpu.make_async_copy(
            routed_ref.at[pl.ds(start, wide)], pair_rows.at[slot], pair_sem.at[slot]
        )

    pair_load(0).start()
    for load in loads:
        load.start()
    greet_all(size, split)

    padded = size * 8
    expert_row = lax.broadcasted_iota(jnp.int32, (padded, tok_rows), 0)
    inner = lax.rem(expert_row, 8)
    expert_row = jnp.where(inner < experts_local, expert_row // 8 * experts_local + inner, -1)
    ones = jnp.ones((8, wide), f32)
    top_count = choices_ref.shape[1] // 2

    @pl.loop(0, pairs)
    def _(pair):
        pair_load(pair).wait()

        @pl.when((pair + 1 < pairs) & (slots > 1))
        def _():
            pair_load(pair + 1).start()

        rows = pair_rows[lax.rem(pair, slots)]
        logits = lax.dot_general(
            router_ref[...], rows, (((1,), (1,)), ((), ())), preferred_element_type=f32
        )
        for side in range(2):
            ids = choices_ref[pair * 2 + side]
            chosen = expert_row == ids[0:1, :]
            for choice in range(1, top_count):
                chosen = chosen | (expert_row == ids[choice : choice + 1, :])
            own = jnp.where(chosen, logits[:, side * tok_rows : (side + 1) * tok_rows], MASKED)
            grown = jnp.where(chosen, jnp.exp(own - jnp.max(own, 0, keepdims=True)), 0.0)
            gates[pair * 2 + side] = grown / jnp.sum(grown, 0, keepdims=True)
        placed = jnp.dot(onehot_ref[pair], rows, preferred_element_type=f32).astype(half)
        for move in range(experts_local):
            piece = placed[move * double : (move + 1) * double]
            if move:
                outgoing[move - 1, pair] = piece
            else:
                arrived[0, pair] = piece
            row = me * 8 + partner_of(member, move)
            weights = jnp.concatenate(
                [gates[pair * 2, pl.ds(row, 1), :], gates[pair * 2 + 1, pl.ds(row, 1), :]], 1
            )
            slot_rows = pl.ds(move * double, double)
            weighted = onehot_ref[pair, slot_rows, :].astype(f32) * weights
            combine_ref[pair, slot_rows, :] = weighted.astype(half)
            gates_out[move, pair] = row_sums(weighted, ones)

        @pl.when((pair + 1 < pairs) & (slots == 1))
        def _():
            pair_load(pair + 1).start()

    def mate(move):
        return {"fsdp": partner_of(mine, move)}

    def rows_copy(move):
        return pltpu.make_async_remote_copy(
            src_ref=outgoing.at[move - 1],
            dst_ref=arrived.at[move],
            send_sem=rows_send.at[move],
            recv_sem=rows_recv.at[move],
            device_id=mate(move),
        )

    def gates_copy(move):
        return pltpu.make_async_remote_copy(
            src_ref=gates_out.at[move],
            dst_ref=gates_in.at[move],
            send_sem=gates_send.at[move],
            recv_sem=gates_recv.at[move],
            device_id=mate(move),
        )

    def back_rows(move):
        return back.at[:, pl.ds(move * double, double), :]

    def back_copy(move):
        return pltpu.make_async_remote_copy(
            src_ref=outgoing.at[move - 1],
            dst_ref=back_rows(move),
            send_sem=back_send.at[move],
            recv_sem=back_recv.at[move],
            device_id=mate(move),
        )

    def dots_copy(move):
        return pltpu.make_async_remote_copy(
            src_ref=dots_out.at[move],
            dst_ref=dots_in.at[move],
            send_sem=dots_send.at[move],
            recv_sem=dots_recv.at[move],
            device_id=mate(move),
        )

    order = list(range(experts_local - 1, 0, -1))
    for move in order:
        gates_copy(move).start()
        rows_copy(move).start()
    gates_in[0] = gates_out[0]
    for load in loads:
        load.wait()

    cols_step = min(256, hidden_width)
    width_step = min(512, model_width)
    spread = (lax.broadcasted_iota(jnp.int32, (8, 128), 0) == 0).astype(f32)
    for move in [0] + order:
        if move:
            gates_copy(move).wait()
            rows_copy(move).wait()
        for pair in range(pairs):
            scales[pair * double : (pair + 1) * double, :] = column_of(
                gates_in[move, pair], spread
            )
        dots_out[move] = jnp.zeros_like(dots_out[move])

        @pl.loop(0, hidden_width // cols_step)
        def _(index):
            cols = pl.ds(pl.multiple_of(index * cols_step, cols_step), cols_step)
            rows = arrived[move].reshape(rows_of, model_width)
            pre = jnp.dot(rows, gate_full[:, cols], preferred_element_type=f32)
            up = jnp.dot(rows, up_full[:, cols], preferred_element_type=f32)
            plain = lax.dot_general(
                upstream[move].reshape(rows_of, model_width),
                down_full[cols, :],
                (((1,), (1,)), ((), ())),
                preferred_element_type=f32,
            )
            sigmoid = 1.0 / (1.0 + jnp.exp(-pre))
            active = pre * sigmoid
            made = (active * up).astype(half)
            hidden[move, :, :, cols] = made.reshape(pairs, double, cols_step)
            dots = made.astype(f32) * plain
            for pair in range(pairs):
                dots_out[move, pair] += row_sums(
                    dots[pair * double : (pair + 1) * double], jnp.ones((8, cols_step), f32)
                )
            scaled = plain * scales[:, 0:1]
            gate_back = scaled * up * sigmoid * (1.0 + pre * (1.0 - sigmoid))
            gate_grad[move, :, :, cols] = gate_back.astype(half).reshape(pairs, double, cols_step)
            up_grad[move, :, :, cols] = (
                (scaled * active).astype(half).reshape(pairs, double, cols_step)
            )

        for pair in range(pairs):
            scale = scales[pair * double : (pair + 1) * double, 0:1]
            upstream[move, pair] = (upstream[move, pair].astype(f32) * scale).astype(half)

        if move:
            dots_copy(move).start()
        else:
            dots_in[0] = dots_out[0]

        @pl.loop(0, model_width // width_step)
        def _(index):
            cols = pl.ds(pl.multiple_of(index * width_step, width_step), width_step)
            rows_grad = lax.dot_general(
                gate_grad[move].reshape(rows_of, hidden_width),
                gate_full[cols, :],
                (((1,), (1,)), ((), ())),
                preferred_element_type=f32,
            )
            rows_grad = rows_grad + lax.dot_general(
                up_grad[move].reshape(rows_of, hidden_width),
                up_full[cols, :],
                (((1,), (1,)), ((), ())),
                preferred_element_type=f32,
            )
            rows_grad = rows_grad.astype(half).reshape(pairs, double, width_step)
            if move:
                outgoing[move - 1, :, :, cols] = rows_grad
            else:
                back[:, 0:double, cols] = rows_grad

        if move:
            back_copy(move).start()

    own_rows = pl.ds(pl.multiple_of(me * tok_rows, tok_rows), tok_rows)
    own_load = pltpu.make_async_copy(
        routed_ref.at[own_rows], pair_rows.at[0, pl.ds(0, tok_rows)], pair_sem.at[0]
    )
    own_load.start()
    hidden_keep = pltpu.make_async_copy(hidden, hidden_out, keep_sem)
    hidden_keep.start()

    total_rows = experts_local * rows_of

    def flat(ref, cols):
        return ref[:, :, :, cols].reshape(total_rows, -1)

    def turned_dot(left, right):
        return lax.dot_general(
            left, right, (((0,), (0,)), ((), ())), preferred_element_type=f32
        )

    every = pl.ds(0, hidden_width)

    @pl.loop(0, split)
    def _(piece):
        cols = pl.ds(pl.multiple_of(piece * part, part), part)
        gate_full[cols, :] = turned_dot(flat(arrived, cols), flat(gate_grad, every)).astype(half)
        up_full[cols, :] = turned_dot(flat(arrived, cols), flat(up_grad, every)).astype(half)
        down_full[:, cols] = turned_dot(flat(hidden, every), flat(upstream, cols)).astype(half)

    grad_keeps = [
        pltpu.make_async_copy(source, target, load_sem.at[index])
        for index, (source, target) in enumerate(
            ((gate_full, grad_gate_ref), (up_full, grad_up_ref), (down_full, grad_down_ref))
        )
    ]
    for keep in grad_keeps:
        keep.start()

    for move in order:
        dots_copy(move).wait()
    token_out[...] = jnp.zeros_like(token_out)

    @pl.loop(0, pairs)
    def _(pair):
        for move in range(experts_local):
            found = jnp.dot(
                dots_in[move, pair],
                onehot_ref[pair, pl.ds(move * double, double), :].astype(f32),
                precision=HIGHEST,
                preferred_element_type=f32,
            )
            row = partner_of(member, move)
            for side in range(2):
                token_out[pair * 2 + side, pl.ds(row, 1), :] = found[
                    0:1, side * tok_rows : (side + 1) * tok_rows
                ]

    def token_copy(shift):
        peer = lax.rem(me + shift, size)
        return pltpu.make_async_remote_copy(
            src_ref=token_out.at[peer],
            dst_ref=token_in.at[me],
            send_sem=token_send.at[shift],
            recv_sem=token_recv.at[shift],
            device_id={"seq": peer},
        )

    for shift in range(1, size):
        token_copy(shift).start()
    token_in[me] = token_out[me]
    for move in order:
        back_copy(move).wait()

    reduce = ChainReduce(chips, residual_grad_ref, reduce_buffers)

    def product(index, store):
        side = pl.ds(pl.multiple_of(lax.rem(index, 2) * tok_rows, tok_rows), tok_rows)
        left = onehot_ref[index // 2, :, side]

        @pl.loop(0, model_width // width_step)
        def _(step):
            cols = pl.ds(pl.multiple_of(step * width_step, width_step), width_step)
            store(cols, turned_dot(left, back[index // 2, :, cols]))

    reduce.run(product)

    for shift in range(1, size):
        token_copy(shift).wait()
    own_gates = gates[me]
    grads = token_in[...].reshape(padded, tok_rows)
    mean = jnp.sum(own_gates * grads, 0, keepdims=True)
    logit_grad = (own_gates * (grads - mean)).astype(half)
    routed_grad = reduce.total[...] + turned_dot(logit_grad, router_ref[...])
    own_load.wait()
    router_grad_ref[...] = jnp.dot(
        logit_grad, pair_rows[0, 0:tok_rows, :], preferred_element_type=f32
    )
    residual = residual_ref[...]
    inverse = lax.rsqrt(jnp.mean(residual * residual, -1, keepdims=True) + EPSILON)
    unit = residual * inverse
    gain_ref[...] = jnp.broadcast_to(
        jnp.sum(routed_grad * unit, 0, keepdims=True), gain_ref.shape
    )
    routed_grad = routed_grad * gains_ref[1:2, :]
    routed_grad = inverse * (
        routed_grad - unit * jnp.mean(routed_grad * unit, -1, keepdims=True)
    )
    residual_grad = cotangent_ref[...].astype(f32) + routed_grad
    residual_grad_ref[...] = residual_grad
    out_grad_ref[...] = residual_grad.astype(half)
    reduce.sent()
    hidden_keep.wait()
    for keep in grad_keeps:
        keep.wait()


def experts(
    sizes,
    routed_seq,
    choices,
    onehot,
    cotangent_rows,
    router_rows,
    gain_rows,
    residual,
    cotangent,
    weights,
    which,
):
    size, split, chips, experts_local = sizes
    gate_full, up_full, down_full = weights
    model_width, hidden_width = gate_full.shape
    tok_rows = residual.shape[0]
    pairs, double = size // 2, 2 * CAP
    f32, half = jnp.float32, jnp.bfloat16
    vmem = pl.BlockSpec(memory_space=pltpu.VMEM)
    anywhere = pl.BlockSpec(memory_space=pl.ANY)
    kind = pltpu.SemaphoreType.DMA
    shape = jax.ShapeDtypeStruct
    few = kind((experts_local,))
    wide_rows = (experts_local, pairs, double, model_width)
    narrow_rows = (experts_local, pairs, double, hidden_width)
    flags = (experts_local, pairs, 8, double)
    return pl.pallas_call(
        functools.partial(experts_kernel, sizes),
        out_shape=(
            shape((tok_rows, model_width), f32),
            shape((tok_rows, model_width), half),
            shape((8, model_width), f32),
            shape((size * 8, model_width), f32),
            shape(onehot.shape, half),
            shape(narrow_rows, half),
            shape(gate_full.shape, half),
            shape(up_full.shape, half),
            shape(down_full.shape, half),
        ),
        in_specs=[anywhere, vmem, vmem, anywhere] + [vmem] * 4 + [anywhere] * 3,
        out_specs=tuple([vmem] * 5 + [anywhere] * 4),
        scratch_shapes=[
            pltpu.VMEM(gate_full.shape, half),
            pltpu.VMEM(up_full.shape, half),
            pltpu.VMEM(down_full.shape, half),
            pltpu.VMEM(wide_rows, half),
            pltpu.VMEM((2 if chips < 8 else 1, 2 * tok_rows, model_width), half),
            pltpu.VMEM((max(experts_local - 1, 1), *wide_rows[1:]), half),
            pltpu.VMEM(wide_rows, half),
            pltpu.VMEM(narrow_rows, half),
            pltpu.VMEM(narrow_rows, half),
            pltpu.VMEM(narrow_rows, half),
            pltpu.VMEM((pairs, experts_local * double, model_width), half),
            pltpu.VMEM((size, size * 8, tok_rows), f32),
            pltpu.VMEM(flags, f32),
            pltpu.VMEM(flags, f32),
            pltpu.VMEM(flags, f32),
            pltpu.VMEM(flags, f32),
            pltpu.VMEM((size, 8, tok_rows), f32),
            pltpu.VMEM((size, 8, tok_rows), f32),
            pltpu.VMEM((pairs * double, 128), f32),
            kind((4,)),
            kind((2,)),
            kind,
            few,
            few,
            few,
            few,
            few,
            few,
            few,
            few,
            kind((size,)),
            kind((size,)),
            *ChainReduce.scratch(chips, tok_rows, model_width),
        ],
        compiler_params=pltpu.CompilerParams(
            collective_id=which, has_side_effects=True, vmem_limit_bytes=63 * 2**20
        ),
        cost_estimate=pl.CostEstimate(
            flops=2 * experts_local * pairs * double * model_width * hidden_width * 8,
            bytes_accessed=500 * 2**20,
            transcendentals=0,
        ),
    )(
        routed_seq,
        choices,
        onehot,
        cotangent_rows,
        router_rows,
        gain_rows,
        residual,
        cotangent,
        gate_full,
        up_full,
        down_full,
    )


def shards(
    tokens,
    norm_gains,
    w_query,
    w_key,
    w_value,
    w_out,
    w_router,
    w_gate,
    w_up,
    w_down,
    segment_ids,
    expert_ids,
    expert_slots,
    cotangent,
):
    half_type = jnp.bfloat16
    float_type = jnp.float32
    tok_rows = tokens.shape[0]
    model_width = tokens.shape[1]
    expert_total = w_router.shape[1]
    top_count = expert_ids.shape[1]
    head_size = HEAD_DIM
    local_width = w_query.shape[1]
    heads_local = local_width // head_size
    capacity = CAP
    column_start = lax.axis_index("seq") * local_width
    experts_local = w_gate.shape[0]
    seq_size = lax.axis_size("seq")
    split = lax.axis_size("fsdp")
    groups = split // experts_local
    shard_index = lax.axis_index("fsdp")

    def pick(stack, index):
        return lax.dynamic_index_in_dim(stack, index, 0, keepdims=False)

    def to_shards(grad, dim):
        part = grad.shape[dim] // split
        shape = [experts_local, *grad.shape]
        shape[dim + 1] = part
        owned = jnp.zeros(shape, float_type)
        for shift in range(split):
            dest = lax.rem(shard_index + shift, split)
            piece = lax.dynamic_slice_in_dim(grad, dest * part, part, dim).astype(half_type)
            if shift:
                links = [(one, (one + shift) % split) for one in range(split)]
                piece = lax.ppermute(piece, "fsdp", links)
            expert = lax.rem(shard_index - shift + split, experts_local)
            piece = piece.astype(float_type)
            if groups > 1:
                piece = piece + pick(owned, expert)
            owned = lax.dynamic_update_index_in_dim(owned, piece, expert, 0)
        return owned

    places = jnp.where(expert_slots < capacity, expert_ids * capacity + expert_slots, -(10**6))
    gain_rows = norm_gains.astype(float_type)
    gain_cols = lax.dynamic_slice_in_dim(gain_rows, column_start, local_width, 1)
    inputs = tokens.astype(float_type)
    inverse_first = inverse_rms(inputs)
    unit_first = inputs * inverse_first
    length = seq_size * tok_rows
    sizes = (seq_size, split, seq_size // 2, experts_local)
    positions = jnp.arange(length, dtype=jnp.int32)
    cosine_table, sine_table = rope_tables(positions, head_size)
    cosine_wide = jnp.concatenate([cosine_table, cosine_table], 1)
    sine_wide = jnp.concatenate([-sine_table, sine_table], 1)
    (
        normed_seq,
        qkv_stack,
        out_stack,
        query_heads,
        key_heads,
        value_heads,
        unit_pair,
        square_sums,
        log_wide,
        attended_heads,
        residual,
        routed_seq,
        cotangent_rows,
        gate_full,
        up_full,
        down_full,
        choices,
        onehot,
    ) = front(
        sizes,
        tokens,
        gain_rows,
        gain_cols,
        cosine_wide,
        sine_wide,
        segment_ids,
        cotangent,
        (w_query, w_key, w_value, w_out, w_gate, w_up, w_down),
        jnp.concatenate([expert_ids, places], 1).T,
        0,
    )
    unit_query, unit_key = unit_pair[0], unit_pair[1]
    inverse_query = lax.rsqrt(square_sums[0] / model_width + EPSILON)[:, None]
    inverse_key = lax.rsqrt(square_sums[1] / model_width + EPSILON)[:, None]
    qkv_cols = jnp.concatenate([qkv_stack[0], qkv_stack[1], qkv_stack[2]], 1)
    out_rows = out_stack.transpose(1, 0, 2).reshape(local_width, model_width)
    block_rows = math.gcd(512, length)
    blocks = length // block_rows
    score_scale = head_size ** (-0.5)
    query_cube = query_heads.reshape(blocks, block_rows, heads_local, head_size)
    key_cube = key_heads.reshape(length, heads_local, head_size)
    value_cube = value_heads.reshape(length, heads_local, head_size)
    segment_blocks = segment_ids.reshape(blocks, block_rows)
    log_sums = log_wide.reshape(blocks, block_rows, heads_local, head_size)[..., 0]
    log_sums = log_sums.transpose(0, 2, 1)

    def block_scores(query_block, segment_block):
        scores = (
            jnp.einsum("qhd,khd->hqk", query_block, key_cube, preferred_element_type=float_type)
            * score_scale
        )
        visible = segment_block[:, None] == segment_ids[None, :]
        return jnp.where(visible[None], scores, MASKED)

    router_rows = jnp.zeros((seq_size, 8, model_width), half_type)
    router_rows = router_rows.at[:, :experts_local].set(
        w_router.T.reshape(seq_size, experts_local, model_width)
    )
    router_rows = router_rows.reshape(seq_size * 8, model_width)
    (
        residual_grad,
        out_grad,
        gain_second_grad,
        router_grad_rows,
        combine,
        hidden,
        grad_gate_full,
        grad_up_full,
        grad_down_full,
    ) = experts(
        sizes,
        routed_seq,
        choices,
        onehot,
        cotangent_rows,
        router_rows,
        gain_rows,
        residual,
        cotangent,
        (gate_full, up_full, down_full),
        1,
    )
    gain_second_grad = gain_second_grad[0]
    grad_router_local = router_grad_rows.reshape(seq_size, 8, model_width)[:, :experts_local]
    grad_router_local = grad_router_local.reshape(expert_total, model_width)
    pairs = seq_size // 2
    returned = jnp.einsum(
        "mpsf,fd->mpsd", hidden, down_full, preferred_element_type=float_type
    ).astype(half_type)
    incoming = []
    for move in range(experts_local):
        piece = returned[move]
        if move:
            piece = lax.ppermute(piece, "fsdp", [(one, one ^ move) for one in range(split)])
        incoming.append(piece)
    mixture = jnp.einsum(
        "pst,psd->ptd",
        combine,
        jnp.concatenate(incoming, 1),
        preferred_element_type=float_type,
    ).astype(half_type)
    mixture = lax.psum_scatter(
        mixture.reshape(length, model_width), "seq", scatter_dimension=0, tiled=True
    ).astype(float_type)
    output = (residual + mixture).astype(half_type)
    out_grad_seq = seq_gather(out_grad, seq_size, 2)
    grad_out_local = jnp.einsum(
        "th,td->hd", attended_heads, out_grad_seq, preferred_element_type=float_type
    )
    attended_grad = jnp.einsum(
        "td,hd->th", out_grad_seq, out_rows, preferred_element_type=float_type
    ).astype(half_type)
    grad_cube = attended_grad.reshape(blocks, block_rows, heads_local, head_size)

    def attend_back(running, pieces):
        key_acc, value_acc = running
        query_block, segment_block, grad_block, log_block = pieces
        scores = block_scores(query_block, segment_block)
        soft_values = jnp.exp(scores - log_block[..., None])
        prob_grad = jnp.einsum(
            "qhd,khd->hqk", grad_block, value_cube, preferred_element_type=float_type
        )
        center = jnp.sum(soft_values * prob_grad, -1, keepdims=True)
        score_grad = (soft_values * (prob_grad - center)).astype(half_type)
        query_grad = (
            jnp.einsum("hqk,khd->qhd", score_grad, key_cube, preferred_element_type=float_type)
            * score_scale
        )
        key_acc = (
            key_acc
            + jnp.einsum("hqk,qhd->khd", score_grad, query_block, preferred_element_type=float_type)
            * score_scale
        )
        value_acc = value_acc + jnp.einsum(
            "hqk,qhd->khd",
            soft_values.astype(half_type),
            grad_block,
            preferred_element_type=float_type,
        )
        return ((key_acc, value_acc), query_grad.astype(half_type))

    empty_acc = jnp.zeros((length, heads_local, head_size), float_type)
    (key_acc, value_acc), query_grads = lax.scan(
        attend_back, (empty_acc, empty_acc), (query_cube, segment_blocks, grad_cube, log_sums)
    )
    query_back = query_grads.reshape(length, local_width)
    key_back = key_acc.reshape(length, local_width).astype(half_type)
    value_back = value_acc.reshape(length, local_width).astype(half_type)
    query_unit_grad = rotate(query_back.astype(float_type), cosine_table, -sine_table, head_size)
    key_unit_grad = rotate(key_back.astype(float_type), cosine_table, -sine_table, head_size)
    gain_query_grad = jnp.sum(query_unit_grad * unit_query, axis=0)
    gain_key_grad = jnp.sum(key_unit_grad * unit_key, axis=0)
    query_scaled = query_unit_grad * gain_cols[2]
    key_scaled = key_unit_grad * gain_cols[3]
    centers = seq_sum(
        (jnp.sum(query_scaled * unit_query, -1), jnp.sum(key_scaled * unit_key, -1)), seq_size, 3
    )
    query_raw_grad = (
        inverse_query * (query_scaled - unit_query * (centers[0] / model_width)[:, None])
    ).astype(half_type)
    key_raw_grad = (
        inverse_key * (key_scaled - unit_key * (centers[1] / model_width)[:, None])
    ).astype(half_type)
    raw_grads = jnp.concatenate([query_raw_grad, key_raw_grad, value_back], 1)
    raw_blocks = raw_grads.reshape(seq_size, tok_rows, 3 * local_width)
    normed_grad = seq_reduce(raw_blocks, qkv_cols, model_width, True, 5)
    grad_qkv_local = jnp.einsum("td,th->dh", normed_seq, raw_grads, preferred_element_type=float_type)
    gain_first_grad = jnp.sum(normed_grad * unit_first, axis=0)
    input_grad = residual_grad + norm_back(normed_grad * gain_rows[0], unit_first, inverse_first)
    zero_row = jnp.zeros((model_width,), float_type)
    gain_query_full = lax.dynamic_update_slice_in_dim(zero_row, gain_query_grad, column_start, 0)
    gain_key_full = lax.dynamic_update_slice_in_dim(zero_row, gain_key_grad, column_start, 0)
    gain_grads = jnp.stack([gain_first_grad, gain_second_grad, gain_query_full, gain_key_full])
    small = jnp.concatenate([gain_grads, jnp.zeros_like(gain_grads), grad_router_local])
    small = total_sum(small, seq_size, split, 6)
    gain_sums, router_grad = small[:4], small[8:].T
    qkv_owned = lax.psum_scatter(
        grad_qkv_local.astype(half_type), "fsdp", scatter_dimension=0, tiled=True
    ).astype(float_type)
    out_owned = lax.psum_scatter(
        grad_out_local.astype(half_type), "fsdp", scatter_dimension=1, tiled=True
    ).astype(float_type)
    return (
        output,
        input_grad,
        gain_sums,
        qkv_owned[:, :local_width],
        qkv_owned[:, local_width : 2 * local_width],
        qkv_owned[:, 2 * local_width :],
        out_owned,
        router_grad,
        to_shards(grad_gate_full, 0),
        to_shards(grad_up_full, 0),
        to_shards(grad_down_full, 1),
    )


def solution(mesh):
    in_specs = (
        P(("fsdp", "seq"), None),
        P(),
        P("fsdp", "seq"),
        P("fsdp", "seq"),
        P("fsdp", "seq"),
        P("seq", "fsdp"),
        P(),
        P("seq", "fsdp", None),
        P("seq", "fsdp", None),
        P("seq", None, "fsdp"),
        P("fsdp"),
        P(("fsdp", "seq"), None),
        P(("fsdp", "seq"), None),
        P(("fsdp", "seq"), None),
    )
    out_specs = (
        P(("fsdp", "seq"), None),
        P(("fsdp", "seq"), None),
        P(),
        P("fsdp", "seq"),
        P("fsdp", "seq"),
        P("fsdp", "seq"),
        P("seq", "fsdp"),
        P(),
        P("seq", "fsdp", None),
        P("seq", "fsdp", None),
        P("seq", None, "fsdp"),
    )
    return jax.shard_map(shards, mesh=mesh, in_specs=in_specs, out_specs=out_specs, check_vma=False)
```

```python
import functools

import jax
import jax.numpy as jnp
from jax import lax
from jax.experimental import pallas as pl
from jax.experimental.pallas import tpu as pltpu
from jax.sharding import PartitionSpec as P

HEAD_DIM = 128
CAP = 40


EPSILON = 1e-06
THETA = 10000.0
MASKED = -1e30
HIGHEST = lax.Precision.HIGHEST


def rope_tables(positions, head_size):
    half_dim = head_size // 2
    frequency = THETA ** (-jnp.arange(half_dim, dtype=jnp.float32) / half_dim)
    angles = positions.astype(jnp.float32)[:, None] * frequency[None, :]
    return (jnp.cos(angles), jnp.sin(angles))


class ChainGather:
    def __init__(self, chips, x_ref, out_ref, local_sem, sends, arrivals):
        self.chips, self.x_ref, self.out_ref = chips, x_ref, out_ref
        self.local_sem, self.sends, self.arrivals = local_sem, sends, arrivals
        me = lax.axis_index("seq")
        self.chip, self.core = me // 2, lax.rem(me, 2)
        self.rows = x_ref.shape[0]

    def block(self, source, core):
        start = pl.multiple_of((source * 2 + core) * self.rows, self.rows)
        return self.out_ref.at[pl.ds(start, self.rows)]

    def hop(self, source, ref, target, way, lane):
        return pltpu.make_async_remote_copy(
            src_ref=ref,
            dst_ref=self.block(source, self.core),
            send_sem=self.sends.at[way, source],
            recv_sem=self.arrivals.at[lane, source],
            device_id={"seq": target},
        )

    def upward(self, source, ref):
        return self.hop(source, ref, self.chip * 2 + 2 + self.core, 0, 0)

    def downward(self, source, ref):
        return self.hop(source, ref, self.chip * 2 - 2 + self.core, 1, 0)

    def sideways(self, source, ref):
        return self.hop(source, ref, self.chip * 2 + 1 - self.core, 2, 1)

    def own(self):
        return pltpu.make_async_copy(
            self.x_ref, self.block(self.chip, self.core), self.local_sem
        )

    def start(self):
        @pl.when(self.chip < self.chips - 1)
        def _():
            self.upward(self.chip, self.x_ref).start()

        @pl.when(self.chip > 0)
        def _():
            self.downward(self.chip, self.x_ref).start()

        self.sideways(self.chip, self.x_ref).start()
        self.own().start()

    def step(self, distance):
        below, above = self.chip - distance, self.chip + distance

        @pl.when(below >= 0)
        def _():
            landed = self.block(below, self.core)
            self.upward(below, landed).wait_recv()

            @pl.when(self.chip < self.chips - 1)
            def _():
                self.upward(below, landed).start()

            self.sideways(below, landed).start()

        @pl.when(above < self.chips)
        def _():
            landed = self.block(above, self.core)
            self.downward(above, landed).wait_recv()

            @pl.when(self.chip > 0)
            def _():
                self.downward(above, landed).start()

            self.sideways(above, landed).start()

    def steps(self):
        for distance in range(1, self.chips):
            self.step(distance)

    def landed(self):
        self.own().wait()
        for source in range(self.chips):
            self.sideways(source, self.block(source, self.core)).wait_recv()

    def sent(self):
        for source in range(self.chips):
            ref = self.block(source, self.core)
            self.sideways(source, ref).wait_send()

            @pl.when((self.chip < self.chips - 1) & (source <= self.chip))
            def _():
                self.upward(source, ref).wait_send()

            @pl.when((self.chip > 0) & (source >= self.chip))
            def _():
                self.downward(source, ref).wait_send()


class ChainReduce:
    def __init__(self, chips, total, buffers):
        self.total = total
        (
            self.side_out,
            self.side_in,
            self.chain_in,
            self.side_send,
            self.side_recv,
            self.chain_send,
            self.chain_recv,
        ) = buffers
        self.chips = chips
        me = lax.axis_index("seq")
        self.chip, self.core = me // 2, lax.rem(me, 2)

    @staticmethod
    def scratch(chips, rows, width):
        half = jnp.bfloat16
        return [
            pltpu.VMEM((chips, rows, width), half),
            pltpu.VMEM((chips, rows, width), half),
            pltpu.VMEM((chips + 1, rows, width), half),
            pltpu.SemaphoreType.DMA((chips,)),
            pltpu.SemaphoreType.DMA((chips,)),
            pltpu.SemaphoreType.DMA((chips,)),
            pltpu.SemaphoreType.DMA((2, chips)),
        ]

    def side_copy(self, dest):
        return pltpu.make_async_remote_copy(
            src_ref=self.side_out.at[dest],
            dst_ref=self.side_in.at[dest],
            send_sem=self.side_send.at[dest],
            recv_sem=self.side_recv.at[dest],
            device_id={"seq": self.chip * 2 + 1 - self.core},
        )

    def chain_copy(self, way, dest, target):
        return pltpu.make_async_remote_copy(
            src_ref=self.side_out.at[dest],
            dst_ref=self.chain_in.at[self.slot(way, dest, target // 2)],
            send_sem=self.chain_send.at[dest],
            recv_sem=self.chain_recv.at[way, dest],
            device_id={"seq": target},
        )

    def slot(self, way, dest, holder):
        return jnp.where(dest == holder, self.chips, dest) if way else dest

    def place(self, index):
        distance = self.chips - 1 - index // 2
        dest = self.chip + (1 - 2 * lax.rem(index, 2)) * distance
        return dest, (dest >= 0) & (dest < self.chips)

    def run(self, product, between=None):
        chips, chip, core, total = self.chips, self.chip, self.core, self.total
        sibling = chip * 2 + 1 - core

        @pl.loop(0, 2 * chips - 1)
        def _(index):
            dest, inside = self.place(index)

            @pl.when(inside)
            def _():
                def store(cols, part):
                    self.side_out[dest, :, cols] = part.astype(self.side_out.dtype)

                product(dest * 2 + 1 - core, store)
                self.side_copy(dest).start()

        if between:
            between()

        @pl.loop(0, 2 * chips - 1)
        def _(index):
            dest, inside = self.place(index)

            @pl.when(inside)
            def _():
                def store(cols, part):
                    total[:, cols] = part

                product(dest * 2 + core, store)
                self.side_copy(dest).wait_recv()
                total[...] += self.side_in[dest].astype(jnp.float32)

                @pl.when((dest >= chip) & (chip > 0))
                def _():
                    self.chain_copy(0, dest, sibling).wait_recv()
                    total[...] += self.chain_in[dest].astype(jnp.float32)

                @pl.when((dest <= chip) & (chip < chips - 1))
                def _():
                    self.chain_copy(1, dest, sibling).wait_recv()
                    total[...] += self.chain_in[self.slot(1, dest, chip)].astype(jnp.float32)

                self.side_copy(dest).wait_send()

                @pl.when(dest != chip)
                def _():
                    self.side_out[dest] = total[...].astype(self.side_out.dtype)

                @pl.when(dest > chip)
                def _():
                    self.chain_copy(0, dest, chip * 2 + 2 + core).start()

                @pl.when(dest < chip)
                def _():
                    self.chain_copy(1, dest, chip * 2 - 2 + core).start()

    def sent(self):
        sibling = self.chip * 2 + 1 - self.core

        @pl.loop(0, self.chips)
        def _(dest):
            @pl.when(dest != self.chip)
            def _():
                self.chain_copy(0, dest, sibling).wait_send()


def partner_of(index, move):
    turned, bit = index, 1
    while bit <= move:
        if move // bit % 2:
            turned = turned + bit - 2 * bit * lax.rem(index // bit, 2)
        bit *= 2
    return turned


def greet_all(size, split):
    me, mine = lax.axis_index("seq"), lax.axis_index("fsdp")
    barrier = pltpu.get_barrier_semaphore()
    for shift in range(1, size):
        pl.semaphore_signal(barrier, inc=1, device_id={"seq": lax.rem(me + shift, size)})
    for shift in range(1, split):
        pl.semaphore_signal(barrier, inc=1, device_id={"fsdp": lax.rem(mine + shift, split)})
    pl.semaphore_wait(barrier, size + split - 2)


def turned_halves(head):
    return pltpu.roll(head, head.shape[-1] // 2, 1)


def row_sums(values, pick):
    return lax.dot_general(
        pick, values, (((1,), (1,)), ((), ())), precision=HIGHEST, preferred_element_type=jnp.float32
    )


def column_of(row_form, pick):
    return lax.dot_general(
        row_form, pick, (((0,), (0,)), ((), ())), precision=HIGHEST, preferred_element_type=jnp.float32
    )


def front_kernel(
    sizes,
    tokens_ref,
    gains_ref,
    gain_cols_ref,
    cos_ref,
    sin_ref,
    seg_col_ref,
    seg_row_ref,
    cotangent_ref,
    wq_ref,
    wk_ref,
    wv_ref,
    wo_ref,
    w_gate_ref,
    w_up_ref,
    w_down_ref,
    choice_ref,
    normed_out,
    qkv_out,
    rows_out,
    q_ref,
    k_ref,
    v_ref,
    unit_ref,
    sums_ref,
    log_ref,
    attended_ref,
    residual_ref,
    routed_out,
    cotangent_rows,
    gate_full,
    up_full,
    down_full,
    choices,
    onehot_ref,
    normed,
    qkv,
    rows_full,
    routed_own,
    cotangent_all,
    placed,
    raw,
    sums_own,
    sums_in,
    gather_local,
    gather_send,
    gather_recv,
    sums_send,
    sums_recv,
    choice_send,
    choice_recv,
    placed_local,
    placed_send,
    placed_recv,
    shard_local,
    shard_send,
    shard_recv,
    expert_local,
    expert_send,
    expert_recv,
    out_sem,
    *reduce_buffers,
):
    size, split, chips, experts_local = sizes
    f32, half = jnp.float32, jnp.bfloat16
    me, mine = lax.axis_index("seq"), lax.axis_index("fsdp")
    tok_rows, model_width = tokens_ref.shape
    length, local_width = q_ref.shape
    part = model_width // split
    head = HEAD_DIM
    heads = local_width // head

    inputs = tokens_ref[...].astype(f32)
    inverse = lax.rsqrt(jnp.mean(inputs * inputs, -1, keepdims=True) + EPSILON)
    own_rows = pl.ds(pl.multiple_of(me * tok_rows, tok_rows), tok_rows)
    routed_own[...] = (inputs * inverse * gains_ref[0:1, :]).astype(half)
    greet_all(size, split)

    def gather(index, x_ref, out_ref):
        return ChainGather(
            chips,
            x_ref,
            out_ref,
            gather_local.at[index],
            gather_send.at[index],
            gather_recv.at[index],
        )

    first = gather(0, routed_own, normed)
    first.start()

    def choice_copy(shift):
        return pltpu.make_async_remote_copy(
            src_ref=choice_ref,
            dst_ref=choices.at[me],
            send_sem=choice_send.at[shift],
            recv_sem=choice_recv.at[shift],
            device_id={"seq": lax.rem(me + shift, size)},
        )

    own_part = pl.ds(pl.multiple_of(mine * part, part), part)
    shard_pairs = (
        (wq_ref, qkv.at[0, own_part]),
        (wk_ref, qkv.at[1, own_part]),
        (wv_ref, qkv.at[2, own_part]),
        (wo_ref, rows_full.at[mine]),
    )

    def shard_copy(index, shift):
        source, target = shard_pairs[index]
        return pltpu.make_async_remote_copy(
            src_ref=source,
            dst_ref=target,
            send_sem=shard_send.at[index, shift],
            recv_sem=shard_recv.at[index, shift],
            device_id={"fsdp": lax.rem(mine + shift, split)},
        )

    def shard_own(index):
        source, target = shard_pairs[index]
        return pltpu.make_async_copy(source, target, shard_local.at[index])

    for index in range(4):
        for shift in range(1, split):
            shard_copy(index, shift).start()
        shard_own(index).start()

    def expert_pair(index, dest):
        expert = lax.rem(dest, experts_local)
        if index == 2:
            return w_down_ref.at[expert], down_full.at[:, own_part]
        source, target = ((w_gate_ref, gate_full), (w_up_ref, up_full))[index]
        return source.at[expert], target.at[own_part]

    def expert_copy(index, shift):
        dest = lax.rem(mine + shift, split)
        source, target = expert_pair(index, dest)
        return pltpu.make_async_remote_copy(
            src_ref=source,
            dst_ref=target,
            send_sem=expert_send.at[index, shift],
            recv_sem=expert_recv.at[index, shift],
            device_id={"fsdp": dest},
        )

    def expert_own(index):
        source, target = expert_pair(index, mine)
        return pltpu.make_async_copy(source, target, expert_local.at[index])

    first.steps()
    for index in range(4):
        shard_own(index).wait()
        for shift in range(1, split):
            shard_copy(index, shift).wait_recv()
    for index in range(3):
        for shift in range(1, split):
            expert_copy(index, shift).start()
        expert_own(index).start()
    first.landed()
    for shift in range(1, size):
        choice_copy(shift).start()
    choices[me] = choice_ref[...]
    second = gather(1, cotangent_ref, cotangent_all)
    second.start()
    keeps = [
        pltpu.make_async_copy(normed, normed_out, out_sem.at[0]),
        pltpu.make_async_copy(qkv, qkv_out, out_sem.at[1]),
        pltpu.make_async_copy(rows_full, rows_out, out_sem.at[2]),
    ]
    for keep in keeps:
        keep.start()

    block = min(512, length)
    lanes = lax.broadcasted_iota(jnp.int32, (8, local_width), 0)
    first_row, second_row = (lanes == 0).astype(f32), (lanes == 1).astype(f32)

    @pl.loop(0, length // block)
    def _(step):
        rows = pl.ds(pl.multiple_of(step * block, block), block)
        left = normed[rows, :]
        query = jnp.dot(left, qkv[0], preferred_element_type=f32)
        raw[0, rows, :] = query
        keys = jnp.dot(left, qkv[1], preferred_element_type=f32)
        raw[1, rows, :] = keys
        sums_own[:, rows] = row_sums(query * query, first_row) + row_sums(keys * keys, second_row)
        v_ref[rows, :] = jnp.dot(left, qkv[2], preferred_element_type=f32).astype(half)

    def sums_copy(shift):
        return pltpu.make_async_remote_copy(
            src_ref=sums_own,
            dst_ref=sums_in.at[me],
            send_sem=sums_send.at[shift],
            recv_sem=sums_recv.at[shift],
            device_id={"seq": lax.rem(me + shift, size)},
        )

    for shift in range(1, size):
        sums_copy(shift).start()
    sums_in[me] = sums_own[...]
    for shift in range(1, size):
        sums_copy(shift).wait()
    sums_ref[...] = jnp.sum(sums_in[...], 0)

    @pl.loop(0, length // block)
    def _(step):
        rows = pl.ds(pl.multiple_of(step * block, block), block)
        square_sums = sums_ref[:, rows]
        for index, pick, target in ((0, first_row, q_ref), (1, second_row, k_ref)):
            scale = lax.rsqrt(column_of(square_sums, pick) / model_width + EPSILON)
            unit = raw[index, rows, :] * scale
            unit_ref[index, rows, :] = unit
            scaled = unit * gain_cols_ref[2 + index : 3 + index, :]
            for number in range(heads):
                cols = slice(number * head, (number + 1) * head)
                piece = scaled[:, cols]
                target[rows, cols] = (
                    piece * cos_ref[rows, :] + turned_halves(piece) * sin_ref[rows, :]
                ).astype(half)

    second.step(1)

    wide = min(256, length)
    for number in range(heads):
        cols = slice(number * head, (number + 1) * head)

        @pl.loop(0, length // wide)
        def _(step):
            rows = pl.ds(pl.multiple_of(step * wide, wide), wide)
            scores = lax.dot_general(
                q_ref[rows, cols],
                k_ref[:, cols],
                (((1,), (1,)), ((), ())),
                preferred_element_type=f32,
            )
            scores = scores * (head**-0.5)
            scores = jnp.where(seg_col_ref[rows, :] == seg_row_ref[...], scores, MASKED)
            peak = jnp.max(scores, -1, keepdims=True)
            grown = jnp.exp(scores - peak)
            weight = jnp.sum(grown, -1, keepdims=True)
            probs = (grown * (1.0 / weight)).astype(half)
            attended_ref[rows, cols] = jnp.dot(
                probs, v_ref[:, cols], preferred_element_type=f32
            ).astype(half)
            log_ref[rows, cols] = jnp.broadcast_to(peak + jnp.log(weight), (wide, head))

        if number + 2 < chips:
            second.step(number + 2)

    for distance in range(heads + 2, chips):
        second.step(distance)

    reduce = ChainReduce(chips, residual_ref, reduce_buffers)

    def product(index, store):
        left = attended_ref[pl.ds(pl.multiple_of(index * tok_rows, tok_rows), tok_rows), :]
        for piece in range(split):
            cols = pl.ds(piece * part, part)
            store(cols, jnp.dot(left, rows_full[piece], preferred_element_type=f32))

    reduce.run(product)
    residual = tokens_ref[...].astype(f32) + reduce.total[...]
    residual_ref[...] = residual
    inverse = lax.rsqrt(jnp.mean(residual * residual, -1, keepdims=True) + EPSILON)
    first.sent()
    routed_own[...] = (residual * inverse * gains_ref[1:2, :]).astype(half)
    third = gather(2, routed_own, routed_out)
    third.start()
    third.steps()
    third.landed()

    second.landed()
    for shift in range(1, size):
        choice_copy(shift).wait()
    double = 2 * CAP
    member = lax.rem(mine, experts_local)
    top_count = choice_ref.shape[0] // 2
    slot_row = lax.broadcasted_iota(jnp.int32, (double, tok_rows), 0)

    @pl.loop(0, size // 2)
    def _(pair):
        for move in range(experts_local):
            base = (me * experts_local + partner_of(member, move)) * CAP
            for side in range(2):
                want = jnp.where(slot_row // CAP == side, slot_row - side * CAP + base, -1)
                places = choices[pair * 2 + side]
                hit = want == places[top_count : top_count + 1, :]
                for choice in range(1, top_count):
                    hit = hit | (want == places[top_count + choice : top_count + choice + 1, :])
                cols = slice(side * tok_rows, (side + 1) * tok_rows)
                onehot_ref[pair, move * double : (move + 1) * double, cols] = jnp.where(
                    hit, 1.0, 0.0
                ).astype(half)
        start = pl.multiple_of(pair * 2 * tok_rows, 2 * tok_rows)
        made = jnp.dot(
            onehot_ref[pair], cotangent_all[pl.ds(start, 2 * tok_rows), :], preferred_element_type=f32
        ).astype(half)
        for move in range(experts_local):
            placed[move, pair] = made[move * double : (move + 1) * double]

    def placed_copy(move):
        return pltpu.make_async_remote_copy(
            src_ref=placed.at[move],
            dst_ref=cotangent_rows.at[move],
            send_sem=placed_send.at[move],
            recv_sem=placed_recv.at[move],
            device_id={"fsdp": partner_of(mine, move)},
        )

    for move in range(experts_local - 1, 0, -1):
        placed_copy(move).start()
    placed_own = pltpu.make_async_copy(placed.at[0], cotangent_rows.at[0], placed_local)
    placed_own.start()

    reduce.sent()
    second.sent()
    third.sent()
    for index in range(4):
        for shift in range(1, split):
            shard_copy(index, shift).wait_send()
    for keep in keeps:
        keep.wait()
    placed_own.wait()
    for move in range(1, experts_local):
        placed_copy(move).wait()
    for index in range(3):
        expert_own(index).wait()
        for shift in range(1, split):
            expert_copy(index, shift).wait()


def front(
    sizes, tokens, gain_rows, gain_cols, cos, sin, segment_ids, cotangent, weights, choice, which
):
    size, split, chips, experts_local = sizes
    w_query, w_key, w_value, w_out, w_gate, w_up, w_down = weights
    tok_rows, model_width = tokens.shape
    length = size * tok_rows
    local_width = w_query.shape[1]
    hidden_width = w_gate.shape[2]
    f32, half = jnp.float32, jnp.bfloat16
    vmem = pl.BlockSpec(memory_space=pltpu.VMEM)
    anywhere = pl.BlockSpec(memory_space=pl.ANY)
    kind = pltpu.SemaphoreType.DMA
    shape = jax.ShapeDtypeStruct
    return pl.pallas_call(
        functools.partial(front_kernel, sizes),
        out_shape=(
            shape((length, model_width), half),
            shape((3, model_width, local_width), half),
            shape((split, *w_out.shape), half),
            shape((length, local_width), half),
            shape((length, local_width), half),
            shape((length, local_width), half),
            shape((2, length, local_width), f32),
            shape((8, length), f32),
            shape((length, local_width), f32),
            shape((length, local_width), half),
            shape((tok_rows, model_width), f32),
            shape((length, model_width), half),
            shape((experts_local, size // 2, 2 * CAP, model_width), half),
            shape((model_width, hidden_width), half),
            shape((model_width, hidden_width), half),
            shape((hidden_width, model_width), half),
            shape((size, *choice.shape), choice.dtype),
            shape((size // 2, experts_local * 2 * CAP, 2 * tok_rows), half),
        ),
        in_specs=[vmem] * 7 + [anywhere] * 8 + [vmem],
        out_specs=tuple([anywhere] * 3 + [vmem] * 8 + [anywhere] * 5 + [vmem] * 2),
        scratch_shapes=[
            pltpu.VMEM((length, model_width), half),
            pltpu.VMEM((3, model_width, local_width), half),
            pltpu.VMEM((split, *w_out.shape), half),
            pltpu.VMEM((tok_rows, model_width), half),
            pltpu.VMEM((length, model_width), half),
            pltpu.VMEM((experts_local, size // 2, 2 * CAP, model_width), half),
            pltpu.VMEM((2, length, local_width), f32),
            pltpu.VMEM((8, length), f32),
            pltpu.VMEM((size, 8, length), f32),
            kind((3,)),
            kind((3, 3, chips)),
            kind((3, 2, chips)),
            kind((size,)),
            kind((size,)),
            kind((size,)),
            kind((size,)),
            kind,
            kind((experts_local,)),
            kind((experts_local,)),
            kind((4,)),
            kind((4, split)),
            kind((4, split)),
            kind((3,)),
            kind((3, split)),
            kind((3, split)),
            kind((3,)),
            *ChainReduce.scratch(chips, tok_rows, model_width),
        ],
        compiler_params=pltpu.CompilerParams(
            collective_id=which, has_side_effects=True, vmem_limit_bytes=58 * 2**20
        ),
        cost_estimate=pl.CostEstimate(
            flops=2 * length * model_width * local_width * 4,
            bytes_accessed=500 * 2**20,
            transcendentals=0,
        ),
    )(
        tokens,
        gain_rows,
        gain_cols,
        cos,
        sin,
        segment_ids.reshape(-1, 1),
        segment_ids.reshape(1, -1),
        cotangent,
        *weights,
        choice,
    )

class ShardSend:
    def __init__(self, split, source, landing, local_sem, sends, arrivals):
        self.split, self.source, self.landing = split, source, landing
        self.local_sem, self.sends, self.arrivals = local_sem, sends, arrivals
        self.mine = lax.axis_index("fsdp")

    def copy(self, shift):
        dest = lax.rem(self.mine + shift, self.split)
        return pltpu.make_async_remote_copy(
            src_ref=self.source(dest),
            dst_ref=self.landing.at[self.mine],
            send_sem=self.sends.at[shift],
            recv_sem=self.arrivals.at[shift],
            device_id={"fsdp": dest},
        )

    def own(self):
        return pltpu.make_async_copy(
            self.source(self.mine), self.landing.at[self.mine], self.local_sem
        )

    def start(self):
        for shift in range(1, self.split):
            self.copy(shift).start()
        self.own().start()

    def wait(self):
        for shift in range(1, self.split):
            self.copy(shift).wait()
        self.own().wait()


def turned_dot(left, right):
    return lax.dot_general(
        left, right, (((0,), (0,)), ((), ())), preferred_element_type=jnp.float32
    )


def cross_dot(left, right):
    return lax.dot_general(
        left, right, (((1,), (1,)), ((), ())), preferred_element_type=jnp.float32
    )


def experts_kernel(
    sizes,
    routed_ref,
    choices_ref,
    onehot_ref,
    cotangent_rows_ref,
    router_ref,
    gains_ref,
    residual_ref,
    cotangent_ref,
    gate_ref,
    up_ref,
    down_ref,
    residual_grad_ref,
    out_grad_ref,
    gain_ref,
    router_grad_ref,
    combine_ref,
    hidden_out,
    grad_gate_ref,
    grad_up_ref,
    down_landing,
    gate_full,
    up_full,
    down_full,
    upstream,
    pair_rows,
    outgoing,
    arrived,
    hidden,
    gate_grad,
    up_grad,
    back,
    gates,
    gates_out,
    gates_in,
    dots_out,
    dots_in,
    token_out,
    token_in,
    scales,
    load_sem,
    pair_sem,
    keep_sem,
    rows_send,
    rows_recv,
    gates_send,
    gates_recv,
    back_send,
    back_recv,
    dots_send,
    dots_recv,
    token_send,
    token_recv,
    down_send,
    down_recv,
    *reduce_buffers,
):
    size, split, chips, experts_local = sizes
    f32, half = jnp.float32, jnp.bfloat16
    me, mine = lax.axis_index("seq"), lax.axis_index("fsdp")
    tok_rows, model_width = residual_ref.shape
    pairs = size // 2
    double = 2 * CAP
    wide = 2 * tok_rows
    hidden_width = gate_full.shape[1]
    rows_of = pairs * double
    part = model_width // split
    member = lax.rem(mine, experts_local)

    loads = [
        pltpu.make_async_copy(source, target, load_sem.at[index])
        for index, (source, target) in enumerate(
            (
                (gate_ref, gate_full),
                (up_ref, up_full),
                (down_ref, down_full),
                (cotangent_rows_ref, upstream),
            )
        )
    ]

    slots = pair_rows.shape[0]

    def pair_load(pair):
        slot = lax.rem(pair, slots)
        start = pl.multiple_of(pair * wide, wide)
        return pltpu.make_async_copy(
            routed_ref.at[pl.ds(start, wide)], pair_rows.at[slot], pair_sem.at[slot]
        )

    pair_load(0).start()
    for load in loads:
        load.start()
    greet_all(size, split)

    padded = size * 8
    expert_row = lax.broadcasted_iota(jnp.int32, (padded, tok_rows), 0)
    inner = lax.rem(expert_row, 8)
    expert_row = jnp.where(inner < experts_local, expert_row // 8 * experts_local + inner, -1)
    ones = jnp.ones((8, wide), f32)
    top_count = choices_ref.shape[1] // 2

    @pl.loop(0, pairs)
    def _(pair):
        pair_load(pair).wait()

        @pl.when((pair + 1 < pairs) & (slots > 1))
        def _():
            pair_load(pair + 1).start()

        rows = pair_rows[lax.rem(pair, slots)]
        logits = lax.dot_general(
            router_ref[...], rows, (((1,), (1,)), ((), ())), preferred_element_type=f32
        )
        for side in range(2):
            ids = choices_ref[pair * 2 + side]
            chosen = expert_row == ids[0:1, :]
            for choice in range(1, top_count):
                chosen = chosen | (expert_row == ids[choice : choice + 1, :])
            own = jnp.where(chosen, logits[:, side * tok_rows : (side + 1) * tok_rows], MASKED)
            grown = jnp.where(chosen, jnp.exp(own - jnp.max(own, 0, keepdims=True)), 0.0)
            gates[pair * 2 + side] = grown / jnp.sum(grown, 0, keepdims=True)
        placed = jnp.dot(onehot_ref[pair], rows, preferred_element_type=f32).astype(half)
        for move in range(experts_local):
            piece = placed[move * double : (move + 1) * double]
            if move:
                outgoing[move - 1, pair] = piece
            else:
                arrived[0, pair] = piece
            row = me * 8 + partner_of(member, move)
            weights = jnp.concatenate(
                [gates[pair * 2, pl.ds(row, 1), :], gates[pair * 2 + 1, pl.ds(row, 1), :]], 1
            )
            slot_rows = pl.ds(move * double, double)
            weighted = onehot_ref[pair, slot_rows, :].astype(f32) * weights
            combine_ref[pair, slot_rows, :] = weighted.astype(half)
            gates_out[move, pair] = row_sums(weighted, ones)

        @pl.when((pair + 1 < pairs) & (slots == 1))
        def _():
            pair_load(pair + 1).start()

    def mate(move):
        return {"fsdp": partner_of(mine, move)}

    def rows_copy(move):
        return pltpu.make_async_remote_copy(
            src_ref=outgoing.at[move - 1],
            dst_ref=arrived.at[move],
            send_sem=rows_send.at[move],
            recv_sem=rows_recv.at[move],
            device_id=mate(move),
        )

    def gates_copy(move):
        return pltpu.make_async_remote_copy(
            src_ref=gates_out.at[move],
            dst_ref=gates_in.at[move],
            send_sem=gates_send.at[move],
            recv_sem=gates_recv.at[move],
            device_id=mate(move),
        )

    def back_rows(move):
        return back.at[:, pl.ds(move * double, double), :]

    def back_copy(move):
        return pltpu.make_async_remote_copy(
            src_ref=outgoing.at[move - 1],
            dst_ref=back_rows(move),
            send_sem=back_send.at[move],
            recv_sem=back_recv.at[move],
            device_id=mate(move),
        )

    def dots_copy(move):
        return pltpu.make_async_remote_copy(
            src_ref=dots_out.at[move],
            dst_ref=dots_in.at[move],
            send_sem=dots_send.at[move],
            recv_sem=dots_recv.at[move],
            device_id=mate(move),
        )

    order = list(range(experts_local - 1, 0, -1))
    for move in order:
        gates_copy(move).start()
        rows_copy(move).start()
    gates_in[0] = gates_out[0]
    for load in loads:
        load.wait()

    cols_step = min(256, hidden_width)
    width_step = min(512, model_width)
    spread = (lax.broadcasted_iota(jnp.int32, (8, 128), 0) == 0).astype(f32)
    for move in [0] + order:
        if move:
            gates_copy(move).wait()
            rows_copy(move).wait()
        for pair in range(pairs):
            scales[pair * double : (pair + 1) * double, :] = column_of(
                gates_in[move, pair], spread
            )
        dots_out[move] = jnp.zeros_like(dots_out[move])

        @pl.loop(0, hidden_width // cols_step)
        def _(index):
            cols = pl.ds(pl.multiple_of(index * cols_step, cols_step), cols_step)
            rows = arrived[move].reshape(rows_of, model_width)
            pre = jnp.dot(rows, gate_full[:, cols], preferred_element_type=f32)
            up = jnp.dot(rows, up_full[:, cols], preferred_element_type=f32)
            plain = lax.dot_general(
                upstream[move].reshape(rows_of, model_width),
                down_full[cols, :],
                (((1,), (1,)), ((), ())),
                preferred_element_type=f32,
            )
            sigmoid = 1.0 / (1.0 + jnp.exp(-pre))
            active = pre * sigmoid
            made = (active * up).astype(half)
            hidden[move, :, :, cols] = made.reshape(pairs, double, cols_step)
            dots = made.astype(f32) * plain
            for pair in range(pairs):
                dots_out[move, pair] += row_sums(
                    dots[pair * double : (pair + 1) * double], jnp.ones((8, cols_step), f32)
                )
            scaled = plain * scales[:, 0:1]
            gate_back = scaled * up * sigmoid * (1.0 + pre * (1.0 - sigmoid))
            gate_grad[move, :, :, cols] = gate_back.astype(half).reshape(pairs, double, cols_step)
            up_grad[move, :, :, cols] = (
                (scaled * active).astype(half).reshape(pairs, double, cols_step)
            )

        for pair in range(pairs):
            scale = scales[pair * double : (pair + 1) * double, 0:1]
            upstream[move, pair] = (upstream[move, pair].astype(f32) * scale).astype(half)

        if move:
            dots_copy(move).start()
        else:
            dots_in[0] = dots_out[0]

        @pl.loop(0, model_width // width_step)
        def _(index):
            cols = pl.ds(pl.multiple_of(index * width_step, width_step), width_step)
            rows_grad = lax.dot_general(
                gate_grad[move].reshape(rows_of, hidden_width),
                gate_full[cols, :],
                (((1,), (1,)), ((), ())),
                preferred_element_type=f32,
            )
            rows_grad = rows_grad + lax.dot_general(
                up_grad[move].reshape(rows_of, hidden_width),
                up_full[cols, :],
                (((1,), (1,)), ((), ())),
                preferred_element_type=f32,
            )
            rows_grad = rows_grad.astype(half).reshape(pairs, double, width_step)
            if move:
                outgoing[move - 1, :, :, cols] = rows_grad
            else:
                back[:, 0:double, cols] = rows_grad

        if move:
            back_copy(move).start()

    own_rows = pl.ds(pl.multiple_of(me * tok_rows, tok_rows), tok_rows)
    own_load = pltpu.make_async_copy(
        routed_ref.at[own_rows], pair_rows.at[0, pl.ds(0, tok_rows)], pair_sem.at[0]
    )
    own_load.start()
    hidden_keep = pltpu.make_async_copy(hidden, hidden_out, keep_sem)
    hidden_keep.start()

    total_rows = experts_local * rows_of

    def flat(ref, cols):
        return ref[:, :, :, cols].reshape(total_rows, -1)

    every = pl.ds(0, hidden_width)

    @pl.loop(0, split)
    def _(piece):
        cols = pl.ds(pl.multiple_of(piece * part, part), part)
        gate_full[cols, :] = turned_dot(flat(arrived, cols), flat(gate_grad, every)).astype(half)
        up_full[cols, :] = turned_dot(flat(arrived, cols), flat(up_grad, every)).astype(half)
        down_full[:, cols] = turned_dot(flat(hidden, every), flat(upstream, cols)).astype(half)

    grad_keeps = [
        pltpu.make_async_copy(source, target, load_sem.at[index])
        for index, (source, target) in enumerate(
            ((gate_full, grad_gate_ref), (up_full, grad_up_ref))
        )
    ]
    for keep in grad_keeps:
        keep.start()
    down_send_all = ShardSend(
        split,
        lambda dest: down_full.at[:, pl.ds(pl.multiple_of(dest * part, part), part)],
        down_landing,
        load_sem.at[2],
        down_send,
        down_recv,
    )

    for move in order:
        dots_copy(move).wait()
    token_out[...] = jnp.zeros_like(token_out)

    @pl.loop(0, pairs)
    def _(pair):
        for move in range(experts_local):
            found = jnp.dot(
                dots_in[move, pair],
                onehot_ref[pair, pl.ds(move * double, double), :].astype(f32),
                precision=HIGHEST,
                preferred_element_type=f32,
            )
            row = partner_of(member, move)
            for side in range(2):
                token_out[pair * 2 + side, pl.ds(row, 1), :] = found[
                    0:1, side * tok_rows : (side + 1) * tok_rows
                ]

    def token_copy(shift):
        peer = lax.rem(me + shift, size)
        return pltpu.make_async_remote_copy(
            src_ref=token_out.at[peer],
            dst_ref=token_in.at[me],
            send_sem=token_send.at[shift],
            recv_sem=token_recv.at[shift],
            device_id={"seq": peer},
        )

    for shift in range(1, size):
        token_copy(shift).start()
    token_in[me] = token_out[me]
    for move in order:
        back_copy(move).wait()
    down_send_all.start()

    reduce = ChainReduce(chips, residual_grad_ref, reduce_buffers)

    def product(index, store):
        side = pl.ds(pl.multiple_of(lax.rem(index, 2) * tok_rows, tok_rows), tok_rows)
        left = onehot_ref[index // 2, :, side]

        @pl.loop(0, model_width // width_step)
        def _(step):
            cols = pl.ds(pl.multiple_of(step * width_step, width_step), width_step)
            store(cols, turned_dot(left, back[index // 2, :, cols]))

    reduce.run(product)

    for shift in range(1, size):
        token_copy(shift).wait()
    own_gates = gates[me]
    grads = token_in[...].reshape(padded, tok_rows)
    mean = jnp.sum(own_gates * grads, 0, keepdims=True)
    logit_grad = (own_gates * (grads - mean)).astype(half)
    routed_grad = reduce.total[...] + turned_dot(logit_grad, router_ref[...])
    own_load.wait()
    router_grad = jnp.dot(logit_grad, pair_rows[0, 0:tok_rows, :], preferred_element_type=f32)
    for device in range(size):
        router_grad_ref[device * experts_local : (device + 1) * experts_local, :] = router_grad[
            device * 8 : device * 8 + experts_local
        ]
    residual = residual_ref[...]
    inverse = lax.rsqrt(jnp.mean(residual * residual, -1, keepdims=True) + EPSILON)
    unit = residual * inverse
    gain_ref[...] = jnp.broadcast_to(
        jnp.sum(routed_grad * unit, 0, keepdims=True), gain_ref.shape
    )
    routed_grad = routed_grad * gains_ref[1:2, :]
    routed_grad = inverse * (
        routed_grad - unit * jnp.mean(routed_grad * unit, -1, keepdims=True)
    )
    residual_grad = cotangent_ref[...].astype(f32) + routed_grad
    residual_grad_ref[...] = residual_grad
    out_grad_ref[...] = residual_grad.astype(half)
    reduce.sent()
    hidden_keep.wait()
    for keep in grad_keeps:
        keep.wait()
    down_send_all.wait()


def experts(
    sizes,
    routed_seq,
    choices,
    onehot,
    cotangent_rows,
    router_rows,
    gain_rows,
    residual,
    cotangent,
    weights,
    which,
):
    size, split, chips, experts_local = sizes
    gate_full, up_full, down_full = weights
    model_width, hidden_width = gate_full.shape
    tok_rows = residual.shape[0]
    pairs, double = size // 2, 2 * CAP
    f32, half = jnp.float32, jnp.bfloat16
    vmem = pl.BlockSpec(memory_space=pltpu.VMEM)
    anywhere = pl.BlockSpec(memory_space=pl.ANY)
    kind = pltpu.SemaphoreType.DMA
    shape = jax.ShapeDtypeStruct
    few = kind((experts_local,))
    wide_rows = (experts_local, pairs, double, model_width)
    narrow_rows = (experts_local, pairs, double, hidden_width)
    flags = (experts_local, pairs, 8, double)
    return pl.pallas_call(
        functools.partial(experts_kernel, sizes),
        out_shape=(
            shape((tok_rows, model_width), f32),
            shape((tok_rows, model_width), half),
            shape((8, model_width), f32),
            shape((size * experts_local, model_width), f32),
            shape(onehot.shape, half),
            shape(narrow_rows, half),
            shape(gate_full.shape, half),
            shape(up_full.shape, half),
            shape((split, hidden_width, model_width // split), half),
        ),
        in_specs=[anywhere, vmem, vmem, anywhere] + [vmem] * 4 + [anywhere] * 3,
        out_specs=tuple([vmem] * 5 + [anywhere] * 4),
        scratch_shapes=[
            pltpu.VMEM(gate_full.shape, half),
            pltpu.VMEM(up_full.shape, half),
            pltpu.VMEM(down_full.shape, half),
            pltpu.VMEM(wide_rows, half),
            pltpu.VMEM((2 if chips < 8 else 1, 2 * tok_rows, model_width), half),
            pltpu.VMEM((max(experts_local - 1, 1), *wide_rows[1:]), half),
            pltpu.VMEM(wide_rows, half),
            pltpu.VMEM(narrow_rows, half),
            pltpu.VMEM(narrow_rows, half),
            pltpu.VMEM(narrow_rows, half),
            pltpu.VMEM((pairs, experts_local * double, model_width), half),
            pltpu.VMEM((size, size * 8, tok_rows), f32),
            pltpu.VMEM(flags, f32),
            pltpu.VMEM(flags, f32),
            pltpu.VMEM(flags, f32),
            pltpu.VMEM(flags, f32),
            pltpu.VMEM((size, 8, tok_rows), f32),
            pltpu.VMEM((size, 8, tok_rows), f32),
            pltpu.VMEM((pairs * double, 128), f32),
            kind((4,)),
            kind((2,)),
            kind,
            few,
            few,
            few,
            few,
            few,
            few,
            few,
            few,
            kind((size,)),
            kind((size,)),
            kind((split,)),
            kind((split,)),
            *ChainReduce.scratch(chips, tok_rows, model_width),
        ],
        compiler_params=pltpu.CompilerParams(
            collective_id=which, has_side_effects=True, vmem_limit_bytes=63 * 2**20
        ),
        cost_estimate=pl.CostEstimate(
            flops=2 * experts_local * pairs * double * model_width * hidden_width * 8,
            bytes_accessed=500 * 2**20,
            transcendentals=0,
        ),
    )(
        routed_seq,
        choices,
        onehot,
        cotangent_rows,
        router_rows,
        gain_rows,
        residual,
        cotangent,
        gate_full,
        up_full,
        down_full,
    )

def back_kernel(
    sizes,
    out_grad_ref,
    tokens_ref,
    residual_grad_ref,
    gains_ref,
    gain_cols_ref,
    second_gain_ref,
    cos_ref,
    sin_ref,
    seg_col_ref,
    seg_row_ref,
    q_ref,
    k_ref,
    v_ref,
    unit_ref,
    sums_ref,
    log_ref,
    attended_ref,
    qkv_ref,
    rows_full_ref,
    normed_ref,
    hidden_ref,
    down_ref,
    grad_gate_ref,
    input_grad_ref,
    gains_out_ref,
    qkv_grad_ref,
    out_w_grad_ref,
    mixed_rows,
    gate_landing,
    down_full,
    out_grads,
    attended_grad,
    hidden,
    returned,
    key_total,
    value_total,
    scaled,
    raw_grads,
    centers_own,
    centers_in,
    qkv_stage,
    qkv_landing,
    out_stage,
    out_landing,
    load_sem,
    gather_local,
    gather_send,
    gather_recv,
    gate_local,
    gate_send,
    gate_recv,
    rows_local,
    rows_send,
    rows_recv,
    centers_send,
    centers_recv,
    qkv_local,
    qkv_send,
    qkv_recv,
    out_local,
    out_send,
    out_recv,
    *reduce_buffers,
):
    size, split, chips, experts_local = sizes
    f32, half = jnp.float32, jnp.bfloat16
    me, mine = lax.axis_index("seq"), lax.axis_index("fsdp")
    tok_rows, model_width = tokens_ref.shape
    length, local_width = q_ref.shape
    hidden_width = down_ref.shape[0]
    part = model_width // split
    head = HEAD_DIM
    heads = local_width // head
    double = 2 * CAP
    pairs = size // 2
    rows_of = pairs * double

    down_load = pltpu.make_async_copy(down_ref, down_full, load_sem.at[0])
    hidden_load = pltpu.make_async_copy(hidden_ref, hidden, load_sem.at[1])
    down_load.start()
    hidden_load.start()
    greet_all(size, split)
    gather = ChainGather(chips, out_grad_ref, out_grads, gather_local, gather_send, gather_recv)
    gather.start()
    gate_send_all = ShardSend(
        split,
        lambda dest: grad_gate_ref.at[pl.ds(pl.multiple_of(dest * part, part), part)],
        gate_landing,
        gate_local,
        gate_send,
        gate_recv,
    )

    down_load.wait()
    hidden_load.wait()
    width_step = min(512, model_width)

    def rows_target(move):
        return mixed_rows.at[:, pl.ds(move * double, double), :]

    def rows_copy(move):
        return pltpu.make_async_remote_copy(
            src_ref=returned.at[move],
            dst_ref=rows_target(move),
            send_sem=rows_send.at[move],
            recv_sem=rows_recv.at[move],
            device_id={"fsdp": partner_of(mine, move)},
        )

    own_rows = pltpu.make_async_copy(returned.at[0], rows_target(0), rows_local)
    for move in range(experts_local - 1, -1, -1):

        @pl.loop(0, model_width // width_step)
        def _(index):
            cols = pl.ds(pl.multiple_of(index * width_step, width_step), width_step)
            made = jnp.dot(
                hidden[move].reshape(rows_of, hidden_width),
                down_full[:, cols],
                preferred_element_type=f32,
            )
            returned[move, :, :, cols] = made.astype(half).reshape(pairs, double, width_step)

        if move:
            rows_copy(move).start()
    own_rows.start()
    gate_send_all.start()
    gather.steps()
    gather.landed()

    block = min(512, length)

    @pl.loop(0, length // block)
    def _(step):
        rows = pl.ds(pl.multiple_of(step * block, block), block)
        total = cross_dot(out_grads[rows, 0:part], rows_full_ref[0])
        for piece in range(1, split):
            total += cross_dot(
                out_grads[rows, piece * part : (piece + 1) * part], rows_full_ref[piece]
            )
        attended_grad[rows, :] = total.astype(half)

    @pl.loop(0, split)
    def _(piece):
        cols = pl.ds(pl.multiple_of(piece * part, part), part)
        out_stage[piece] = turned_dot(attended_ref[...], out_grads[:, cols]).astype(half)

    out_send_all = ShardSend(
        split, lambda dest: out_stage.at[dest], out_landing, out_local, out_send, out_recv
    )
    out_send_all.start()
    gather.sent()
    normed_load = pltpu.make_async_copy(normed_ref, out_grads, load_sem.at[0])
    normed_load.start()

    wide = min(256, length) if length <= 1024 else 128
    scale = head**-0.5
    for number in range(heads):
        cols = slice(number * head, (number + 1) * head)
        key_total[...] = jnp.zeros_like(key_total)
        value_total[...] = jnp.zeros_like(value_total)

        @pl.loop(0, length // wide)
        def _(step):
            rows = pl.ds(pl.multiple_of(step * wide, wide), wide)
            scores = cross_dot(q_ref[rows, cols], k_ref[:, cols]) * scale
            scores = jnp.where(seg_col_ref[rows, :] == seg_row_ref[...], scores, MASKED)
            probs = jnp.exp(scores - log_ref[rows, cols][:, 0:1])
            grads = attended_grad[rows, cols]
            prob_grad = cross_dot(grads, v_ref[:, cols])
            center = jnp.sum(probs * prob_grad, -1, keepdims=True)
            score_grad = (probs * (prob_grad - center)).astype(half)
            query_grad = jnp.dot(score_grad, k_ref[:, cols], preferred_element_type=f32) * scale
            raw_grads[0, rows, cols] = query_grad.astype(half)
            key_total[...] += turned_dot(score_grad, q_ref[rows, cols])
            value_total[...] += turned_dot(probs.astype(half), grads)

        raw_grads[1, :, cols] = (key_total[...] * scale).astype(half)
        raw_grads[2, :, cols] = value_total[...].astype(half)

    lanes = lax.broadcasted_iota(jnp.int32, (8, local_width), 0)
    first_row, second_row = (lanes == 0).astype(f32), (lanes == 1).astype(f32)
    gains_out_ref[...] = jnp.zeros_like(gains_out_ref)
    own_cols = pl.ds(pl.multiple_of(me * local_width, local_width), local_width)
    gains_out_ref[1:2, :] = second_gain_ref[0:1, :]

    @pl.loop(0, length // block)
    def _(step):
        rows = pl.ds(pl.multiple_of(step * block, block), block)
        found = jnp.zeros((8, block), f32)
        for index, pick in ((0, first_row), (1, second_row)):
            unit = unit_ref[index, rows, :]
            pieces = []
            for number in range(heads):
                cols = slice(number * head, (number + 1) * head)
                piece = raw_grads[index, rows, cols].astype(f32)
                pieces.append(piece * cos_ref[rows, :] - turned_halves(piece) * sin_ref[rows, :])
            unit_grad = pieces[0] if heads == 1 else jnp.concatenate(pieces, 1)
            gains_out_ref[2 + index : 3 + index, own_cols] += jnp.sum(
                unit_grad * unit, 0, keepdims=True
            )
            grown = unit_grad * gain_cols_ref[2 + index : 3 + index, :]
            scaled[index, rows, :] = grown
            found += row_sums(grown * unit, pick)
        centers_own[:, rows] = found

    def centers_copy(shift):
        return pltpu.make_async_remote_copy(
            src_ref=centers_own,
            dst_ref=centers_in.at[me],
            send_sem=centers_send.at[shift],
            recv_sem=centers_recv.at[shift],
            device_id={"seq": lax.rem(me + shift, size)},
        )

    for shift in range(1, size):
        centers_copy(shift).start()
    centers_in[me] = centers_own[...]
    for shift in range(1, size):
        centers_copy(shift).wait()
    centers_own[...] = jnp.sum(centers_in[...], 0) * (1.0 / model_width)

    @pl.loop(0, length // block)
    def _(step):
        rows = pl.ds(pl.multiple_of(step * block, block), block)
        for index, pick in ((0, first_row), (1, second_row)):
            inverse = lax.rsqrt(column_of(sums_ref[:, rows], pick) / model_width + EPSILON)
            center = column_of(centers_own[:, rows], pick)
            raw_grads[index, rows, :] = (
                inverse * (scaled[index, rows, :] - unit_ref[index, rows, :] * center)
            ).astype(half)

    reduce = ChainReduce(chips, input_grad_ref, reduce_buffers)

    def product(index, store):
        rows = pl.ds(pl.multiple_of(index * tok_rows, tok_rows), tok_rows)

        @pl.loop(0, model_width // width_step)
        def _(step):
            cols = pl.ds(pl.multiple_of(step * width_step, width_step), width_step)
            total = cross_dot(raw_grads[0, rows, :], qkv_ref[0, cols, :])
            total += cross_dot(raw_grads[1, rows, :], qkv_ref[1, cols, :])
            total += cross_dot(raw_grads[2, rows, :], qkv_ref[2, cols, :])
            store(cols, total)

    qkv_send_all = ShardSend(
        split, lambda dest: qkv_stage.at[dest], qkv_landing, qkv_local, qkv_send, qkv_recv
    )

    def between():
        normed_load.wait()

        @pl.loop(0, split)
        def _(piece):
            cols = pl.ds(pl.multiple_of(piece * part, part), part)
            left = out_grads[:, cols]
            for index in range(3):
                qkv_stage[piece, index] = turned_dot(left, raw_grads[index]).astype(half)

        qkv_send_all.start()

    reduce.run(product, between)

    inputs = tokens_ref[...].astype(f32)
    inverse = lax.rsqrt(jnp.mean(inputs * inputs, -1, keepdims=True) + EPSILON)
    unit = inputs * inverse
    grads = input_grad_ref[...]
    gains_out_ref[0:1, :] = jnp.sum(grads * unit, 0, keepdims=True)
    grads = grads * gains_ref[0:1, :]
    input_grad_ref[...] = residual_grad_ref[...] + inverse * (
        grads - unit * jnp.mean(grads * unit, -1, keepdims=True)
    )

    out_send_all.wait()
    total = out_landing[0].astype(f32)
    for index in range(1, split):
        total += out_landing[index].astype(f32)
    out_w_grad_ref[...] = total
    qkv_send_all.wait()
    for index in range(3):
        total = qkv_landing[0, index].astype(f32)
        for piece in range(1, split):
            total += qkv_landing[piece, index].astype(f32)
        qkv_grad_ref[index] = total
    reduce.sent()
    own_rows.wait()
    for move in range(1, experts_local):
        rows_copy(move).wait()
    gate_send_all.wait()


def back(sizes, out_grad, tokens, residual_grad, gains, kept, big_ones, which):
    size, split, chips, experts_local = sizes
    f32, half = jnp.float32, jnp.bfloat16
    tok_rows, model_width = tokens.shape
    query_heads, qkv_stack, out_stack = kept[4], kept[11], kept[12]
    length, local_width = query_heads.shape
    normed_seq, hidden, down_full, grad_gate = big_ones
    hidden_width = down_full.shape[0]
    part = model_width // split
    vmem = pl.BlockSpec(memory_space=pltpu.VMEM)
    anywhere = pl.BlockSpec(memory_space=pl.ANY)
    kind = pltpu.SemaphoreType.DMA
    shape = jax.ShapeDtypeStruct
    few, fsdp = kind((experts_local,)), kind((split,))
    return pl.pallas_call(
        functools.partial(back_kernel, sizes),
        out_shape=(
            shape((tok_rows, model_width), f32),
            shape((8, model_width), f32),
            shape((3, part, local_width), f32),
            shape((local_width, part), f32),
            shape((size // 2, experts_local * 2 * CAP, model_width), half),
            shape((split, part, hidden_width), half),
        ),
        in_specs=[vmem] * 19 + [anywhere] * 4,
        out_specs=tuple([vmem] * 4 + [anywhere] * 2),
        scratch_shapes=[
            pltpu.VMEM(down_full.shape, half),
            pltpu.VMEM((length, model_width), half),
            pltpu.VMEM((length, local_width), half),
            pltpu.VMEM(hidden.shape, half),
            pltpu.VMEM((experts_local, size // 2, 2 * CAP, model_width), half),
            pltpu.VMEM((length, HEAD_DIM), f32),
            pltpu.VMEM((length, HEAD_DIM), f32),
            pltpu.VMEM((2, length, local_width), f32),
            pltpu.VMEM((3, length, local_width), half),
            pltpu.VMEM((8, length), f32),
            pltpu.VMEM((size, 8, length), f32),
            pltpu.VMEM((split, 3, part, local_width), half),
            pltpu.VMEM((split, 3, part, local_width), half),
            pltpu.VMEM((split, local_width, part), half),
            pltpu.VMEM((split, local_width, part), half),
            kind((2,)),
            kind,
            kind((3, chips)),
            kind((2, chips)),
            kind,
            fsdp,
            fsdp,
            kind,
            few,
            few,
            kind((size,)),
            kind((size,)),
            kind,
            fsdp,
            fsdp,
            kind,
            fsdp,
            fsdp,
            *ChainReduce.scratch(chips, tok_rows, model_width),
        ],
        compiler_params=pltpu.CompilerParams(
            collective_id=which, has_side_effects=True, vmem_limit_bytes=63 * 2**20
        ),
        cost_estimate=pl.CostEstimate(
            flops=2 * length * model_width * local_width * 8,
            bytes_accessed=500 * 2**20,
            transcendentals=0,
        ),
    )(out_grad, tokens, residual_grad, *gains, *kept, *big_ones)


def close_kernel(
    sizes,
    mixed_rows_ref,
    combine_ref,
    residual_ref,
    gains_ref,
    router_ref,
    grad_up_ref,
    output_ref,
    small_ref,
    up_landing,
    total,
    small,
    first,
    second,
    final,
    up_local,
    up_send,
    up_recv,
    send_one,
    recv_one,
    send_two,
    recv_two,
    send_three,
    recv_three,
    *reduce_buffers,
):
    size, split, chips, experts_local = sizes
    f32 = jnp.float32
    me, mine = lax.axis_index("seq"), lax.axis_index("fsdp")
    tok_rows, model_width = residual_ref.shape
    part = model_width // split
    slice_width = model_width // size
    experts_all = router_ref.shape[0]
    small[0:8, :] = gains_ref[...]
    small[8 : 8 + experts_all, :] = router_ref[...]
    greet_all(size, split)
    up_send_all = ShardSend(
        split,
        lambda dest: grad_up_ref.at[pl.ds(pl.multiple_of(dest * part, part), part)],
        up_landing,
        up_local,
        up_send,
        up_recv,
    )
    up_send_all.start()

    def columns(index):
        return pl.ds(pl.multiple_of(index * slice_width, slice_width), slice_width)

    def scatter(shift):
        peer = lax.rem(me + shift, size)
        return pltpu.make_async_remote_copy(
            src_ref=small.at[:, columns(peer)],
            dst_ref=first.at[me],
            send_sem=send_one.at[shift],
            recv_sem=recv_one.at[shift],
            device_id={"seq": peer},
        )

    def share(shift):
        return pltpu.make_async_remote_copy(
            src_ref=second.at[mine],
            dst_ref=second.at[mine],
            send_sem=send_two.at[shift],
            recv_sem=recv_two.at[shift],
            device_id={"fsdp": lax.rem(mine + shift, split)},
        )

    def collect(shift):
        return pltpu.make_async_remote_copy(
            src_ref=final.at[me],
            dst_ref=final.at[me],
            send_sem=send_three.at[shift],
            recv_sem=recv_three.at[shift],
            device_id={"seq": lax.rem(me + shift, size)},
        )

    for shift in range(1, size):
        scatter(shift).start()
    first[me] = small[:, columns(me)]

    reduce = ChainReduce(chips, total, reduce_buffers)
    width_step = min(512, model_width)

    def product(index, store):
        side = pl.ds(pl.multiple_of(lax.rem(index, 2) * tok_rows, tok_rows), tok_rows)
        left = combine_ref[index // 2, :, side]

        @pl.loop(0, model_width // width_step)
        def _(step):
            cols = pl.ds(pl.multiple_of(step * width_step, width_step), width_step)
            store(cols, turned_dot(left, mixed_rows_ref[index // 2, :, cols]))

    def between():
        for shift in range(1, size):
            scatter(shift).wait_recv()
        second[mine] = jnp.sum(first[...], 0)
        for shift in range(1, split):
            share(shift).start()

    reduce.run(product, between)
    for shift in range(1, split):
        share(shift).wait_recv()
    final[me] = jnp.sum(second[...], 0)
    for shift in range(1, size):
        collect(shift).start()
    output_ref[...] = (residual_ref[...] + total[...]).astype(output_ref.dtype)
    for shift in range(1, size):
        scatter(shift).wait_send()
    for shift in range(1, split):
        share(shift).wait_send()
    for shift in range(1, size):
        collect(shift).wait()
    for index in range(size):
        small_ref[:, index * slice_width : (index + 1) * slice_width] = final[index]
    reduce.sent()
    up_send_all.wait()


def close(sizes, mixed_rows, combine, residual, gains, router_grad, grad_up, which):
    size, split, chips, experts_local = sizes
    f32, half = jnp.float32, jnp.bfloat16
    tok_rows, model_width = residual.shape
    hidden_width = grad_up.shape[1]
    part, slice_width = model_width // split, model_width // size
    rows = 8 + router_grad.shape[0]
    vmem = pl.BlockSpec(memory_space=pltpu.VMEM)
    anywhere = pl.BlockSpec(memory_space=pl.ANY)
    kind = pltpu.SemaphoreType.DMA
    shape = jax.ShapeDtypeStruct
    seq, fsdp = kind((size,)), kind((split,))
    return pl.pallas_call(
        functools.partial(close_kernel, sizes),
        out_shape=(
            shape((tok_rows, model_width), half),
            shape((rows, model_width), f32),
            shape((split, part, hidden_width), half),
        ),
        in_specs=[vmem] * 5 + [anywhere],
        out_specs=(vmem, vmem, anywhere),
        scratch_shapes=[
            pltpu.VMEM((tok_rows, model_width), f32),
            pltpu.VMEM((rows, model_width), f32),
            pltpu.VMEM((size, rows, slice_width), f32),
            pltpu.VMEM((split, rows, slice_width), f32),
            pltpu.VMEM((size, rows, slice_width), f32),
            kind,
            fsdp,
            fsdp,
            seq,
            seq,
            fsdp,
            fsdp,
            seq,
            seq,
            *ChainReduce.scratch(chips, tok_rows, model_width),
        ],
        compiler_params=pltpu.CompilerParams(
            collective_id=which, has_side_effects=True, vmem_limit_bytes=56 * 2**20
        ),
    )(mixed_rows, combine, residual, gains, router_grad, grad_up)


def shards(
    tokens,
    norm_gains,
    w_query,
    w_key,
    w_value,
    w_out,
    w_router,
    w_gate,
    w_up,
    w_down,
    segment_ids,
    expert_ids,
    expert_slots,
    cotangent,
):
    half_type = jnp.bfloat16
    float_type = jnp.float32
    tok_rows = tokens.shape[0]
    model_width = tokens.shape[1]
    expert_total = w_router.shape[1]
    top_count = expert_ids.shape[1]
    head_size = HEAD_DIM
    local_width = w_query.shape[1]
    capacity = CAP
    column_start = lax.axis_index("seq") * local_width
    experts_local = w_gate.shape[0]
    seq_size = lax.axis_size("seq")
    split = lax.axis_size("fsdp")
    places = jnp.where(expert_slots < capacity, expert_ids * capacity + expert_slots, -(10**6))
    gain_rows = norm_gains.astype(float_type)
    gain_cols = lax.dynamic_slice_in_dim(gain_rows, column_start, local_width, 1)
    length = seq_size * tok_rows
    sizes = (seq_size, split, seq_size // 2, experts_local)
    positions = jnp.arange(length, dtype=jnp.int32)
    cosine_table, sine_table = rope_tables(positions, head_size)
    cosine_wide = jnp.concatenate([cosine_table, cosine_table], 1)
    sine_wide = jnp.concatenate([-sine_table, sine_table], 1)
    (
        normed_seq,
        qkv_stack,
        out_stack,
        query_heads,
        key_heads,
        value_heads,
        unit_pair,
        square_sums,
        log_wide,
        attended_heads,
        residual,
        routed_seq,
        cotangent_rows,
        gate_full,
        up_full,
        down_full,
        choices,
        onehot,
    ) = front(
        sizes,
        tokens,
        gain_rows,
        gain_cols,
        cosine_wide,
        sine_wide,
        segment_ids,
        cotangent,
        (w_query, w_key, w_value, w_out, w_gate, w_up, w_down),
        jnp.concatenate([expert_ids, places], 1).T,
        0,
    )
    router_rows = jnp.zeros((seq_size, 8, model_width), half_type)
    router_rows = router_rows.at[:, :experts_local].set(
        w_router.T.reshape(seq_size, experts_local, model_width)
    )
    router_rows = router_rows.reshape(seq_size * 8, model_width)
    (
        residual_grad,
        out_grad,
        gain_second_grad,
        router_grad,
        combine,
        hidden,
        grad_gate_full,
        grad_up_full,
        down_landing,
    ) = experts(
        sizes,
        routed_seq,
        choices,
        onehot,
        cotangent_rows,
        router_rows,
        gain_rows,
        residual,
        cotangent,
        (gate_full, up_full, down_full),
        1,
    )
    input_grad, gain_grads, qkv_owned, out_owned, mixed_rows, gate_landing = back(
        sizes,
        out_grad,
        tokens,
        residual_grad,
        (gain_rows, gain_cols, gain_second_grad),
        (
            cosine_wide,
            sine_wide,
            segment_ids.reshape(-1, 1),
            segment_ids.reshape(1, -1),
            query_heads,
            key_heads,
            value_heads,
            unit_pair,
            square_sums,
            log_wide,
            attended_heads,
            qkv_stack,
            out_stack,
        ),
        (normed_seq, hidden, down_full, grad_gate_full),
        2,
    )
    output, small, up_landing = close(
        sizes, mixed_rows, combine, residual, gain_grads, router_grad, grad_up_full, 3
    )

    def owned(landing):
        shape = (split // experts_local, experts_local, *landing.shape[1:])
        return landing.astype(float_type).reshape(shape).sum(0)

    return (
        output,
        input_grad,
        small[:4],
        qkv_owned[0],
        qkv_owned[1],
        qkv_owned[2],
        out_owned,
        small[8:].T,
        owned(gate_landing),
        owned(up_landing),
        owned(down_landing),
    )


def solution(mesh):
    in_specs = (
        P(("fsdp", "seq"), None),
        P(),
        P("fsdp", "seq"),
        P("fsdp", "seq"),
        P("fsdp", "seq"),
        P("seq", "fsdp"),
        P(),
        P("seq", "fsdp", None),
        P("seq", "fsdp", None),
        P("seq", None, "fsdp"),
        P("fsdp"),
        P(("fsdp", "seq"), None),
        P(("fsdp", "seq"), None),
        P(("fsdp", "seq"), None),
    )
    out_specs = (
        P(("fsdp", "seq"), None),
        P(("fsdp", "seq"), None),
        P(),
        P("fsdp", "seq"),
        P("fsdp", "seq"),
        P("fsdp", "seq"),
        P("seq", "fsdp"),
        P(),
        P("seq", "fsdp", None),
        P("seq", "fsdp", None),
        P("seq", None, "fsdp"),
    )
    return jax.shard_map(shards, mesh=mesh, in_specs=in_specs, out_specs=out_specs, check_vma=False)
```

```python
import functools

import jax
import jax.numpy as jnp
import numpy as np
from jax import lax
from jax.experimental import pallas as pl
from jax.experimental.pallas import tpu as pltpu
from jax.sharding import PartitionSpec as P

HEAD_DIM = 128
CAP = 40


EPSILON = 1e-06
THETA = 10000.0
MASKED = -1e30
HIGHEST = lax.Precision.HIGHEST


def rope_tables(length, head_size):
    half_dim = head_size // 2
    frequency = THETA ** (-np.arange(half_dim, dtype=np.float64) / half_dim)
    angles = np.arange(length, dtype=np.float64)[:, None] * frequency.astype(np.float32)
    cosine, sine = np.cos(angles), np.sin(angles)
    return (
        jnp.asarray(np.concatenate([cosine, cosine], 1), jnp.float32),
        jnp.asarray(np.concatenate([-sine, sine], 1), jnp.float32),
    )


class ChainGather:
    def __init__(self, chips, x_ref, out_ref, local_sem, sends, arrivals):
        self.chips, self.x_ref, self.out_ref = chips, x_ref, out_ref
        self.local_sem, self.sends, self.arrivals = local_sem, sends, arrivals
        me = lax.axis_index("seq")
        self.chip, self.core = me // 2, lax.rem(me, 2)
        self.rows = x_ref.shape[0]

    def block(self, source, core):
        start = pl.multiple_of((source * 2 + core) * self.rows, self.rows)
        return self.out_ref.at[pl.ds(start, self.rows)]

    def hop(self, source, ref, target, way, lane):
        return pltpu.make_async_remote_copy(
            src_ref=ref,
            dst_ref=self.block(source, self.core),
            send_sem=self.sends.at[way, source],
            recv_sem=self.arrivals.at[lane, source],
            device_id={"seq": target},
        )

    def upward(self, source, ref):
        return self.hop(source, ref, self.chip * 2 + 2 + self.core, 0, 0)

    def downward(self, source, ref):
        return self.hop(source, ref, self.chip * 2 - 2 + self.core, 1, 0)

    def sideways(self, source, ref):
        return self.hop(source, ref, self.chip * 2 + 1 - self.core, 2, 1)

    def own(self):
        return pltpu.make_async_copy(
            self.x_ref, self.block(self.chip, self.core), self.local_sem
        )

    def start(self):
        @pl.when(self.chip < self.chips - 1)
        def _():
            self.upward(self.chip, self.x_ref).start()

        @pl.when(self.chip > 0)
        def _():
            self.downward(self.chip, self.x_ref).start()

        self.sideways(self.chip, self.x_ref).start()
        self.own().start()

    def step(self, distance):
        below, above = self.chip - distance, self.chip + distance

        @pl.when(below >= 0)
        def _():
            landed = self.block(below, self.core)
            self.upward(below, landed).wait_recv()

            @pl.when(self.chip < self.chips - 1)
            def _():
                self.upward(below, landed).start()

            self.sideways(below, landed).start()

        @pl.when(above < self.chips)
        def _():
            landed = self.block(above, self.core)
            self.downward(above, landed).wait_recv()

            @pl.when(self.chip > 0)
            def _():
                self.downward(above, landed).start()

            self.sideways(above, landed).start()

    def steps(self):
        for distance in range(1, self.chips):
            self.step(distance)

    def landed(self):
        self.own().wait()
        for source in range(self.chips):
            self.sideways(source, self.block(source, self.core)).wait_recv()

    def sent(self):
        for source in range(self.chips):
            ref = self.block(source, self.core)
            self.sideways(source, ref).wait_send()

            @pl.when((self.chip < self.chips - 1) & (source <= self.chip))
            def _():
                self.upward(source, ref).wait_send()

            @pl.when((self.chip > 0) & (source >= self.chip))
            def _():
                self.downward(source, ref).wait_send()


class ChainReduce:
    def __init__(self, chips, total, buffers):
        self.total = total
        (
            self.side_out,
            self.side_in,
            self.chain_in,
            self.side_send,
            self.side_recv,
            self.chain_send,
            self.chain_recv,
        ) = buffers
        self.chips = chips
        me = lax.axis_index("seq")
        self.chip, self.core = me // 2, lax.rem(me, 2)

    @staticmethod
    def scratch(chips, rows, width):
        half = jnp.bfloat16
        return [
            pltpu.VMEM((chips, rows, width), half),
            pltpu.VMEM((chips, rows, width), half),
            pltpu.VMEM((chips + 1, rows, width), half),
            pltpu.SemaphoreType.DMA((chips,)),
            pltpu.SemaphoreType.DMA((chips,)),
            pltpu.SemaphoreType.DMA((chips,)),
            pltpu.SemaphoreType.DMA((2, chips)),
        ]

    def side_copy(self, dest):
        return pltpu.make_async_remote_copy(
            src_ref=self.side_out.at[dest],
            dst_ref=self.side_in.at[dest],
            send_sem=self.side_send.at[dest],
            recv_sem=self.side_recv.at[dest],
            device_id={"seq": self.chip * 2 + 1 - self.core},
        )

    def chain_copy(self, way, dest, target):
        return pltpu.make_async_remote_copy(
            src_ref=self.side_out.at[dest],
            dst_ref=self.chain_in.at[self.slot(way, dest, target // 2)],
            send_sem=self.chain_send.at[dest],
            recv_sem=self.chain_recv.at[way, dest],
            device_id={"seq": target},
        )

    def slot(self, way, dest, holder):
        return jnp.where(dest == holder, self.chips, dest) if way else dest

    def place(self, index):
        distance = self.chips - 1 - index // 2
        dest = self.chip + (1 - 2 * lax.rem(index, 2)) * distance
        return dest, (dest >= 0) & (dest < self.chips)

    def run(self, product, between=None):
        chips, chip, core, total = self.chips, self.chip, self.core, self.total
        sibling = chip * 2 + 1 - core

        @pl.loop(0, 2 * chips - 1)
        def _(index):
            dest, inside = self.place(index)

            @pl.when(inside)
            def _():
                def store(cols, part):
                    self.side_out[dest, :, cols] = part.astype(self.side_out.dtype)

                product(dest * 2 + 1 - core, store)
                self.side_copy(dest).start()

        if between:
            between()

        @pl.loop(0, 2 * chips - 1)
        def _(index):
            dest, inside = self.place(index)

            @pl.when(inside)
            def _():
                def store(cols, part):
                    total[:, cols] = part

                product(dest * 2 + core, store)
                self.side_copy(dest).wait_recv()
                total[...] += self.side_in[dest].astype(jnp.float32)

                @pl.when((dest >= chip) & (chip > 0))
                def _():
                    self.chain_copy(0, dest, sibling).wait_recv()
                    total[...] += self.chain_in[dest].astype(jnp.float32)

                @pl.when((dest <= chip) & (chip < chips - 1))
                def _():
                    self.chain_copy(1, dest, sibling).wait_recv()
                    total[...] += self.chain_in[self.slot(1, dest, chip)].astype(jnp.float32)

                self.side_copy(dest).wait_send()

                @pl.when(dest != chip)
                def _():
                    self.side_out[dest] = total[...].astype(self.side_out.dtype)

                @pl.when(dest > chip)
                def _():
                    self.chain_copy(0, dest, chip * 2 + 2 + core).start()

                @pl.when(dest < chip)
                def _():
                    self.chain_copy(1, dest, chip * 2 - 2 + core).start()

    def sent(self):
        sibling = self.chip * 2 + 1 - self.core

        @pl.loop(0, self.chips)
        def _(dest):
            @pl.when(dest != self.chip)
            def _():
                self.chain_copy(0, dest, sibling).wait_send()


def partner_of(index, move):
    turned, bit = index, 1
    while bit <= move:
        if move // bit % 2:
            turned = turned + bit - 2 * bit * lax.rem(index // bit, 2)
        bit *= 2
    return turned


def greet_all(size, split):
    me, mine = lax.axis_index("seq"), lax.axis_index("fsdp")
    barrier = pltpu.get_barrier_semaphore()
    for shift in range(1, size):
        pl.semaphore_signal(barrier, inc=1, device_id={"seq": lax.rem(me + shift, size)})
    for shift in range(1, split):
        pl.semaphore_signal(barrier, inc=1, device_id={"fsdp": lax.rem(mine + shift, split)})
    pl.semaphore_wait(barrier, size + split - 2)


def turned_halves(head):
    return pltpu.roll(head, head.shape[-1] // 2, 1)


def row_sums(values, pick):
    return lax.dot_general(
        pick, values, (((1,), (1,)), ((), ())), precision=HIGHEST, preferred_element_type=jnp.float32
    )


def column_of(row_form, pick):
    return lax.dot_general(
        row_form, pick, (((0,), (0,)), ((), ())), precision=HIGHEST, preferred_element_type=jnp.float32
    )


def front_kernel(
    sizes,
    tokens_ref,
    gains_in_ref,
    cos_ref,
    sin_ref,
    seg_row_ref,
    ids_ref,
    slots_ref,
    cotangent_ref,
    wq_ref,
    wk_ref,
    wv_ref,
    wo_ref,
    w_gate_ref,
    w_up_ref,
    w_down_ref,
    normed_out,
    qkv_out,
    rows_out,
    q_ref,
    k_ref,
    v_ref,
    unit_ref,
    sums_ref,
    log_ref,
    attended_ref,
    residual_ref,
    gains_ref,
    seg_col_ref,
    routed_out,
    cotangent_rows,
    gate_full,
    up_full,
    down_full,
    choices,
    onehot_ref,
    normed,
    qkv,
    rows_full,
    routed_own,
    choice_own,
    cotangent_pair,
    cotangent_all,
    mate_choices,
    mate_onehot,
    placed,
    raw,
    sums_own,
    sums_in,
    gather_local,
    gather_send,
    gather_recv,
    sums_send,
    sums_recv,
    choice_send,
    choice_recv,
    mate_send,
    mate_recv,
    cross_local,
    cross_send,
    cross_recv,
    placed_local,
    placed_send,
    placed_recv,
    shard_local,
    shard_send,
    shard_recv,
    expert_local,
    expert_send,
    expert_recv,
    out_sem,
    *reduce_buffers,
):
    size, split, chips, experts_local = sizes
    f32, half = jnp.float32, jnp.bfloat16
    me, mine = lax.axis_index("seq"), lax.axis_index("fsdp")
    tok_rows, model_width = tokens_ref.shape
    length, local_width = q_ref.shape
    part = model_width // split
    head = HEAD_DIM
    heads = local_width // head

    inputs = tokens_ref[...].astype(f32)
    inverse = lax.rsqrt(jnp.mean(inputs * inputs, -1, keepdims=True) + EPSILON)
    gains_ref[...] = gains_in_ref[...].astype(f32)
    routed_own[...] = (inputs * inverse * gains_ref[0:1, :]).astype(half)
    crossed = split == experts_local == 4
    half_width = model_width // 2
    x_mate, y_mate = {"fsdp": partner_of(mine, 1)}, {"fsdp": partner_of(mine, 2)}
    greet_all(size, split)

    def gather(index, x_ref, out_ref):
        return ChainGather(
            chips,
            x_ref,
            out_ref,
            gather_local.at[index],
            gather_send.at[index],
            gather_recv.at[index],
        )

    first = gather(0, routed_own, normed)
    first.start()

    cross_rows = pl.ds(tok_rows, tok_rows)
    lower, upper = pl.ds(0, half_width), pl.ds(half_width, half_width)

    def cross_copy(index):
        cols = (lower, upper)[index]
        return pltpu.make_async_remote_copy(
            src_ref=cotangent_ref.at[:, cols],
            dst_ref=cotangent_pair.at[cross_rows, cols],
            send_sem=cross_send.at[index],
            recv_sem=cross_recv.at[index],
            device_id=(x_mate, y_mate)[index],
        )

    if crossed:
        cross_own = pltpu.make_async_copy(
            cotangent_ref, cotangent_pair.at[pl.ds(0, tok_rows)], cross_local
        )
        cross_copy(0).start()
        cross_copy(1).start()
        cross_own.start()

    top_count = ids_ref.shape[1]
    same = lax.broadcasted_iota(jnp.int32, (top_count, top_count), 0) == (
        lax.broadcasted_iota(jnp.int32, (top_count, top_count), 1)
    )
    ids_row = row_sums(ids_ref[...].astype(f32), same.astype(f32))
    slots_row = row_sums(slots_ref[...].astype(f32), same.astype(f32))
    choice_own[0:top_count, :] = ids_row.astype(jnp.int32)
    choice_own[top_count : 2 * top_count, :] = jnp.where(
        slots_row < CAP, ids_row * CAP + slots_row, -1e6
    ).astype(jnp.int32)

    def choice_copy(shift):
        return pltpu.make_async_remote_copy(
            src_ref=choice_own,
            dst_ref=choices.at[me],
            send_sem=choice_send.at[shift],
            recv_sem=choice_recv.at[shift],
            device_id={"seq": lax.rem(me + shift, size)},
        )

    own_part = pl.ds(pl.multiple_of(mine * part, part), part)
    shard_pairs = (
        (wq_ref, qkv.at[0, own_part]),
        (wk_ref, qkv.at[1, own_part]),
        (wv_ref, qkv.at[2, own_part]),
        (wo_ref, rows_full.at[mine]),
    )

    def shard_copy(index, shift):
        source, target = shard_pairs[index]
        return pltpu.make_async_remote_copy(
            src_ref=source,
            dst_ref=target,
            send_sem=shard_send.at[index, shift],
            recv_sem=shard_recv.at[index, shift],
            device_id={"fsdp": lax.rem(mine + shift, split)},
        )

    def landed_half(index, owner, side):
        if index == 3:
            rows = local_width // 2
            return rows_full.at[owner, pl.ds(side * rows, rows)]
        rows = part // 2
        start = pl.multiple_of(owner * part + side * rows, rows)
        return qkv.at[index, pl.ds(start, rows)]

    def relay_copy(index, step):
        if step < 2:
            source, target = shard_pairs[index]
        else:
            source = target = landed_half(index, partner_of(mine, step - 1), step - 2)
        return pltpu.make_async_remote_copy(
            src_ref=source,
            dst_ref=target,
            send_sem=shard_send.at[index, step],
            recv_sem=shard_recv.at[index, step],
            device_id=(x_mate, y_mate, y_mate, x_mate)[step],
        )

    def shard_own(index):
        source, target = shard_pairs[index]
        return pltpu.make_async_copy(source, target, shard_local.at[index])

    for index in range(4):
        if split == 4:
            relay_copy(index, 0).start()
            relay_copy(index, 1).start()
        else:
            for shift in range(1, split):
                shard_copy(index, shift).start()
        shard_own(index).start()

    def expert_pair(index, dest):
        expert = lax.rem(dest, experts_local)
        if index == 2:
            return w_down_ref.at[expert], down_full.at[:, own_part]
        source, target = ((w_gate_ref, gate_full), (w_up_ref, up_full))[index]
        return source.at[expert], target.at[own_part]

    def expert_copy(index, shift):
        dest = lax.rem(mine + shift, split)
        source, target = expert_pair(index, dest)
        return pltpu.make_async_remote_copy(
            src_ref=source,
            dst_ref=target,
            send_sem=expert_send.at[index, shift],
            recv_sem=expert_recv.at[index, shift],
            device_id={"fsdp": dest},
        )

    def expert_own(index):
        source, target = expert_pair(index, mine)
        return pltpu.make_async_copy(source, target, expert_local.at[index])

    for distance in range(1, chips):
        first.step(distance)
        if split == 4 and distance == min(2, chips - 1):
            for index in range(4):
                for step in range(2):
                    relay_copy(index, step).wait_recv()
                    relay_copy(index, step + 2).start()
    for index in range(4):
        shard_own(index).wait()
        if split == 4:
            relay_copy(index, 2).wait_recv()
            relay_copy(index, 3).wait_recv()
        else:
            for shift in range(1, split):
                shard_copy(index, shift).wait_recv()
    for index in range(3):
        for shift in range(1, split):
            expert_copy(index, shift).start()
        expert_own(index).start()
    first.landed()
    for shift in range(1, size):
        choice_copy(shift).start()
    choices[me] = choice_own[...]
    if crossed:
        cross_own.wait()
        cross_copy(0).wait()
        cross_copy(1).wait()
        second = gather(1, cotangent_pair, cotangent_all)
    else:
        second = gather(1, cotangent_ref, cotangent_all)
    second.start()
    keeps = [
        pltpu.make_async_copy(normed, normed_out, out_sem.at[0]),
        pltpu.make_async_copy(qkv, qkv_out, out_sem.at[1]),
        pltpu.make_async_copy(rows_full, rows_out, out_sem.at[2]),
    ]
    for keep in keeps:
        keep.start()

    own_cols = pl.ds(pl.multiple_of(me * local_width, local_width), local_width)
    block = min(512, length)
    lanes = lax.broadcasted_iota(jnp.int32, (8, local_width), 0)
    first_row, second_row = (lanes == 0).astype(f32), (lanes == 1).astype(f32)

    @pl.loop(0, length // block)
    def _(step):
        rows = pl.ds(pl.multiple_of(step * block, block), block)
        left = normed[rows, :]
        query = jnp.dot(left, qkv[0], preferred_element_type=f32)
        raw[0, rows, :] = query
        keys = jnp.dot(left, qkv[1], preferred_element_type=f32)
        raw[1, rows, :] = keys
        sums_own[:, rows] = row_sums(query * query, first_row) + row_sums(keys * keys, second_row)
        v_ref[rows, :] = jnp.dot(left, qkv[2], preferred_element_type=f32).astype(half)

    def sums_copy(shift):
        return pltpu.make_async_remote_copy(
            src_ref=sums_own,
            dst_ref=sums_in.at[me],
            send_sem=sums_send.at[shift],
            recv_sem=sums_recv.at[shift],
            device_id={"seq": lax.rem(me + shift, size)},
        )

    for shift in range(1, size):
        sums_copy(shift).start()
    sums_in[me] = sums_own[...]
    for shift in range(1, size):
        sums_copy(shift).wait()
    sums_ref[...] = jnp.sum(sums_in[...], 0)
    for shift in range(1, size):
        choice_copy(shift).wait()

    def mate_copy(index):
        return pltpu.make_async_remote_copy(
            src_ref=choices,
            dst_ref=mate_choices.at[index],
            send_sem=mate_send.at[index],
            recv_sem=mate_recv.at[index],
            device_id=(x_mate, y_mate)[index],
        )

    if crossed:
        mate_copy(0).start()
        mate_copy(1).start()
    segments = seg_row_ref[...].astype(f32)
    narrow = first_row[:, 0:128]

    @pl.loop(0, length // block)
    def _(step):
        rows = pl.ds(pl.multiple_of(step * block, block), block)
        square_sums = sums_ref[:, rows]
        seg_col_ref[rows, :] = column_of(
            jnp.broadcast_to(seg_row_ref[:, rows].astype(f32), (8, block)), narrow
        )
        for index, pick, target in ((0, first_row, q_ref), (1, second_row, k_ref)):
            scale = lax.rsqrt(column_of(square_sums, pick) / model_width + EPSILON)
            unit = raw[index, rows, :] * scale
            unit_ref[index, rows, :] = unit
            scaled = unit * gains_ref[2 + index : 3 + index, own_cols]
            for number in range(heads):
                cols = slice(number * head, (number + 1) * head)
                piece = scaled[:, cols]
                target[rows, cols] = (
                    piece * cos_ref[rows, :] + turned_halves(piece) * sin_ref[rows, :]
                ).astype(half)

    second.step(1)

    wide = min(256, length)
    for number in range(heads):
        cols = slice(number * head, (number + 1) * head)

        @pl.loop(0, length // wide)
        def _(step):
            rows = pl.ds(pl.multiple_of(step * wide, wide), wide)
            scores = lax.dot_general(
                q_ref[rows, cols],
                k_ref[:, cols],
                (((1,), (1,)), ((), ())),
                preferred_element_type=f32,
            )
            scores = scores * (head**-0.5)
            scores = jnp.where(seg_col_ref[rows, 0:1] == segments, scores, MASKED)
            peak = jnp.max(scores, -1, keepdims=True)
            grown = jnp.exp(scores - peak)
            weight = jnp.sum(grown, -1, keepdims=True)
            probs = (grown * (1.0 / weight)).astype(half)
            attended_ref[rows, cols] = jnp.dot(
                probs, v_ref[:, cols], preferred_element_type=f32
            ).astype(half)
            log_ref[rows, cols] = jnp.broadcast_to(peak + jnp.log(weight), (wide, head))

        if number + 2 < chips:
            second.step(number + 2)

    for distance in range(heads + 2, chips):
        second.step(distance)

    reduce = ChainReduce(chips, residual_ref, reduce_buffers)

    def product(index, store):
        left = attended_ref[pl.ds(pl.multiple_of(index * tok_rows, tok_rows), tok_rows), :]
        for piece in range(split):
            cols = pl.ds(piece * part, part)
            store(cols, jnp.dot(left, rows_full[piece], preferred_element_type=f32))

    reduce.run(product)
    residual = tokens_ref[...].astype(f32) + reduce.total[...]
    residual_ref[...] = residual
    inverse = lax.rsqrt(jnp.mean(residual * residual, -1, keepdims=True) + EPSILON)
    first.sent()
    routed_own[...] = (residual * inverse * gains_ref[1:2, :]).astype(half)
    third = gather(2, routed_own, routed_out)
    third.start()

    second.landed()
    double = 2 * CAP
    member = lax.rem(mine, experts_local)
    slot_row = lax.broadcasted_iota(jnp.int32, (double, tok_rows), 0)
    if crossed:
        mate_copy(0).wait()
        mate_copy(1).wait()

    def one_hot(places, target, rows, expert):
        base = (me * experts_local + expert) * CAP
        for side in range(2):
            want = jnp.where(slot_row // CAP == side, slot_row - side * CAP + base, -1)
            hit = want == places(side)[top_count : top_count + 1, :]
            for choice in range(1, top_count):
                hit = hit | (want == places(side)[top_count + choice : top_count + choice + 1, :])
            cols = slice(side * tok_rows, (side + 1) * tok_rows)
            target[rows, cols] = jnp.where(hit, 1.0, 0.0).astype(half)

    def slot_range(move):
        return slice(move * double, (move + 1) * double)

    @pl.loop(0, size // 2)
    def _(pair):
        for move in range(experts_local):
            one_hot(
                lambda side: choices[pair * 2 + side],
                onehot_ref.at[pair],
                slot_range(move),
                partner_of(member, move),
            )
        if crossed:
            start = pl.multiple_of(pair * 4 * tok_rows, 4 * tok_rows)
            four = cotangent_all[pl.ds(start, 4 * tok_rows), :]
            own = jnp.concatenate(
                [four[0:tok_rows], four[2 * tok_rows : 3 * tok_rows]], 0
            )
            mates = jnp.concatenate(
                [four[tok_rows : 2 * tok_rows], four[3 * tok_rows : 4 * tok_rows]], 0
            )
            made = jnp.dot(onehot_ref[pair], own, preferred_element_type=f32).astype(half)
            placed[0, pair] = made[slot_range(0)]
            placed[1, pair, :, upper] = made[slot_range(1), half_width:]
            placed[2, pair, :, lower] = made[slot_range(2), :half_width]
            for index in range(2):
                for row, expert in enumerate((member, partner_of(member, 2 - index))):
                    one_hot(
                        lambda side: mate_choices[index, pair * 2 + side],
                        mate_onehot.at[index],
                        slot_range(row),
                        expert,
                    )
                cols = (lower, upper)[index]
                taken = mates[:, :half_width] if index == 0 else mates[:, half_width:]
                made = jnp.dot(mate_onehot[index], taken, preferred_element_type=f32).astype(half)
                placed[index + 1, pair, :, cols] = made[slot_range(0)]
                placed[3, pair, :, cols] = made[slot_range(1)]
        else:
            start = pl.multiple_of(pair * 2 * tok_rows, 2 * tok_rows)
            made = jnp.dot(
                onehot_ref[pair],
                cotangent_all[pl.ds(start, 2 * tok_rows), :],
                preferred_element_type=f32,
            ).astype(half)
            for move in range(experts_local):
                placed[move, pair] = made[slot_range(move)]

    def placed_copy(index):
        if crossed:
            move, cols = ((1, upper), (2, lower), (3, upper), (3, lower))[index]
            source, target = placed.at[move, :, :, cols], cotangent_rows.at[move, :, :, cols]
            mate = (x_mate, y_mate)[index % 2]
        else:
            source, target = placed.at[index], cotangent_rows.at[index]
            mate = {"fsdp": partner_of(mine, index)}
        return pltpu.make_async_remote_copy(
            src_ref=source,
            dst_ref=target,
            send_sem=placed_send.at[index],
            recv_sem=placed_recv.at[index],
            device_id=mate,
        )

    if crossed:
        placed_pieces = [
            (placed.at[0], cotangent_rows.at[0]),
            (placed.at[1, :, :, lower], cotangent_rows.at[1, :, :, lower]),
            (placed.at[2, :, :, upper], cotangent_rows.at[2, :, :, upper]),
        ]
    else:
        placed_pieces = [(placed.at[0], cotangent_rows.at[0])]
    placed_sends = [placed_copy(index) for index in range(0 if crossed else 1, experts_local)]
    placed_owns = [
        pltpu.make_async_copy(source, target, placed_local.at[index])
        for index, (source, target) in enumerate(placed_pieces)
    ]
    for copy in placed_sends + placed_owns:
        copy.start()
    third.steps()
    third.landed()
    reduce.sent()
    second.sent()
    third.sent()
    for index in range(4):
        if split == 4:
            for step in range(4):
                relay_copy(index, step).wait_send()
        else:
            for shift in range(1, split):
                shard_copy(index, shift).wait_send()
    for keep in keeps:
        keep.wait()
    for copy in placed_sends + placed_owns:
        copy.wait()
    for index in range(3):
        expert_own(index).wait()
        for shift in range(1, split):
            expert_copy(index, shift).wait()


def front(sizes, tokens, gains, cos, sin, segment_row, ids, slots, cotangent, weights, which):
    size, split, chips, experts_local = sizes
    w_query, w_key, w_value, w_out, w_gate, w_up, w_down = weights
    tok_rows, model_width = tokens.shape
    length = size * tok_rows
    local_width = w_query.shape[1]
    hidden_width = w_gate.shape[2]
    f32, half = jnp.float32, jnp.bfloat16
    vmem = pl.BlockSpec(memory_space=pltpu.VMEM)
    anywhere = pl.BlockSpec(memory_space=pl.ANY)
    kind = pltpu.SemaphoreType.DMA
    shape = jax.ShapeDtypeStruct
    crossed = split == experts_local == 4
    choices = (size, 2 * ids.shape[1], tok_rows)
    return pl.pallas_call(
        functools.partial(front_kernel, sizes),
        out_shape=(
            shape((length, model_width), half),
            shape((3, model_width, local_width), half),
            shape((split, *w_out.shape), half),
            shape((length, local_width), half),
            shape((length, local_width), half),
            shape((length, local_width), half),
            shape((2, length, local_width), f32),
            shape((8, length), f32),
            shape((length, local_width), f32),
            shape((length, local_width), half),
            shape((tok_rows, model_width), f32),
            shape(gains.shape, f32),
            shape((length, 128), f32),
            shape((length, model_width), half),
            shape((experts_local, size // 2, 2 * CAP, model_width), half),
            shape((model_width, hidden_width), half),
            shape((model_width, hidden_width), half),
            shape((hidden_width, model_width), half),
            shape((size, 2 * ids.shape[1], tok_rows), jnp.int32),
            shape((size // 2, experts_local * 2 * CAP, 2 * tok_rows), half),
        ),
        in_specs=[vmem] * 7 + [anywhere] * 8,
        out_specs=tuple([anywhere] * 3 + [vmem] * 10 + [anywhere] * 5 + [vmem] * 2),
        scratch_shapes=[
            pltpu.VMEM((length, model_width), half),
            pltpu.VMEM((3, model_width, local_width), half),
            pltpu.VMEM((split, *w_out.shape), half),
            pltpu.VMEM((tok_rows, model_width), half),
            pltpu.VMEM((2 * ids.shape[1], tok_rows), jnp.int32),
            pltpu.VMEM((2 * tok_rows if crossed else 16, model_width), half),
            pltpu.VMEM(((2 if crossed else 1) * length, model_width), half),
            pltpu.VMEM((2, *(choices if crossed else (1, 8, 128))), jnp.int32),
            pltpu.VMEM((2, 4 * CAP if crossed else 16, 2 * tok_rows), half),
            pltpu.VMEM((experts_local, size // 2, 2 * CAP, model_width), half),
            pltpu.VMEM((2, length, local_width), f32),
            pltpu.VMEM((8, length), f32),
            pltpu.VMEM((size, 8, length), f32),
            kind((3,)),
            kind((3, 3, chips)),
            kind((3, 2, chips)),
            kind((size,)),
            kind((size,)),
            kind((size,)),
            kind((size,)),
            kind((2,)),
            kind((2,)),
            kind,
            kind((2,)),
            kind((2,)),
            kind((3,)),
            kind((experts_local,)),
            kind((experts_local,)),
            kind((4,)),
            kind((4, split)),
            kind((4, split)),
            kind((3,)),
            kind((3, split)),
            kind((3, split)),
            kind((3,)),
            *ChainReduce.scratch(chips, tok_rows, model_width),
        ],
        compiler_params=pltpu.CompilerParams(
            collective_id=which, has_side_effects=True, vmem_limit_bytes=58 * 2**20
        ),
        cost_estimate=pl.CostEstimate(
            flops=2 * length * model_width * local_width * 4,
            bytes_accessed=500 * 2**20,
            transcendentals=0,
        ),
    )(
        tokens, gains, cos, sin, segment_row, ids, slots, cotangent, *weights
    )


class ShardSend:
    def __init__(self, split, source, landing, local_sem, sends, arrivals):
        self.split, self.source, self.landing = split, source, landing
        self.local_sem, self.sends, self.arrivals = local_sem, sends, arrivals
        self.mine = lax.axis_index("fsdp")

    def copy(self, shift):
        dest = lax.rem(self.mine + shift, self.split)
        return pltpu.make_async_remote_copy(
            src_ref=self.source(dest),
            dst_ref=self.landing.at[self.mine],
            send_sem=self.sends.at[shift],
            recv_sem=self.arrivals.at[shift],
            device_id={"fsdp": dest},
        )

    def own(self):
        return pltpu.make_async_copy(
            self.source(self.mine), self.landing.at[self.mine], self.local_sem
        )

    def start(self):
        for shift in range(1, self.split):
            self.copy(shift).start()
        self.own().start()

    def wait(self):
        for shift in range(1, self.split):
            self.copy(shift).wait()
        self.own().wait()


def turned_dot(left, right):
    return lax.dot_general(
        left, right, (((0,), (0,)), ((), ())), preferred_element_type=jnp.float32
    )


def cross_dot(left, right):
    return lax.dot_general(
        left, right, (((1,), (1,)), ((), ())), preferred_element_type=jnp.float32
    )


def experts_kernel(
    sizes,
    routed_ref,
    choices_ref,
    onehot_ref,
    cotangent_rows_ref,
    router_ref,
    gains_ref,
    residual_ref,
    cotangent_ref,
    gate_ref,
    up_ref,
    down_ref,
    residual_grad_ref,
    out_grad_ref,
    gain_ref,
    router_grad_ref,
    combine_ref,
    hidden_out,
    grad_gate_ref,
    grad_up_ref,
    down_landing,
    gate_full,
    up_full,
    down_full,
    upstream,
    pair_rows,
    outgoing,
    arrived,
    hidden,
    gate_grad,
    up_grad,
    back,
    gates,
    gates_out,
    gates_in,
    dots_out,
    dots_in,
    token_out,
    token_in,
    scales,
    load_sem,
    pair_sem,
    keep_sem,
    rows_send,
    rows_recv,
    gates_send,
    gates_recv,
    back_send,
    back_recv,
    dots_send,
    dots_recv,
    token_send,
    token_recv,
    down_send,
    down_recv,
    *reduce_buffers,
):
    size, split, chips, experts_local = sizes
    f32, half = jnp.float32, jnp.bfloat16
    me, mine = lax.axis_index("seq"), lax.axis_index("fsdp")
    tok_rows, model_width = residual_ref.shape
    pairs = size // 2
    double = 2 * CAP
    wide = 2 * tok_rows
    hidden_width = gate_full.shape[1]
    rows_of = pairs * double
    part = model_width // split
    member = lax.rem(mine, experts_local)

    loads = [
        pltpu.make_async_copy(source, target, load_sem.at[index])
        for index, (source, target) in enumerate(
            (
                (gate_ref, gate_full),
                (up_ref, up_full),
                (down_ref, down_full),
                (cotangent_rows_ref, upstream),
            )
        )
    ]

    slots = pair_rows.shape[0]

    def pair_load(pair):
        slot = lax.rem(pair, slots)
        start = pl.multiple_of(pair * wide, wide)
        return pltpu.make_async_copy(
            routed_ref.at[pl.ds(start, wide)], pair_rows.at[slot], pair_sem.at[slot]
        )

    pair_load(0).start()
    for load in loads:
        load.start()
    greet_all(size, split)

    padded = size * 8
    expert_row = lax.broadcasted_iota(jnp.int32, (padded, tok_rows), 0)
    inner = lax.rem(expert_row, 8)
    expert_row = jnp.where(inner < experts_local, expert_row // 8 * experts_local + inner, -1)
    ones = jnp.ones((8, wide), f32)
    top_count = choices_ref.shape[1] // 2

    @pl.loop(0, pairs)
    def _(pair):
        pair_load(pair).wait()

        @pl.when((pair + 1 < pairs) & (slots > 1))
        def _():
            pair_load(pair + 1).start()

        rows = pair_rows[lax.rem(pair, slots)]
        logits = lax.dot_general(
            router_ref[...], rows, (((1,), (1,)), ((), ())), preferred_element_type=f32
        )
        for side in range(2):
            ids = choices_ref[pair * 2 + side]
            chosen = expert_row == ids[0:1, :]
            for choice in range(1, top_count):
                chosen = chosen | (expert_row == ids[choice : choice + 1, :])
            own = jnp.where(chosen, logits[:, side * tok_rows : (side + 1) * tok_rows], MASKED)
            grown = jnp.where(chosen, jnp.exp(own - jnp.max(own, 0, keepdims=True)), 0.0)
            gates[pair * 2 + side] = grown / jnp.sum(grown, 0, keepdims=True)
        placed = jnp.dot(onehot_ref[pair], rows, preferred_element_type=f32).astype(half)
        for move in range(experts_local):
            piece = placed[move * double : (move + 1) * double]
            if move:
                outgoing[move - 1, pair] = piece
            else:
                arrived[0, pair] = piece
            row = me * 8 + partner_of(member, move)
            weights = jnp.concatenate(
                [gates[pair * 2, pl.ds(row, 1), :], gates[pair * 2 + 1, pl.ds(row, 1), :]], 1
            )
            slot_rows = pl.ds(move * double, double)
            weighted = onehot_ref[pair, slot_rows, :].astype(f32) * weights
            combine_ref[pair, slot_rows, :] = weighted.astype(half)
            gates_out[move, pair] = row_sums(weighted, ones)

        @pl.when((pair + 1 < pairs) & (slots == 1))
        def _():
            pair_load(pair + 1).start()

    def mate(move):
        return {"fsdp": partner_of(mine, move)}

    def rows_copy(move):
        return pltpu.make_async_remote_copy(
            src_ref=outgoing.at[move - 1],
            dst_ref=arrived.at[move],
            send_sem=rows_send.at[move],
            recv_sem=rows_recv.at[move],
            device_id=mate(move),
        )

    def gates_copy(move):
        return pltpu.make_async_remote_copy(
            src_ref=gates_out.at[move],
            dst_ref=gates_in.at[move],
            send_sem=gates_send.at[move],
            recv_sem=gates_recv.at[move],
            device_id=mate(move),
        )

    def back_rows(move):
        return back.at[:, pl.ds(move * double, double), :]

    def back_copy(move):
        return pltpu.make_async_remote_copy(
            src_ref=outgoing.at[move - 1],
            dst_ref=back_rows(move),
            send_sem=back_send.at[move],
            recv_sem=back_recv.at[move],
            device_id=mate(move),
        )

    def dots_copy(move):
        return pltpu.make_async_remote_copy(
            src_ref=dots_out.at[move],
            dst_ref=dots_in.at[move],
            send_sem=dots_send.at[move],
            recv_sem=dots_recv.at[move],
            device_id=mate(move),
        )

    order = list(range(experts_local - 1, 0, -1))
    for move in order:
        gates_copy(move).start()
        rows_copy(move).start()
    gates_in[0] = gates_out[0]
    for load in loads:
        load.wait()

    cols_step = min(256, hidden_width)
    width_step = min(512, model_width)
    spread = (lax.broadcasted_iota(jnp.int32, (8, 128), 0) == 0).astype(f32)
    for move in [0] + order:
        if move:
            gates_copy(move).wait()
            rows_copy(move).wait()
        for pair in range(pairs):
            scales[pair * double : (pair + 1) * double, :] = column_of(
                gates_in[move, pair], spread
            )
        dots_out[move] = jnp.zeros_like(dots_out[move])

        @pl.loop(0, hidden_width // cols_step)
        def _(index):
            cols = pl.ds(pl.multiple_of(index * cols_step, cols_step), cols_step)
            rows = arrived[move].reshape(rows_of, model_width)
            pre = jnp.dot(rows, gate_full[:, cols], preferred_element_type=f32)
            up = jnp.dot(rows, up_full[:, cols], preferred_element_type=f32)
            plain = lax.dot_general(
                upstream[move].reshape(rows_of, model_width),
                down_full[cols, :],
                (((1,), (1,)), ((), ())),
                preferred_element_type=f32,
            )
            sigmoid = 1.0 / (1.0 + jnp.exp(-pre))
            active = pre * sigmoid
            made = (active * up).astype(half)
            hidden[move, :, :, cols] = made.reshape(pairs, double, cols_step)
            dots = made.astype(f32) * plain
            for pair in range(pairs):
                dots_out[move, pair] += row_sums(
                    dots[pair * double : (pair + 1) * double], jnp.ones((8, cols_step), f32)
                )
            scaled = plain * scales[:, 0:1]
            gate_back = scaled * up * sigmoid * (1.0 + pre * (1.0 - sigmoid))
            gate_grad[move, :, :, cols] = gate_back.astype(half).reshape(pairs, double, cols_step)
            up_grad[move, :, :, cols] = (
                (scaled * active).astype(half).reshape(pairs, double, cols_step)
            )

        for pair in range(pairs):
            scale = scales[pair * double : (pair + 1) * double, 0:1]
            upstream[move, pair] = (upstream[move, pair].astype(f32) * scale).astype(half)

        if move:
            dots_copy(move).start()
        else:
            dots_in[0] = dots_out[0]

        @pl.loop(0, model_width // width_step)
        def _(index):
            cols = pl.ds(pl.multiple_of(index * width_step, width_step), width_step)
            rows_grad = lax.dot_general(
                gate_grad[move].reshape(rows_of, hidden_width),
                gate_full[cols, :],
                (((1,), (1,)), ((), ())),
                preferred_element_type=f32,
            )
            rows_grad = rows_grad + lax.dot_general(
                up_grad[move].reshape(rows_of, hidden_width),
                up_full[cols, :],
                (((1,), (1,)), ((), ())),
                preferred_element_type=f32,
            )
            rows_grad = rows_grad.astype(half).reshape(pairs, double, width_step)
            if move:
                outgoing[move - 1, :, :, cols] = rows_grad
            else:
                back[:, 0:double, cols] = rows_grad

        if move:
            back_copy(move).start()

    own_rows = pl.ds(pl.multiple_of(me * tok_rows, tok_rows), tok_rows)
    own_load = pltpu.make_async_copy(
        routed_ref.at[own_rows], pair_rows.at[0, pl.ds(0, tok_rows)], pair_sem.at[0]
    )
    own_load.start()
    hidden_keep = pltpu.make_async_copy(hidden, hidden_out, keep_sem)
    hidden_keep.start()

    total_rows = experts_local * rows_of

    def flat(ref, cols):
        return ref[:, :, :, cols].reshape(total_rows, -1)

    every = pl.ds(0, hidden_width)

    @pl.loop(0, split)
    def _(piece):
        cols = pl.ds(pl.multiple_of(piece * part, part), part)
        gate_full[cols, :] = turned_dot(flat(arrived, cols), flat(gate_grad, every)).astype(half)
        up_full[cols, :] = turned_dot(flat(arrived, cols), flat(up_grad, every)).astype(half)
        down_full[:, cols] = turned_dot(flat(hidden, every), flat(upstream, cols)).astype(half)

    grad_keeps = [
        pltpu.make_async_copy(source, target, load_sem.at[index])
        for index, (source, target) in enumerate(
            ((gate_full, grad_gate_ref), (up_full, grad_up_ref))
        )
    ]
    for keep in grad_keeps:
        keep.start()
    down_send_all = ShardSend(
        split,
        lambda dest: down_full.at[:, pl.ds(pl.multiple_of(dest * part, part), part)],
        down_landing,
        load_sem.at[2],
        down_send,
        down_recv,
    )

    for move in order:
        dots_copy(move).wait()
    token_out[...] = jnp.zeros_like(token_out)

    @pl.loop(0, pairs)
    def _(pair):
        for move in range(experts_local):
            found = jnp.dot(
                dots_in[move, pair],
                onehot_ref[pair, pl.ds(move * double, double), :].astype(f32),
                precision=HIGHEST,
                preferred_element_type=f32,
            )
            row = partner_of(member, move)
            for side in range(2):
                token_out[pair * 2 + side, pl.ds(row, 1), :] = found[
                    0:1, side * tok_rows : (side + 1) * tok_rows
                ]

    def token_copy(shift):
        peer = lax.rem(me + shift, size)
        return pltpu.make_async_remote_copy(
            src_ref=token_out.at[peer],
            dst_ref=token_in.at[me],
            send_sem=token_send.at[shift],
            recv_sem=token_recv.at[shift],
            device_id={"seq": peer},
        )

    for shift in range(1, size):
        token_copy(shift).start()
    token_in[me] = token_out[me]
    for move in order:
        back_copy(move).wait()
    down_send_all.start()

    reduce = ChainReduce(chips, residual_grad_ref, reduce_buffers)

    def product(index, store):
        side = pl.ds(pl.multiple_of(lax.rem(index, 2) * tok_rows, tok_rows), tok_rows)
        left = onehot_ref[index // 2, :, side]

        @pl.loop(0, model_width // width_step)
        def _(step):
            cols = pl.ds(pl.multiple_of(step * width_step, width_step), width_step)
            store(cols, turned_dot(left, back[index // 2, :, cols]))

    reduce.run(product)

    for shift in range(1, size):
        token_copy(shift).wait()
    own_gates = gates[me]
    grads = token_in[...].reshape(padded, tok_rows)
    mean = jnp.sum(own_gates * grads, 0, keepdims=True)
    logit_grad = (own_gates * (grads - mean)).astype(half)
    routed_grad = reduce.total[...] + turned_dot(logit_grad, router_ref[...])
    own_load.wait()
    router_grad = jnp.dot(logit_grad, pair_rows[0, 0:tok_rows, :], preferred_element_type=f32)
    for device in range(size):
        router_grad_ref[device * experts_local : (device + 1) * experts_local, :] = router_grad[
            device * 8 : device * 8 + experts_local
        ]
    residual = residual_ref[...]
    inverse = lax.rsqrt(jnp.mean(residual * residual, -1, keepdims=True) + EPSILON)
    unit = residual * inverse
    gain_ref[...] = jnp.broadcast_to(
        jnp.sum(routed_grad * unit, 0, keepdims=True), gain_ref.shape
    )
    routed_grad = routed_grad * gains_ref[1:2, :]
    routed_grad = inverse * (
        routed_grad - unit * jnp.mean(routed_grad * unit, -1, keepdims=True)
    )
    residual_grad = cotangent_ref[...].astype(f32) + routed_grad
    residual_grad_ref[...] = residual_grad
    out_grad_ref[...] = residual_grad.astype(half)
    reduce.sent()
    hidden_keep.wait()
    for keep in grad_keeps:
        keep.wait()
    down_send_all.wait()


def experts(
    sizes,
    routed_seq,
    choices,
    onehot,
    cotangent_rows,
    router_rows,
    gain_rows,
    residual,
    cotangent,
    weights,
    which,
):
    size, split, chips, experts_local = sizes
    gate_full, up_full, down_full = weights
    model_width, hidden_width = gate_full.shape
    tok_rows = residual.shape[0]
    pairs, double = size // 2, 2 * CAP
    f32, half = jnp.float32, jnp.bfloat16
    vmem = pl.BlockSpec(memory_space=pltpu.VMEM)
    anywhere = pl.BlockSpec(memory_space=pl.ANY)
    kind = pltpu.SemaphoreType.DMA
    shape = jax.ShapeDtypeStruct
    few = kind((experts_local,))
    wide_rows = (experts_local, pairs, double, model_width)
    narrow_rows = (experts_local, pairs, double, hidden_width)
    flags = (experts_local, pairs, 8, double)
    return pl.pallas_call(
        functools.partial(experts_kernel, sizes),
        out_shape=(
            shape((tok_rows, model_width), f32),
            shape((tok_rows, model_width), half),
            shape((8, model_width), f32),
            shape((size * experts_local, model_width), f32),
            shape(onehot.shape, half),
            shape(narrow_rows, half),
            shape(gate_full.shape, half),
            shape(up_full.shape, half),
            shape((split, hidden_width, model_width // split), half),
        ),
        in_specs=[anywhere, vmem, vmem, anywhere] + [vmem] * 4 + [anywhere] * 3,
        out_specs=tuple([vmem] * 5 + [anywhere] * 4),
        scratch_shapes=[
            pltpu.VMEM(gate_full.shape, half),
            pltpu.VMEM(up_full.shape, half),
            pltpu.VMEM(down_full.shape, half),
            pltpu.VMEM(wide_rows, half),
            pltpu.VMEM((2 if chips < 8 else 1, 2 * tok_rows, model_width), half),
            pltpu.VMEM((max(experts_local - 1, 1), *wide_rows[1:]), half),
            pltpu.VMEM(wide_rows, half),
            pltpu.VMEM(narrow_rows, half),
            pltpu.VMEM(narrow_rows, half),
            pltpu.VMEM(narrow_rows, half),
            pltpu.VMEM((pairs, experts_local * double, model_width), half),
            pltpu.VMEM((size, size * 8, tok_rows), f32),
            pltpu.VMEM(flags, f32),
            pltpu.VMEM(flags, f32),
            pltpu.VMEM(flags, f32),
            pltpu.VMEM(flags, f32),
            pltpu.VMEM((size, 8, tok_rows), f32),
            pltpu.VMEM((size, 8, tok_rows), f32),
            pltpu.VMEM((pairs * double, 128), f32),
            kind((4,)),
            kind((2,)),
            kind,
            few,
            few,
            few,
            few,
            few,
            few,
            few,
            few,
            kind((size,)),
            kind((size,)),
            kind((split,)),
            kind((split,)),
            *ChainReduce.scratch(chips, tok_rows, model_width),
        ],
        compiler_params=pltpu.CompilerParams(
            collective_id=which, has_side_effects=True, vmem_limit_bytes=63 * 2**20
        ),
        cost_estimate=pl.CostEstimate(
            flops=2 * experts_local * pairs * double * model_width * hidden_width * 8,
            bytes_accessed=500 * 2**20,
            transcendentals=0,
        ),
    )(
        routed_seq,
        choices,
        onehot,
        cotangent_rows,
        router_rows,
        gain_rows,
        residual,
        cotangent,
        gate_full,
        up_full,
        down_full,
    )

def back_kernel(
    sizes,
    out_grad_ref,
    tokens_ref,
    residual_grad_ref,
    gains_ref,
    second_gain_ref,
    cos_ref,
    sin_ref,
    seg_col_ref,
    seg_row_ref,
    q_ref,
    k_ref,
    v_ref,
    unit_ref,
    sums_ref,
    log_ref,
    attended_ref,
    qkv_ref,
    rows_full_ref,
    normed_ref,
    hidden_ref,
    down_ref,
    grad_gate_ref,
    input_grad_ref,
    gains_out_ref,
    query_w_grad_ref,
    key_w_grad_ref,
    value_w_grad_ref,
    out_w_grad_ref,
    mixed_rows,
    gate_landing,
    down_full,
    out_grads,
    attended_grad,
    hidden,
    returned,
    key_total,
    value_total,
    scaled,
    raw_grads,
    centers_own,
    centers_in,
    qkv_stage,
    qkv_landing,
    out_stage,
    out_landing,
    load_sem,
    gather_local,
    gather_send,
    gather_recv,
    gate_local,
    gate_send,
    gate_recv,
    rows_local,
    rows_send,
    rows_recv,
    centers_send,
    centers_recv,
    qkv_local,
    qkv_send,
    qkv_recv,
    out_local,
    out_send,
    out_recv,
    *reduce_buffers,
):
    size, split, chips, experts_local = sizes
    f32, half = jnp.float32, jnp.bfloat16
    me, mine = lax.axis_index("seq"), lax.axis_index("fsdp")
    tok_rows, model_width = tokens_ref.shape
    length, local_width = q_ref.shape
    hidden_width = down_ref.shape[0]
    part = model_width // split
    head = HEAD_DIM
    heads = local_width // head
    double = 2 * CAP
    pairs = size // 2
    rows_of = pairs * double

    down_load = pltpu.make_async_copy(down_ref, down_full, load_sem.at[0])
    hidden_load = pltpu.make_async_copy(hidden_ref, hidden, load_sem.at[1])
    down_load.start()
    hidden_load.start()
    greet_all(size, split)
    gather = ChainGather(chips, out_grad_ref, out_grads, gather_local, gather_send, gather_recv)
    gather.start()
    gate_send_all = ShardSend(
        split,
        lambda dest: grad_gate_ref.at[pl.ds(pl.multiple_of(dest * part, part), part)],
        gate_landing,
        gate_local,
        gate_send,
        gate_recv,
    )

    gate_send_all.start()

    down_load.wait()
    hidden_load.wait()
    width_step = min(512, model_width)

    def rows_target(move):
        return mixed_rows.at[:, pl.ds(move * double, double), :]

    def rows_copy(move):
        return pltpu.make_async_remote_copy(
            src_ref=returned.at[move],
            dst_ref=rows_target(move),
            send_sem=rows_send.at[move],
            recv_sem=rows_recv.at[move],
            device_id={"fsdp": partner_of(mine, move)},
        )

    own_rows = pltpu.make_async_copy(returned.at[0], rows_target(0), rows_local)
    for move in range(experts_local - 1, -1, -1):

        @pl.loop(0, model_width // width_step)
        def _(index):
            cols = pl.ds(pl.multiple_of(index * width_step, width_step), width_step)
            made = jnp.dot(
                hidden[move].reshape(rows_of, hidden_width),
                down_full[:, cols],
                preferred_element_type=f32,
            )
            returned[move, :, :, cols] = made.astype(half).reshape(pairs, double, width_step)

        if move:
            rows_copy(move).start()
    own_rows.start()
    gather.steps()
    gather.landed()

    block = min(512, length)

    @pl.loop(0, length // block)
    def _(step):
        rows = pl.ds(pl.multiple_of(step * block, block), block)
        total = cross_dot(out_grads[rows, 0:part], rows_full_ref[0])
        for piece in range(1, split):
            total += cross_dot(
                out_grads[rows, piece * part : (piece + 1) * part], rows_full_ref[piece]
            )
        attended_grad[rows, :] = total.astype(half)

    @pl.loop(0, split)
    def _(piece):
        cols = pl.ds(pl.multiple_of(piece * part, part), part)
        out_stage[piece] = turned_dot(attended_ref[...], out_grads[:, cols]).astype(half)

    out_send_all = ShardSend(
        split, lambda dest: out_stage.at[dest], out_landing, out_local, out_send, out_recv
    )
    out_send_all.start()
    gather.sent()
    normed_load = pltpu.make_async_copy(normed_ref, out_grads, load_sem.at[0])
    normed_load.start()

    wide = min(256, length) if length <= 1024 else 128
    scale = head**-0.5
    segments = seg_row_ref[...].astype(f32)
    for number in range(heads):
        cols = slice(number * head, (number + 1) * head)
        key_total[...] = jnp.zeros_like(key_total)
        value_total[...] = jnp.zeros_like(value_total)

        @pl.loop(0, length // wide)
        def _(step):
            rows = pl.ds(pl.multiple_of(step * wide, wide), wide)
            scores = cross_dot(q_ref[rows, cols], k_ref[:, cols]) * scale
            scores = jnp.where(seg_col_ref[rows, 0:1] == segments, scores, MASKED)
            probs = jnp.exp(scores - log_ref[rows, cols][:, 0:1])
            grads = attended_grad[rows, cols]
            prob_grad = cross_dot(grads, v_ref[:, cols])
            center = jnp.sum(probs * prob_grad, -1, keepdims=True)
            score_grad = (probs * (prob_grad - center)).astype(half)
            query_grad = jnp.dot(score_grad, k_ref[:, cols], preferred_element_type=f32) * scale
            raw_grads[0, rows, cols] = query_grad.astype(half)
            key_total[...] += turned_dot(score_grad, q_ref[rows, cols])
            value_total[...] += turned_dot(probs.astype(half), grads)

        raw_grads[1, :, cols] = (key_total[...] * scale).astype(half)
        raw_grads[2, :, cols] = value_total[...].astype(half)

    lanes = lax.broadcasted_iota(jnp.int32, (8, local_width), 0)
    first_row, second_row = (lanes == 0).astype(f32), (lanes == 1).astype(f32)
    gains_out_ref[...] = jnp.zeros_like(gains_out_ref)
    own_cols = pl.ds(pl.multiple_of(me * local_width, local_width), local_width)
    gains_out_ref[1:2, :] = second_gain_ref[0:1, :]

    @pl.loop(0, length // block)
    def _(step):
        rows = pl.ds(pl.multiple_of(step * block, block), block)
        found = jnp.zeros((8, block), f32)
        for index, pick in ((0, first_row), (1, second_row)):
            unit = unit_ref[index, rows, :]
            pieces = []
            for number in range(heads):
                cols = slice(number * head, (number + 1) * head)
                piece = raw_grads[index, rows, cols].astype(f32)
                pieces.append(piece * cos_ref[rows, :] - turned_halves(piece) * sin_ref[rows, :])
            unit_grad = pieces[0] if heads == 1 else jnp.concatenate(pieces, 1)
            gains_out_ref[2 + index : 3 + index, own_cols] += jnp.sum(
                unit_grad * unit, 0, keepdims=True
            )
            grown = unit_grad * gains_ref[2 + index : 3 + index, own_cols]
            scaled[index, rows, :] = grown
            found += row_sums(grown * unit, pick)
        centers_own[:, rows] = found

    def centers_copy(shift):
        return pltpu.make_async_remote_copy(
            src_ref=centers_own,
            dst_ref=centers_in.at[me],
            send_sem=centers_send.at[shift],
            recv_sem=centers_recv.at[shift],
            device_id={"seq": lax.rem(me + shift, size)},
        )

    for shift in range(1, size):
        centers_copy(shift).start()
    centers_in[me] = centers_own[...]
    for shift in range(1, size):
        centers_copy(shift).wait()
    centers_own[...] = jnp.sum(centers_in[...], 0) * (1.0 / model_width)

    @pl.loop(0, length // block)
    def _(step):
        rows = pl.ds(pl.multiple_of(step * block, block), block)
        for index, pick in ((0, first_row), (1, second_row)):
            inverse = lax.rsqrt(column_of(sums_ref[:, rows], pick) / model_width + EPSILON)
            center = column_of(centers_own[:, rows], pick)
            raw_grads[index, rows, :] = (
                inverse * (scaled[index, rows, :] - unit_ref[index, rows, :] * center)
            ).astype(half)

    reduce = ChainReduce(chips, input_grad_ref, reduce_buffers)

    def product(index, store):
        rows = pl.ds(pl.multiple_of(index * tok_rows, tok_rows), tok_rows)

        @pl.loop(0, model_width // width_step)
        def _(step):
            cols = pl.ds(pl.multiple_of(step * width_step, width_step), width_step)
            total = cross_dot(raw_grads[0, rows, :], qkv_ref[0, cols, :])
            total += cross_dot(raw_grads[1, rows, :], qkv_ref[1, cols, :])
            total += cross_dot(raw_grads[2, rows, :], qkv_ref[2, cols, :])
            store(cols, total)

    qkv_send_all = ShardSend(
        split, lambda dest: qkv_stage.at[dest], qkv_landing, qkv_local, qkv_send, qkv_recv
    )

    def between():
        normed_load.wait()

        @pl.loop(0, split)
        def _(piece):
            cols = pl.ds(pl.multiple_of(piece * part, part), part)
            left = out_grads[:, cols]
            for index in range(3):
                qkv_stage[piece, index] = turned_dot(left, raw_grads[index]).astype(half)

        qkv_send_all.start()

    reduce.run(product, between)

    inputs = tokens_ref[...].astype(f32)
    inverse = lax.rsqrt(jnp.mean(inputs * inputs, -1, keepdims=True) + EPSILON)
    unit = inputs * inverse
    grads = input_grad_ref[...]
    gains_out_ref[0:1, :] = jnp.sum(grads * unit, 0, keepdims=True)
    grads = grads * gains_ref[0:1, :]
    input_grad_ref[...] = residual_grad_ref[...] + inverse * (
        grads - unit * jnp.mean(grads * unit, -1, keepdims=True)
    )

    out_send_all.wait()
    total = out_landing[0].astype(f32)
    for index in range(1, split):
        total += out_landing[index].astype(f32)
    out_w_grad_ref[...] = total
    qkv_send_all.wait()
    for index, target in enumerate((query_w_grad_ref, key_w_grad_ref, value_w_grad_ref)):
        total = qkv_landing[0, index].astype(f32)
        for piece in range(1, split):
            total += qkv_landing[piece, index].astype(f32)
        target[...] = total
    reduce.sent()
    own_rows.wait()
    for move in range(1, experts_local):
        rows_copy(move).wait()
    gate_send_all.wait()


def back(sizes, out_grad, tokens, residual_grad, gains, kept, big_ones, which):
    size, split, chips, experts_local = sizes
    f32, half = jnp.float32, jnp.bfloat16
    tok_rows, model_width = tokens.shape
    query_heads = kept[4]
    length, local_width = query_heads.shape
    normed_seq, hidden, down_full, grad_gate = big_ones
    hidden_width = down_full.shape[0]
    part = model_width // split
    vmem = pl.BlockSpec(memory_space=pltpu.VMEM)
    anywhere = pl.BlockSpec(memory_space=pl.ANY)
    kind = pltpu.SemaphoreType.DMA
    shape = jax.ShapeDtypeStruct
    few, fsdp = kind((experts_local,)), kind((split,))
    return pl.pallas_call(
        functools.partial(back_kernel, sizes),
        out_shape=(
            shape((tok_rows, model_width), f32),
            shape((8, model_width), f32),
            shape((part, local_width), f32),
            shape((part, local_width), f32),
            shape((part, local_width), f32),
            shape((local_width, part), f32),
            shape((size // 2, experts_local * 2 * CAP, model_width), half),
            shape((split, part, hidden_width), half),
        ),
        in_specs=[vmem] * 18 + [anywhere] * 4,
        out_specs=tuple([vmem] * 6 + [anywhere] * 2),
        scratch_shapes=[
            pltpu.VMEM(down_full.shape, half),
            pltpu.VMEM((length, model_width), half),
            pltpu.VMEM((length, local_width), half),
            pltpu.VMEM(hidden.shape, half),
            pltpu.VMEM((experts_local, size // 2, 2 * CAP, model_width), half),
            pltpu.VMEM((length, HEAD_DIM), f32),
            pltpu.VMEM((length, HEAD_DIM), f32),
            pltpu.VMEM((2, length, local_width), f32),
            pltpu.VMEM((3, length, local_width), half),
            pltpu.VMEM((8, length), f32),
            pltpu.VMEM((size, 8, length), f32),
            pltpu.VMEM((split, 3, part, local_width), half),
            pltpu.VMEM((split, 3, part, local_width), half),
            pltpu.VMEM((split, local_width, part), half),
            pltpu.VMEM((split, local_width, part), half),
            kind((2,)),
            kind,
            kind((3, chips)),
            kind((2, chips)),
            kind,
            fsdp,
            fsdp,
            kind,
            few,
            few,
            kind((size,)),
            kind((size,)),
            kind,
            fsdp,
            fsdp,
            kind,
            fsdp,
            fsdp,
            *ChainReduce.scratch(chips, tok_rows, model_width),
        ],
        compiler_params=pltpu.CompilerParams(
            collective_id=which, has_side_effects=True, vmem_limit_bytes=63 * 2**20
        ),
        cost_estimate=pl.CostEstimate(
            flops=2 * length * model_width * local_width * 8,
            bytes_accessed=500 * 2**20,
            transcendentals=0,
        ),
    )(out_grad, tokens, residual_grad, *gains, *kept, *big_ones)


def close_kernel(
    sizes,
    mixed_rows_ref,
    combine_ref,
    residual_ref,
    gains_ref,
    router_ref,
    grad_up_ref,
    output_ref,
    gains_out_ref,
    router_out_ref,
    up_landing,
    total,
    small,
    first,
    second,
    final,
    up_local,
    up_send,
    up_recv,
    send_one,
    recv_one,
    send_two,
    recv_two,
    send_three,
    recv_three,
    *reduce_buffers,
):
    size, split, chips, experts_local = sizes
    f32 = jnp.float32
    me, mine = lax.axis_index("seq"), lax.axis_index("fsdp")
    tok_rows, model_width = residual_ref.shape
    part = model_width // split
    slice_width = model_width // size
    experts_all = router_ref.shape[0]
    small[0:8, :] = gains_ref[...]
    small[8 : 8 + experts_all, :] = router_ref[...]
    greet_all(size, split)
    up_send_all = ShardSend(
        split,
        lambda dest: grad_up_ref.at[pl.ds(pl.multiple_of(dest * part, part), part)],
        up_landing,
        up_local,
        up_send,
        up_recv,
    )
    up_send_all.start()

    def columns(index):
        return pl.ds(pl.multiple_of(index * slice_width, slice_width), slice_width)

    def scatter(shift):
        peer = lax.rem(me + shift, size)
        return pltpu.make_async_remote_copy(
            src_ref=small.at[:, columns(peer)],
            dst_ref=first.at[me],
            send_sem=send_one.at[shift],
            recv_sem=recv_one.at[shift],
            device_id={"seq": peer},
        )

    def share(shift):
        return pltpu.make_async_remote_copy(
            src_ref=second.at[mine],
            dst_ref=second.at[mine],
            send_sem=send_two.at[shift],
            recv_sem=recv_two.at[shift],
            device_id={"fsdp": lax.rem(mine + shift, split)},
        )

    def collect(shift):
        return pltpu.make_async_remote_copy(
            src_ref=final.at[me],
            dst_ref=final.at[me],
            send_sem=send_three.at[shift],
            recv_sem=recv_three.at[shift],
            device_id={"seq": lax.rem(me + shift, size)},
        )

    for shift in range(1, size):
        scatter(shift).start()
    first[me] = small[:, columns(me)]

    reduce = ChainReduce(chips, total, reduce_buffers)
    width_step = min(512, model_width)

    def product(index, store):
        side = pl.ds(pl.multiple_of(lax.rem(index, 2) * tok_rows, tok_rows), tok_rows)
        left = combine_ref[index // 2, :, side]

        @pl.loop(0, model_width // width_step)
        def _(step):
            cols = pl.ds(pl.multiple_of(step * width_step, width_step), width_step)
            store(cols, turned_dot(left, mixed_rows_ref[index // 2, :, cols]))

    def between():
        for shift in range(1, size):
            scatter(shift).wait_recv()
        second[mine] = jnp.sum(first[...], 0)
        for shift in range(1, split):
            share(shift).start()

    reduce.run(product, between)
    for shift in range(1, split):
        share(shift).wait_recv()
    final[me] = jnp.sum(second[...], 0)
    for shift in range(1, size):
        collect(shift).start()
    output_ref[...] = (residual_ref[...] + total[...]).astype(output_ref.dtype)
    for shift in range(1, size):
        scatter(shift).wait_send()
    for shift in range(1, split):
        share(shift).wait_send()
    for shift in range(1, size):
        collect(shift).wait()
    for index in range(size):
        cols = slice(index * slice_width, (index + 1) * slice_width)
        gains_out_ref[:, cols] = final[index, 0:4]
        router_out_ref[:, cols] = final[index, 8:]
    reduce.sent()
    up_send_all.wait()


def close(sizes, mixed_rows, combine, residual, gains, router_grad, grad_up, which):
    size, split, chips, experts_local = sizes
    f32, half = jnp.float32, jnp.bfloat16
    tok_rows, model_width = residual.shape
    hidden_width = grad_up.shape[1]
    part, slice_width = model_width // split, model_width // size
    rows = 8 + router_grad.shape[0]
    vmem = pl.BlockSpec(memory_space=pltpu.VMEM)
    anywhere = pl.BlockSpec(memory_space=pl.ANY)
    kind = pltpu.SemaphoreType.DMA
    shape = jax.ShapeDtypeStruct
    seq, fsdp = kind((size,)), kind((split,))
    return pl.pallas_call(
        functools.partial(close_kernel, sizes),
        out_shape=(
            shape((tok_rows, model_width), half),
            shape((4, model_width), f32),
            shape(router_grad.shape, f32),
            shape((split, part, hidden_width), half),
        ),
        in_specs=[vmem] * 5 + [anywhere],
        out_specs=(vmem, vmem, vmem, anywhere),
        scratch_shapes=[
            pltpu.VMEM((tok_rows, model_width), f32),
            pltpu.VMEM((rows, model_width), f32),
            pltpu.VMEM((size, rows, slice_width), f32),
            pltpu.VMEM((split, rows, slice_width), f32),
            pltpu.VMEM((size, rows, slice_width), f32),
            kind,
            fsdp,
            fsdp,
            seq,
            seq,
            fsdp,
            fsdp,
            seq,
            seq,
            *ChainReduce.scratch(chips, tok_rows, model_width),
        ],
        compiler_params=pltpu.CompilerParams(
            collective_id=which, has_side_effects=True, vmem_limit_bytes=56 * 2**20
        ),
    )(mixed_rows, combine, residual, gains, router_grad, grad_up)


def shards(
    tokens,
    norm_gains,
    w_query,
    w_key,
    w_value,
    w_out,
    w_router,
    w_gate,
    w_up,
    w_down,
    segment_ids,
    expert_ids,
    expert_slots,
    cotangent,
):
    half_type = jnp.bfloat16
    model_width = tokens.shape[1]
    experts_local = w_gate.shape[0]
    seq_size = lax.axis_size("seq")
    split = lax.axis_size("fsdp")
    length = seq_size * tokens.shape[0]
    sizes = (seq_size, split, seq_size // 2, experts_local)
    cosine_wide, sine_wide = rope_tables(length, HEAD_DIM)
    segment_row = segment_ids.reshape(1, -1)
    (
        normed_seq,
        qkv_stack,
        out_stack,
        query_heads,
        key_heads,
        value_heads,
        unit_pair,
        square_sums,
        log_wide,
        attended_heads,
        residual,
        gain_rows,
        segment_cols,
        routed_seq,
        cotangent_rows,
        gate_full,
        up_full,
        down_full,
        choices,
        onehot,
    ) = front(
        sizes,
        tokens,
        norm_gains,
        cosine_wide,
        sine_wide,
        segment_row,
        expert_ids,
        expert_slots,
        cotangent,
        (w_query, w_key, w_value, w_out, w_gate, w_up, w_down),
        0,
    )
    router_rows = jnp.zeros((seq_size, 8, model_width), half_type)
    router_rows = router_rows.at[:, :experts_local].set(
        w_router.T.reshape(seq_size, experts_local, model_width)
    )
    router_rows = router_rows.reshape(seq_size * 8, model_width)
    (
        residual_grad,
        out_grad,
        gain_second_grad,
        router_grad,
        combine,
        hidden,
        grad_gate_full,
        grad_up_full,
        down_landing,
    ) = experts(
        sizes,
        routed_seq,
        choices,
        onehot,
        cotangent_rows,
        router_rows,
        gain_rows,
        residual,
        cotangent,
        (gate_full, up_full, down_full),
        1,
    )
    (
        input_grad,
        gain_grads,
        query_owned,
        key_owned,
        value_owned,
        out_owned,
        mixed_rows,
        gate_landing,
    ) = back(
        sizes,
        out_grad,
        tokens,
        residual_grad,
        (gain_rows, gain_second_grad),
        (
            cosine_wide,
            sine_wide,
            segment_cols,
            segment_row,
            query_heads,
            key_heads,
            value_heads,
            unit_pair,
            square_sums,
            log_wide,
            attended_heads,
            qkv_stack,
            out_stack,
        ),
        (normed_seq, hidden, down_full, grad_gate_full),
        2,
    )
    output, gain_sums, router_sums, up_landing = close(
        sizes, mixed_rows, combine, residual, gain_grads, router_grad, grad_up_full, 3
    )

    def owned(landing):
        shape = (split // experts_local, experts_local, *landing.shape[1:])
        return landing.astype(jnp.float32).reshape(shape).sum(0)

    return (
        output,
        input_grad,
        gain_sums,
        query_owned,
        key_owned,
        value_owned,
        out_owned,
        router_sums.T,
        owned(gate_landing),
        owned(up_landing),
        owned(down_landing),
    )


def solution(mesh):
    in_specs = (
        P(("fsdp", "seq"), None),
        P(),
        P("fsdp", "seq"),
        P("fsdp", "seq"),
        P("fsdp", "seq"),
        P("seq", "fsdp"),
        P(),
        P("seq", "fsdp", None),
        P("seq", "fsdp", None),
        P("seq", None, "fsdp"),
        P("fsdp"),
        P(("fsdp", "seq"), None),
        P(("fsdp", "seq"), None),
        P(("fsdp", "seq"), None),
    )
    out_specs = (
        P(("fsdp", "seq"), None),
        P(("fsdp", "seq"), None),
        P(),
        P("fsdp", "seq"),
        P("fsdp", "seq"),
        P("fsdp", "seq"),
        P("seq", "fsdp"),
        P(),
        P("seq", "fsdp", None),
        P("seq", "fsdp", None),
        P("seq", None, "fsdp"),
    )
    return jax.shard_map(shards, mesh=mesh, in_specs=in_specs, out_specs=out_specs, check_vma=False)
```

```python
import functools

import jax
import jax.numpy as jnp
import numpy as np
from jax import lax
from jax.experimental import pallas as pl
from jax.experimental.pallas import tpu as pltpu
from jax.sharding import PartitionSpec as P

HEAD_DIM = 128
CAP = 40


EPSILON = 1e-06
THETA = 10000.0
MASKED = -1e30
HIGHEST = lax.Precision.HIGHEST


def rope_tables(length, head_size):
    half_dim = head_size // 2
    frequency = THETA ** (-np.arange(half_dim, dtype=np.float64) / half_dim)
    angles = np.arange(length, dtype=np.float64)[:, None] * frequency.astype(np.float32)
    cosine, sine = np.cos(angles), np.sin(angles)
    return (
        jnp.asarray(np.concatenate([cosine, cosine], 1), jnp.float32),
        jnp.asarray(np.concatenate([-sine, sine], 1), jnp.float32),
    )


class ChainGather:
    def __init__(self, chips, x_ref, out_ref, local_sem, sends, arrivals):
        self.chips, self.x_ref, self.out_ref = chips, x_ref, out_ref
        self.local_sem, self.sends, self.arrivals = local_sem, sends, arrivals
        me = lax.axis_index("seq")
        self.chip, self.core = me // 2, lax.rem(me, 2)
        self.rows = x_ref.shape[0]

    def block(self, source, core):
        start = pl.multiple_of((source * 2 + core) * self.rows, self.rows)
        return self.out_ref.at[pl.ds(start, self.rows)]

    def hop(self, source, ref, target, way, lane):
        return pltpu.make_async_remote_copy(
            src_ref=ref,
            dst_ref=self.block(source, self.core),
            send_sem=self.sends.at[way, source],
            recv_sem=self.arrivals.at[lane, source],
            device_id={"seq": target},
        )

    def upward(self, source, ref):
        return self.hop(source, ref, self.chip * 2 + 2 + self.core, 0, 0)

    def downward(self, source, ref):
        return self.hop(source, ref, self.chip * 2 - 2 + self.core, 1, 0)

    def sideways(self, source, ref):
        return self.hop(source, ref, self.chip * 2 + 1 - self.core, 2, 1)

    def own(self):
        return pltpu.make_async_copy(
            self.x_ref, self.block(self.chip, self.core), self.local_sem
        )

    def start(self):
        @pl.when(self.chip < self.chips - 1)
        def _():
            self.upward(self.chip, self.x_ref).start()

        @pl.when(self.chip > 0)
        def _():
            self.downward(self.chip, self.x_ref).start()

        self.sideways(self.chip, self.x_ref).start()
        self.own().start()

    def step(self, distance):
        below, above = self.chip - distance, self.chip + distance

        @pl.when(below >= 0)
        def _():
            landed = self.block(below, self.core)
            self.upward(below, landed).wait_recv()

            @pl.when(self.chip < self.chips - 1)
            def _():
                self.upward(below, landed).start()

            self.sideways(below, landed).start()

        @pl.when(above < self.chips)
        def _():
            landed = self.block(above, self.core)
            self.downward(above, landed).wait_recv()

            @pl.when(self.chip > 0)
            def _():
                self.downward(above, landed).start()

            self.sideways(above, landed).start()

    def steps(self):
        for distance in range(1, self.chips):
            self.step(distance)

    def landed(self):
        self.own().wait()
        for source in range(self.chips):
            self.sideways(source, self.block(source, self.core)).wait_recv()

    def sent(self):
        for source in range(self.chips):
            ref = self.block(source, self.core)
            self.sideways(source, ref).wait_send()

            @pl.when((self.chip < self.chips - 1) & (source <= self.chip))
            def _():
                self.upward(source, ref).wait_send()

            @pl.when((self.chip > 0) & (source >= self.chip))
            def _():
                self.downward(source, ref).wait_send()


class ChainReduce:
    def __init__(self, chips, total, buffers):
        self.total = total
        (
            self.side_out,
            self.side_in,
            self.chain_in,
            self.side_send,
            self.side_recv,
            self.chain_send,
            self.chain_recv,
        ) = buffers
        self.chips = chips
        me = lax.axis_index("seq")
        self.chip, self.core = me // 2, lax.rem(me, 2)

    @staticmethod
    def scratch(chips, rows, width):
        half = jnp.bfloat16
        return [
            pltpu.VMEM((chips, rows, width), half),
            pltpu.VMEM((chips, rows, width), half),
            pltpu.VMEM((chips + 1, rows, width), half),
            pltpu.SemaphoreType.DMA((chips,)),
            pltpu.SemaphoreType.DMA((chips,)),
            pltpu.SemaphoreType.DMA((chips,)),
            pltpu.SemaphoreType.DMA((2, chips)),
        ]

    def side_copy(self, dest):
        return pltpu.make_async_remote_copy(
            src_ref=self.side_out.at[dest],
            dst_ref=self.side_in.at[dest],
            send_sem=self.side_send.at[dest],
            recv_sem=self.side_recv.at[dest],
            device_id={"seq": self.chip * 2 + 1 - self.core},
        )

    def chain_copy(self, way, dest, target):
        return pltpu.make_async_remote_copy(
            src_ref=self.side_out.at[dest],
            dst_ref=self.chain_in.at[self.slot(way, dest, target // 2)],
            send_sem=self.chain_send.at[dest],
            recv_sem=self.chain_recv.at[way, dest],
            device_id={"seq": target},
        )

    def slot(self, way, dest, holder):
        return jnp.where(dest == holder, self.chips, dest) if way else dest

    def place(self, index):
        distance = self.chips - 1 - index // 2
        dest = self.chip + (1 - 2 * lax.rem(index, 2)) * distance
        return dest, (dest >= 0) & (dest < self.chips)

    def run(self, product, between=None):
        chips, chip, core, total = self.chips, self.chip, self.core, self.total
        sibling = chip * 2 + 1 - core

        @pl.loop(0, 2 * chips - 1)
        def _(index):
            dest, inside = self.place(index)

            @pl.when(inside)
            def _():
                def store(cols, part):
                    self.side_out[dest, :, cols] = part.astype(self.side_out.dtype)

                product(dest * 2 + 1 - core, store)
                self.side_copy(dest).start()

        if between:
            between()

        @pl.loop(0, 2 * chips - 1)
        def _(index):
            dest, inside = self.place(index)

            @pl.when(inside)
            def _():
                def store(cols, part):
                    total[:, cols] = part

                product(dest * 2 + core, store)
                self.side_copy(dest).wait_recv()
                total[...] += self.side_in[dest].astype(jnp.float32)

                @pl.when((dest >= chip) & (chip > 0))
                def _():
                    self.chain_copy(0, dest, sibling).wait_recv()
                    total[...] += self.chain_in[dest].astype(jnp.float32)

                @pl.when((dest <= chip) & (chip < chips - 1))
                def _():
                    self.chain_copy(1, dest, sibling).wait_recv()
                    total[...] += self.chain_in[self.slot(1, dest, chip)].astype(jnp.float32)

                self.side_copy(dest).wait_send()

                @pl.when(dest != chip)
                def _():
                    self.side_out[dest] = total[...].astype(self.side_out.dtype)

                @pl.when(dest > chip)
                def _():
                    self.chain_copy(0, dest, chip * 2 + 2 + core).start()

                @pl.when(dest < chip)
                def _():
                    self.chain_copy(1, dest, chip * 2 - 2 + core).start()

    def sent(self):
        sibling = self.chip * 2 + 1 - self.core

        @pl.loop(0, self.chips)
        def _(dest):
            @pl.when(dest != self.chip)
            def _():
                self.chain_copy(0, dest, sibling).wait_send()


def partner_of(index, move):
    turned, bit = index, 1
    while bit <= move:
        if move // bit % 2:
            turned = turned + bit - 2 * bit * lax.rem(index // bit, 2)
        bit *= 2
    return turned


def greet_all(size, split):
    me, mine = lax.axis_index("seq"), lax.axis_index("fsdp")
    barrier = pltpu.get_barrier_semaphore()
    for shift in range(1, size):
        pl.semaphore_signal(barrier, inc=1, device_id={"seq": lax.rem(me + shift, size)})
    for shift in range(1, split):
        pl.semaphore_signal(barrier, inc=1, device_id={"fsdp": lax.rem(mine + shift, split)})
    pl.semaphore_wait(barrier, size + split - 2)


def turned_halves(head):
    return pltpu.roll(head, head.shape[-1] // 2, 1)


def row_sums(values, pick):
    return lax.dot_general(
        pick, values, (((1,), (1,)), ((), ())), precision=HIGHEST, preferred_element_type=jnp.float32
    )


def column_of(row_form, pick):
    return lax.dot_general(
        row_form, pick, (((0,), (0,)), ((), ())), precision=HIGHEST, preferred_element_type=jnp.float32
    )


def front_kernel(
    sizes,
    tokens_ref,
    gains_in_ref,
    cos_ref,
    sin_ref,
    seg_row_ref,
    ids_ref,
    slots_ref,
    cotangent_ref,
    wq_ref,
    wk_ref,
    wv_ref,
    wo_ref,
    w_gate_ref,
    w_up_ref,
    w_down_ref,
    normed_out,
    qkv_out,
    rows_out,
    q_out,
    k_out,
    v_out,
    unit_out,
    log_out,
    attended_out,
    sums_ref,
    residual_ref,
    gains_ref,
    seg_col_ref,
    routed_out,
    cotangent_rows,
    gate_full,
    up_full,
    down_full,
    choices,
    onehot_ref,
    q_ref,
    k_ref,
    v_ref,
    unit_ref,
    log_ref,
    attended_ref,
    normed,
    qkv,
    rows_full,
    routed_own,
    choice_own,
    cotangent_pair,
    cotangent_all,
    mate_choices,
    mate_onehot,
    placed,
    raw,
    sums_own,
    sums_in,
    gather_local,
    gather_send,
    gather_recv,
    sums_send,
    sums_recv,
    choice_send,
    choice_recv,
    mate_send,
    mate_recv,
    cross_local,
    cross_send,
    cross_recv,
    placed_local,
    placed_send,
    placed_recv,
    shard_local,
    shard_send,
    shard_recv,
    expert_local,
    expert_send,
    expert_recv,
    out_sem,
    *reduce_buffers,
):
    size, split, chips, experts_local = sizes
    f32, half = jnp.float32, jnp.bfloat16
    me, mine = lax.axis_index("seq"), lax.axis_index("fsdp")
    tok_rows, model_width = tokens_ref.shape
    length, local_width = q_ref.shape
    part = model_width // split
    head = HEAD_DIM
    heads = local_width // head

    inputs = tokens_ref[...].astype(f32)
    inverse = lax.rsqrt(jnp.mean(inputs * inputs, -1, keepdims=True) + EPSILON)
    gains_ref[...] = gains_in_ref[...].astype(f32)
    routed_own[...] = (inputs * inverse * gains_ref[0:1, :]).astype(half)
    crossed = split == experts_local == 4
    half_width = model_width // 2
    x_mate, y_mate = {"fsdp": partner_of(mine, 1)}, {"fsdp": partner_of(mine, 2)}
    greet_all(size, split)

    def gather(index, x_ref, out_ref):
        return ChainGather(
            chips,
            x_ref,
            out_ref,
            gather_local.at[index],
            gather_send.at[index],
            gather_recv.at[index],
        )

    first = gather(0, routed_own, normed)
    first.start()

    cross_rows = pl.ds(tok_rows, tok_rows)
    lower, upper = pl.ds(0, half_width), pl.ds(half_width, half_width)

    def cross_copy(index):
        cols = (lower, upper)[index]
        return pltpu.make_async_remote_copy(
            src_ref=cotangent_ref.at[:, cols],
            dst_ref=cotangent_pair.at[cross_rows, cols],
            send_sem=cross_send.at[index],
            recv_sem=cross_recv.at[index],
            device_id=(x_mate, y_mate)[index],
        )

    if crossed:
        cross_own = pltpu.make_async_copy(
            cotangent_ref, cotangent_pair.at[pl.ds(0, tok_rows)], cross_local
        )
        cross_copy(0).start()
        cross_copy(1).start()
        cross_own.start()

    top_count = ids_ref.shape[1]
    same = lax.broadcasted_iota(jnp.int32, (top_count, top_count), 0) == (
        lax.broadcasted_iota(jnp.int32, (top_count, top_count), 1)
    )
    ids_row = row_sums(ids_ref[...].astype(f32), same.astype(f32))
    slots_row = row_sums(slots_ref[...].astype(f32), same.astype(f32))
    choice_own[0:top_count, :] = ids_row.astype(jnp.int32)
    choice_own[top_count : 2 * top_count, :] = jnp.where(
        slots_row < CAP, ids_row * CAP + slots_row, -1e6
    ).astype(jnp.int32)

    def choice_copy(shift):
        return pltpu.make_async_remote_copy(
            src_ref=choice_own,
            dst_ref=choices.at[me],
            send_sem=choice_send.at[shift],
            recv_sem=choice_recv.at[shift],
            device_id={"seq": lax.rem(me + shift, size)},
        )

    own_part = pl.ds(pl.multiple_of(mine * part, part), part)
    shard_pairs = (
        (wq_ref, qkv.at[0, own_part]),
        (wk_ref, qkv.at[1, own_part]),
        (wv_ref, qkv.at[2, own_part]),
        (wo_ref, rows_full.at[mine]),
    )

    def shard_copy(index, shift):
        source, target = shard_pairs[index]
        return pltpu.make_async_remote_copy(
            src_ref=source,
            dst_ref=target,
            send_sem=shard_send.at[index, shift],
            recv_sem=shard_recv.at[index, shift],
            device_id={"fsdp": lax.rem(mine + shift, split)},
        )

    def landed_half(index, owner, side):
        if index == 3:
            rows = local_width // 2
            return rows_full.at[owner, pl.ds(side * rows, rows)]
        rows = part // 2
        start = pl.multiple_of(owner * part + side * rows, rows)
        return qkv.at[index, pl.ds(start, rows)]

    def relay_copy(index, step):
        if step < 2:
            source, target = shard_pairs[index]
        else:
            source = target = landed_half(index, partner_of(mine, step - 1), step - 2)
        return pltpu.make_async_remote_copy(
            src_ref=source,
            dst_ref=target,
            send_sem=shard_send.at[index, step],
            recv_sem=shard_recv.at[index, step],
            device_id=(x_mate, y_mate, y_mate, x_mate)[step],
        )

    def shard_own(index):
        source, target = shard_pairs[index]
        return pltpu.make_async_copy(source, target, shard_local.at[index])

    for index in range(4):
        if split == 4:
            relay_copy(index, 0).start()
            relay_copy(index, 1).start()
        else:
            for shift in range(1, split):
                shard_copy(index, shift).start()
        shard_own(index).start()

    def expert_pair(index, dest):
        expert = lax.rem(dest, experts_local)
        if index == 2:
            return w_down_ref.at[expert], down_full.at[:, own_part]
        source, target = ((w_gate_ref, gate_full), (w_up_ref, up_full))[index]
        return source.at[expert], target.at[own_part]

    def expert_copy(index, shift):
        dest = lax.rem(mine + shift, split)
        source, target = expert_pair(index, dest)
        return pltpu.make_async_remote_copy(
            src_ref=source,
            dst_ref=target,
            send_sem=expert_send.at[index, shift],
            recv_sem=expert_recv.at[index, shift],
            device_id={"fsdp": dest},
        )

    def expert_own(index):
        source, target = expert_pair(index, mine)
        return pltpu.make_async_copy(source, target, expert_local.at[index])

    for distance in range(1, chips):
        first.step(distance)
        if split == 4 and distance == min(2, chips - 1):
            for index in range(4):
                for step in range(2):
                    relay_copy(index, step).wait_recv()
                    relay_copy(index, step + 2).start()
    for index in range(4):
        shard_own(index).wait()
        if split == 4:
            relay_copy(index, 2).wait_recv()
            relay_copy(index, 3).wait_recv()
        else:
            for shift in range(1, split):
                shard_copy(index, shift).wait_recv()
    for index in range(3):
        for shift in range(1, split):
            expert_copy(index, shift).start()
        expert_own(index).start()
    first.landed()
    for shift in range(1, size):
        choice_copy(shift).start()
    choices[me] = choice_own[...]
    if crossed:
        cross_own.wait()
        cross_copy(0).wait()
        cross_copy(1).wait()
        second = gather(1, cotangent_pair, cotangent_all)
    else:
        second = gather(1, cotangent_ref, cotangent_all)
    second.start()
    keeps = [
        pltpu.make_async_copy(normed, normed_out, out_sem.at[0]),
        pltpu.make_async_copy(qkv, qkv_out, out_sem.at[1]),
        pltpu.make_async_copy(rows_full, rows_out, out_sem.at[2]),
    ]
    for keep in keeps:
        keep.start()

    own_cols = pl.ds(pl.multiple_of(me * local_width, local_width), local_width)
    block = min(512, length)
    lanes = lax.broadcasted_iota(jnp.int32, (8, local_width), 0)
    first_row, second_row = (lanes == 0).astype(f32), (lanes == 1).astype(f32)

    @pl.loop(0, length // block)
    def _(step):
        rows = pl.ds(pl.multiple_of(step * block, block), block)
        left = normed[rows, :]
        query = jnp.dot(left, qkv[0], preferred_element_type=f32)
        raw[0, rows, :] = query
        keys = jnp.dot(left, qkv[1], preferred_element_type=f32)
        raw[1, rows, :] = keys
        sums_own[:, rows] = row_sums(query * query, first_row) + row_sums(keys * keys, second_row)
        v_ref[rows, :] = jnp.dot(left, qkv[2], preferred_element_type=f32).astype(half)

    def sums_copy(shift):
        return pltpu.make_async_remote_copy(
            src_ref=sums_own,
            dst_ref=sums_in.at[me],
            send_sem=sums_send.at[shift],
            recv_sem=sums_recv.at[shift],
            device_id={"seq": lax.rem(me + shift, size)},
        )

    for shift in range(1, size):
        sums_copy(shift).start()
    sums_in[me] = sums_own[...]
    for shift in range(1, size):
        sums_copy(shift).wait()
    sums_ref[...] = jnp.sum(sums_in[...], 0)
    for shift in range(1, size):
        choice_copy(shift).wait()

    def mate_copy(index):
        return pltpu.make_async_remote_copy(
            src_ref=choices,
            dst_ref=mate_choices.at[index],
            send_sem=mate_send.at[index],
            recv_sem=mate_recv.at[index],
            device_id=(x_mate, y_mate)[index],
        )

    if crossed:
        mate_copy(0).start()
        mate_copy(1).start()
    segments = seg_row_ref[...].astype(f32)
    narrow = first_row[:, 0:128]

    @pl.loop(0, length // block)
    def _(step):
        rows = pl.ds(pl.multiple_of(step * block, block), block)
        square_sums = sums_ref[:, rows]
        seg_col_ref[rows, :] = column_of(
            jnp.broadcast_to(seg_row_ref[:, rows].astype(f32), (8, block)), narrow
        )
        for index, pick, target in ((0, first_row, q_ref), (1, second_row, k_ref)):
            scale = lax.rsqrt(column_of(square_sums, pick) / model_width + EPSILON)
            unit = raw[index, rows, :] * scale
            unit_ref[index, rows, :] = unit
            scaled = unit * gains_ref[2 + index : 3 + index, own_cols]
            for number in range(heads):
                cols = slice(number * head, (number + 1) * head)
                piece = scaled[:, cols]
                target[rows, cols] = (
                    piece * cos_ref[rows, :] + turned_halves(piece) * sin_ref[rows, :]
                ).astype(half)

    second.step(1)

    wide = min(256, length)
    for number in range(heads):
        cols = slice(number * head, (number + 1) * head)

        @pl.loop(0, length // wide)
        def _(step):
            rows = pl.ds(pl.multiple_of(step * wide, wide), wide)
            scores = lax.dot_general(
                q_ref[rows, cols],
                k_ref[:, cols],
                (((1,), (1,)), ((), ())),
                preferred_element_type=f32,
            )
            scores = scores * (head**-0.5)
            scores = jnp.where(seg_col_ref[rows, 0:1] == segments, scores, MASKED)
            peak = jnp.max(scores, -1, keepdims=True)
            grown = jnp.exp(scores - peak)
            weight = jnp.sum(grown, -1, keepdims=True)
            probs = (grown * (1.0 / weight)).astype(half)
            attended_ref[rows, cols] = jnp.dot(
                probs, v_ref[:, cols], preferred_element_type=f32
            ).astype(half)
            log_ref[rows, cols] = jnp.broadcast_to(peak + jnp.log(weight), (wide, head))

        if number + 2 < chips:
            second.step(number + 2)

    for distance in range(heads + 2, chips):
        second.step(distance)

    for index, (source, target) in enumerate(
        (
            (q_ref, q_out),
            (k_ref, k_out),
            (v_ref, v_out),
            (unit_ref, unit_out),
            (log_ref, log_out),
            (attended_ref, attended_out),
        )
    ):
        keeps.append(pltpu.make_async_copy(source, target, out_sem.at[3 + index]))
        keeps[-1].start()

    reduce = ChainReduce(chips, residual_ref, reduce_buffers)

    def product(index, store):
        left = attended_ref[pl.ds(pl.multiple_of(index * tok_rows, tok_rows), tok_rows), :]
        for piece in range(split):
            cols = pl.ds(piece * part, part)
            store(cols, jnp.dot(left, rows_full[piece], preferred_element_type=f32))

    reduce.run(product)
    residual = tokens_ref[...].astype(f32) + reduce.total[...]
    residual_ref[...] = residual
    inverse = lax.rsqrt(jnp.mean(residual * residual, -1, keepdims=True) + EPSILON)
    first.sent()
    routed_own[...] = (residual * inverse * gains_ref[1:2, :]).astype(half)
    third = gather(2, routed_own, routed_out)
    third.start()

    second.landed()
    double = 2 * CAP
    member = lax.rem(mine, experts_local)
    slot_row = lax.broadcasted_iota(jnp.int32, (double, tok_rows), 0)
    if crossed:
        mate_copy(0).wait()
        mate_copy(1).wait()

    def one_hot(places, target, rows, expert):
        base = (me * experts_local + expert) * CAP
        for side in range(2):
            want = jnp.where(slot_row // CAP == side, slot_row - side * CAP + base, -1)
            hit = want == places(side)[top_count : top_count + 1, :]
            for choice in range(1, top_count):
                hit = hit | (want == places(side)[top_count + choice : top_count + choice + 1, :])
            cols = slice(side * tok_rows, (side + 1) * tok_rows)
            target[rows, cols] = jnp.where(hit, 1.0, 0.0).astype(half)

    def slot_range(move):
        return slice(move * double, (move + 1) * double)

    @pl.loop(0, size // 2)
    def _(pair):
        for move in range(experts_local):
            one_hot(
                lambda side: choices[pair * 2 + side],
                onehot_ref.at[pair],
                slot_range(move),
                partner_of(member, move),
            )
        if crossed:
            start = pl.multiple_of(pair * 4 * tok_rows, 4 * tok_rows)
            four = cotangent_all[pl.ds(start, 4 * tok_rows), :]
            own = jnp.concatenate(
                [four[0:tok_rows], four[2 * tok_rows : 3 * tok_rows]], 0
            )
            mates = jnp.concatenate(
                [four[tok_rows : 2 * tok_rows], four[3 * tok_rows : 4 * tok_rows]], 0
            )
            made = jnp.dot(onehot_ref[pair], own, preferred_element_type=f32).astype(half)
            placed[0, pair] = made[slot_range(0)]
            placed[1, pair, :, upper] = made[slot_range(1), half_width:]
            placed[2, pair, :, lower] = made[slot_range(2), :half_width]
            for index in range(2):
                for row, expert in enumerate((member, partner_of(member, 2 - index))):
                    one_hot(
                        lambda side: mate_choices[index, pair * 2 + side],
                        mate_onehot.at[index],
                        slot_range(row),
                        expert,
                    )
                cols = (lower, upper)[index]
                taken = mates[:, :half_width] if index == 0 else mates[:, half_width:]
                made = jnp.dot(mate_onehot[index], taken, preferred_element_type=f32).astype(half)
                placed[index + 1, pair, :, cols] = made[slot_range(0)]
                placed[3, pair, :, cols] = made[slot_range(1)]
        else:
            start = pl.multiple_of(pair * 2 * tok_rows, 2 * tok_rows)
            made = jnp.dot(
                onehot_ref[pair],
                cotangent_all[pl.ds(start, 2 * tok_rows), :],
                preferred_element_type=f32,
            ).astype(half)
            for move in range(experts_local):
                placed[move, pair] = made[slot_range(move)]

    def placed_copy(index):
        if crossed:
            move, cols = ((1, upper), (2, lower), (3, upper), (3, lower))[index]
            source, target = placed.at[move, :, :, cols], cotangent_rows.at[move, :, :, cols]
            mate = (x_mate, y_mate)[index % 2]
        else:
            source, target = placed.at[index], cotangent_rows.at[index]
            mate = {"fsdp": partner_of(mine, index)}
        return pltpu.make_async_remote_copy(
            src_ref=source,
            dst_ref=target,
            send_sem=placed_send.at[index],
            recv_sem=placed_recv.at[index],
            device_id=mate,
        )

    if crossed:
        placed_pieces = [
            (placed.at[0], cotangent_rows.at[0]),
            (placed.at[1, :, :, lower], cotangent_rows.at[1, :, :, lower]),
            (placed.at[2, :, :, upper], cotangent_rows.at[2, :, :, upper]),
        ]
    else:
        placed_pieces = [(placed.at[0], cotangent_rows.at[0])]
    placed_sends = [placed_copy(index) for index in range(0 if crossed else 1, experts_local)]
    placed_owns = [
        pltpu.make_async_copy(source, target, placed_local.at[index])
        for index, (source, target) in enumerate(placed_pieces)
    ]
    for copy in placed_sends + placed_owns:
        copy.start()
    third.steps()
    third.landed()
    reduce.sent()
    second.sent()
    third.sent()
    for index in range(4):
        if split == 4:
            for step in range(4):
                relay_copy(index, step).wait_send()
        else:
            for shift in range(1, split):
                shard_copy(index, shift).wait_send()
    for keep in keeps:
        keep.wait()
    for copy in placed_sends + placed_owns:
        copy.wait()
    for index in range(3):
        expert_own(index).wait()
        for shift in range(1, split):
            expert_copy(index, shift).wait()


def front(sizes, tokens, gains, cos, sin, segment_row, ids, slots, cotangent, weights, which):
    size, split, chips, experts_local = sizes
    w_query, w_key, w_value, w_out, w_gate, w_up, w_down = weights
    tok_rows, model_width = tokens.shape
    length = size * tok_rows
    local_width = w_query.shape[1]
    hidden_width = w_gate.shape[2]
    f32, half = jnp.float32, jnp.bfloat16
    vmem = pl.BlockSpec(memory_space=pltpu.VMEM)
    anywhere = pl.BlockSpec(memory_space=pl.ANY)
    kind = pltpu.SemaphoreType.DMA
    shape = jax.ShapeDtypeStruct
    crossed = split == experts_local == 4
    choices = (size, 2 * ids.shape[1], tok_rows)
    return pl.pallas_call(
        functools.partial(front_kernel, sizes),
        out_shape=(
            shape((length, model_width), half),
            shape((3, model_width, local_width), half),
            shape((split, *w_out.shape), half),
            shape((length, local_width), half),
            shape((length, local_width), half),
            shape((length, local_width), half),
            shape((2, length, local_width), f32),
            shape((length, local_width), f32),
            shape((length, local_width), half),
            shape((8, length), f32),
            shape((tok_rows, model_width), f32),
            shape(gains.shape, f32),
            shape((length, 128), f32),
            shape((length, model_width), half),
            shape((experts_local, size // 2, 2 * CAP, model_width), half),
            shape((model_width, hidden_width), half),
            shape((model_width, hidden_width), half),
            shape((hidden_width, model_width), half),
            shape((size, 2 * ids.shape[1], tok_rows), jnp.int32),
            shape((size // 2, experts_local * 2 * CAP, 2 * tok_rows), half),
        ),
        in_specs=[vmem] * 7 + [anywhere] * 8,
        out_specs=tuple([anywhere] * 9 + [vmem] * 4 + [anywhere] * 5 + [vmem] * 2),
        scratch_shapes=[
            pltpu.VMEM((length, local_width), half),
            pltpu.VMEM((length, local_width), half),
            pltpu.VMEM((length, local_width), half),
            pltpu.VMEM((2, length, local_width), f32),
            pltpu.VMEM((length, local_width), f32),
            pltpu.VMEM((length, local_width), half),
            pltpu.VMEM((length, model_width), half),
            pltpu.VMEM((3, model_width, local_width), half),
            pltpu.VMEM((split, *w_out.shape), half),
            pltpu.VMEM((tok_rows, model_width), half),
            pltpu.VMEM((2 * ids.shape[1], tok_rows), jnp.int32),
            pltpu.VMEM((2 * tok_rows if crossed else 16, model_width), half),
            pltpu.VMEM(((2 if crossed else 1) * length, model_width), half),
            pltpu.VMEM((2, *(choices if crossed else (1, 8, 128))), jnp.int32),
            pltpu.VMEM((2, 4 * CAP if crossed else 16, 2 * tok_rows), half),
            pltpu.VMEM((experts_local, size // 2, 2 * CAP, model_width), half),
            pltpu.VMEM((2, length, local_width), f32),
            pltpu.VMEM((8, length), f32),
            pltpu.VMEM((size, 8, length), f32),
            kind((3,)),
            kind((3, 3, chips)),
            kind((3, 2, chips)),
            kind((size,)),
            kind((size,)),
            kind((size,)),
            kind((size,)),
            kind((2,)),
            kind((2,)),
            kind,
            kind((2,)),
            kind((2,)),
            kind((3,)),
            kind((experts_local,)),
            kind((experts_local,)),
            kind((4,)),
            kind((4, split)),
            kind((4, split)),
            kind((3,)),
            kind((3, split)),
            kind((3, split)),
            kind((9,)),
            *ChainReduce.scratch(chips, tok_rows, model_width),
        ],
        compiler_params=pltpu.CompilerParams(
            collective_id=which, has_side_effects=True, vmem_limit_bytes=58 * 2**20
        ),
        cost_estimate=pl.CostEstimate(
            flops=2 * length * model_width * local_width * 4,
            bytes_accessed=500 * 2**20,
            transcendentals=0,
        ),
    )(
        tokens, gains, cos, sin, segment_row, ids, slots, cotangent, *weights
    )


class ShardSend:
    def __init__(self, split, source, landing, local_sem, sends, arrivals):
        self.split, self.source, self.landing = split, source, landing
        self.local_sem, self.sends, self.arrivals = local_sem, sends, arrivals
        self.mine = lax.axis_index("fsdp")

    def copy(self, shift):
        dest = lax.rem(self.mine + shift, self.split)
        return pltpu.make_async_remote_copy(
            src_ref=self.source(dest),
            dst_ref=self.landing.at[self.mine],
            send_sem=self.sends.at[shift],
            recv_sem=self.arrivals.at[shift],
            device_id={"fsdp": dest},
        )

    def own(self):
        return pltpu.make_async_copy(
            self.source(self.mine), self.landing.at[self.mine], self.local_sem
        )

    def start(self):
        for shift in range(1, self.split):
            self.copy(shift).start()
        self.own().start()

    def wait(self):
        for shift in range(1, self.split):
            self.copy(shift).wait()
        self.own().wait()


def turned_dot(left, right):
    return lax.dot_general(
        left, right, (((0,), (0,)), ((), ())), preferred_element_type=jnp.float32
    )


def cross_dot(left, right):
    return lax.dot_general(
        left, right, (((1,), (1,)), ((), ())), preferred_element_type=jnp.float32
    )


def experts_kernel(
    sizes,
    routed_ref,
    choices_ref,
    onehot_ref,
    cotangent_rows_ref,
    router_ref,
    gains_ref,
    residual_ref,
    cotangent_ref,
    gate_ref,
    up_ref,
    down_ref,
    residual_grad_ref,
    out_grad_ref,
    gain_ref,
    router_grad_ref,
    hidden_out,
    grad_gate_ref,
    grad_up_ref,
    down_landing,
    gate_full,
    up_full,
    down_full,
    upstream,
    pair_rows,
    outgoing,
    arrived,
    hidden,
    gate_grad,
    up_grad,
    back,
    gates,
    gates_out,
    gates_in,
    dots_out,
    dots_in,
    token_out,
    token_in,
    scales,
    load_sem,
    pair_sem,
    keep_sem,
    rows_send,
    rows_recv,
    gates_send,
    gates_recv,
    back_send,
    back_recv,
    dots_send,
    dots_recv,
    token_send,
    token_recv,
    down_send,
    down_recv,
    *reduce_buffers,
):
    size, split, chips, experts_local = sizes
    f32, half = jnp.float32, jnp.bfloat16
    me, mine = lax.axis_index("seq"), lax.axis_index("fsdp")
    tok_rows, model_width = residual_ref.shape
    pairs = size // 2
    double = 2 * CAP
    wide = 2 * tok_rows
    hidden_width = gate_full.shape[1]
    rows_of = pairs * double
    part = model_width // split
    member = lax.rem(mine, experts_local)

    loads = [
        pltpu.make_async_copy(source, target, load_sem.at[index])
        for index, (source, target) in enumerate(
            (
                (gate_ref, gate_full),
                (up_ref, up_full),
                (down_ref, down_full),
                (cotangent_rows_ref, upstream),
            )
        )
    ]

    slots = pair_rows.shape[0]

    def pair_load(pair):
        slot = lax.rem(pair, slots)
        start = pl.multiple_of(pair * wide, wide)
        return pltpu.make_async_copy(
            routed_ref.at[pl.ds(start, wide)], pair_rows.at[slot], pair_sem.at[slot]
        )

    pair_load(0).start()
    for load in loads:
        load.start()
    greet_all(size, split)

    padded = size * 8
    expert_row = lax.broadcasted_iota(jnp.int32, (padded, tok_rows), 0)
    inner = lax.rem(expert_row, 8)
    expert_row = jnp.where(inner < experts_local, expert_row // 8 * experts_local + inner, -1)
    ones = jnp.ones((8, wide), f32)
    top_count = choices_ref.shape[1] // 2

    @pl.loop(0, pairs)
    def _(pair):
        pair_load(pair).wait()

        @pl.when((pair + 1 < pairs) & (slots > 1))
        def _():
            pair_load(pair + 1).start()

        rows = pair_rows[lax.rem(pair, slots)]
        logits = lax.dot_general(
            router_ref[...], rows, (((1,), (1,)), ((), ())), preferred_element_type=f32
        )
        for side in range(2):
            ids = choices_ref[pair * 2 + side]
            chosen = expert_row == ids[0:1, :]
            for choice in range(1, top_count):
                chosen = chosen | (expert_row == ids[choice : choice + 1, :])
            own = jnp.where(chosen, logits[:, side * tok_rows : (side + 1) * tok_rows], MASKED)
            grown = jnp.where(chosen, jnp.exp(own - jnp.max(own, 0, keepdims=True)), 0.0)
            gates[pair * 2 + side] = grown / jnp.sum(grown, 0, keepdims=True)
        placed = jnp.dot(onehot_ref[pair], rows, preferred_element_type=f32).astype(half)
        for move in range(experts_local):
            piece = placed[move * double : (move + 1) * double]
            if move:
                outgoing[move - 1, pair] = piece
            else:
                arrived[0, pair] = piece
            row = me * 8 + partner_of(member, move)
            weights = jnp.concatenate(
                [gates[pair * 2, pl.ds(row, 1), :], gates[pair * 2 + 1, pl.ds(row, 1), :]], 1
            )
            slot_rows = pl.ds(move * double, double)
            weighted = onehot_ref[pair, slot_rows, :].astype(f32) * weights
            gates_out[move, pair] = row_sums(weighted, ones)

        @pl.when((pair + 1 < pairs) & (slots == 1))
        def _():
            pair_load(pair + 1).start()

    def mate(move):
        return {"fsdp": partner_of(mine, move)}

    def rows_copy(move):
        return pltpu.make_async_remote_copy(
            src_ref=outgoing.at[move - 1],
            dst_ref=arrived.at[move],
            send_sem=rows_send.at[move],
            recv_sem=rows_recv.at[move],
            device_id=mate(move),
        )

    def gates_copy(move):
        return pltpu.make_async_remote_copy(
            src_ref=gates_out.at[move],
            dst_ref=gates_in.at[move],
            send_sem=gates_send.at[move],
            recv_sem=gates_recv.at[move],
            device_id=mate(move),
        )

    def back_rows(move):
        return back.at[:, pl.ds(move * double, double), :]

    def back_copy(move):
        return pltpu.make_async_remote_copy(
            src_ref=outgoing.at[move - 1],
            dst_ref=back_rows(move),
            send_sem=back_send.at[move],
            recv_sem=back_recv.at[move],
            device_id=mate(move),
        )

    def dots_copy(move):
        return pltpu.make_async_remote_copy(
            src_ref=dots_out.at[move],
            dst_ref=dots_in.at[move],
            send_sem=dots_send.at[move],
            recv_sem=dots_recv.at[move],
            device_id=mate(move),
        )

    order = list(range(experts_local - 1, 0, -1))
    for move in order:
        gates_copy(move).start()
        rows_copy(move).start()
    gates_in[0] = gates_out[0]
    for load in loads:
        load.wait()

    cols_step = min(256, hidden_width)
    width_step = min(512, model_width)
    spread = (lax.broadcasted_iota(jnp.int32, (8, 128), 0) == 0).astype(f32)
    for move in [0] + order:
        if move:
            gates_copy(move).wait()
            rows_copy(move).wait()
        for pair in range(pairs):
            scales[pair * double : (pair + 1) * double, :] = column_of(
                gates_in[move, pair], spread
            )
        dots_out[move] = jnp.zeros_like(dots_out[move])

        @pl.loop(0, hidden_width // cols_step)
        def _(index):
            cols = pl.ds(pl.multiple_of(index * cols_step, cols_step), cols_step)
            rows = arrived[move].reshape(rows_of, model_width)
            pre = jnp.dot(rows, gate_full[:, cols], preferred_element_type=f32)
            up = jnp.dot(rows, up_full[:, cols], preferred_element_type=f32)
            plain = lax.dot_general(
                upstream[move].reshape(rows_of, model_width),
                down_full[cols, :],
                (((1,), (1,)), ((), ())),
                preferred_element_type=f32,
            )
            sigmoid = 1.0 / (1.0 + jnp.exp(-pre))
            active = pre * sigmoid
            made = (active * up).astype(half)
            weighted = made.astype(f32) * scales[:, 0:1]
            hidden[move, :, :, cols] = weighted.astype(half).reshape(pairs, double, cols_step)
            dots = made.astype(f32) * plain
            for pair in range(pairs):
                dots_out[move, pair] += row_sums(
                    dots[pair * double : (pair + 1) * double], jnp.ones((8, cols_step), f32)
                )
            scaled = plain * scales[:, 0:1]
            gate_back = scaled * up * sigmoid * (1.0 + pre * (1.0 - sigmoid))
            gate_grad[move, :, :, cols] = gate_back.astype(half).reshape(pairs, double, cols_step)
            up_grad[move, :, :, cols] = (
                (scaled * active).astype(half).reshape(pairs, double, cols_step)
            )

        if move:
            dots_copy(move).start()
        else:
            dots_in[0] = dots_out[0]

        @pl.loop(0, model_width // width_step)
        def _(index):
            cols = pl.ds(pl.multiple_of(index * width_step, width_step), width_step)
            rows_grad = lax.dot_general(
                gate_grad[move].reshape(rows_of, hidden_width),
                gate_full[cols, :],
                (((1,), (1,)), ((), ())),
                preferred_element_type=f32,
            )
            rows_grad = rows_grad + lax.dot_general(
                up_grad[move].reshape(rows_of, hidden_width),
                up_full[cols, :],
                (((1,), (1,)), ((), ())),
                preferred_element_type=f32,
            )
            rows_grad = rows_grad.astype(half).reshape(pairs, double, width_step)
            if move:
                outgoing[move - 1, :, :, cols] = rows_grad
            else:
                back[:, 0:double, cols] = rows_grad

        if move:
            back_copy(move).start()

    own_rows = pl.ds(pl.multiple_of(me * tok_rows, tok_rows), tok_rows)
    own_load = pltpu.make_async_copy(
        routed_ref.at[own_rows], pair_rows.at[0, pl.ds(0, tok_rows)], pair_sem.at[0]
    )
    own_load.start()
    hidden_keep = pltpu.make_async_copy(hidden, hidden_out, keep_sem)
    hidden_keep.start()

    total_rows = experts_local * rows_of

    def flat(ref, cols):
        return ref[:, :, :, cols].reshape(total_rows, -1)

    every = pl.ds(0, hidden_width)

    @pl.loop(0, split)
    def _(piece):
        cols = pl.ds(pl.multiple_of(piece * part, part), part)
        gate_full[cols, :] = turned_dot(flat(arrived, cols), flat(gate_grad, every)).astype(half)
        up_full[cols, :] = turned_dot(flat(arrived, cols), flat(up_grad, every)).astype(half)
        down_full[:, cols] = turned_dot(flat(hidden, every), flat(upstream, cols)).astype(half)

    grad_keeps = [
        pltpu.make_async_copy(source, target, load_sem.at[index])
        for index, (source, target) in enumerate(
            ((gate_full, grad_gate_ref), (up_full, grad_up_ref))
        )
    ]
    for keep in grad_keeps:
        keep.start()
    down_send_all = ShardSend(
        split,
        lambda dest: down_full.at[:, pl.ds(pl.multiple_of(dest * part, part), part)],
        down_landing,
        load_sem.at[2],
        down_send,
        down_recv,
    )

    for move in order:
        dots_copy(move).wait()
    token_out[...] = jnp.zeros_like(token_out)

    @pl.loop(0, pairs)
    def _(pair):
        for move in range(experts_local):
            found = jnp.dot(
                dots_in[move, pair],
                onehot_ref[pair, pl.ds(move * double, double), :].astype(f32),
                precision=HIGHEST,
                preferred_element_type=f32,
            )
            row = partner_of(member, move)
            for side in range(2):
                token_out[pair * 2 + side, pl.ds(row, 1), :] = found[
                    0:1, side * tok_rows : (side + 1) * tok_rows
                ]

    def token_copy(shift):
        peer = lax.rem(me + shift, size)
        return pltpu.make_async_remote_copy(
            src_ref=token_out.at[peer],
            dst_ref=token_in.at[me],
            send_sem=token_send.at[shift],
            recv_sem=token_recv.at[shift],
            device_id={"seq": peer},
        )

    for shift in range(1, size):
        token_copy(shift).start()
    token_in[me] = token_out[me]
    for move in order:
        back_copy(move).wait()
    down_send_all.start()

    reduce = ChainReduce(chips, residual_grad_ref, reduce_buffers)

    def product(index, store):
        side = pl.ds(pl.multiple_of(lax.rem(index, 2) * tok_rows, tok_rows), tok_rows)
        left = onehot_ref[index // 2, :, side]

        @pl.loop(0, model_width // width_step)
        def _(step):
            cols = pl.ds(pl.multiple_of(step * width_step, width_step), width_step)
            store(cols, turned_dot(left, back[index // 2, :, cols]))

    reduce.run(product)

    for shift in range(1, size):
        token_copy(shift).wait()
    own_gates = gates[me]
    grads = token_in[...].reshape(padded, tok_rows)
    mean = jnp.sum(own_gates * grads, 0, keepdims=True)
    logit_grad = (own_gates * (grads - mean)).astype(half)
    routed_grad = reduce.total[...] + turned_dot(logit_grad, router_ref[...])
    own_load.wait()
    router_grad = jnp.dot(logit_grad, pair_rows[0, 0:tok_rows, :], preferred_element_type=f32)
    for device in range(size):
        router_grad_ref[device * experts_local : (device + 1) * experts_local, :] = router_grad[
            device * 8 : device * 8 + experts_local
        ]
    residual = residual_ref[...]
    inverse = lax.rsqrt(jnp.mean(residual * residual, -1, keepdims=True) + EPSILON)
    unit = residual * inverse
    gain_ref[...] = jnp.broadcast_to(
        jnp.sum(routed_grad * unit, 0, keepdims=True), gain_ref.shape
    )
    routed_grad = routed_grad * gains_ref[1:2, :]
    routed_grad = inverse * (
        routed_grad - unit * jnp.mean(routed_grad * unit, -1, keepdims=True)
    )
    residual_grad = cotangent_ref[...].astype(f32) + routed_grad
    residual_grad_ref[...] = residual_grad
    out_grad_ref[...] = residual_grad.astype(half)
    reduce.sent()
    hidden_keep.wait()
    for keep in grad_keeps:
        keep.wait()
    down_send_all.wait()


def experts(
    sizes,
    routed_seq,
    choices,
    onehot,
    cotangent_rows,
    router_rows,
    gain_rows,
    residual,
    cotangent,
    weights,
    which,
):
    size, split, chips, experts_local = sizes
    gate_full, up_full, down_full = weights
    model_width, hidden_width = gate_full.shape
    tok_rows = residual.shape[0]
    pairs, double = size // 2, 2 * CAP
    f32, half = jnp.float32, jnp.bfloat16
    vmem = pl.BlockSpec(memory_space=pltpu.VMEM)
    anywhere = pl.BlockSpec(memory_space=pl.ANY)
    kind = pltpu.SemaphoreType.DMA
    shape = jax.ShapeDtypeStruct
    few = kind((experts_local,))
    wide_rows = (experts_local, pairs, double, model_width)
    narrow_rows = (experts_local, pairs, double, hidden_width)
    flags = (experts_local, pairs, 8, double)
    return pl.pallas_call(
        functools.partial(experts_kernel, sizes),
        out_shape=(
            shape((tok_rows, model_width), f32),
            shape((tok_rows, model_width), half),
            shape((8, model_width), f32),
            shape((size * experts_local, model_width), f32),
            shape(narrow_rows, half),
            shape(gate_full.shape, half),
            shape(up_full.shape, half),
            shape((split, hidden_width, model_width // split), half),
        ),
        in_specs=[anywhere, vmem, vmem, anywhere] + [vmem] * 4 + [anywhere] * 3,
        out_specs=tuple([vmem] * 4 + [anywhere] * 4),
        scratch_shapes=[
            pltpu.VMEM(gate_full.shape, half),
            pltpu.VMEM(up_full.shape, half),
            pltpu.VMEM(down_full.shape, half),
            pltpu.VMEM(wide_rows, half),
            pltpu.VMEM((2 if chips < 8 else 1, 2 * tok_rows, model_width), half),
            pltpu.VMEM((max(experts_local - 1, 1), *wide_rows[1:]), half),
            pltpu.VMEM(wide_rows, half),
            pltpu.VMEM(narrow_rows, half),
            pltpu.VMEM(narrow_rows, half),
            pltpu.VMEM(narrow_rows, half),
            pltpu.VMEM((pairs, experts_local * double, model_width), half),
            pltpu.VMEM((size, size * 8, tok_rows), f32),
            pltpu.VMEM(flags, f32),
            pltpu.VMEM(flags, f32),
            pltpu.VMEM(flags, f32),
            pltpu.VMEM(flags, f32),
            pltpu.VMEM((size, 8, tok_rows), f32),
            pltpu.VMEM((size, 8, tok_rows), f32),
            pltpu.VMEM((pairs * double, 128), f32),
            kind((4,)),
            kind((2,)),
            kind,
            few,
            few,
            few,
            few,
            few,
            few,
            few,
            few,
            kind((size,)),
            kind((size,)),
            kind((split,)),
            kind((split,)),
            *ChainReduce.scratch(chips, tok_rows, model_width),
        ],
        compiler_params=pltpu.CompilerParams(
            collective_id=which, has_side_effects=True, vmem_limit_bytes=63 * 2**20
        ),
        cost_estimate=pl.CostEstimate(
            flops=2 * experts_local * pairs * double * model_width * hidden_width * 8,
            bytes_accessed=500 * 2**20,
            transcendentals=0,
        ),
    )(
        routed_seq,
        choices,
        onehot,
        cotangent_rows,
        router_rows,
        gain_rows,
        residual,
        cotangent,
        gate_full,
        up_full,
        down_full,
    )

def back_kernel(
    sizes,
    out_grad_ref,
    gains_ref,
    second_gain_ref,
    seg_row_ref,
    sums_ref,
    *refs,
):
    kept_count = 13
    kept, refs = refs[:kept_count], refs[kept_count:]
    back_body(sizes, out_grad_ref, gains_ref, second_gain_ref, seg_row_ref, sums_ref, kept, *refs)


def back_body(
    sizes,
    out_grad_ref,
    gains_ref,
    second_gain_ref,
    seg_row_ref,
    sums_ref,
    kept,
    normed_ref,
    hidden_ref,
    down_ref,
    grad_gate_ref,
    input_grad_ref,
    gains_out_ref,
    out_w_grad_ref,
    mixed_rows,
    gate_landing,
    qkv_out,
    rows_full_ref,
    attended_ref,
    q_ref,
    k_ref,
    v_ref,
    seg_col_ref,
    log_ref,
    cos_ref,
    sin_ref,
    unit_ref,
    qkv_ref,
    tokens_ref,
    residual_grad_ref,
    down_full,
    out_grads,
    attended_grad,
    hidden,
    returned,
    key_total,
    value_total,
    scaled,
    raw_grads,
    centers_own,
    centers_in,
    qkv_stage,
    out_stage,
    out_landing,
    load_sem,
    gather_local,
    gather_send,
    gather_recv,
    gate_local,
    gate_send,
    gate_recv,
    rows_local,
    rows_send,
    rows_recv,
    centers_send,
    centers_recv,
    kept_sem,
    out_local,
    out_send,
    out_recv,
    *reduce_buffers,
):
    size, split, chips, experts_local = sizes
    f32, half = jnp.float32, jnp.bfloat16
    me, mine = lax.axis_index("seq"), lax.axis_index("fsdp")
    tok_rows, model_width = out_grad_ref.shape
    length, local_width = q_ref.shape
    hidden_width = down_ref.shape[0]
    part = model_width // split
    head = HEAD_DIM
    heads = local_width // head
    double = 2 * CAP
    pairs = size // 2
    rows_of = pairs * double

    down_load = pltpu.make_async_copy(down_ref, down_full, load_sem.at[0])
    hidden_load = pltpu.make_async_copy(hidden_ref, hidden, load_sem.at[1])
    down_load.start()
    hidden_load.start()
    targets = (
        rows_full_ref,
        attended_ref,
        q_ref,
        k_ref,
        v_ref,
        seg_col_ref,
        log_ref,
        cos_ref,
        sin_ref,
        unit_ref,
        qkv_ref,
        tokens_ref,
        residual_grad_ref,
    )
    kept_loads = [
        pltpu.make_async_copy(source, target, kept_sem.at[index])
        for index, (source, target) in enumerate(zip(kept, targets))
    ]
    greet_all(size, split)
    gather = ChainGather(chips, out_grad_ref, out_grads, gather_local, gather_send, gather_recv)
    gather.start()
    gate_send_all = ShardSend(
        split,
        lambda dest: grad_gate_ref.at[pl.ds(pl.multiple_of(dest * part, part), part)],
        gate_landing,
        gate_local,
        gate_send,
        gate_recv,
    )

    gate_send_all.start()
    for load in kept_loads:
        load.start()

    down_load.wait()
    hidden_load.wait()
    width_step = min(512, model_width)

    def rows_target(move):
        return mixed_rows.at[:, pl.ds(move * double, double), :]

    def rows_copy(move):
        return pltpu.make_async_remote_copy(
            src_ref=returned.at[move],
            dst_ref=rows_target(move),
            send_sem=rows_send.at[move],
            recv_sem=rows_recv.at[move],
            device_id={"fsdp": partner_of(mine, move)},
        )

    own_rows = pltpu.make_async_copy(returned.at[0], rows_target(0), rows_local)
    for move in range(experts_local - 1, -1, -1):

        @pl.loop(0, model_width // width_step)
        def _(index):
            cols = pl.ds(pl.multiple_of(index * width_step, width_step), width_step)
            made = jnp.dot(
                hidden[move].reshape(rows_of, hidden_width),
                down_full[:, cols],
                preferred_element_type=f32,
            )
            returned[move, :, :, cols] = made.astype(half).reshape(pairs, double, width_step)

        if move:
            rows_copy(move).start()
    own_rows.start()
    gather.steps()
    for load in kept_loads:
        load.wait()
    gather.landed()

    block = min(512, length)

    @pl.loop(0, length // block)
    def _(step):
        rows = pl.ds(pl.multiple_of(step * block, block), block)
        total = cross_dot(out_grads[rows, 0:part], rows_full_ref[0])
        for piece in range(1, split):
            total += cross_dot(
                out_grads[rows, piece * part : (piece + 1) * part], rows_full_ref[piece]
            )
        attended_grad[rows, :] = total.astype(half)

    @pl.loop(0, split)
    def _(piece):
        cols = pl.ds(pl.multiple_of(piece * part, part), part)
        out_stage[piece] = turned_dot(attended_ref[...], out_grads[:, cols]).astype(half)

    out_send_all = ShardSend(
        split, lambda dest: out_stage.at[dest], out_landing, out_local, out_send, out_recv
    )
    out_send_all.start()
    gather.sent()
    normed_load = pltpu.make_async_copy(normed_ref, out_grads, load_sem.at[0])
    normed_load.start()

    wide = min(256, length) if length <= 1024 else 128
    scale = head**-0.5
    segments = seg_row_ref[...].astype(f32)
    for number in range(heads):
        cols = slice(number * head, (number + 1) * head)
        key_total[...] = jnp.zeros_like(key_total)
        value_total[...] = jnp.zeros_like(value_total)

        @pl.loop(0, length // wide)
        def _(step):
            rows = pl.ds(pl.multiple_of(step * wide, wide), wide)
            scores = cross_dot(q_ref[rows, cols], k_ref[:, cols]) * scale
            scores = jnp.where(seg_col_ref[rows, 0:1] == segments, scores, MASKED)
            probs = jnp.exp(scores - log_ref[rows, cols][:, 0:1])
            grads = attended_grad[rows, cols]
            prob_grad = cross_dot(grads, v_ref[:, cols])
            center = jnp.sum(probs * prob_grad, -1, keepdims=True)
            score_grad = (probs * (prob_grad - center)).astype(half)
            query_grad = jnp.dot(score_grad, k_ref[:, cols], preferred_element_type=f32) * scale
            raw_grads[0, rows, cols] = query_grad.astype(half)
            key_total[...] += turned_dot(score_grad, q_ref[rows, cols])
            value_total[...] += turned_dot(probs.astype(half), grads)

        raw_grads[1, :, cols] = (key_total[...] * scale).astype(half)
        raw_grads[2, :, cols] = value_total[...].astype(half)

    lanes = lax.broadcasted_iota(jnp.int32, (8, local_width), 0)
    first_row, second_row = (lanes == 0).astype(f32), (lanes == 1).astype(f32)
    gains_out_ref[...] = jnp.zeros_like(gains_out_ref)
    own_cols = pl.ds(pl.multiple_of(me * local_width, local_width), local_width)
    gains_out_ref[1:2, :] = second_gain_ref[0:1, :]

    @pl.loop(0, length // block)
    def _(step):
        rows = pl.ds(pl.multiple_of(step * block, block), block)
        found = jnp.zeros((8, block), f32)
        for index, pick in ((0, first_row), (1, second_row)):
            unit = unit_ref[index, rows, :]
            pieces = []
            for number in range(heads):
                cols = slice(number * head, (number + 1) * head)
                piece = raw_grads[index, rows, cols].astype(f32)
                pieces.append(piece * cos_ref[rows, :] - turned_halves(piece) * sin_ref[rows, :])
            unit_grad = pieces[0] if heads == 1 else jnp.concatenate(pieces, 1)
            gains_out_ref[2 + index : 3 + index, own_cols] += jnp.sum(
                unit_grad * unit, 0, keepdims=True
            )
            grown = unit_grad * gains_ref[2 + index : 3 + index, own_cols]
            scaled[index, rows, :] = grown
            found += row_sums(grown * unit, pick)
        centers_own[:, rows] = found

    def centers_copy(shift):
        return pltpu.make_async_remote_copy(
            src_ref=centers_own,
            dst_ref=centers_in.at[me],
            send_sem=centers_send.at[shift],
            recv_sem=centers_recv.at[shift],
            device_id={"seq": lax.rem(me + shift, size)},
        )

    for shift in range(1, size):
        centers_copy(shift).start()
    centers_in[me] = centers_own[...]
    for shift in range(1, size):
        centers_copy(shift).wait()
    centers_own[...] = jnp.sum(centers_in[...], 0) * (1.0 / model_width)

    @pl.loop(0, length // block)
    def _(step):
        rows = pl.ds(pl.multiple_of(step * block, block), block)
        for index, pick in ((0, first_row), (1, second_row)):
            inverse = lax.rsqrt(column_of(sums_ref[:, rows], pick) / model_width + EPSILON)
            center = column_of(centers_own[:, rows], pick)
            raw_grads[index, rows, :] = (
                inverse * (scaled[index, rows, :] - unit_ref[index, rows, :] * center)
            ).astype(half)

    reduce = ChainReduce(chips, input_grad_ref, reduce_buffers)

    def product(index, store):
        rows = pl.ds(pl.multiple_of(index * tok_rows, tok_rows), tok_rows)

        @pl.loop(0, model_width // width_step)
        def _(step):
            cols = pl.ds(pl.multiple_of(step * width_step, width_step), width_step)
            total = cross_dot(raw_grads[0, rows, :], qkv_ref[0, cols, :])
            total += cross_dot(raw_grads[1, rows, :], qkv_ref[1, cols, :])
            total += cross_dot(raw_grads[2, rows, :], qkv_ref[2, cols, :])
            store(cols, total)

    qkv_keep = pltpu.make_async_copy(qkv_stage, qkv_out, load_sem.at[1])

    def between():
        normed_load.wait()

        @pl.loop(0, split)
        def _(piece):
            cols = pl.ds(pl.multiple_of(piece * part, part), part)
            left = out_grads[:, cols]
            for index in range(3):
                qkv_stage[piece, index] = turned_dot(left, raw_grads[index]).astype(half)

        qkv_keep.start()

    reduce.run(product, between)

    inputs = tokens_ref[...].astype(f32)
    inverse = lax.rsqrt(jnp.mean(inputs * inputs, -1, keepdims=True) + EPSILON)
    unit = inputs * inverse
    grads = input_grad_ref[...]
    gains_out_ref[0:1, :] = jnp.sum(grads * unit, 0, keepdims=True)
    grads = grads * gains_ref[0:1, :]
    input_grad_ref[...] = residual_grad_ref[...] + inverse * (
        grads - unit * jnp.mean(grads * unit, -1, keepdims=True)
    )

    out_send_all.wait()
    total = out_landing[0].astype(f32)
    for index in range(1, split):
        total += out_landing[index].astype(f32)
    out_w_grad_ref[...] = total
    qkv_keep.wait()
    reduce.sent()
    own_rows.wait()
    for move in range(1, experts_local):
        rows_copy(move).wait()
    gate_send_all.wait()


def back(sizes, out_grad, small, kept, big_ones, which):
    size, split, chips, experts_local = sizes
    f32, half = jnp.float32, jnp.bfloat16
    tok_rows, model_width = out_grad.shape
    length, local_width = kept[1].shape
    normed_seq, hidden, down_full, grad_gate = big_ones
    hidden_width = down_full.shape[0]
    part = model_width // split
    vmem = pl.BlockSpec(memory_space=pltpu.VMEM)
    anywhere = pl.BlockSpec(memory_space=pl.ANY)
    kind = pltpu.SemaphoreType.DMA
    shape = jax.ShapeDtypeStruct
    few, fsdp = kind((experts_local,)), kind((split,))
    return pl.pallas_call(
        functools.partial(back_kernel, sizes),
        out_shape=(
            shape((tok_rows, model_width), f32),
            shape((8, model_width), f32),
            shape((local_width, part), f32),
            shape((size // 2, experts_local * 2 * CAP, model_width), half),
            shape((split, part, hidden_width), half),
            shape((split, 3, part, local_width), half),
        ),
        in_specs=[vmem] * 5 + [anywhere] * (len(kept) + 4),
        out_specs=tuple([vmem] * 3 + [anywhere] * 3),
        scratch_shapes=[
            *[pltpu.VMEM(one.shape, one.dtype) for one in kept],
            pltpu.VMEM(down_full.shape, half),
            pltpu.VMEM((length, model_width), half),
            pltpu.VMEM((length, local_width), half),
            pltpu.VMEM(hidden.shape, half),
            pltpu.VMEM((experts_local, size // 2, 2 * CAP, model_width), half),
            pltpu.VMEM((length, HEAD_DIM), f32),
            pltpu.VMEM((length, HEAD_DIM), f32),
            pltpu.VMEM((2, length, local_width), f32),
            pltpu.VMEM((3, length, local_width), half),
            pltpu.VMEM((8, length), f32),
            pltpu.VMEM((size, 8, length), f32),
            pltpu.VMEM((split, 3, part, local_width), half),
            pltpu.VMEM((split, local_width, part), half),
            pltpu.VMEM((split, local_width, part), half),
            kind((2,)),
            kind,
            kind((3, chips)),
            kind((2, chips)),
            kind,
            fsdp,
            fsdp,
            kind,
            few,
            few,
            kind((size,)),
            kind((size,)),
            kind((len(kept),)),
            kind,
            fsdp,
            fsdp,
            *ChainReduce.scratch(chips, tok_rows, model_width),
        ],
        compiler_params=pltpu.CompilerParams(
            collective_id=which, has_side_effects=True, vmem_limit_bytes=63 * 2**20
        ),
        cost_estimate=pl.CostEstimate(
            flops=2 * length * model_width * local_width * 8,
            bytes_accessed=500 * 2**20,
            transcendentals=0,
        ),
    )(out_grad, *small, *kept, *big_ones)


def close_kernel(
    sizes,
    onehot_ref,
    gains_ref,
    router_ref,
    mixed_rows_any,
    residual_any,
    qkv_any,
    grad_up_ref,
    output_ref,
    gains_out_ref,
    router_out_ref,
    query_w_grad_ref,
    key_w_grad_ref,
    value_w_grad_ref,
    up_landing,
    mixed_rows_ref,
    residual_ref,
    qkv_ref,
    qkv_in,
    qkv_sum,
    load_sem,
    qkv_send,
    qkv_recv,
    total,
    small,
    first,
    second,
    final,
    up_local,
    up_send,
    up_recv,
    send_one,
    recv_one,
    send_two,
    recv_two,
    send_three,
    recv_three,
    *reduce_buffers,
):
    size, split, chips, experts_local = sizes
    f32 = jnp.float32
    me, mine = lax.axis_index("seq"), lax.axis_index("fsdp")
    tok_rows, model_width = residual_ref.shape
    part = model_width // split
    slice_width = model_width // size
    experts_all = router_ref.shape[0]
    loads = [
        pltpu.make_async_copy(source, target, load_sem.at[index])
        for index, (source, target) in enumerate(
            ((qkv_any, qkv_ref), (mixed_rows_any, mixed_rows_ref), (residual_any, residual_ref))
        )
    ]
    for load in loads:
        load.start()
    small[0:8, :] = gains_ref[...]
    small[8 : 8 + experts_all, :] = router_ref[...]
    greet_all(size, split)
    up_send_all = ShardSend(
        split,
        lambda dest: grad_up_ref.at[pl.ds(pl.multiple_of(dest * part, part), part)],
        up_landing,
        up_local,
        up_send,
        up_recv,
    )
    loads[0].wait()

    half_part = qkv_ref.shape[2] // 2
    lower, upper = pl.ds(0, half_part), pl.ds(half_part, half_part)
    mates = (partner_of(mine, 1), partner_of(mine, 2), partner_of(mine, 3)) if split == 4 else ()

    def qkv_copy(index):
        side = index % 2
        rows = (lower, upper)[side]
        if index < 4:
            dest = mates[side] if index < 2 else mates[2]
            source, mate = qkv_ref.at[dest, :, rows], mates[side]
        else:
            source, mate = qkv_sum.at[side], mates[1 - side]
        return pltpu.make_async_remote_copy(
            src_ref=source,
            dst_ref=qkv_in.at[index],
            send_sem=qkv_send.at[index],
            recv_sem=qkv_recv.at[index],
            device_id={"fsdp": mate},
        )

    def qkv_shift(shift):
        dest = lax.rem(mine + shift, split)
        return pltpu.make_async_remote_copy(
            src_ref=qkv_ref.at[dest],
            dst_ref=qkv_in.at[shift],
            send_sem=qkv_send.at[shift],
            recv_sem=qkv_recv.at[shift],
            device_id={"fsdp": dest},
        )

    if split == 4:
        for index in range(4):
            qkv_copy(index).start()
    else:
        for shift in range(1, split):
            qkv_shift(shift).start()
    up_send_all.start()

    def columns(index):
        return pl.ds(pl.multiple_of(index * slice_width, slice_width), slice_width)

    def scatter(shift):
        peer = lax.rem(me + shift, size)
        return pltpu.make_async_remote_copy(
            src_ref=small.at[:, columns(peer)],
            dst_ref=first.at[me],
            send_sem=send_one.at[shift],
            recv_sem=recv_one.at[shift],
            device_id={"seq": peer},
        )

    def share(shift):
        return pltpu.make_async_remote_copy(
            src_ref=second.at[mine],
            dst_ref=second.at[mine],
            send_sem=send_two.at[shift],
            recv_sem=recv_two.at[shift],
            device_id={"fsdp": lax.rem(mine + shift, split)},
        )

    def collect(shift):
        return pltpu.make_async_remote_copy(
            src_ref=final.at[me],
            dst_ref=final.at[me],
            send_sem=send_three.at[shift],
            recv_sem=recv_three.at[shift],
            device_id={"seq": lax.rem(me + shift, size)},
        )

    for shift in range(1, size):
        scatter(shift).start()
    first[me] = small[:, columns(me)]

    reduce = ChainReduce(chips, total, reduce_buffers)
    width_step = min(512, model_width)

    def product(index, store):
        side = pl.ds(pl.multiple_of(lax.rem(index, 2) * tok_rows, tok_rows), tok_rows)
        left = onehot_ref[index // 2, :, side]

        @pl.loop(0, model_width // width_step)
        def _(step):
            cols = pl.ds(pl.multiple_of(step * width_step, width_step), width_step)
            store(cols, turned_dot(left, mixed_rows_ref[index // 2, :, cols]))

    def between():
        for shift in range(1, size):
            scatter(shift).wait_recv()
        second[mine] = jnp.sum(first[...], 0)
        for shift in range(1, split):
            share(shift).start()

    loads[1].wait()
    reduce.run(product, between)
    if split == 4:
        for side in range(2):
            qkv_copy(2 + side).wait_recv()
            rows = (lower, upper)[side]
            qkv_sum[side] = (
                qkv_ref[mates[1 - side], :, rows].astype(f32) + qkv_in[2 + side].astype(f32)
            ).astype(qkv_sum.dtype)
            qkv_copy(4 + side).start()
    loads[2].wait()
    for shift in range(1, split):
        share(shift).wait_recv()
    final[me] = jnp.sum(second[...], 0)
    for shift in range(1, size):
        collect(shift).start()
    output_ref[...] = (residual_ref[...] + total[...]).astype(output_ref.dtype)
    for shift in range(1, size):
        scatter(shift).wait_send()
    for shift in range(1, split):
        share(shift).wait_send()
    for shift in range(1, size):
        collect(shift).wait()
    for index in range(size):
        cols = slice(index * slice_width, (index + 1) * slice_width)
        gains_out_ref[:, cols] = final[index, 0:4]
        router_out_ref[:, cols] = final[index, 8:]
    targets = (query_w_grad_ref, key_w_grad_ref, value_w_grad_ref)
    if split == 4:
        for side in range(2):
            for index in (side, 2 + side, 5 - side):
                copy = qkv_copy(index)
                copy.wait() if index < 2 or index > 3 else copy.wait_send()
        for side in range(2):
            rows = (lower, upper)[side]
            for index, target in enumerate(targets):
                target[rows, :] = (
                    qkv_ref[mine, index, rows].astype(f32)
                    + qkv_in[side, index].astype(f32)
                    + qkv_in[4 + side, index].astype(f32)
                )
    else:
        for shift in range(1, split):
            qkv_shift(shift).wait()
        for index, target in enumerate(targets):
            sums = qkv_ref[mine, index].astype(f32)
            for shift in range(1, split):
                sums += qkv_in[shift, index].astype(f32)
            target[...] = sums
    reduce.sent()
    up_send_all.wait()


def close(sizes, onehot, gains, router_grad, mixed_rows, residual, qkv_parts, grad_up, which):
    size, split, chips, experts_local = sizes
    f32, half = jnp.float32, jnp.bfloat16
    tok_rows, model_width = residual.shape
    hidden_width = grad_up.shape[1]
    part, slice_width = model_width // split, model_width // size
    rows = 8 + router_grad.shape[0]
    vmem = pl.BlockSpec(memory_space=pltpu.VMEM)
    anywhere = pl.BlockSpec(memory_space=pl.ANY)
    kind = pltpu.SemaphoreType.DMA
    shape = jax.ShapeDtypeStruct
    seq, fsdp = kind((size,)), kind((split,))
    share = qkv_parts.shape[2:]
    return pl.pallas_call(
        functools.partial(close_kernel, sizes),
        out_shape=(
            shape((tok_rows, model_width), half),
            shape((4, model_width), f32),
            shape(router_grad.shape, f32),
            shape(share, f32),
            shape(share, f32),
            shape(share, f32),
            shape((split, part, hidden_width), half),
        ),
        in_specs=[vmem] * 3 + [anywhere] * 4,
        out_specs=tuple([vmem] * 6 + [anywhere]),
        scratch_shapes=[
            pltpu.VMEM(mixed_rows.shape, half),
            pltpu.VMEM(residual.shape, f32),
            pltpu.VMEM(qkv_parts.shape, half),
            pltpu.VMEM((6, 3, share[0] // 2, share[1]) if split == 4 else qkv_parts.shape, half),
            pltpu.VMEM((2, 3, share[0] // 2, share[1]), half),
            kind((3,)),
            kind((max(6, split),)),
            kind((max(6, split),)),
            pltpu.VMEM((tok_rows, model_width), f32),
            pltpu.VMEM((rows, model_width), f32),
            pltpu.VMEM((size, rows, slice_width), f32),
            pltpu.VMEM((split, rows, slice_width), f32),
            pltpu.VMEM((size, rows, slice_width), f32),
            kind,
            fsdp,
            fsdp,
            seq,
            seq,
            fsdp,
            fsdp,
            seq,
            seq,
            *ChainReduce.scratch(chips, tok_rows, model_width),
        ],
        compiler_params=pltpu.CompilerParams(
            collective_id=which, has_side_effects=True, vmem_limit_bytes=56 * 2**20
        ),
    )(onehot, gains, router_grad, mixed_rows, residual, qkv_parts, grad_up)


def finish_kernel(count, *refs):
    sources, targets = refs[: len(refs) // 2], refs[len(refs) // 2 :]
    for source, target in zip(sources[:count], targets[:count]):
        target[...] = source[...]
    for source, target in zip(sources[count:], targets[count:]):
        total = source[0].astype(target.dtype)
        for index in range(1, source.shape[0]):
            total += source[index].astype(target.dtype)
        target[...] = total


def finish(results, landings, experts_local):
    halves = 2
    steps = experts_local * halves
    in_specs, out_specs, shapes = [], [], []
    for one in results:
        rows = one.shape[0] // steps
        spec = pl.BlockSpec((rows, one.shape[1]), lambda step: (step, 0))
        if one.shape[0] % (steps * 16):
            spec = pl.BlockSpec(one.shape, lambda step: (0, 0))
        in_specs.append(spec)
        out_specs.append(spec)
        shapes.append(jax.ShapeDtypeStruct(one.shape, one.dtype))
    grouped = []
    for one in landings:
        groups = one.shape[0] // experts_local
        grouped.append(one.reshape(groups, experts_local, *one.shape[1:]))
        block = (one.shape[1] // halves, one.shape[2])
        in_specs.append(
            pl.BlockSpec(
                (groups, 1, *block), lambda step: (0, step // halves, step % halves, 0)
            )
        )
        out_specs.append(
            pl.BlockSpec((1, *block), lambda step: (step // halves, step % halves, 0))
        )
        shapes.append(jax.ShapeDtypeStruct((experts_local, *one.shape[1:]), jnp.float32))
    return pl.pallas_call(
        functools.partial(finish_kernel, len(results)),
        grid=(steps,),
        in_specs=in_specs,
        out_specs=out_specs,
        out_shape=shapes,
        compiler_params=pltpu.CompilerParams(vmem_limit_bytes=63 * 2**20),
    )(*results, *grouped)


def shards(
    tokens,
    norm_gains,
    w_query,
    w_key,
    w_value,
    w_out,
    w_router,
    w_gate,
    w_up,
    w_down,
    segment_ids,
    expert_ids,
    expert_slots,
    cotangent,
):
    half_type = jnp.bfloat16
    model_width = tokens.shape[1]
    experts_local = w_gate.shape[0]
    seq_size = lax.axis_size("seq")
    split = lax.axis_size("fsdp")
    length = seq_size * tokens.shape[0]
    sizes = (seq_size, split, seq_size // 2, experts_local)
    cosine_wide, sine_wide = rope_tables(length, HEAD_DIM)
    segment_row = segment_ids.reshape(1, -1)
    (
        normed_seq,
        qkv_stack,
        out_stack,
        query_heads,
        key_heads,
        value_heads,
        unit_pair,
        log_wide,
        attended_heads,
        square_sums,
        residual,
        gain_rows,
        segment_cols,
        routed_seq,
        cotangent_rows,
        gate_full,
        up_full,
        down_full,
        choices,
        onehot,
    ) = front(
        sizes,
        tokens,
        norm_gains,
        cosine_wide,
        sine_wide,
        segment_row,
        expert_ids,
        expert_slots,
        cotangent,
        (w_query, w_key, w_value, w_out, w_gate, w_up, w_down),
        0,
    )
    router_rows = jnp.zeros((seq_size, 8, model_width), half_type)
    router_rows = router_rows.at[:, :experts_local].set(
        w_router.T.reshape(seq_size, experts_local, model_width)
    )
    router_rows = router_rows.reshape(seq_size * 8, model_width)
    (
        residual_grad,
        out_grad,
        gain_second_grad,
        router_grad,
        hidden,
        grad_gate_full,
        grad_up_full,
        down_landing,
    ) = experts(
        sizes,
        routed_seq,
        choices,
        onehot,
        cotangent_rows,
        router_rows,
        gain_rows,
        residual,
        cotangent,
        (gate_full, up_full, down_full),
        1,
    )
    input_grad, gain_grads, out_owned, mixed_rows, gate_landing, qkv_parts = back(
        sizes,
        out_grad,
        (gain_rows, gain_second_grad, segment_row, square_sums),
        (
            out_stack,
            attended_heads,
            query_heads,
            key_heads,
            value_heads,
            segment_cols,
            log_wide,
            cosine_wide,
            sine_wide,
            unit_pair,
            qkv_stack,
            tokens,
            residual_grad,
        ),
        (normed_seq, hidden, down_full, grad_gate_full),
        2,
    )
    output, gain_sums, router_sums, query_owned, key_owned, value_owned, up_landing = close(
        sizes, onehot, gain_grads, router_grad, mixed_rows, residual, qkv_parts, grad_up_full, 3
    )
    (
        output,
        input_grad,
        gain_sums,
        query_owned,
        key_owned,
        value_owned,
        out_owned,
        router_sums,
        gate_owned,
        up_owned,
        down_owned,
    ) = finish(
        (
            output,
            input_grad,
            gain_sums,
            query_owned,
            key_owned,
            value_owned,
            out_owned,
            router_sums,
        ),
        (gate_landing, up_landing, down_landing),
        experts_local,
    )
    return (
        output,
        input_grad,
        gain_sums,
        query_owned,
        key_owned,
        value_owned,
        out_owned,
        router_sums.T,
        gate_owned,
        up_owned,
        down_owned,
    )


def solution(mesh):
    in_specs = (
        P(("fsdp", "seq"), None),
        P(),
        P("fsdp", "seq"),
        P("fsdp", "seq"),
        P("fsdp", "seq"),
        P("seq", "fsdp"),
        P(),
        P("seq", "fsdp", None),
        P("seq", "fsdp", None),
        P("seq", None, "fsdp"),
        P("fsdp"),
        P(("fsdp", "seq"), None),
        P(("fsdp", "seq"), None),
        P(("fsdp", "seq"), None),
    )
    out_specs = (
        P(("fsdp", "seq"), None),
        P(("fsdp", "seq"), None),
        P(),
        P("fsdp", "seq"),
        P("fsdp", "seq"),
        P("fsdp", "seq"),
        P("seq", "fsdp"),
        P(),
        P("seq", "fsdp", None),
        P("seq", "fsdp", None),
        P("seq", None, "fsdp"),
    )
    return jax.shard_map(shards, mesh=mesh, in_specs=in_specs, out_specs=out_specs, check_vma=False)
```

```python
import functools

import jax
import jax.numpy as jnp
import numpy as np
from jax import lax
from jax.experimental import pallas as pl
from jax.experimental.pallas import tpu as pltpu
from jax.sharding import PartitionSpec as P

HEAD_DIM = 128
CAP = 40


EPSILON = 1e-06
THETA = 10000.0
MASKED = -1e30
HIGHEST = lax.Precision.HIGHEST


def rope_tables(length, head_size):
    half_dim = head_size // 2
    frequency = THETA ** (-np.arange(half_dim, dtype=np.float64) / half_dim)
    angles = np.arange(length, dtype=np.float64)[:, None] * frequency.astype(np.float32)
    cosine, sine = np.cos(angles), np.sin(angles)
    return (
        jnp.asarray(np.concatenate([cosine, cosine], 1), jnp.float32),
        jnp.asarray(np.concatenate([-sine, sine], 1), jnp.float32),
    )


class ChainGather:
    def __init__(self, chips, x_ref, out_ref, local_sem, sends, arrivals):
        self.chips, self.x_ref, self.out_ref = chips, x_ref, out_ref
        self.local_sem, self.sends, self.arrivals = local_sem, sends, arrivals
        me = lax.axis_index("seq")
        self.chip, self.core = me // 2, lax.rem(me, 2)
        self.rows = x_ref.shape[0]

    def block(self, source, core):
        start = pl.multiple_of((source * 2 + core) * self.rows, self.rows)
        return self.out_ref.at[pl.ds(start, self.rows)]

    def hop(self, source, ref, target, way, lane):
        return pltpu.make_async_remote_copy(
            src_ref=ref,
            dst_ref=self.block(source, self.core),
            send_sem=self.sends.at[way, source],
            recv_sem=self.arrivals.at[lane, source],
            device_id={"seq": target},
        )

    def upward(self, source, ref):
        return self.hop(source, ref, self.chip * 2 + 2 + self.core, 0, 0)

    def downward(self, source, ref):
        return self.hop(source, ref, self.chip * 2 - 2 + self.core, 1, 0)

    def sideways(self, source, ref):
        return self.hop(source, ref, self.chip * 2 + 1 - self.core, 2, 1)

    def own(self):
        return pltpu.make_async_copy(
            self.x_ref, self.block(self.chip, self.core), self.local_sem
        )

    def start(self):
        @pl.when(self.chip < self.chips - 1)
        def _():
            self.upward(self.chip, self.x_ref).start()

        @pl.when(self.chip > 0)
        def _():
            self.downward(self.chip, self.x_ref).start()

        self.sideways(self.chip, self.x_ref).start()
        self.own().start()

    def step(self, distance):
        below, above = self.chip - distance, self.chip + distance

        @pl.when(below >= 0)
        def _():
            landed = self.block(below, self.core)
            self.upward(below, landed).wait_recv()

            @pl.when(self.chip < self.chips - 1)
            def _():
                self.upward(below, landed).start()

            self.sideways(below, landed).start()

        @pl.when(above < self.chips)
        def _():
            landed = self.block(above, self.core)
            self.downward(above, landed).wait_recv()

            @pl.when(self.chip > 0)
            def _():
                self.downward(above, landed).start()

            self.sideways(above, landed).start()

    def steps(self):
        for distance in range(1, self.chips):
            self.step(distance)

    def landed(self):
        self.own().wait()
        for source in range(self.chips):
            self.sideways(source, self.block(source, self.core)).wait_recv()

    def sent(self):
        for source in range(self.chips):
            ref = self.block(source, self.core)
            self.sideways(source, ref).wait_send()

            @pl.when((self.chip < self.chips - 1) & (source <= self.chip))
            def _():
                self.upward(source, ref).wait_send()

            @pl.when((self.chip > 0) & (source >= self.chip))
            def _():
                self.downward(source, ref).wait_send()


class ChainReduce:
    def __init__(self, chips, total, buffers):
        self.total = total
        (
            self.side_out,
            self.side_in,
            self.chain_in,
            self.side_send,
            self.side_recv,
            self.chain_send,
            self.chain_recv,
        ) = buffers
        self.chips = chips
        me = lax.axis_index("seq")
        self.chip, self.core = me // 2, lax.rem(me, 2)

    @staticmethod
    def scratch(chips, rows, width):
        half = jnp.bfloat16
        return [
            pltpu.VMEM((chips, rows, width), half),
            pltpu.VMEM((chips, rows, width), half),
            pltpu.VMEM((chips + 1, rows, width), half),
            pltpu.SemaphoreType.DMA((chips,)),
            pltpu.SemaphoreType.DMA((chips,)),
            pltpu.SemaphoreType.DMA((chips,)),
            pltpu.SemaphoreType.DMA((2, chips)),
        ]

    def side_copy(self, dest):
        return pltpu.make_async_remote_copy(
            src_ref=self.side_out.at[dest],
            dst_ref=self.side_in.at[dest],
            send_sem=self.side_send.at[dest],
            recv_sem=self.side_recv.at[dest],
            device_id={"seq": self.chip * 2 + 1 - self.core},
        )

    def chain_copy(self, way, dest, target):
        return pltpu.make_async_remote_copy(
            src_ref=self.side_out.at[dest],
            dst_ref=self.chain_in.at[self.slot(way, dest, target // 2)],
            send_sem=self.chain_send.at[dest],
            recv_sem=self.chain_recv.at[way, dest],
            device_id={"seq": target},
        )

    def slot(self, way, dest, holder):
        return jnp.where(dest == holder, self.chips, dest) if way else dest

    def place(self, index):
        distance = self.chips - 1 - index // 2
        dest = self.chip + (1 - 2 * lax.rem(index, 2)) * distance
        return dest, (dest >= 0) & (dest < self.chips)

    def run(self, product, between=None, hook=None):
        chips, chip, core, total = self.chips, self.chip, self.core, self.total
        sibling = chip * 2 + 1 - core

        @pl.loop(0, 2 * chips - 1)
        def _(index):
            dest, inside = self.place(index)

            @pl.when(inside)
            def _():
                def store(cols, part):
                    self.side_out[dest, :, cols] = part.astype(self.side_out.dtype)

                product(dest * 2 + 1 - core, store)
                self.side_copy(dest).start()

        if between:
            between()

        @pl.loop(0, 2 * chips - 1)
        def _(index):
            dest, inside = self.place(index)
            if hook:
                hook(index)

            @pl.when(inside)
            def _():
                def store(cols, part):
                    total[:, cols] = part

                product(dest * 2 + core, store)
                self.side_copy(dest).wait_recv()
                total[...] += self.side_in[dest].astype(jnp.float32)

                @pl.when((dest >= chip) & (chip > 0))
                def _():
                    self.chain_copy(0, dest, sibling).wait_recv()
                    total[...] += self.chain_in[dest].astype(jnp.float32)

                @pl.when((dest <= chip) & (chip < chips - 1))
                def _():
                    self.chain_copy(1, dest, sibling).wait_recv()
                    total[...] += self.chain_in[self.slot(1, dest, chip)].astype(jnp.float32)

                self.side_copy(dest).wait_send()

                @pl.when(dest != chip)
                def _():
                    self.side_out[dest] = total[...].astype(self.side_out.dtype)

                @pl.when(dest > chip)
                def _():
                    self.chain_copy(0, dest, chip * 2 + 2 + core).start()

                @pl.when(dest < chip)
                def _():
                    self.chain_copy(1, dest, chip * 2 - 2 + core).start()

    def sent(self):
        sibling = self.chip * 2 + 1 - self.core

        @pl.loop(0, self.chips)
        def _(dest):
            @pl.when(dest != self.chip)
            def _():
                self.chain_copy(0, dest, sibling).wait_send()


def partner_of(index, move):
    turned, bit = index, 1
    while bit <= move:
        if move // bit % 2:
            turned = turned + bit - 2 * bit * lax.rem(index // bit, 2)
        bit *= 2
    return turned


def greet_all(size, split):
    me, mine = lax.axis_index("seq"), lax.axis_index("fsdp")
    barrier = pltpu.get_barrier_semaphore()
    for shift in range(1, size):
        pl.semaphore_signal(barrier, inc=1, device_id={"seq": lax.rem(me + shift, size)})
    for shift in range(1, split):
        pl.semaphore_signal(barrier, inc=1, device_id={"fsdp": lax.rem(mine + shift, split)})
    pl.semaphore_wait(barrier, size + split - 2)


def turned_halves(head):
    return pltpu.roll(head, head.shape[-1] // 2, 1)


def row_sums(values, pick):
    return lax.dot_general(
        pick, values, (((1,), (1,)), ((), ())), precision=HIGHEST, preferred_element_type=jnp.float32
    )


def column_of(row_form, pick):
    return lax.dot_general(
        row_form, pick, (((0,), (0,)), ((), ())), precision=HIGHEST, preferred_element_type=jnp.float32
    )


def front_kernel(
    sizes,
    tokens_ref,
    gains_in_ref,
    cos_ref,
    sin_ref,
    seg_row_ref,
    ids_ref,
    slots_ref,
    cotangent_ref,
    wq_ref,
    wk_ref,
    wv_ref,
    wo_ref,
    w_gate_ref,
    w_up_ref,
    w_down_ref,
    normed_out,
    qkv_out,
    rows_out,
    q_out,
    k_out,
    v_out,
    unit_out,
    log_out,
    attended_out,
    sums_ref,
    residual_ref,
    gains_ref,
    seg_col_ref,
    routed_out,
    routed_cross,
    placed_out,
    gate_full,
    up_full,
    down_full,
    choices,
    onehot_ref,
    mate_onehot,
    q_ref,
    k_ref,
    v_ref,
    unit_ref,
    log_ref,
    attended_ref,
    normed,
    qkv,
    rows_full,
    routed_own,
    choice_own,
    cotangent_pair,
    cotangent_all,
    mate_choices,
    placed,
    raw,
    sums_own,
    sums_in,
    gather_local,
    gather_send,
    gather_recv,
    sums_send,
    sums_recv,
    choice_send,
    choice_recv,
    mate_send,
    mate_recv,
    cross_local,
    cross_send,
    cross_recv,
    placed_local,
    shard_local,
    shard_send,
    shard_recv,
    expert_local,
    expert_send,
    expert_recv,
    out_sem,
    *reduce_buffers,
):
    size, split, chips, experts_local = sizes
    f32, half = jnp.float32, jnp.bfloat16
    me, mine = lax.axis_index("seq"), lax.axis_index("fsdp")
    tok_rows, model_width = tokens_ref.shape
    length, local_width = q_ref.shape
    part = model_width // split
    head = HEAD_DIM
    heads = local_width // head

    inputs = tokens_ref[...].astype(f32)
    inverse = lax.rsqrt(jnp.mean(inputs * inputs, -1, keepdims=True) + EPSILON)
    gains_ref[...] = gains_in_ref[...].astype(f32)
    routed_half = routed_own.at[pl.ds(0, tok_rows)]
    routed_half[...] = (inputs * inverse * gains_ref[0:1, :]).astype(half)
    crossed = split == experts_local == 4
    half_width = model_width // 2
    x_mate, y_mate = {"fsdp": partner_of(mine, 1)}, {"fsdp": partner_of(mine, 2)}
    greet_all(size, split)

    def gather(index, x_ref, out_ref):
        return ChainGather(
            chips,
            x_ref,
            out_ref,
            gather_local.at[index],
            gather_send.at[index],
            gather_recv.at[index],
        )

    first = gather(0, routed_half, normed)
    first.start()

    cross_rows = pl.ds(tok_rows, tok_rows)
    lower, upper = pl.ds(0, half_width), pl.ds(half_width, half_width)

    def cross_copy(index):
        cols = (lower, upper)[index % 2]
        source, target = (
            (cotangent_ref, cotangent_pair) if index < 2 else (routed_half, routed_own)
        )
        return pltpu.make_async_remote_copy(
            src_ref=source.at[:, cols],
            dst_ref=target.at[cross_rows, cols],
            send_sem=cross_send.at[index],
            recv_sem=cross_recv.at[index],
            device_id=(x_mate, y_mate)[index % 2],
        )

    if crossed:
        cross_own = pltpu.make_async_copy(
            cotangent_ref, cotangent_pair.at[pl.ds(0, tok_rows)], cross_local
        )
        cross_copy(0).start()
        cross_copy(1).start()
        cross_own.start()

    top_count = ids_ref.shape[1]
    same = lax.broadcasted_iota(jnp.int32, (top_count, top_count), 0) == (
        lax.broadcasted_iota(jnp.int32, (top_count, top_count), 1)
    )
    ids_row = row_sums(ids_ref[...].astype(f32), same.astype(f32))
    slots_row = row_sums(slots_ref[...].astype(f32), same.astype(f32))
    choice_own[0:top_count, :] = ids_row.astype(jnp.int32)
    choice_own[top_count : 2 * top_count, :] = jnp.where(
        slots_row < CAP, ids_row * CAP + slots_row, -1e6
    ).astype(jnp.int32)

    def choice_copy(shift):
        return pltpu.make_async_remote_copy(
            src_ref=choice_own,
            dst_ref=choices.at[me],
            send_sem=choice_send.at[shift],
            recv_sem=choice_recv.at[shift],
            device_id={"seq": lax.rem(me + shift, size)},
        )

    own_part = pl.ds(pl.multiple_of(mine * part, part), part)
    shard_pairs = (
        (wq_ref, qkv.at[0, own_part]),
        (wk_ref, qkv.at[1, own_part]),
        (wv_ref, qkv.at[2, own_part]),
        (wo_ref, rows_full.at[mine]),
    )

    def shard_copy(index, shift):
        source, target = shard_pairs[index]
        return pltpu.make_async_remote_copy(
            src_ref=source,
            dst_ref=target,
            send_sem=shard_send.at[index, shift],
            recv_sem=shard_recv.at[index, shift],
            device_id={"fsdp": lax.rem(mine + shift, split)},
        )

    def landed_half(index, owner, side):
        if index == 3:
            rows = local_width // 2
            return rows_full.at[owner, pl.ds(side * rows, rows)]
        rows = part // 2
        start = pl.multiple_of(owner * part + side * rows, rows)
        return qkv.at[index, pl.ds(start, rows)]

    def relay_copy(index, step):
        if step < 2:
            source, target = shard_pairs[index]
        else:
            source = target = landed_half(index, partner_of(mine, step - 1), step - 2)
        return pltpu.make_async_remote_copy(
            src_ref=source,
            dst_ref=target,
            send_sem=shard_send.at[index, step],
            recv_sem=shard_recv.at[index, step],
            device_id=(x_mate, y_mate, y_mate, x_mate)[step],
        )

    def shard_own(index):
        source, target = shard_pairs[index]
        return pltpu.make_async_copy(source, target, shard_local.at[index])

    for index in range(4):
        if split == 4:
            relay_copy(index, 0).start()
            relay_copy(index, 1).start()
        else:
            for shift in range(1, split):
                shard_copy(index, shift).start()
        shard_own(index).start()

    def expert_pair(index, dest):
        expert = lax.rem(dest, experts_local)
        if index == 2:
            return w_down_ref.at[expert], down_full.at[:, own_part]
        source, target = ((w_gate_ref, gate_full), (w_up_ref, up_full))[index]
        return source.at[expert], target.at[own_part]

    def expert_copy(index, shift):
        dest = lax.rem(mine + shift, split)
        source, target = expert_pair(index, dest)
        return pltpu.make_async_remote_copy(
            src_ref=source,
            dst_ref=target,
            send_sem=expert_send.at[index, shift],
            recv_sem=expert_recv.at[index, shift],
            device_id={"fsdp": dest},
        )

    def expert_own(index):
        source, target = expert_pair(index, mine)
        return pltpu.make_async_copy(source, target, expert_local.at[index])

    for distance in range(1, chips):
        first.step(distance)
        if split == 4 and distance == min(2, chips - 1):
            for index in range(4):
                for step in range(2):
                    relay_copy(index, step).wait_recv()
                    relay_copy(index, step + 2).start()
    for index in range(4):
        shard_own(index).wait()
        if split == 4:
            relay_copy(index, 2).wait_recv()
            relay_copy(index, 3).wait_recv()
        else:
            for shift in range(1, split):
                shard_copy(index, shift).wait_recv()

    def expert_start(index):
        for shift in range(1, split):
            expert_copy(index, shift).start()
        expert_own(index).start()

    expert_start(0)
    first.landed()
    for shift in range(1, size):
        choice_copy(shift).start()
    choices[me] = choice_own[...]
    if crossed:
        cross_own.wait()
        cross_copy(0).wait()
        cross_copy(1).wait()
        second = gather(1, cotangent_pair, cotangent_all)
    else:
        second = gather(1, cotangent_ref, cotangent_all)
    second.start()
    keeps = [
        pltpu.make_async_copy(normed, normed_out, out_sem.at[0]),
        pltpu.make_async_copy(qkv, qkv_out, out_sem.at[1]),
        pltpu.make_async_copy(rows_full, rows_out, out_sem.at[2]),
    ]
    for keep in keeps:
        keep.start()

    own_cols = pl.ds(pl.multiple_of(me * local_width, local_width), local_width)
    block = min(512, length)
    lanes = lax.broadcasted_iota(jnp.int32, (8, local_width), 0)
    first_row, second_row = (lanes == 0).astype(f32), (lanes == 1).astype(f32)

    @pl.loop(0, length // block)
    def _(step):
        rows = pl.ds(pl.multiple_of(step * block, block), block)
        left = normed[rows, :]
        query = jnp.dot(left, qkv[0], preferred_element_type=f32)
        raw[0, rows, :] = query
        keys = jnp.dot(left, qkv[1], preferred_element_type=f32)
        raw[1, rows, :] = keys
        sums_own[:, rows] = row_sums(query * query, first_row) + row_sums(keys * keys, second_row)
        v_ref[rows, :] = jnp.dot(left, qkv[2], preferred_element_type=f32).astype(half)

    def sums_copy(shift):
        return pltpu.make_async_remote_copy(
            src_ref=sums_own,
            dst_ref=sums_in.at[me],
            send_sem=sums_send.at[shift],
            recv_sem=sums_recv.at[shift],
            device_id={"seq": lax.rem(me + shift, size)},
        )

    for shift in range(1, size):
        sums_copy(shift).start()
    sums_in[me] = sums_own[...]
    for shift in range(1, size):
        sums_copy(shift).wait()
    sums_ref[...] = jnp.sum(sums_in[...], 0)
    for shift in range(1, size):
        choice_copy(shift).wait()

    def mate_copy(index):
        return pltpu.make_async_remote_copy(
            src_ref=choices,
            dst_ref=mate_choices.at[index],
            send_sem=mate_send.at[index],
            recv_sem=mate_recv.at[index],
            device_id=(x_mate, y_mate)[index],
        )

    if crossed:
        mate_copy(0).start()
        mate_copy(1).start()
    segments = seg_row_ref[...].astype(f32)
    narrow = first_row[:, 0:128]

    @pl.loop(0, length // block)
    def _(step):
        rows = pl.ds(pl.multiple_of(step * block, block), block)
        square_sums = sums_ref[:, rows]
        seg_col_ref[rows, :] = column_of(
            jnp.broadcast_to(seg_row_ref[:, rows].astype(f32), (8, block)), narrow
        )
        for index, pick, target in ((0, first_row, q_ref), (1, second_row, k_ref)):
            scale = lax.rsqrt(column_of(square_sums, pick) / model_width + EPSILON)
            unit = raw[index, rows, :] * scale
            unit_ref[index, rows, :] = unit
            scaled = unit * gains_ref[2 + index : 3 + index, own_cols]
            for number in range(heads):
                cols = slice(number * head, (number + 1) * head)
                piece = scaled[:, cols]
                target[rows, cols] = (
                    piece * cos_ref[rows, :] + turned_halves(piece) * sin_ref[rows, :]
                ).astype(half)

    second.step(1)

    wide = min(256, length)
    for number in range(heads):
        cols = slice(number * head, (number + 1) * head)

        @pl.loop(0, length // wide)
        def _(step):
            rows = pl.ds(pl.multiple_of(step * wide, wide), wide)
            scores = lax.dot_general(
                q_ref[rows, cols],
                k_ref[:, cols],
                (((1,), (1,)), ((), ())),
                preferred_element_type=f32,
            )
            scores = scores * (head**-0.5)
            scores = jnp.where(seg_col_ref[rows, 0:1] == segments, scores, MASKED)
            peak = jnp.max(scores, -1, keepdims=True)
            grown = jnp.exp(scores - peak)
            weight = jnp.sum(grown, -1, keepdims=True)
            probs = (grown * (1.0 / weight)).astype(half)
            attended_ref[rows, cols] = jnp.dot(
                probs, v_ref[:, cols], preferred_element_type=f32
            ).astype(half)
            log_ref[rows, cols] = jnp.broadcast_to(peak + jnp.log(weight), (wide, head))

    expert_start(1)
    for index, (source, target) in enumerate(
        (
            (q_ref, q_out),
            (k_ref, k_out),
            (v_ref, v_out),
            (unit_ref, unit_out),
            (log_ref, log_out),
            (attended_ref, attended_out),
        )
    ):
        keeps.append(pltpu.make_async_copy(source, target, out_sem.at[3 + index]))
        keeps[-1].start()

    reduce = ChainReduce(chips, residual_ref, reduce_buffers)

    def product(index, store):
        left = attended_ref[pl.ds(pl.multiple_of(index * tok_rows, tok_rows), tok_rows), :]
        for piece in range(split):
            cols = pl.ds(piece * part, part)
            store(cols, jnp.dot(left, rows_full[piece], preferred_element_type=f32))

    def hook(index):
        for distance in range(2, chips - 1):

            @pl.when(index == 2 * distance)
            def _():
                second.step(distance)

    reduce.run(product, hook=hook)
    residual = tokens_ref[...].astype(f32) + reduce.total[...]
    residual_ref[...] = residual
    inverse = lax.rsqrt(jnp.mean(residual * residual, -1, keepdims=True) + EPSILON)
    first.sent()
    routed_half[...] = (residual * inverse * gains_ref[1:2, :]).astype(half)
    if crossed:
        cross_copy(2).start()
        cross_copy(3).start()
    third = gather(2, routed_half, routed_out)
    third.start()
    if chips > 2:
        second.step(chips - 1)
    expert_start(2)

    second.landed()
    double = 2 * CAP
    member = lax.rem(mine, experts_local)
    slot_row = lax.broadcasted_iota(jnp.int32, (double, tok_rows), 0)
    if crossed:
        mate_copy(0).wait()
        mate_copy(1).wait()

    def one_hot(places, target, rows, expert):
        base = (me * experts_local + expert) * CAP
        for side in range(2):
            want = jnp.where(slot_row // CAP == side, slot_row - side * CAP + base, -1)
            hit = want == places(side)[top_count : top_count + 1, :]
            for choice in range(1, top_count):
                hit = hit | (want == places(side)[top_count + choice : top_count + choice + 1, :])
            cols = slice(side * tok_rows, (side + 1) * tok_rows)
            target[rows, cols] = jnp.where(hit, 1.0, 0.0).astype(half)

    def slot_range(move):
        return slice(move * double, (move + 1) * double)

    @pl.loop(0, size // 2)
    def _(pair):
        for move in range(experts_local):
            one_hot(
                lambda side: choices[pair * 2 + side],
                onehot_ref.at[pair],
                slot_range(move),
                partner_of(member, move),
            )
        if crossed:
            start = pl.multiple_of(pair * 4 * tok_rows, 4 * tok_rows)
            four = cotangent_all[pl.ds(start, 4 * tok_rows), :]
            own = jnp.concatenate(
                [four[0:tok_rows], four[2 * tok_rows : 3 * tok_rows]], 0
            )
            mates = jnp.concatenate(
                [four[tok_rows : 2 * tok_rows], four[3 * tok_rows : 4 * tok_rows]], 0
            )
            made = jnp.dot(onehot_ref[pair], own, preferred_element_type=f32).astype(half)
            placed[0, pair] = made[slot_range(0)]
            placed[1, pair, :, upper] = made[slot_range(1), half_width:]
            placed[2, pair, :, lower] = made[slot_range(2), :half_width]
            for index in range(2):
                for row, expert in enumerate((member, partner_of(member, 2 - index))):
                    one_hot(
                        lambda side: mate_choices[index, pair * 2 + side],
                        mate_onehot.at[pair, index],
                        slot_range(row),
                        expert,
                    )
                cols = (lower, upper)[index]
                taken = mates[:, :half_width] if index == 0 else mates[:, half_width:]
                made = jnp.dot(
                    mate_onehot[pair, index], taken, preferred_element_type=f32
                ).astype(half)
                placed[index + 1, pair, :, cols] = made[slot_range(0)]
                placed[3, pair, :, cols] = made[slot_range(1)]
        else:
            start = pl.multiple_of(pair * 2 * tok_rows, 2 * tok_rows)
            made = jnp.dot(
                onehot_ref[pair],
                cotangent_all[pl.ds(start, 2 * tok_rows), :],
                preferred_element_type=f32,
            ).astype(half)
            for move in range(experts_local):
                placed[move, pair] = made[slot_range(move)]

    placed_keep = pltpu.make_async_copy(placed, placed_out, placed_local.at[0])
    placed_keep.start()
    third.steps()
    third.landed()
    if crossed:
        cross_copy(2).wait()
        cross_copy(3).wait()
        cross_keep = pltpu.make_async_copy(
            routed_own.at[cross_rows], routed_cross, placed_local.at[1]
        )
        cross_keep.start()
    reduce.sent()
    second.sent()
    third.sent()
    for index in range(4):
        if split == 4:
            for step in range(4):
                relay_copy(index, step).wait_send()
        else:
            for shift in range(1, split):
                shard_copy(index, shift).wait_send()
    for keep in keeps:
        keep.wait()
    placed_keep.wait()
    if crossed:
        cross_keep.wait()
    for index in range(3):
        expert_own(index).wait()
        for shift in range(1, split):
            expert_copy(index, shift).wait()


def front(sizes, tokens, gains, cos, sin, segment_row, ids, slots, cotangent, weights, which):
    size, split, chips, experts_local = sizes
    w_query, w_key, w_value, w_out, w_gate, w_up, w_down = weights
    tok_rows, model_width = tokens.shape
    length = size * tok_rows
    local_width = w_query.shape[1]
    hidden_width = w_gate.shape[2]
    f32, half = jnp.float32, jnp.bfloat16
    vmem = pl.BlockSpec(memory_space=pltpu.VMEM)
    anywhere = pl.BlockSpec(memory_space=pl.ANY)
    kind = pltpu.SemaphoreType.DMA
    shape = jax.ShapeDtypeStruct
    crossed = split == experts_local == 4
    choices = (size, 2 * ids.shape[1], tok_rows)
    return pl.pallas_call(
        functools.partial(front_kernel, sizes),
        out_shape=(
            shape((length, model_width), half),
            shape((3, model_width, local_width), half),
            shape((split, *w_out.shape), half),
            shape((length, local_width), half),
            shape((length, local_width), half),
            shape((length, local_width), half),
            shape((2, length, local_width), f32),
            shape((length, local_width), f32),
            shape((length, local_width), half),
            shape((8, length), f32),
            shape((tok_rows, model_width), f32),
            shape(gains.shape, f32),
            shape((length, 128), f32),
            shape((length, model_width), half),
            shape((tok_rows, model_width), half),
            shape((experts_local, size // 2, 2 * CAP, model_width), half),
            shape((model_width, hidden_width), half),
            shape((model_width, hidden_width), half),
            shape((hidden_width, model_width), half),
            shape((size, 2 * ids.shape[1], tok_rows), jnp.int32),
            shape((size // 2, experts_local * 2 * CAP, 2 * tok_rows), half),
            shape((size // 2 if crossed else 1, 2, 4 * CAP, 2 * tok_rows), half),
        ),
        in_specs=[vmem] * 7 + [anywhere] * 8,
        out_specs=tuple([anywhere] * 9 + [vmem] * 4 + [anywhere] * 6 + [vmem] * 3),
        scratch_shapes=[
            pltpu.VMEM((length, local_width), half),
            pltpu.VMEM((length, local_width), half),
            pltpu.VMEM((length, local_width), half),
            pltpu.VMEM((2, length, local_width), f32),
            pltpu.VMEM((length, local_width), f32),
            pltpu.VMEM((length, local_width), half),
            pltpu.VMEM((length, model_width), half),
            pltpu.VMEM((3, model_width, local_width), half),
            pltpu.VMEM((split, *w_out.shape), half),
            pltpu.VMEM((2 * tok_rows, model_width), half),
            pltpu.VMEM((2 * ids.shape[1], tok_rows), jnp.int32),
            pltpu.VMEM((2 * tok_rows if crossed else 16, model_width), half),
            pltpu.VMEM(((2 if crossed else 1) * length, model_width), half),
            pltpu.VMEM((2, *(choices if crossed else (1, 8, 128))), jnp.int32),
            pltpu.VMEM((experts_local, size // 2, 2 * CAP, model_width), half),
            pltpu.VMEM((2, length, local_width), f32),
            pltpu.VMEM((8, length), f32),
            pltpu.VMEM((size, 8, length), f32),
            kind((3,)),
            kind((3, 3, chips)),
            kind((3, 2, chips)),
            kind((size,)),
            kind((size,)),
            kind((size,)),
            kind((size,)),
            kind((2,)),
            kind((2,)),
            kind,
            kind((4,)),
            kind((4,)),
            kind((2,)),
            kind((4,)),
            kind((4, split)),
            kind((4, split)),
            kind((3,)),
            kind((3, split)),
            kind((3, split)),
            kind((9,)),
            *ChainReduce.scratch(chips, tok_rows, model_width),
        ],
        compiler_params=pltpu.CompilerParams(
            collective_id=which, has_side_effects=True, vmem_limit_bytes=58 * 2**20
        ),
        cost_estimate=pl.CostEstimate(
            flops=2 * length * model_width * local_width * 4,
            bytes_accessed=500 * 2**20,
            transcendentals=0,
        ),
    )(
        tokens, gains, cos, sin, segment_row, ids, slots, cotangent, *weights
    )


class ShardSend:
    def __init__(self, split, source, landing, local_sem, sends, arrivals):
        self.split, self.source, self.landing = split, source, landing
        self.local_sem, self.sends, self.arrivals = local_sem, sends, arrivals
        self.mine = lax.axis_index("fsdp")

    def copy(self, shift):
        dest = lax.rem(self.mine + shift, self.split)
        return pltpu.make_async_remote_copy(
            src_ref=self.source(dest),
            dst_ref=self.landing.at[self.mine],
            send_sem=self.sends.at[shift],
            recv_sem=self.arrivals.at[shift],
            device_id={"fsdp": dest},
        )

    def own(self):
        return pltpu.make_async_copy(
            self.source(self.mine), self.landing.at[self.mine], self.local_sem
        )

    def start(self):
        for shift in range(1, self.split):
            self.copy(shift).start()
        self.own().start()

    def wait(self):
        for shift in range(1, self.split):
            self.copy(shift).wait()
        self.own().wait()


def turned_dot(left, right):
    return lax.dot_general(
        left, right, (((0,), (0,)), ((), ())), preferred_element_type=jnp.float32
    )


def cross_dot(left, right):
    return lax.dot_general(
        left, right, (((1,), (1,)), ((), ())), preferred_element_type=jnp.float32
    )


def experts_kernel(
    sizes,
    routed_ref,
    routed_cross_ref,
    choices_ref,
    onehot_ref,
    mate_onehot_ref,
    placed_ref,
    router_ref,
    gains_ref,
    residual_ref,
    cotangent_ref,
    gate_ref,
    up_ref,
    down_ref,
    residual_grad_ref,
    out_grad_ref,
    gain_ref,
    router_grad_ref,
    hidden_out,
    grad_gate_ref,
    grad_up_ref,
    down_landing,
    routed_mates,
    gate_full,
    up_full,
    down_full,
    upstream,
    pair_rows,
    outgoing,
    arrived,
    hidden,
    gate_grad,
    up_grad,
    back,
    gates,
    gates_out,
    gates_in,
    dots_out,
    dots_in,
    token_out,
    token_in,
    scales,
    load_sem,
    pair_sem,
    keep_sem,
    gather_local,
    gather_send,
    gather_recv,
    upstream_send,
    upstream_recv,
    rows_send,
    rows_recv,
    gates_send,
    gates_recv,
    back_send,
    back_recv,
    dots_send,
    dots_recv,
    token_send,
    token_recv,
    down_send,
    down_recv,
    *reduce_buffers,
):
    size, split, chips, experts_local = sizes
    f32, half = jnp.float32, jnp.bfloat16
    me, mine = lax.axis_index("seq"), lax.axis_index("fsdp")
    tok_rows, model_width = residual_ref.shape
    pairs = size // 2
    double = 2 * CAP
    wide = 2 * tok_rows
    hidden_width = gate_full.shape[1]
    rows_of = pairs * double
    part = model_width // split
    member = lax.rem(mine, experts_local)
    crossed = split == experts_local == 4
    half_width = model_width // 2
    lower, upper = pl.ds(0, half_width), pl.ds(half_width, half_width)

    loads = [
        pltpu.make_async_copy(source, target, load_sem.at[index])
        for index, (source, target) in enumerate(
            (
                (gate_ref, gate_full),
                (up_ref, up_full),
                (down_ref, down_full),
            )
        )
    ]
    if crossed:
        pieces = (
            (placed_ref.at[0], upstream.at[0]),
            (placed_ref.at[1, :, :, lower], upstream.at[1, :, :, lower]),
            (placed_ref.at[2, :, :, upper], upstream.at[2, :, :, upper]),
        )
    else:
        pieces = ((placed_ref.at[0], upstream.at[0]),)
    loads += [
        pltpu.make_async_copy(source, target, load_sem.at[3 + index])
        for index, (source, target) in enumerate(pieces)
    ]

    slots = pair_rows.shape[0]

    def pair_load(source, pair):
        slot = lax.rem(pair, slots)
        start = pl.multiple_of(pair * wide, wide)
        return pltpu.make_async_copy(
            source.at[pl.ds(start, wide)], pair_rows.at[slot], pair_sem.at[slot]
        )

    pair_load(routed_ref, 0).start()
    for load in loads:
        load.start()
    greet_all(size, split)

    def mate(move):
        return {"fsdp": partner_of(mine, move)}

    def upstream_piece(move, index, cols, target):
        return pltpu.make_async_remote_copy(
            src_ref=placed_ref.at[move, :, :, cols],
            dst_ref=upstream.at[move, :, :, cols],
            send_sem=upstream_send.at[index],
            recv_sem=upstream_recv.at[index],
            device_id=mate(target),
        )

    def halves_of(piece, move):
        if not crossed:
            return [piece(move, move, pl.ds(0, model_width), move)]
        if move == 3:
            return [piece(3, 3, upper, 1), piece(3, 0, lower, 2)]
        return [piece(move, move, (upper, lower)[move - 1], move)]

    order = [1, 2, 3] if crossed else list(range(experts_local - 1, 0, -1))
    if crossed:
        gather = ChainGather(
            chips, routed_cross_ref, routed_mates, gather_local, gather_send, gather_recv
        )
        gather.start()
    for move in order:
        for copy in halves_of(upstream_piece, move):
            copy.start()

    padded = size * 8
    expert_row = lax.broadcasted_iota(jnp.int32, (padded, tok_rows), 0)
    inner = lax.rem(expert_row, 8)
    expert_row = jnp.where(inner < experts_local, expert_row // 8 * experts_local + inner, -1)
    ones = jnp.ones((8, wide), f32)
    top_count = choices_ref.shape[1] // 2

    @pl.loop(0, pairs)
    def _(pair):
        pair_load(routed_ref, pair).wait()

        @pl.when((pair + 1 < pairs) & (slots > 1))
        def _():
            pair_load(routed_ref, pair + 1).start()

        rows = pair_rows[lax.rem(pair, slots)]
        logits = lax.dot_general(
            router_ref[...], rows, (((1,), (1,)), ((), ())), preferred_element_type=f32
        )
        for side in range(2):
            ids = choices_ref[pair * 2 + side]
            chosen = expert_row == ids[0:1, :]
            for choice in range(1, top_count):
                chosen = chosen | (expert_row == ids[choice : choice + 1, :])
            own = jnp.where(chosen, logits[:, side * tok_rows : (side + 1) * tok_rows], MASKED)
            grown = jnp.where(chosen, jnp.exp(own - jnp.max(own, 0, keepdims=True)), 0.0)
            gates[pair * 2 + side] = grown / jnp.sum(grown, 0, keepdims=True)
        placed = jnp.dot(onehot_ref[pair], rows, preferred_element_type=f32).astype(half)
        for move in range(experts_local):
            piece = placed[move * double : (move + 1) * double]
            if move == 0:
                arrived[0, pair] = piece
            elif not crossed:
                outgoing[move - 1, pair] = piece
            elif move < 3:
                cols = (upper, lower)[move - 1]
                outgoing[move - 1, pair, :, cols] = (
                    piece[:, half_width:] if move == 1 else piece[:, :half_width]
                )
            row = me * 8 + partner_of(member, move)
            weights = jnp.concatenate(
                [gates[pair * 2, pl.ds(row, 1), :], gates[pair * 2 + 1, pl.ds(row, 1), :]], 1
            )
            slot_rows = pl.ds(move * double, double)
            weighted = onehot_ref[pair, slot_rows, :].astype(f32) * weights
            gates_out[move, pair] = row_sums(weighted, ones)

        @pl.when((pair + 1 < pairs) & (slots == 1))
        def _():
            pair_load(routed_ref, pair + 1).start()

    def rows_piece(move, index, cols, target):
        return pltpu.make_async_remote_copy(
            src_ref=outgoing.at[move - 1, :, :, cols],
            dst_ref=arrived.at[move, :, :, cols],
            send_sem=rows_send.at[index],
            recv_sem=rows_recv.at[index],
            device_id=mate(target),
        )

    def gates_copy(move):
        return pltpu.make_async_remote_copy(
            src_ref=gates_out.at[move],
            dst_ref=gates_in.at[move],
            send_sem=gates_send.at[move],
            recv_sem=gates_recv.at[move],
            device_id=mate(move),
        )

    def back_rows(move):
        return back.at[:, pl.ds(move * double, double), :]

    def back_copy(move):
        return pltpu.make_async_remote_copy(
            src_ref=outgoing.at[move - 1],
            dst_ref=back_rows(move),
            send_sem=back_send.at[move],
            recv_sem=back_recv.at[move],
            device_id=mate(move),
        )

    def dots_copy(move):
        return pltpu.make_async_remote_copy(
            src_ref=dots_out.at[move],
            dst_ref=dots_in.at[move],
            send_sem=dots_send.at[move],
            recv_sem=dots_recv.at[move],
            device_id=mate(move),
        )

    for move in order:
        gates_copy(move).start()
        if not crossed or move < 3:
            for copy in halves_of(rows_piece, move):
                copy.start()
    gates_in[0] = gates_out[0]
    for load in loads:
        load.wait()
    if crossed:
        gather.step(1)

    def mates_rows():
        for distance in range(3, chips):
            gather.step(distance)
        gather.landed()
        pair_load(routed_mates, 0).start()

        @pl.loop(0, pairs)
        def _(pair):
            pair_load(routed_mates, pair).wait()

            @pl.when(pair + 1 < pairs)
            def _():
                pair_load(routed_mates, pair + 1).start()

            for index, cols in enumerate((lower, upper)):
                made = jnp.dot(
                    mate_onehot_ref[pair, index],
                    pair_rows[lax.rem(pair, slots), :, cols],
                    preferred_element_type=f32,
                ).astype(half)
                arrived[index + 1, pair, :, cols] = made[0:double]
                outgoing[2, pair, :, cols] = made[double:]

        for copy in halves_of(rows_piece, 3):
            copy.start()
        gather.sent()

    cols_step = min(256, hidden_width)
    width_step = min(512, model_width)
    spread = (lax.broadcasted_iota(jnp.int32, (8, 128), 0) == 0).astype(f32)
    for move in [0] + order:
        if move:
            gates_copy(move).wait()
            for copy in halves_of(rows_piece, move) + halves_of(upstream_piece, move):
                copy.wait()
        for pair in range(pairs):
            scales[pair * double : (pair + 1) * double, :] = column_of(
                gates_in[move, pair], spread
            )
        dots_out[move] = jnp.zeros_like(dots_out[move])

        @pl.loop(0, hidden_width // cols_step)
        def _(index):
            cols = pl.ds(pl.multiple_of(index * cols_step, cols_step), cols_step)
            rows = arrived[move].reshape(rows_of, model_width)
            pre = jnp.dot(rows, gate_full[:, cols], preferred_element_type=f32)
            up = jnp.dot(rows, up_full[:, cols], preferred_element_type=f32)
            plain = lax.dot_general(
                upstream[move].reshape(rows_of, model_width),
                down_full[cols, :],
                (((1,), (1,)), ((), ())),
                preferred_element_type=f32,
            )
            sigmoid = 1.0 / (1.0 + jnp.exp(-pre))
            active = pre * sigmoid
            made = (active * up).astype(half)
            weighted = made.astype(f32) * scales[:, 0:1]
            hidden[move, :, :, cols] = weighted.astype(half).reshape(pairs, double, cols_step)
            dots = made.astype(f32) * plain
            for pair in range(pairs):
                dots_out[move, pair] += row_sums(
                    dots[pair * double : (pair + 1) * double], jnp.ones((8, cols_step), f32)
                )
            scaled = plain * scales[:, 0:1]
            gate_back = scaled * up * sigmoid * (1.0 + pre * (1.0 - sigmoid))
            gate_grad[move, :, :, cols] = gate_back.astype(half).reshape(pairs, double, cols_step)
            up_grad[move, :, :, cols] = (
                (scaled * active).astype(half).reshape(pairs, double, cols_step)
            )

        if move:
            dots_copy(move).start()
        else:
            dots_in[0] = dots_out[0]
            if crossed and chips > 2:
                gather.step(2)

        @pl.loop(0, model_width // width_step)
        def _(index):
            cols = pl.ds(pl.multiple_of(index * width_step, width_step), width_step)
            rows_grad = lax.dot_general(
                gate_grad[move].reshape(rows_of, hidden_width),
                gate_full[cols, :],
                (((1,), (1,)), ((), ())),
                preferred_element_type=f32,
            )
            rows_grad = rows_grad + lax.dot_general(
                up_grad[move].reshape(rows_of, hidden_width),
                up_full[cols, :],
                (((1,), (1,)), ((), ())),
                preferred_element_type=f32,
            )
            rows_grad = rows_grad.astype(half).reshape(pairs, double, width_step)
            if move:
                outgoing[move - 1, :, :, cols] = rows_grad
            else:
                back[:, 0:double, cols] = rows_grad

        if move:
            back_copy(move).start()
        elif crossed:
            mates_rows()

    own_rows = pl.ds(pl.multiple_of(me * tok_rows, tok_rows), tok_rows)
    own_load = pltpu.make_async_copy(
        routed_ref.at[own_rows], pair_rows.at[0, pl.ds(0, tok_rows)], pair_sem.at[0]
    )
    own_load.start()
    hidden_keep = pltpu.make_async_copy(hidden, hidden_out, keep_sem)
    hidden_keep.start()

    total_rows = experts_local * rows_of

    def flat(ref, cols):
        return ref[:, :, :, cols].reshape(total_rows, -1)

    every = pl.ds(0, hidden_width)

    @pl.loop(0, split)
    def _(piece):
        cols = pl.ds(pl.multiple_of(piece * part, part), part)
        gate_full[cols, :] = turned_dot(flat(arrived, cols), flat(gate_grad, every)).astype(half)
        up_full[cols, :] = turned_dot(flat(arrived, cols), flat(up_grad, every)).astype(half)
        down_full[:, cols] = turned_dot(flat(hidden, every), flat(upstream, cols)).astype(half)

    grad_keeps = [
        pltpu.make_async_copy(source, target, load_sem.at[index])
        for index, (source, target) in enumerate(
            ((gate_full, grad_gate_ref), (up_full, grad_up_ref))
        )
    ]
    for keep in grad_keeps:
        keep.start()
    down_send_all = ShardSend(
        split,
        lambda dest: down_full.at[:, pl.ds(pl.multiple_of(dest * part, part), part)],
        down_landing,
        load_sem.at[2],
        down_send,
        down_recv,
    )

    for move in order:
        dots_copy(move).wait()
    token_out[...] = jnp.zeros_like(token_out)

    @pl.loop(0, pairs)
    def _(pair):
        for move in range(experts_local):
            found = jnp.dot(
                dots_in[move, pair],
                onehot_ref[pair, pl.ds(move * double, double), :].astype(f32),
                precision=HIGHEST,
                preferred_element_type=f32,
            )
            row = partner_of(member, move)
            for side in range(2):
                token_out[pair * 2 + side, pl.ds(row, 1), :] = found[
                    0:1, side * tok_rows : (side + 1) * tok_rows
                ]

    def token_copy(shift):
        peer = lax.rem(me + shift, size)
        return pltpu.make_async_remote_copy(
            src_ref=token_out.at[peer],
            dst_ref=token_in.at[me],
            send_sem=token_send.at[shift],
            recv_sem=token_recv.at[shift],
            device_id={"seq": peer},
        )

    for shift in range(1, size):
        token_copy(shift).start()
    token_in[me] = token_out[me]
    for move in order:
        back_copy(move).wait()
    down_send_all.start()

    reduce = ChainReduce(chips, residual_grad_ref, reduce_buffers)

    def product(index, store):
        side = pl.ds(pl.multiple_of(lax.rem(index, 2) * tok_rows, tok_rows), tok_rows)
        left = onehot_ref[index // 2, :, side]

        @pl.loop(0, model_width // width_step)
        def _(step):
            cols = pl.ds(pl.multiple_of(step * width_step, width_step), width_step)
            store(cols, turned_dot(left, back[index // 2, :, cols]))

    reduce.run(product)

    for shift in range(1, size):
        token_copy(shift).wait()
    own_gates = gates[me]
    grads = token_in[...].reshape(padded, tok_rows)
    mean = jnp.sum(own_gates * grads, 0, keepdims=True)
    logit_grad = (own_gates * (grads - mean)).astype(half)
    routed_grad = reduce.total[...] + turned_dot(logit_grad, router_ref[...])
    own_load.wait()
    router_grad = jnp.dot(logit_grad, pair_rows[0, 0:tok_rows, :], preferred_element_type=f32)
    for device in range(size):
        router_grad_ref[device * experts_local : (device + 1) * experts_local, :] = router_grad[
            device * 8 : device * 8 + experts_local
        ]
    residual = residual_ref[...]
    inverse = lax.rsqrt(jnp.mean(residual * residual, -1, keepdims=True) + EPSILON)
    unit = residual * inverse
    gain_ref[...] = jnp.broadcast_to(
        jnp.sum(routed_grad * unit, 0, keepdims=True), gain_ref.shape
    )
    routed_grad = routed_grad * gains_ref[1:2, :]
    routed_grad = inverse * (
        routed_grad - unit * jnp.mean(routed_grad * unit, -1, keepdims=True)
    )
    residual_grad = cotangent_ref[...].astype(f32) + routed_grad
    residual_grad_ref[...] = residual_grad
    out_grad_ref[...] = residual_grad.astype(half)
    reduce.sent()
    hidden_keep.wait()
    for keep in grad_keeps:
        keep.wait()
    down_send_all.wait()


def experts(
    sizes,
    routed_seq,
    routed_cross,
    choices,
    onehot,
    mate_onehot,
    placed,
    router_rows,
    gain_rows,
    residual,
    cotangent,
    weights,
    which,
):
    size, split, chips, experts_local = sizes
    gate_full, up_full, down_full = weights
    model_width, hidden_width = gate_full.shape
    tok_rows = residual.shape[0]
    pairs, double = size // 2, 2 * CAP
    f32, half = jnp.float32, jnp.bfloat16
    vmem = pl.BlockSpec(memory_space=pltpu.VMEM)
    anywhere = pl.BlockSpec(memory_space=pl.ANY)
    kind = pltpu.SemaphoreType.DMA
    shape = jax.ShapeDtypeStruct
    few = kind((experts_local,))
    crossed = split == experts_local == 4
    wide_rows = (experts_local, pairs, double, model_width)
    narrow_rows = (experts_local, pairs, double, hidden_width)
    flags = (experts_local, pairs, 8, double)
    return pl.pallas_call(
        functools.partial(experts_kernel, sizes),
        out_shape=(
            shape((tok_rows, model_width), f32),
            shape((tok_rows, model_width), half),
            shape((8, model_width), f32),
            shape((size * experts_local, model_width), f32),
            shape(narrow_rows, half),
            shape(gate_full.shape, half),
            shape(up_full.shape, half),
            shape((split, hidden_width, model_width // split), half),
            shape(routed_seq.shape if crossed else (16, model_width), half),
        ),
        in_specs=[anywhere] * 2 + [vmem] * 3 + [anywhere] + [vmem] * 4 + [anywhere] * 3,
        out_specs=tuple([vmem] * 4 + [anywhere] * 5),
        scratch_shapes=[
            pltpu.VMEM(gate_full.shape, half),
            pltpu.VMEM(up_full.shape, half),
            pltpu.VMEM(down_full.shape, half),
            pltpu.VMEM(wide_rows, half),
            pltpu.VMEM((2 if chips < 8 else 1, 2 * tok_rows, model_width), half),
            pltpu.VMEM((max(experts_local - 1, 1), *wide_rows[1:]), half),
            pltpu.VMEM(wide_rows, half),
            pltpu.VMEM(narrow_rows, half),
            pltpu.VMEM(narrow_rows, half),
            pltpu.VMEM(narrow_rows, half),
            pltpu.VMEM((pairs, experts_local * double, model_width), half),
            pltpu.VMEM((size, size * 8, tok_rows), f32),
            pltpu.VMEM(flags, f32),
            pltpu.VMEM(flags, f32),
            pltpu.VMEM(flags, f32),
            pltpu.VMEM(flags, f32),
            pltpu.VMEM((size, 8, tok_rows), f32),
            pltpu.VMEM((size, 8, tok_rows), f32),
            pltpu.VMEM((pairs * double, 128), f32),
            kind((6,)),
            kind((2,)),
            kind,
            kind,
            kind((3, chips)),
            kind((2, chips)),
            few,
            few,
            few,
            few,
            few,
            few,
            few,
            few,
            few,
            few,
            kind((size,)),
            kind((size,)),
            kind((split,)),
            kind((split,)),
            *ChainReduce.scratch(chips, tok_rows, model_width),
        ],
        compiler_params=pltpu.CompilerParams(
            collective_id=which, has_side_effects=True, vmem_limit_bytes=63 * 2**20
        ),
        cost_estimate=pl.CostEstimate(
            flops=2 * experts_local * pairs * double * model_width * hidden_width * 8,
            bytes_accessed=500 * 2**20,
            transcendentals=0,
        ),
    )(
        routed_seq,
        routed_cross,
        choices,
        onehot,
        mate_onehot,
        placed,
        router_rows,
        gain_rows,
        residual,
        cotangent,
        gate_full,
        up_full,
        down_full,
    )

def back_kernel(
    sizes,
    out_grad_ref,
    gains_ref,
    second_gain_ref,
    seg_row_ref,
    sums_ref,
    *refs,
):
    kept_count = 13
    kept, refs = refs[:kept_count], refs[kept_count:]
    back_body(sizes, out_grad_ref, gains_ref, second_gain_ref, seg_row_ref, sums_ref, kept, *refs)


def back_body(
    sizes,
    out_grad_ref,
    gains_ref,
    second_gain_ref,
    seg_row_ref,
    sums_ref,
    kept,
    normed_ref,
    hidden_ref,
    down_ref,
    grad_gate_ref,
    input_grad_ref,
    gains_out_ref,
    out_w_grad_ref,
    mixed_rows,
    gate_landing,
    qkv_out,
    rows_full_ref,
    attended_ref,
    q_ref,
    k_ref,
    v_ref,
    seg_col_ref,
    log_ref,
    cos_ref,
    sin_ref,
    unit_ref,
    qkv_ref,
    tokens_ref,
    residual_grad_ref,
    down_full,
    out_grads,
    attended_grad,
    hidden,
    returned,
    key_total,
    value_total,
    scaled,
    raw_grads,
    centers_own,
    centers_in,
    qkv_stage,
    out_stage,
    out_landing,
    load_sem,
    gather_local,
    gather_send,
    gather_recv,
    gate_local,
    gate_send,
    gate_recv,
    rows_local,
    rows_send,
    rows_recv,
    centers_send,
    centers_recv,
    kept_sem,
    out_local,
    out_send,
    out_recv,
    *reduce_buffers,
):
    size, split, chips, experts_local = sizes
    f32, half = jnp.float32, jnp.bfloat16
    me, mine = lax.axis_index("seq"), lax.axis_index("fsdp")
    tok_rows, model_width = out_grad_ref.shape
    length, local_width = q_ref.shape
    hidden_width = down_ref.shape[0]
    part = model_width // split
    head = HEAD_DIM
    heads = local_width // head
    double = 2 * CAP
    pairs = size // 2
    rows_of = pairs * double

    down_load = pltpu.make_async_copy(down_ref, down_full, load_sem.at[0])
    hidden_load = pltpu.make_async_copy(hidden_ref, hidden, load_sem.at[1])
    down_load.start()
    hidden_load.start()
    targets = (
        rows_full_ref,
        attended_ref,
        q_ref,
        k_ref,
        v_ref,
        seg_col_ref,
        log_ref,
        cos_ref,
        sin_ref,
        unit_ref,
        qkv_ref,
        tokens_ref,
        residual_grad_ref,
    )
    kept_loads = [
        pltpu.make_async_copy(source, target, kept_sem.at[index])
        for index, (source, target) in enumerate(zip(kept, targets))
    ]
    greet_all(size, split)
    gather = ChainGather(chips, out_grad_ref, out_grads, gather_local, gather_send, gather_recv)
    gather.start()
    gate_send_all = ShardSend(
        split,
        lambda dest: grad_gate_ref.at[pl.ds(pl.multiple_of(dest * part, part), part)],
        gate_landing,
        gate_local,
        gate_send,
        gate_recv,
    )

    gate_send_all.start()
    for load in kept_loads:
        load.start()

    down_load.wait()
    hidden_load.wait()
    width_step = min(512, model_width)

    def rows_target(move):
        return mixed_rows.at[:, pl.ds(move * double, double), :]

    def rows_copy(move):
        return pltpu.make_async_remote_copy(
            src_ref=returned.at[move],
            dst_ref=rows_target(move),
            send_sem=rows_send.at[move],
            recv_sem=rows_recv.at[move],
            device_id={"fsdp": partner_of(mine, move)},
        )

    own_rows = pltpu.make_async_copy(returned.at[0], rows_target(0), rows_local)
    for move in range(experts_local - 1, -1, -1):

        @pl.loop(0, model_width // width_step)
        def _(index):
            cols = pl.ds(pl.multiple_of(index * width_step, width_step), width_step)
            made = jnp.dot(
                hidden[move].reshape(rows_of, hidden_width),
                down_full[:, cols],
                preferred_element_type=f32,
            )
            returned[move, :, :, cols] = made.astype(half).reshape(pairs, double, width_step)

        if move:
            rows_copy(move).start()
    own_rows.start()
    gather.steps()
    for load in kept_loads:
        load.wait()
    gather.landed()

    block = min(512, length)

    @pl.loop(0, length // block)
    def _(step):
        rows = pl.ds(pl.multiple_of(step * block, block), block)
        total = cross_dot(out_grads[rows, 0:part], rows_full_ref[0])
        for piece in range(1, split):
            total += cross_dot(
                out_grads[rows, piece * part : (piece + 1) * part], rows_full_ref[piece]
            )
        attended_grad[rows, :] = total.astype(half)

    @pl.loop(0, split)
    def _(piece):
        cols = pl.ds(pl.multiple_of(piece * part, part), part)
        out_stage[piece] = turned_dot(attended_ref[...], out_grads[:, cols]).astype(half)

    out_send_all = ShardSend(
        split, lambda dest: out_stage.at[dest], out_landing, out_local, out_send, out_recv
    )
    out_send_all.start()
    gather.sent()
    normed_load = pltpu.make_async_copy(normed_ref, out_grads, load_sem.at[0])
    normed_load.start()

    wide = min(256, length) if length <= 1024 else 128
    scale = head**-0.5
    segments = seg_row_ref[...].astype(f32)
    for number in range(heads):
        cols = slice(number * head, (number + 1) * head)
        key_total[...] = jnp.zeros_like(key_total)
        value_total[...] = jnp.zeros_like(value_total)

        @pl.loop(0, length // wide)
        def _(step):
            rows = pl.ds(pl.multiple_of(step * wide, wide), wide)
            scores = cross_dot(q_ref[rows, cols], k_ref[:, cols]) * scale
            scores = jnp.where(seg_col_ref[rows, 0:1] == segments, scores, MASKED)
            probs = jnp.exp(scores - log_ref[rows, cols][:, 0:1])
            grads = attended_grad[rows, cols]
            prob_grad = cross_dot(grads, v_ref[:, cols])
            center = jnp.sum(probs * prob_grad, -1, keepdims=True)
            score_grad = (probs * (prob_grad - center)).astype(half)
            query_grad = jnp.dot(score_grad, k_ref[:, cols], preferred_element_type=f32) * scale
            raw_grads[0, rows, cols] = query_grad.astype(half)
            key_total[...] += turned_dot(score_grad, q_ref[rows, cols])
            value_total[...] += turned_dot(probs.astype(half), grads)

        raw_grads[1, :, cols] = (key_total[...] * scale).astype(half)
        raw_grads[2, :, cols] = value_total[...].astype(half)

    lanes = lax.broadcasted_iota(jnp.int32, (8, local_width), 0)
    first_row, second_row = (lanes == 0).astype(f32), (lanes == 1).astype(f32)
    gains_out_ref[...] = jnp.zeros_like(gains_out_ref)
    own_cols = pl.ds(pl.multiple_of(me * local_width, local_width), local_width)
    gains_out_ref[1:2, :] = second_gain_ref[0:1, :]

    @pl.loop(0, length // block)
    def _(step):
        rows = pl.ds(pl.multiple_of(step * block, block), block)
        found = jnp.zeros((8, block), f32)
        for index, pick in ((0, first_row), (1, second_row)):
            unit = unit_ref[index, rows, :]
            pieces = []
            for number in range(heads):
                cols = slice(number * head, (number + 1) * head)
                piece = raw_grads[index, rows, cols].astype(f32)
                pieces.append(piece * cos_ref[rows, :] - turned_halves(piece) * sin_ref[rows, :])
            unit_grad = pieces[0] if heads == 1 else jnp.concatenate(pieces, 1)
            gains_out_ref[2 + index : 3 + index, own_cols] += jnp.sum(
                unit_grad * unit, 0, keepdims=True
            )
            grown = unit_grad * gains_ref[2 + index : 3 + index, own_cols]
            scaled[index, rows, :] = grown
            found += row_sums(grown * unit, pick)
        centers_own[:, rows] = found

    def centers_copy(shift):
        return pltpu.make_async_remote_copy(
            src_ref=centers_own,
            dst_ref=centers_in.at[me],
            send_sem=centers_send.at[shift],
            recv_sem=centers_recv.at[shift],
            device_id={"seq": lax.rem(me + shift, size)},
        )

    for shift in range(1, size):
        centers_copy(shift).start()
    centers_in[me] = centers_own[...]
    for shift in range(1, size):
        centers_copy(shift).wait()
    centers_own[...] = jnp.sum(centers_in[...], 0) * (1.0 / model_width)

    @pl.loop(0, length // block)
    def _(step):
        rows = pl.ds(pl.multiple_of(step * block, block), block)
        for index, pick in ((0, first_row), (1, second_row)):
            inverse = lax.rsqrt(column_of(sums_ref[:, rows], pick) / model_width + EPSILON)
            center = column_of(centers_own[:, rows], pick)
            raw_grads[index, rows, :] = (
                inverse * (scaled[index, rows, :] - unit_ref[index, rows, :] * center)
            ).astype(half)

    reduce = ChainReduce(chips, input_grad_ref, reduce_buffers)

    def product(index, store):
        rows = pl.ds(pl.multiple_of(index * tok_rows, tok_rows), tok_rows)

        @pl.loop(0, model_width // width_step)
        def _(step):
            cols = pl.ds(pl.multiple_of(step * width_step, width_step), width_step)
            total = cross_dot(raw_grads[0, rows, :], qkv_ref[0, cols, :])
            total += cross_dot(raw_grads[1, rows, :], qkv_ref[1, cols, :])
            total += cross_dot(raw_grads[2, rows, :], qkv_ref[2, cols, :])
            store(cols, total)

    qkv_keep = pltpu.make_async_copy(qkv_stage, qkv_out, load_sem.at[1])

    def between():
        normed_load.wait()

        @pl.loop(0, split)
        def _(piece):
            cols = pl.ds(pl.multiple_of(piece * part, part), part)
            left = out_grads[:, cols]
            for index in range(3):
                qkv_stage[piece, index] = turned_dot(left, raw_grads[index]).astype(half)

        qkv_keep.start()

    reduce.run(product, between)

    inputs = tokens_ref[...].astype(f32)
    inverse = lax.rsqrt(jnp.mean(inputs * inputs, -1, keepdims=True) + EPSILON)
    unit = inputs * inverse
    grads = input_grad_ref[...]
    gains_out_ref[0:1, :] = jnp.sum(grads * unit, 0, keepdims=True)
    grads = grads * gains_ref[0:1, :]
    input_grad_ref[...] = residual_grad_ref[...] + inverse * (
        grads - unit * jnp.mean(grads * unit, -1, keepdims=True)
    )

    out_send_all.wait()
    total = out_landing[0].astype(f32)
    for index in range(1, split):
        total += out_landing[index].astype(f32)
    out_w_grad_ref[...] = total
    qkv_keep.wait()
    reduce.sent()
    own_rows.wait()
    for move in range(1, experts_local):
        rows_copy(move).wait()
    gate_send_all.wait()


def back(sizes, out_grad, small, kept, big_ones, which):
    size, split, chips, experts_local = sizes
    f32, half = jnp.float32, jnp.bfloat16
    tok_rows, model_width = out_grad.shape
    length, local_width = kept[1].shape
    normed_seq, hidden, down_full, grad_gate = big_ones
    hidden_width = down_full.shape[0]
    part = model_width // split
    vmem = pl.BlockSpec(memory_space=pltpu.VMEM)
    anywhere = pl.BlockSpec(memory_space=pl.ANY)
    kind = pltpu.SemaphoreType.DMA
    shape = jax.ShapeDtypeStruct
    few, fsdp = kind((experts_local,)), kind((split,))
    return pl.pallas_call(
        functools.partial(back_kernel, sizes),
        out_shape=(
            shape((tok_rows, model_width), f32),
            shape((8, model_width), f32),
            shape((local_width, part), f32),
            shape((size // 2, experts_local * 2 * CAP, model_width), half),
            shape((split, part, hidden_width), half),
            shape((split, 3, part, local_width), half),
        ),
        in_specs=[vmem] * 5 + [anywhere] * (len(kept) + 4),
        out_specs=tuple([vmem] * 3 + [anywhere] * 3),
        scratch_shapes=[
            *[pltpu.VMEM(one.shape, one.dtype) for one in kept],
            pltpu.VMEM(down_full.shape, half),
            pltpu.VMEM((length, model_width), half),
            pltpu.VMEM((length, local_width), half),
            pltpu.VMEM(hidden.shape, half),
            pltpu.VMEM((experts_local, size // 2, 2 * CAP, model_width), half),
            pltpu.VMEM((length, HEAD_DIM), f32),
            pltpu.VMEM((length, HEAD_DIM), f32),
            pltpu.VMEM((2, length, local_width), f32),
            pltpu.VMEM((3, length, local_width), half),
            pltpu.VMEM((8, length), f32),
            pltpu.VMEM((size, 8, length), f32),
            pltpu.VMEM((split, 3, part, local_width), half),
            pltpu.VMEM((split, local_width, part), half),
            pltpu.VMEM((split, local_width, part), half),
            kind((2,)),
            kind,
            kind((3, chips)),
            kind((2, chips)),
            kind,
            fsdp,
            fsdp,
            kind,
            few,
            few,
            kind((size,)),
            kind((size,)),
            kind((len(kept),)),
            kind,
            fsdp,
            fsdp,
            *ChainReduce.scratch(chips, tok_rows, model_width),
        ],
        compiler_params=pltpu.CompilerParams(
            collective_id=which, has_side_effects=True, vmem_limit_bytes=63 * 2**20
        ),
        cost_estimate=pl.CostEstimate(
            flops=2 * length * model_width * local_width * 8,
            bytes_accessed=500 * 2**20,
            transcendentals=0,
        ),
    )(out_grad, *small, *kept, *big_ones)


def close_kernel(
    sizes,
    onehot_ref,
    gains_ref,
    router_ref,
    mixed_rows_any,
    residual_any,
    qkv_any,
    grad_up_ref,
    output_ref,
    gains_out_ref,
    router_out_ref,
    query_w_grad_ref,
    key_w_grad_ref,
    value_w_grad_ref,
    up_landing,
    mixed_rows_ref,
    residual_ref,
    qkv_ref,
    qkv_in,
    qkv_sum,
    load_sem,
    qkv_send,
    qkv_recv,
    total,
    small,
    first,
    second,
    final,
    up_local,
    up_send,
    up_recv,
    send_one,
    recv_one,
    send_two,
    recv_two,
    send_three,
    recv_three,
    *reduce_buffers,
):
    size, split, chips, experts_local = sizes
    f32 = jnp.float32
    me, mine = lax.axis_index("seq"), lax.axis_index("fsdp")
    tok_rows, model_width = residual_ref.shape
    part = model_width // split
    slice_width = model_width // size
    experts_all = router_ref.shape[0]
    loads = [
        pltpu.make_async_copy(source, target, load_sem.at[index])
        for index, (source, target) in enumerate(
            ((qkv_any, qkv_ref), (mixed_rows_any, mixed_rows_ref), (residual_any, residual_ref))
        )
    ]
    for load in loads:
        load.start()
    small[0:8, :] = gains_ref[...]
    small[8 : 8 + experts_all, :] = router_ref[...]
    greet_all(size, split)
    up_send_all = ShardSend(
        split,
        lambda dest: grad_up_ref.at[pl.ds(pl.multiple_of(dest * part, part), part)],
        up_landing,
        up_local,
        up_send,
        up_recv,
    )
    loads[0].wait()

    half_part = qkv_ref.shape[2] // 2
    lower, upper = pl.ds(0, half_part), pl.ds(half_part, half_part)
    mates = (partner_of(mine, 1), partner_of(mine, 2), partner_of(mine, 3)) if split == 4 else ()

    def qkv_copy(index):
        side = index % 2
        rows = (lower, upper)[side]
        if index < 4:
            dest = mates[side] if index < 2 else mates[2]
            source, mate = qkv_ref.at[dest, :, rows], mates[side]
        else:
            source, mate = qkv_sum.at[side], mates[1 - side]
        return pltpu.make_async_remote_copy(
            src_ref=source,
            dst_ref=qkv_in.at[index],
            send_sem=qkv_send.at[index],
            recv_sem=qkv_recv.at[index],
            device_id={"fsdp": mate},
        )

    def qkv_shift(shift):
        dest = lax.rem(mine + shift, split)
        return pltpu.make_async_remote_copy(
            src_ref=qkv_ref.at[dest],
            dst_ref=qkv_in.at[shift],
            send_sem=qkv_send.at[shift],
            recv_sem=qkv_recv.at[shift],
            device_id={"fsdp": dest},
        )

    if split == 4:
        for index in range(4):
            qkv_copy(index).start()
    else:
        for shift in range(1, split):
            qkv_shift(shift).start()
    up_send_all.start()

    def columns(index):
        return pl.ds(pl.multiple_of(index * slice_width, slice_width), slice_width)

    def scatter(shift):
        peer = lax.rem(me + shift, size)
        return pltpu.make_async_remote_copy(
            src_ref=small.at[:, columns(peer)],
            dst_ref=first.at[me],
            send_sem=send_one.at[shift],
            recv_sem=recv_one.at[shift],
            device_id={"seq": peer},
        )

    def share(shift):
        return pltpu.make_async_remote_copy(
            src_ref=second.at[mine],
            dst_ref=second.at[mine],
            send_sem=send_two.at[shift],
            recv_sem=recv_two.at[shift],
            device_id={"fsdp": lax.rem(mine + shift, split)},
        )

    def collect(shift):
        return pltpu.make_async_remote_copy(
            src_ref=final.at[me],
            dst_ref=final.at[me],
            send_sem=send_three.at[shift],
            recv_sem=recv_three.at[shift],
            device_id={"seq": lax.rem(me + shift, size)},
        )

    for shift in range(1, size):
        scatter(shift).start()
    first[me] = small[:, columns(me)]

    reduce = ChainReduce(chips, total, reduce_buffers)
    width_step = min(512, model_width)

    def product(index, store):
        side = pl.ds(pl.multiple_of(lax.rem(index, 2) * tok_rows, tok_rows), tok_rows)
        left = onehot_ref[index // 2, :, side]

        @pl.loop(0, model_width // width_step)
        def _(step):
            cols = pl.ds(pl.multiple_of(step * width_step, width_step), width_step)
            store(cols, turned_dot(left, mixed_rows_ref[index // 2, :, cols]))

    def between():
        for shift in range(1, size):
            scatter(shift).wait_recv()
        second[mine] = jnp.sum(first[...], 0)
        for shift in range(1, split):
            share(shift).start()

    loads[1].wait()
    reduce.run(product, between)
    if split == 4:
        for side in range(2):
            qkv_copy(2 + side).wait_recv()
            rows = (lower, upper)[side]
            qkv_sum[side] = (
                qkv_ref[mates[1 - side], :, rows].astype(f32) + qkv_in[2 + side].astype(f32)
            ).astype(qkv_sum.dtype)
            qkv_copy(4 + side).start()
    loads[2].wait()
    for shift in range(1, split):
        share(shift).wait_recv()
    final[me] = jnp.sum(second[...], 0)
    for shift in range(1, size):
        collect(shift).start()
    output_ref[...] = (residual_ref[...] + total[...]).astype(output_ref.dtype)
    for shift in range(1, size):
        scatter(shift).wait_send()
    for shift in range(1, split):
        share(shift).wait_send()
    for shift in range(1, size):
        collect(shift).wait()
    for index in range(size):
        cols = slice(index * slice_width, (index + 1) * slice_width)
        gains_out_ref[:, cols] = final[index, 0:4]
        router_out_ref[:, cols] = final[index, 8:]
    targets = (query_w_grad_ref, key_w_grad_ref, value_w_grad_ref)
    if split == 4:
        for side in range(2):
            for index in (side, 2 + side, 5 - side):
                copy = qkv_copy(index)
                copy.wait() if index < 2 or index > 3 else copy.wait_send()
        for side in range(2):
            rows = (lower, upper)[side]
            for index, target in enumerate(targets):
                target[rows, :] = (
                    qkv_ref[mine, index, rows].astype(f32)
                    + qkv_in[side, index].astype(f32)
                    + qkv_in[4 + side, index].astype(f32)
                )
    else:
        for shift in range(1, split):
            qkv_shift(shift).wait()
        for index, target in enumerate(targets):
            sums = qkv_ref[mine, index].astype(f32)
            for shift in range(1, split):
                sums += qkv_in[shift, index].astype(f32)
            target[...] = sums
    reduce.sent()
    up_send_all.wait()


def close(sizes, onehot, gains, router_grad, mixed_rows, residual, qkv_parts, grad_up, which):
    size, split, chips, experts_local = sizes
    f32, half = jnp.float32, jnp.bfloat16
    tok_rows, model_width = residual.shape
    hidden_width = grad_up.shape[1]
    part, slice_width = model_width // split, model_width // size
    rows = 8 + router_grad.shape[0]
    vmem = pl.BlockSpec(memory_space=pltpu.VMEM)
    anywhere = pl.BlockSpec(memory_space=pl.ANY)
    kind = pltpu.SemaphoreType.DMA
    shape = jax.ShapeDtypeStruct
    seq, fsdp = kind((size,)), kind((split,))
    share = qkv_parts.shape[2:]
    return pl.pallas_call(
        functools.partial(close_kernel, sizes),
        out_shape=(
            shape((tok_rows, model_width), half),
            shape((4, model_width), f32),
            shape(router_grad.shape, f32),
            shape(share, f32),
            shape(share, f32),
            shape(share, f32),
            shape((split, part, hidden_width), half),
        ),
        in_specs=[vmem] * 3 + [anywhere] * 4,
        out_specs=tuple([vmem] * 6 + [anywhere]),
        scratch_shapes=[
            pltpu.VMEM(mixed_rows.shape, half),
            pltpu.VMEM(residual.shape, f32),
            pltpu.VMEM(qkv_parts.shape, half),
            pltpu.VMEM((6, 3, share[0] // 2, share[1]) if split == 4 else qkv_parts.shape, half),
            pltpu.VMEM((2, 3, share[0] // 2, share[1]), half),
            kind((3,)),
            kind((max(6, split),)),
            kind((max(6, split),)),
            pltpu.VMEM((tok_rows, model_width), f32),
            pltpu.VMEM((rows, model_width), f32),
            pltpu.VMEM((size, rows, slice_width), f32),
            pltpu.VMEM((split, rows, slice_width), f32),
            pltpu.VMEM((size, rows, slice_width), f32),
            kind,
            fsdp,
            fsdp,
            seq,
            seq,
            fsdp,
            fsdp,
            seq,
            seq,
            *ChainReduce.scratch(chips, tok_rows, model_width),
        ],
        compiler_params=pltpu.CompilerParams(
            collective_id=which, has_side_effects=True, vmem_limit_bytes=56 * 2**20
        ),
    )(onehot, gains, router_grad, mixed_rows, residual, qkv_parts, grad_up)


def finish_kernel(count, *refs):
    sources, targets = refs[: len(refs) // 2], refs[len(refs) // 2 :]
    for source, target in zip(sources[:count], targets[:count]):
        target[...] = source[...]
    for source, target in zip(sources[count:], targets[count:]):
        total = source[0].astype(target.dtype)
        for index in range(1, source.shape[0]):
            total += source[index].astype(target.dtype)
        target[...] = total


def finish(results, landings, experts_local):
    halves = 2
    steps = experts_local * halves
    in_specs, out_specs, shapes = [], [], []
    for one in results:
        rows = one.shape[0] // steps
        spec = pl.BlockSpec((rows, one.shape[1]), lambda step: (step, 0))
        if one.shape[0] % (steps * 16):
            spec = pl.BlockSpec(one.shape, lambda step: (0, 0))
        in_specs.append(spec)
        out_specs.append(spec)
        shapes.append(jax.ShapeDtypeStruct(one.shape, one.dtype))
    grouped = []
    for one in landings:
        groups = one.shape[0] // experts_local
        grouped.append(one.reshape(groups, experts_local, *one.shape[1:]))
        block = (one.shape[1] // halves, one.shape[2])
        in_specs.append(
            pl.BlockSpec(
                (groups, 1, *block), lambda step: (0, step // halves, step % halves, 0)
            )
        )
        out_specs.append(
            pl.BlockSpec((1, *block), lambda step: (step // halves, step % halves, 0))
        )
        shapes.append(jax.ShapeDtypeStruct((experts_local, *one.shape[1:]), jnp.float32))
    return pl.pallas_call(
        functools.partial(finish_kernel, len(results)),
        grid=(steps,),
        in_specs=in_specs,
        out_specs=out_specs,
        out_shape=shapes,
        compiler_params=pltpu.CompilerParams(vmem_limit_bytes=63 * 2**20),
    )(*results, *grouped)


def shards(
    tokens,
    norm_gains,
    w_query,
    w_key,
    w_value,
    w_out,
    w_router,
    w_gate,
    w_up,
    w_down,
    segment_ids,
    expert_ids,
    expert_slots,
    cotangent,
):
    half_type = jnp.bfloat16
    model_width = tokens.shape[1]
    experts_local = w_gate.shape[0]
    seq_size = lax.axis_size("seq")
    split = lax.axis_size("fsdp")
    length = seq_size * tokens.shape[0]
    sizes = (seq_size, split, seq_size // 2, experts_local)
    cosine_wide, sine_wide = rope_tables(length, HEAD_DIM)
    segment_row = segment_ids.reshape(1, -1)
    (
        normed_seq,
        qkv_stack,
        out_stack,
        query_heads,
        key_heads,
        value_heads,
        unit_pair,
        log_wide,
        attended_heads,
        square_sums,
        residual,
        gain_rows,
        segment_cols,
        routed_seq,
        routed_cross,
        placed,
        gate_full,
        up_full,
        down_full,
        choices,
        onehot,
        mate_onehot,
    ) = front(
        sizes,
        tokens,
        norm_gains,
        cosine_wide,
        sine_wide,
        segment_row,
        expert_ids,
        expert_slots,
        cotangent,
        (w_query, w_key, w_value, w_out, w_gate, w_up, w_down),
        0,
    )
    router_rows = jnp.zeros((seq_size, 8, model_width), half_type)
    router_rows = router_rows.at[:, :experts_local].set(
        w_router.T.reshape(seq_size, experts_local, model_width)
    )
    router_rows = router_rows.reshape(seq_size * 8, model_width)
    (
        residual_grad,
        out_grad,
        gain_second_grad,
        router_grad,
        hidden,
        grad_gate_full,
        grad_up_full,
        down_landing,
        _,
    ) = experts(
        sizes,
        routed_seq,
        routed_cross,
        choices,
        onehot,
        mate_onehot,
        placed,
        router_rows,
        gain_rows,
        residual,
        cotangent,
        (gate_full, up_full, down_full),
        1,
    )
    input_grad, gain_grads, out_owned, mixed_rows, gate_landing, qkv_parts = back(
        sizes,
        out_grad,
        (gain_rows, gain_second_grad, segment_row, square_sums),
        (
            out_stack,
            attended_heads,
            query_heads,
            key_heads,
            value_heads,
            segment_cols,
            log_wide,
            cosine_wide,
            sine_wide,
            unit_pair,
            qkv_stack,
            tokens,
            residual_grad,
        ),
        (normed_seq, hidden, down_full, grad_gate_full),
        2,
    )
    output, gain_sums, router_sums, query_owned, key_owned, value_owned, up_landing = close(
        sizes, onehot, gain_grads, router_grad, mixed_rows, residual, qkv_parts, grad_up_full, 3
    )
    (
        output,
        input_grad,
        gain_sums,
        query_owned,
        key_owned,
        value_owned,
        out_owned,
        router_sums,
        gate_owned,
        up_owned,
        down_owned,
    ) = finish(
        (
            output,
            input_grad,
            gain_sums,
            query_owned,
            key_owned,
            value_owned,
            out_owned,
            router_sums,
        ),
        (gate_landing, up_landing, down_landing),
        experts_local,
    )
    return (
        output,
        input_grad,
        gain_sums,
        query_owned,
        key_owned,
        value_owned,
        out_owned,
        router_sums.T,
        gate_owned,
        up_owned,
        down_owned,
    )


def solution(mesh):
    in_specs = (
        P(("fsdp", "seq"), None),
        P(),
        P("fsdp", "seq"),
        P("fsdp", "seq"),
        P("fsdp", "seq"),
        P("seq", "fsdp"),
        P(),
        P("seq", "fsdp", None),
        P("seq", "fsdp", None),
        P("seq", None, "fsdp"),
        P("fsdp"),
        P(("fsdp", "seq"), None),
        P(("fsdp", "seq"), None),
        P(("fsdp", "seq"), None),
    )
    out_specs = (
        P(("fsdp", "seq"), None),
        P(("fsdp", "seq"), None),
        P(),
        P("fsdp", "seq"),
        P("fsdp", "seq"),
        P("fsdp", "seq"),
        P("seq", "fsdp"),
        P(),
        P("seq", "fsdp", None),
        P("seq", "fsdp", None),
        P("seq", None, "fsdp"),
    )
    return jax.shard_map(shards, mesh=mesh, in_specs=in_specs, out_specs=out_specs, check_vma=False)
```

```python
import functools

import jax
import jax.numpy as jnp
import numpy as np
from jax import lax
from jax.experimental import pallas as pl
from jax.experimental.pallas import tpu as pltpu
from jax.sharding import PartitionSpec as P

HEAD_DIM = 128
CAP = 40


EPSILON = 1e-06
THETA = 10000.0
MASKED = -1e30
HIGHEST = lax.Precision.HIGHEST


def rope_tables(length, head_size):
    half_dim = head_size // 2
    frequency = THETA ** (-np.arange(half_dim, dtype=np.float64) / half_dim)
    angles = np.arange(length, dtype=np.float64)[:, None] * frequency.astype(np.float32)
    cosine, sine = np.cos(angles), np.sin(angles)
    return (
        jnp.asarray(np.concatenate([cosine, cosine], 1), jnp.float32),
        jnp.asarray(np.concatenate([-sine, sine], 1), jnp.float32),
    )


class ChainGather:
    def __init__(self, chips, x_ref, out_ref, local_sem, sends, arrivals):
        self.chips, self.x_ref, self.out_ref = chips, x_ref, out_ref
        self.local_sem, self.sends, self.arrivals = local_sem, sends, arrivals
        me = lax.axis_index("seq")
        self.chip, self.core = me // 2, lax.rem(me, 2)
        self.rows = x_ref.shape[0]

    def block(self, source, core):
        start = pl.multiple_of((source * 2 + core) * self.rows, self.rows)
        return self.out_ref.at[pl.ds(start, self.rows)]

    def hop(self, source, ref, target, way, lane):
        return pltpu.make_async_remote_copy(
            src_ref=ref,
            dst_ref=self.block(source, self.core),
            send_sem=self.sends.at[way, source],
            recv_sem=self.arrivals.at[lane, source],
            device_id={"seq": target},
        )

    def upward(self, source, ref):
        return self.hop(source, ref, self.chip * 2 + 2 + self.core, 0, 0)

    def downward(self, source, ref):
        return self.hop(source, ref, self.chip * 2 - 2 + self.core, 1, 0)

    def sideways(self, source, ref):
        return self.hop(source, ref, self.chip * 2 + 1 - self.core, 2, 1)

    def own(self):
        return pltpu.make_async_copy(
            self.x_ref, self.block(self.chip, self.core), self.local_sem
        )

    def start(self):
        @pl.when(self.chip < self.chips - 1)
        def _():
            self.upward(self.chip, self.x_ref).start()

        @pl.when(self.chip > 0)
        def _():
            self.downward(self.chip, self.x_ref).start()

        self.sideways(self.chip, self.x_ref).start()
        self.own().start()

    def step(self, distance):
        below, above = self.chip - distance, self.chip + distance

        @pl.when(below >= 0)
        def _():
            landed = self.block(below, self.core)
            self.upward(below, landed).wait_recv()

            @pl.when(self.chip < self.chips - 1)
            def _():
                self.upward(below, landed).start()

            self.sideways(below, landed).start()

        @pl.when(above < self.chips)
        def _():
            landed = self.block(above, self.core)
            self.downward(above, landed).wait_recv()

            @pl.when(self.chip > 0)
            def _():
                self.downward(above, landed).start()

            self.sideways(above, landed).start()

    def steps(self):
        for distance in range(1, self.chips):
            self.step(distance)

    def landed(self):
        self.own().wait()
        for source in range(self.chips):
            self.sideways(source, self.block(source, self.core)).wait_recv()

    def sent(self):
        for source in range(self.chips):
            ref = self.block(source, self.core)
            self.sideways(source, ref).wait_send()

            @pl.when((self.chip < self.chips - 1) & (source <= self.chip))
            def _():
                self.upward(source, ref).wait_send()

            @pl.when((self.chip > 0) & (source >= self.chip))
            def _():
                self.downward(source, ref).wait_send()


class ChainReduce:
    def __init__(self, chips, total, buffers):
        self.total = total
        (
            self.side_out,
            self.side_in,
            self.chain_in,
            self.side_send,
            self.side_recv,
            self.chain_send,
            self.chain_recv,
        ) = buffers
        self.chips = chips
        me = lax.axis_index("seq")
        self.chip, self.core = me // 2, lax.rem(me, 2)

    @staticmethod
    def scratch(chips, rows, width):
        half = jnp.bfloat16
        return [
            pltpu.VMEM((chips, rows, width), half),
            pltpu.VMEM((chips, rows, width), half),
            pltpu.VMEM((chips + 1, rows, width), half),
            pltpu.SemaphoreType.DMA((chips,)),
            pltpu.SemaphoreType.DMA((chips,)),
            pltpu.SemaphoreType.DMA((chips,)),
            pltpu.SemaphoreType.DMA((2, chips)),
        ]

    def side_copy(self, dest):
        return pltpu.make_async_remote_copy(
            src_ref=self.side_out.at[dest],
            dst_ref=self.side_in.at[dest],
            send_sem=self.side_send.at[dest],
            recv_sem=self.side_recv.at[dest],
            device_id={"seq": self.chip * 2 + 1 - self.core},
        )

    def chain_copy(self, way, dest, target):
        return pltpu.make_async_remote_copy(
            src_ref=self.side_out.at[dest],
            dst_ref=self.chain_in.at[self.slot(way, dest, target // 2)],
            send_sem=self.chain_send.at[dest],
            recv_sem=self.chain_recv.at[way, dest],
            device_id={"seq": target},
        )

    def slot(self, way, dest, holder):
        return jnp.where(dest == holder, self.chips, dest) if way else dest

    def place(self, index):
        distance = self.chips - 1 - index // 2
        dest = self.chip + (1 - 2 * lax.rem(index, 2)) * distance
        return dest, (dest >= 0) & (dest < self.chips)

    def run(self, product, between=None, hook=None):
        chips, chip, core, total = self.chips, self.chip, self.core, self.total
        sibling = chip * 2 + 1 - core

        @pl.loop(0, 2 * chips - 1)
        def _(index):
            dest, inside = self.place(index)

            @pl.when(inside)
            def _():
                def store(cols, part):
                    self.side_out[dest, :, cols] = part.astype(self.side_out.dtype)

                product(dest * 2 + 1 - core, store)
                self.side_copy(dest).start()

        if between:
            between()

        @pl.loop(0, 2 * chips - 1)
        def _(index):
            dest, inside = self.place(index)
            if hook:
                hook(index)

            @pl.when(inside)
            def _():
                def store(cols, part):
                    total[:, cols] = part

                product(dest * 2 + core, store)
                self.side_copy(dest).wait_recv()
                total[...] += self.side_in[dest].astype(jnp.float32)

                @pl.when((dest >= chip) & (chip > 0))
                def _():
                    self.chain_copy(0, dest, sibling).wait_recv()
                    total[...] += self.chain_in[dest].astype(jnp.float32)

                @pl.when((dest <= chip) & (chip < chips - 1))
                def _():
                    self.chain_copy(1, dest, sibling).wait_recv()
                    total[...] += self.chain_in[self.slot(1, dest, chip)].astype(jnp.float32)

                self.side_copy(dest).wait_send()

                @pl.when(dest != chip)
                def _():
                    self.side_out[dest] = total[...].astype(self.side_out.dtype)

                @pl.when(dest > chip)
                def _():
                    self.chain_copy(0, dest, chip * 2 + 2 + core).start()

                @pl.when(dest < chip)
                def _():
                    self.chain_copy(1, dest, chip * 2 - 2 + core).start()

    def sent(self):
        sibling = self.chip * 2 + 1 - self.core

        @pl.loop(0, self.chips)
        def _(dest):
            @pl.when(dest != self.chip)
            def _():
                self.chain_copy(0, dest, sibling).wait_send()


def partner_of(index, move):
    turned, bit = index, 1
    while bit <= move:
        if move // bit % 2:
            turned = turned + bit - 2 * bit * lax.rem(index // bit, 2)
        bit *= 2
    return turned


def greet_all(size, split):
    me, mine = lax.axis_index("seq"), lax.axis_index("fsdp")
    barrier = pltpu.get_barrier_semaphore()
    for shift in range(1, size):
        pl.semaphore_signal(barrier, inc=1, device_id={"seq": lax.rem(me + shift, size)})
    for shift in range(1, split):
        pl.semaphore_signal(barrier, inc=1, device_id={"fsdp": lax.rem(mine + shift, split)})
    pl.semaphore_wait(barrier, size + split - 2)


def turned_halves(head):
    return pltpu.roll(head, head.shape[-1] // 2, 1)


def row_sums(values, pick):
    return lax.dot_general(
        pick, values, (((1,), (1,)), ((), ())), precision=HIGHEST, preferred_element_type=jnp.float32
    )


def column_of(row_form, pick):
    return lax.dot_general(
        row_form, pick, (((0,), (0,)), ((), ())), precision=HIGHEST, preferred_element_type=jnp.float32
    )


def front_kernel(
    sizes,
    tokens_ref,
    gains_in_ref,
    cos_ref,
    sin_ref,
    seg_row_ref,
    ids_ref,
    slots_ref,
    cotangent_ref,
    wq_ref,
    wk_ref,
    wv_ref,
    wo_ref,
    w_gate_ref,
    w_up_ref,
    w_down_ref,
    normed_out,
    qkv_out,
    rows_out,
    q_out,
    k_out,
    v_out,
    unit_out,
    log_out,
    attended_out,
    sums_ref,
    residual_ref,
    gains_ref,
    seg_col_ref,
    routed_out,
    routed_cross,
    placed_out,
    gate_full,
    up_full,
    down_full,
    choices,
    onehot_ref,
    mate_onehot,
    q_ref,
    k_ref,
    v_ref,
    unit_ref,
    log_ref,
    attended_ref,
    normed,
    qkv,
    rows_full,
    routed_own,
    choice_own,
    cotangent_pair,
    cotangent_all,
    mate_choices,
    placed,
    raw,
    sums_own,
    sums_in,
    gather_local,
    gather_send,
    gather_recv,
    sums_send,
    sums_recv,
    choice_send,
    choice_recv,
    mate_send,
    mate_recv,
    cross_local,
    cross_send,
    cross_recv,
    placed_local,
    shard_local,
    shard_send,
    shard_recv,
    expert_local,
    expert_send,
    expert_recv,
    out_sem,
    *reduce_buffers,
):
    size, split, chips, experts_local = sizes
    f32, half = jnp.float32, jnp.bfloat16
    me, mine = lax.axis_index("seq"), lax.axis_index("fsdp")
    tok_rows, model_width = tokens_ref.shape
    length, local_width = q_ref.shape
    part = model_width // split
    head = HEAD_DIM
    heads = local_width // head

    inputs = tokens_ref[...].astype(f32)
    inverse = lax.rsqrt(jnp.mean(inputs * inputs, -1, keepdims=True) + EPSILON)
    gains_ref[...] = gains_in_ref[...].astype(f32)
    routed_half = routed_own.at[pl.ds(0, tok_rows)]
    routed_half[...] = (inputs * inverse * gains_ref[0:1, :]).astype(half)
    crossed = split == experts_local == 4
    half_width = model_width // 2
    x_mate, y_mate = {"fsdp": partner_of(mine, 1)}, {"fsdp": partner_of(mine, 2)}
    greet_all(size, split)

    def gather(index, x_ref, out_ref):
        return ChainGather(
            chips,
            x_ref,
            out_ref,
            gather_local.at[index],
            gather_send.at[index],
            gather_recv.at[index],
        )

    first = gather(0, routed_half, normed)
    first.start()

    cross_rows = pl.ds(tok_rows, tok_rows)
    lower, upper = pl.ds(0, half_width), pl.ds(half_width, half_width)

    def cross_copy(index):
        cols = (lower, upper)[index % 2]
        source, target = (
            (cotangent_ref, cotangent_pair) if index < 2 else (routed_half, routed_own)
        )
        return pltpu.make_async_remote_copy(
            src_ref=source.at[:, cols],
            dst_ref=target.at[cross_rows, cols],
            send_sem=cross_send.at[index],
            recv_sem=cross_recv.at[index],
            device_id=(x_mate, y_mate)[index % 2],
        )

    if crossed:
        cross_own = pltpu.make_async_copy(
            cotangent_ref, cotangent_pair.at[pl.ds(0, tok_rows)], cross_local
        )
        cross_copy(0).start()
        cross_copy(1).start()
        cross_own.start()

    top_count = ids_ref.shape[0]
    ids_row, slots_row = ids_ref[...], slots_ref[...]
    choice_own[0:top_count, :] = ids_row
    choice_own[top_count : 2 * top_count, :] = jnp.where(
        slots_row < CAP, ids_row * CAP + slots_row, -(10**6)
    )

    def choice_copy(shift):
        return pltpu.make_async_remote_copy(
            src_ref=choice_own,
            dst_ref=choices.at[me],
            send_sem=choice_send.at[shift],
            recv_sem=choice_recv.at[shift],
            device_id={"seq": lax.rem(me + shift, size)},
        )

    own_part = pl.ds(pl.multiple_of(mine * part, part), part)
    shard_pairs = (
        (wq_ref, qkv.at[0, own_part]),
        (wk_ref, qkv.at[1, own_part]),
        (wv_ref, qkv.at[2, own_part]),
        (wo_ref, rows_full.at[mine]),
    )

    def shard_copy(index, shift):
        source, target = shard_pairs[index]
        return pltpu.make_async_remote_copy(
            src_ref=source,
            dst_ref=target,
            send_sem=shard_send.at[index, shift],
            recv_sem=shard_recv.at[index, shift],
            device_id={"fsdp": lax.rem(mine + shift, split)},
        )

    def landed_half(index, owner, side):
        if index == 3:
            rows = local_width // 2
            return rows_full.at[owner, pl.ds(side * rows, rows)]
        rows = part // 2
        start = pl.multiple_of(owner * part + side * rows, rows)
        return qkv.at[index, pl.ds(start, rows)]

    def relay_copy(index, step):
        if step < 2:
            source, target = shard_pairs[index]
        else:
            source = target = landed_half(index, partner_of(mine, step - 1), step - 2)
        return pltpu.make_async_remote_copy(
            src_ref=source,
            dst_ref=target,
            send_sem=shard_send.at[index, step],
            recv_sem=shard_recv.at[index, step],
            device_id=(x_mate, y_mate, y_mate, x_mate)[step],
        )

    def shard_own(index):
        source, target = shard_pairs[index]
        return pltpu.make_async_copy(source, target, shard_local.at[index])

    for index in range(4):
        if split == 4:
            relay_copy(index, 0).start()
            relay_copy(index, 1).start()
        else:
            for shift in range(1, split):
                shard_copy(index, shift).start()
        shard_own(index).start()

    def expert_pair(index, dest):
        expert = lax.rem(dest, experts_local)
        if index == 2:
            return w_down_ref.at[expert], down_full.at[:, own_part]
        source, target = ((w_gate_ref, gate_full), (w_up_ref, up_full))[index]
        return source.at[expert], target.at[own_part]

    def expert_copy(index, shift):
        dest = lax.rem(mine + shift, split)
        source, target = expert_pair(index, dest)
        return pltpu.make_async_remote_copy(
            src_ref=source,
            dst_ref=target,
            send_sem=expert_send.at[index, shift],
            recv_sem=expert_recv.at[index, shift],
            device_id={"fsdp": dest},
        )

    def expert_own(index):
        source, target = expert_pair(index, mine)
        return pltpu.make_async_copy(source, target, expert_local.at[index])

    for distance in range(1, chips):
        first.step(distance)
        if split == 4 and distance == min(2, chips - 1):
            for index in range(4):
                for step in range(2):
                    relay_copy(index, step).wait_recv()
                    relay_copy(index, step + 2).start()
    for index in range(4):
        shard_own(index).wait()
        if split == 4:
            relay_copy(index, 2).wait_recv()
            relay_copy(index, 3).wait_recv()
        else:
            for shift in range(1, split):
                shard_copy(index, shift).wait_recv()

    def expert_start(index):
        for shift in range(1, split):
            expert_copy(index, shift).start()
        expert_own(index).start()

    expert_start(0)
    first.landed()
    for shift in range(1, size):
        choice_copy(shift).start()
    choices[me] = choice_own[...]
    if crossed:
        cross_own.wait()
        cross_copy(0).wait()
        cross_copy(1).wait()
        second = gather(1, cotangent_pair, cotangent_all)
    else:
        second = gather(1, cotangent_ref, cotangent_all)
    second.start()
    keeps = [
        pltpu.make_async_copy(normed, normed_out, out_sem.at[0]),
        pltpu.make_async_copy(qkv, qkv_out, out_sem.at[1]),
        pltpu.make_async_copy(rows_full, rows_out, out_sem.at[2]),
    ]
    for keep in keeps:
        keep.start()

    own_cols = pl.ds(pl.multiple_of(me * local_width, local_width), local_width)
    block = min(512, length)
    lanes = lax.broadcasted_iota(jnp.int32, (8, local_width), 0)
    first_row, second_row = (lanes == 0).astype(f32), (lanes == 1).astype(f32)

    @pl.loop(0, length // block)
    def _(step):
        rows = pl.ds(pl.multiple_of(step * block, block), block)
        left = normed[rows, :]
        query = jnp.dot(left, qkv[0], preferred_element_type=f32)
        raw[0, rows, :] = query
        keys = jnp.dot(left, qkv[1], preferred_element_type=f32)
        raw[1, rows, :] = keys
        sums_own[:, rows] = row_sums(query * query, first_row) + row_sums(keys * keys, second_row)
        v_ref[rows, :] = jnp.dot(left, qkv[2], preferred_element_type=f32).astype(half)

    def sums_copy(shift):
        return pltpu.make_async_remote_copy(
            src_ref=sums_own,
            dst_ref=sums_in.at[me],
            send_sem=sums_send.at[shift],
            recv_sem=sums_recv.at[shift],
            device_id={"seq": lax.rem(me + shift, size)},
        )

    for shift in range(1, size):
        sums_copy(shift).start()
    sums_in[me] = sums_own[...]
    for shift in range(1, size):
        sums_copy(shift).wait()
    sums_ref[...] = jnp.sum(sums_in[...], 0)
    for shift in range(1, size):
        choice_copy(shift).wait()

    def mate_copy(index):
        return pltpu.make_async_remote_copy(
            src_ref=choices,
            dst_ref=mate_choices.at[index],
            send_sem=mate_send.at[index],
            recv_sem=mate_recv.at[index],
            device_id=(x_mate, y_mate)[index],
        )

    if crossed:
        mate_copy(0).start()
        mate_copy(1).start()
    segments = seg_row_ref[...].astype(f32)
    narrow = first_row[:, 0:128]

    @pl.loop(0, length // block)
    def _(step):
        rows = pl.ds(pl.multiple_of(step * block, block), block)
        square_sums = sums_ref[:, rows]
        seg_col_ref[rows, :] = column_of(
            jnp.broadcast_to(seg_row_ref[:, rows].astype(f32), (8, block)), narrow
        )
        for index, pick, target in ((0, first_row, q_ref), (1, second_row, k_ref)):
            scale = lax.rsqrt(column_of(square_sums, pick) / model_width + EPSILON)
            unit = raw[index, rows, :] * scale
            unit_ref[index, rows, :] = unit
            scaled = unit * gains_ref[2 + index : 3 + index, own_cols]
            for number in range(heads):
                cols = slice(number * head, (number + 1) * head)
                piece = scaled[:, cols]
                target[rows, cols] = (
                    piece * cos_ref[rows, :] + turned_halves(piece) * sin_ref[rows, :]
                ).astype(half)

    second.step(1)

    wide = min(256, length)
    for number in range(heads):
        cols = slice(number * head, (number + 1) * head)

        @pl.loop(0, length // wide)
        def _(step):
            rows = pl.ds(pl.multiple_of(step * wide, wide), wide)
            scores = lax.dot_general(
                q_ref[rows, cols],
                k_ref[:, cols],
                (((1,), (1,)), ((), ())),
                preferred_element_type=f32,
            )
            scores = scores * (head**-0.5)
            scores = jnp.where(seg_col_ref[rows, 0:1] == segments, scores, MASKED)
            peak = jnp.max(scores, -1, keepdims=True)
            grown = jnp.exp(scores - peak)
            weight = jnp.sum(grown, -1, keepdims=True)
            probs = (grown * (1.0 / weight)).astype(half)
            attended_ref[rows, cols] = jnp.dot(
                probs, v_ref[:, cols], preferred_element_type=f32
            ).astype(half)
            log_ref[rows, cols] = jnp.broadcast_to(peak + jnp.log(weight), (wide, head))

    expert_start(1)
    for index, (source, target) in enumerate(
        (
            (q_ref, q_out),
            (k_ref, k_out),
            (v_ref, v_out),
            (unit_ref, unit_out),
            (log_ref, log_out),
            (attended_ref, attended_out),
        )
    ):
        keeps.append(pltpu.make_async_copy(source, target, out_sem.at[3 + index]))
        keeps[-1].start()

    reduce = ChainReduce(chips, residual_ref, reduce_buffers)

    def product(index, store):
        left = attended_ref[pl.ds(pl.multiple_of(index * tok_rows, tok_rows), tok_rows), :]
        for piece in range(split):
            cols = pl.ds(piece * part, part)
            store(cols, jnp.dot(left, rows_full[piece], preferred_element_type=f32))

    def hook(index):
        for distance in range(2, chips - 1):

            @pl.when(index == 2 * distance)
            def _():
                second.step(distance)

    reduce.run(product, hook=hook)
    residual = tokens_ref[...].astype(f32) + reduce.total[...]
    residual_ref[...] = residual
    inverse = lax.rsqrt(jnp.mean(residual * residual, -1, keepdims=True) + EPSILON)
    first.sent()
    routed_half[...] = (residual * inverse * gains_ref[1:2, :]).astype(half)
    if crossed:
        cross_copy(2).start()
        cross_copy(3).start()
    third = gather(2, routed_half, routed_out)
    third.start()
    if chips > 2:
        second.step(chips - 1)
    expert_start(2)

    second.landed()
    double = 2 * CAP
    member = lax.rem(mine, experts_local)
    slot_row = lax.broadcasted_iota(jnp.int32, (double, tok_rows), 0)
    if crossed:
        mate_copy(0).wait()
        mate_copy(1).wait()

    def one_hot(places, target, rows, expert):
        base = (me * experts_local + expert) * CAP
        for side in range(2):
            want = jnp.where(slot_row // CAP == side, slot_row - side * CAP + base, -1)
            hit = want == places(side)[top_count : top_count + 1, :]
            for choice in range(1, top_count):
                hit = hit | (want == places(side)[top_count + choice : top_count + choice + 1, :])
            cols = slice(side * tok_rows, (side + 1) * tok_rows)
            target[rows, cols] = jnp.where(hit, 1.0, 0.0).astype(half)

    def slot_range(move):
        return slice(move * double, (move + 1) * double)

    @pl.loop(0, size // 2)
    def _(pair):
        for move in range(experts_local):
            one_hot(
                lambda side: choices[pair * 2 + side],
                onehot_ref.at[pair],
                slot_range(move),
                partner_of(member, move),
            )
        if crossed:
            start = pl.multiple_of(pair * 4 * tok_rows, 4 * tok_rows)
            four = cotangent_all[pl.ds(start, 4 * tok_rows), :]
            own = jnp.concatenate(
                [four[0:tok_rows], four[2 * tok_rows : 3 * tok_rows]], 0
            )
            mates = jnp.concatenate(
                [four[tok_rows : 2 * tok_rows], four[3 * tok_rows : 4 * tok_rows]], 0
            )
            made = jnp.dot(onehot_ref[pair], own, preferred_element_type=f32).astype(half)
            placed[0, pair] = made[slot_range(0)]
            placed[1, pair, :, upper] = made[slot_range(1), half_width:]
            placed[2, pair, :, lower] = made[slot_range(2), :half_width]
            for index in range(2):
                for row, expert in enumerate((member, partner_of(member, 2 - index))):
                    one_hot(
                        lambda side: mate_choices[index, pair * 2 + side],
                        mate_onehot.at[pair, index],
                        slot_range(row),
                        expert,
                    )
                cols = (lower, upper)[index]
                taken = mates[:, :half_width] if index == 0 else mates[:, half_width:]
                made = jnp.dot(
                    mate_onehot[pair, index], taken, preferred_element_type=f32
                ).astype(half)
                placed[index + 1, pair, :, cols] = made[slot_range(0)]
                placed[3, pair, :, cols] = made[slot_range(1)]
        else:
            start = pl.multiple_of(pair * 2 * tok_rows, 2 * tok_rows)
            made = jnp.dot(
                onehot_ref[pair],
                cotangent_all[pl.ds(start, 2 * tok_rows), :],
                preferred_element_type=f32,
            ).astype(half)
            for move in range(experts_local):
                placed[move, pair] = made[slot_range(move)]

    placed_keep = pltpu.make_async_copy(placed, placed_out, placed_local.at[0])
    placed_keep.start()
    third.steps()
    third.landed()
    if crossed:
        cross_copy(2).wait()
        cross_copy(3).wait()
        cross_keep = pltpu.make_async_copy(
            routed_own.at[cross_rows], routed_cross, placed_local.at[1]
        )
        cross_keep.start()
    reduce.sent()
    second.sent()
    third.sent()
    for index in range(4):
        if split == 4:
            for step in range(4):
                relay_copy(index, step).wait_send()
        else:
            for shift in range(1, split):
                shard_copy(index, shift).wait_send()
    for keep in keeps:
        keep.wait()
    placed_keep.wait()
    if crossed:
        cross_keep.wait()
    for index in range(3):
        expert_own(index).wait()
        for shift in range(1, split):
            expert_copy(index, shift).wait()


def front(sizes, tokens, gains, cos, sin, segment_row, ids, slots, cotangent, weights, which):
    size, split, chips, experts_local = sizes
    w_query, w_key, w_value, w_out, w_gate, w_up, w_down = weights
    tok_rows, model_width = tokens.shape
    length = size * tok_rows
    local_width = w_query.shape[1]
    hidden_width = w_gate.shape[2]
    f32, half = jnp.float32, jnp.bfloat16
    vmem = pl.BlockSpec(memory_space=pltpu.VMEM)
    anywhere = pl.BlockSpec(memory_space=pl.ANY)
    kind = pltpu.SemaphoreType.DMA
    shape = jax.ShapeDtypeStruct
    crossed = split == experts_local == 4
    choices = (size, 2 * ids.shape[0], tok_rows)
    return pl.pallas_call(
        functools.partial(front_kernel, sizes),
        out_shape=(
            shape((length, model_width), half),
            shape((3, model_width, local_width), half),
            shape((split, *w_out.shape), half),
            shape((length, local_width), half),
            shape((length, local_width), half),
            shape((length, local_width), half),
            shape((2, length, local_width), f32),
            shape((length, local_width), f32),
            shape((length, local_width), half),
            shape((8, length), f32),
            shape((tok_rows, model_width), f32),
            shape(gains.shape, f32),
            shape((length, 128), f32),
            shape((length, model_width), half),
            shape((tok_rows, model_width), half),
            shape((experts_local, size // 2, 2 * CAP, model_width), half),
            shape((model_width, hidden_width), half),
            shape((model_width, hidden_width), half),
            shape((hidden_width, model_width), half),
            shape((size, 2 * ids.shape[0], tok_rows), jnp.int32),
            shape((size // 2, experts_local * 2 * CAP, 2 * tok_rows), half),
            shape((size // 2 if crossed else 1, 2, 4 * CAP, 2 * tok_rows), half),
        ),
        in_specs=[vmem] * 7 + [anywhere] * 8,
        out_specs=tuple([anywhere] * 9 + [vmem] * 4 + [anywhere] * 6 + [vmem] * 3),
        scratch_shapes=[
            pltpu.VMEM((length, local_width), half),
            pltpu.VMEM((length, local_width), half),
            pltpu.VMEM((length, local_width), half),
            pltpu.VMEM((2, length, local_width), f32),
            pltpu.VMEM((length, local_width), f32),
            pltpu.VMEM((length, local_width), half),
            pltpu.VMEM((length, model_width), half),
            pltpu.VMEM((3, model_width, local_width), half),
            pltpu.VMEM((split, *w_out.shape), half),
            pltpu.VMEM((2 * tok_rows, model_width), half),
            pltpu.VMEM((2 * ids.shape[0], tok_rows), jnp.int32),
            pltpu.VMEM((2 * tok_rows if crossed else 16, model_width), half),
            pltpu.VMEM(((2 if crossed else 1) * length, model_width), half),
            pltpu.VMEM((2, *(choices if crossed else (1, 8, 128))), jnp.int32),
            pltpu.VMEM((experts_local, size // 2, 2 * CAP, model_width), half),
            pltpu.VMEM((2, length, local_width), f32),
            pltpu.VMEM((8, length), f32),
            pltpu.VMEM((size, 8, length), f32),
            kind((3,)),
            kind((3, 3, chips)),
            kind((3, 2, chips)),
            kind((size,)),
            kind((size,)),
            kind((size,)),
            kind((size,)),
            kind((2,)),
            kind((2,)),
            kind,
            kind((4,)),
            kind((4,)),
            kind((2,)),
            kind((4,)),
            kind((4, split)),
            kind((4, split)),
            kind((3,)),
            kind((3, split)),
            kind((3, split)),
            kind((9,)),
            *ChainReduce.scratch(chips, tok_rows, model_width),
        ],
        compiler_params=pltpu.CompilerParams(
            collective_id=which, has_side_effects=True, vmem_limit_bytes=58 * 2**20
        ),
        cost_estimate=pl.CostEstimate(
            flops=2 * length * model_width * local_width * 4,
            bytes_accessed=500 * 2**20,
            transcendentals=0,
        ),
    )(
        tokens, gains, cos, sin, segment_row, ids, slots, cotangent, *weights
    )


class ShardSend:
    def __init__(self, split, source, landing, local_sem, sends, arrivals):
        self.split, self.source, self.landing = split, source, landing
        self.local_sem, self.sends, self.arrivals = local_sem, sends, arrivals
        self.mine = lax.axis_index("fsdp")

    def copy(self, shift):
        dest = lax.rem(self.mine + shift, self.split)
        return pltpu.make_async_remote_copy(
            src_ref=self.source(dest),
            dst_ref=self.landing.at[self.mine],
            send_sem=self.sends.at[shift],
            recv_sem=self.arrivals.at[shift],
            device_id={"fsdp": dest},
        )

    def own(self):
        return pltpu.make_async_copy(
            self.source(self.mine), self.landing.at[self.mine], self.local_sem
        )

    def start(self):
        for shift in range(1, self.split):
            self.copy(shift).start()
        self.own().start()

    def wait(self):
        for shift in range(1, self.split):
            self.copy(shift).wait()
        self.own().wait()


def turned_dot(left, right):
    return lax.dot_general(
        left, right, (((0,), (0,)), ((), ())), preferred_element_type=jnp.float32
    )


def cross_dot(left, right):
    return lax.dot_general(
        left, right, (((1,), (1,)), ((), ())), preferred_element_type=jnp.float32
    )


def experts_kernel(
    sizes,
    routed_ref,
    routed_cross_ref,
    choices_ref,
    onehot_ref,
    mate_onehot_ref,
    placed_ref,
    router_ref,
    gains_ref,
    residual_ref,
    cotangent_ref,
    gate_ref,
    up_ref,
    down_ref,
    residual_grad_ref,
    out_grad_ref,
    gain_ref,
    router_grad_ref,
    hidden_out,
    grad_gate_ref,
    grad_up_ref,
    down_landing,
    routed_mates,
    gate_full,
    up_full,
    down_full,
    upstream,
    pair_rows,
    outgoing,
    arrived,
    hidden,
    gate_grad,
    up_grad,
    back,
    gates,
    gates_out,
    gates_in,
    dots_out,
    dots_in,
    token_out,
    token_in,
    scales,
    load_sem,
    pair_sem,
    keep_sem,
    gather_local,
    gather_send,
    gather_recv,
    upstream_send,
    upstream_recv,
    rows_send,
    rows_recv,
    gates_send,
    gates_recv,
    back_send,
    back_recv,
    dots_send,
    dots_recv,
    token_send,
    token_recv,
    down_send,
    down_recv,
    *reduce_buffers,
):
    size, split, chips, experts_local = sizes
    f32, half = jnp.float32, jnp.bfloat16
    me, mine = lax.axis_index("seq"), lax.axis_index("fsdp")
    tok_rows, model_width = residual_ref.shape
    pairs = size // 2
    double = 2 * CAP
    wide = 2 * tok_rows
    hidden_width = gate_full.shape[1]
    rows_of = pairs * double
    part = model_width // split
    member = lax.rem(mine, experts_local)
    crossed = split == experts_local == 4
    half_width = model_width // 2
    lower, upper = pl.ds(0, half_width), pl.ds(half_width, half_width)

    loads = [
        pltpu.make_async_copy(source, target, load_sem.at[index])
        for index, (source, target) in enumerate(
            (
                (gate_ref, gate_full),
                (up_ref, up_full),
                (down_ref, down_full),
            )
        )
    ]
    if crossed:
        pieces = (
            (placed_ref.at[0], upstream.at[0]),
            (placed_ref.at[1, :, :, lower], upstream.at[1, :, :, lower]),
            (placed_ref.at[2, :, :, upper], upstream.at[2, :, :, upper]),
        )
    else:
        pieces = ((placed_ref.at[0], upstream.at[0]),)
    loads += [
        pltpu.make_async_copy(source, target, load_sem.at[3 + index])
        for index, (source, target) in enumerate(pieces)
    ]

    slots = pair_rows.shape[0]

    def pair_load(source, pair):
        slot = lax.rem(pair, slots)
        start = pl.multiple_of(pair * wide, wide)
        return pltpu.make_async_copy(
            source.at[pl.ds(start, wide)], pair_rows.at[slot], pair_sem.at[slot]
        )

    pair_load(routed_ref, 0).start()
    for load in loads:
        load.start()
    greet_all(size, split)

    def mate(move):
        return {"fsdp": partner_of(mine, move)}

    def upstream_piece(move, index, cols, target):
        return pltpu.make_async_remote_copy(
            src_ref=placed_ref.at[move, :, :, cols],
            dst_ref=upstream.at[move, :, :, cols],
            send_sem=upstream_send.at[index],
            recv_sem=upstream_recv.at[index],
            device_id=mate(target),
        )

    def halves_of(piece, move):
        if not crossed:
            return [piece(move, move, pl.ds(0, model_width), move)]
        if move == 3:
            return [piece(3, 3, upper, 1), piece(3, 0, lower, 2)]
        return [piece(move, move, (upper, lower)[move - 1], move)]

    order = [1, 2, 3] if crossed else list(range(experts_local - 1, 0, -1))
    if crossed:
        gather = ChainGather(
            chips, routed_cross_ref, routed_mates, gather_local, gather_send, gather_recv
        )
        gather.start()
    for move in order:
        for copy in halves_of(upstream_piece, move):
            copy.start()

    padded = size * 8
    expert_row = lax.broadcasted_iota(jnp.int32, (padded, tok_rows), 0)
    inner = lax.rem(expert_row, 8)
    expert_row = jnp.where(inner < experts_local, expert_row // 8 * experts_local + inner, -1)
    ones = jnp.ones((8, wide), f32)
    top_count = choices_ref.shape[1] // 2

    @pl.loop(0, pairs)
    def _(pair):
        pair_load(routed_ref, pair).wait()

        @pl.when((pair + 1 < pairs) & (slots > 1))
        def _():
            pair_load(routed_ref, pair + 1).start()

        rows = pair_rows[lax.rem(pair, slots)]
        logits = lax.dot_general(
            router_ref[...], rows, (((1,), (1,)), ((), ())), preferred_element_type=f32
        )
        for side in range(2):
            ids = choices_ref[pair * 2 + side]
            chosen = expert_row == ids[0:1, :]
            for choice in range(1, top_count):
                chosen = chosen | (expert_row == ids[choice : choice + 1, :])
            own = jnp.where(chosen, logits[:, side * tok_rows : (side + 1) * tok_rows], MASKED)
            grown = jnp.where(chosen, jnp.exp(own - jnp.max(own, 0, keepdims=True)), 0.0)
            gates[pair * 2 + side] = grown / jnp.sum(grown, 0, keepdims=True)
        placed = jnp.dot(onehot_ref[pair], rows, preferred_element_type=f32).astype(half)
        for move in range(experts_local):
            piece = placed[move * double : (move + 1) * double]
            if move == 0:
                arrived[0, pair] = piece
            elif not crossed:
                outgoing[move - 1, pair] = piece
            elif move < 3:
                cols = (upper, lower)[move - 1]
                outgoing[move - 1, pair, :, cols] = (
                    piece[:, half_width:] if move == 1 else piece[:, :half_width]
                )
            row = me * 8 + partner_of(member, move)
            weights = jnp.concatenate(
                [gates[pair * 2, pl.ds(row, 1), :], gates[pair * 2 + 1, pl.ds(row, 1), :]], 1
            )
            slot_rows = pl.ds(move * double, double)
            weighted = onehot_ref[pair, slot_rows, :].astype(f32) * weights
            gates_out[move, pair] = row_sums(weighted, ones)

        @pl.when((pair + 1 < pairs) & (slots == 1))
        def _():
            pair_load(routed_ref, pair + 1).start()

    def rows_piece(move, index, cols, target):
        return pltpu.make_async_remote_copy(
            src_ref=outgoing.at[move - 1, :, :, cols],
            dst_ref=arrived.at[move, :, :, cols],
            send_sem=rows_send.at[index],
            recv_sem=rows_recv.at[index],
            device_id=mate(target),
        )

    def gates_copy(move):
        return pltpu.make_async_remote_copy(
            src_ref=gates_out.at[move],
            dst_ref=gates_in.at[move],
            send_sem=gates_send.at[move],
            recv_sem=gates_recv.at[move],
            device_id=mate(move),
        )

    def back_rows(move):
        return back.at[:, pl.ds(move * double, double), :]

    def back_copy(move):
        return pltpu.make_async_remote_copy(
            src_ref=outgoing.at[move - 1],
            dst_ref=back_rows(move),
            send_sem=back_send.at[move],
            recv_sem=back_recv.at[move],
            device_id=mate(move),
        )

    def dots_copy(move):
        return pltpu.make_async_remote_copy(
            src_ref=dots_out.at[move],
            dst_ref=dots_in.at[move],
            send_sem=dots_send.at[move],
            recv_sem=dots_recv.at[move],
            device_id=mate(move),
        )

    for move in order:
        gates_copy(move).start()
        if not crossed or move < 3:
            for copy in halves_of(rows_piece, move):
                copy.start()
    gates_in[0] = gates_out[0]
    for load in loads:
        load.wait()
    if crossed:
        gather.step(1)

    def mates_rows():
        for distance in range(3, chips):
            gather.step(distance)
        gather.landed()
        pair_load(routed_mates, 0).start()

        @pl.loop(0, pairs)
        def _(pair):
            pair_load(routed_mates, pair).wait()

            @pl.when(pair + 1 < pairs)
            def _():
                pair_load(routed_mates, pair + 1).start()

            for index, cols in enumerate((lower, upper)):
                made = jnp.dot(
                    mate_onehot_ref[pair, index],
                    pair_rows[lax.rem(pair, slots), :, cols],
                    preferred_element_type=f32,
                ).astype(half)
                arrived[index + 1, pair, :, cols] = made[0:double]
                outgoing[2, pair, :, cols] = made[double:]

        for copy in halves_of(rows_piece, 3):
            copy.start()
        gather.sent()

    cols_step = min(256, hidden_width)
    width_step = min(512, model_width)
    spread = (lax.broadcasted_iota(jnp.int32, (8, 128), 0) == 0).astype(f32)
    for move in [0] + order:
        if move:
            gates_copy(move).wait()
            for copy in halves_of(rows_piece, move) + halves_of(upstream_piece, move):
                copy.wait()
        for pair in range(pairs):
            scales[pair * double : (pair + 1) * double, :] = column_of(
                gates_in[move, pair], spread
            )
        dots_out[move] = jnp.zeros_like(dots_out[move])

        @pl.loop(0, hidden_width // cols_step)
        def _(index):
            cols = pl.ds(pl.multiple_of(index * cols_step, cols_step), cols_step)
            rows = arrived[move].reshape(rows_of, model_width)
            pre = jnp.dot(rows, gate_full[:, cols], preferred_element_type=f32)
            up = jnp.dot(rows, up_full[:, cols], preferred_element_type=f32)
            plain = lax.dot_general(
                upstream[move].reshape(rows_of, model_width),
                down_full[cols, :],
                (((1,), (1,)), ((), ())),
                preferred_element_type=f32,
            )
            sigmoid = 1.0 / (1.0 + jnp.exp(-pre))
            active = pre * sigmoid
            made = (active * up).astype(half)
            weighted = made.astype(f32) * scales[:, 0:1]
            hidden[move, :, :, cols] = weighted.astype(half).reshape(pairs, double, cols_step)
            dots = made.astype(f32) * plain
            for pair in range(pairs):
                dots_out[move, pair] += row_sums(
                    dots[pair * double : (pair + 1) * double], jnp.ones((8, cols_step), f32)
                )
            scaled = plain * scales[:, 0:1]
            gate_back = scaled * up * sigmoid * (1.0 + pre * (1.0 - sigmoid))
            gate_grad[move, :, :, cols] = gate_back.astype(half).reshape(pairs, double, cols_step)
            up_grad[move, :, :, cols] = (
                (scaled * active).astype(half).reshape(pairs, double, cols_step)
            )

        if move:
            dots_copy(move).start()
        else:
            dots_in[0] = dots_out[0]
            if crossed and chips > 2:
                gather.step(2)

        @pl.loop(0, model_width // width_step)
        def _(index):
            cols = pl.ds(pl.multiple_of(index * width_step, width_step), width_step)
            rows_grad = lax.dot_general(
                gate_grad[move].reshape(rows_of, hidden_width),
                gate_full[cols, :],
                (((1,), (1,)), ((), ())),
                preferred_element_type=f32,
            )
            rows_grad = rows_grad + lax.dot_general(
                up_grad[move].reshape(rows_of, hidden_width),
                up_full[cols, :],
                (((1,), (1,)), ((), ())),
                preferred_element_type=f32,
            )
            rows_grad = rows_grad.astype(half).reshape(pairs, double, width_step)
            if move:
                outgoing[move - 1, :, :, cols] = rows_grad
            else:
                back[:, 0:double, cols] = rows_grad

        if move:
            back_copy(move).start()
        elif crossed:
            mates_rows()

    own_rows = pl.ds(pl.multiple_of(me * tok_rows, tok_rows), tok_rows)
    own_load = pltpu.make_async_copy(
        routed_ref.at[own_rows], pair_rows.at[0, pl.ds(0, tok_rows)], pair_sem.at[0]
    )
    own_load.start()
    hidden_keep = pltpu.make_async_copy(hidden, hidden_out, keep_sem)
    hidden_keep.start()

    total_rows = experts_local * rows_of

    def flat(ref, cols):
        return ref[:, :, :, cols].reshape(total_rows, -1)

    every = pl.ds(0, hidden_width)

    @pl.loop(0, split)
    def _(piece):
        cols = pl.ds(pl.multiple_of(piece * part, part), part)
        gate_full[cols, :] = turned_dot(flat(arrived, cols), flat(gate_grad, every)).astype(half)
        up_full[cols, :] = turned_dot(flat(arrived, cols), flat(up_grad, every)).astype(half)
        down_full[:, cols] = turned_dot(flat(hidden, every), flat(upstream, cols)).astype(half)

    grad_keeps = [
        pltpu.make_async_copy(source, target, load_sem.at[index])
        for index, (source, target) in enumerate(
            ((gate_full, grad_gate_ref), (up_full, grad_up_ref))
        )
    ]
    for keep in grad_keeps:
        keep.start()
    down_send_all = ShardSend(
        split,
        lambda dest: down_full.at[:, pl.ds(pl.multiple_of(dest * part, part), part)],
        down_landing,
        load_sem.at[2],
        down_send,
        down_recv,
    )

    for move in order:
        dots_copy(move).wait()
    token_out[...] = jnp.zeros_like(token_out)

    @pl.loop(0, pairs)
    def _(pair):
        for move in range(experts_local):
            found = jnp.dot(
                dots_in[move, pair],
                onehot_ref[pair, pl.ds(move * double, double), :].astype(f32),
                precision=HIGHEST,
                preferred_element_type=f32,
            )
            row = partner_of(member, move)
            for side in range(2):
                token_out[pair * 2 + side, pl.ds(row, 1), :] = found[
                    0:1, side * tok_rows : (side + 1) * tok_rows
                ]

    def token_copy(shift):
        peer = lax.rem(me + shift, size)
        return pltpu.make_async_remote_copy(
            src_ref=token_out.at[peer],
            dst_ref=token_in.at[me],
            send_sem=token_send.at[shift],
            recv_sem=token_recv.at[shift],
            device_id={"seq": peer},
        )

    for shift in range(1, size):
        token_copy(shift).start()
    token_in[me] = token_out[me]
    for move in order:
        back_copy(move).wait()
    down_send_all.start()

    reduce = ChainReduce(chips, residual_grad_ref, reduce_buffers)

    def product(index, store):
        side = pl.ds(pl.multiple_of(lax.rem(index, 2) * tok_rows, tok_rows), tok_rows)
        left = onehot_ref[index // 2, :, side]

        @pl.loop(0, model_width // width_step)
        def _(step):
            cols = pl.ds(pl.multiple_of(step * width_step, width_step), width_step)
            store(cols, turned_dot(left, back[index // 2, :, cols]))

    reduce.run(product)

    for shift in range(1, size):
        token_copy(shift).wait()
    own_gates = gates[me]
    grads = token_in[...].reshape(padded, tok_rows)
    mean = jnp.sum(own_gates * grads, 0, keepdims=True)
    logit_grad = (own_gates * (grads - mean)).astype(half)
    routed_grad = reduce.total[...] + turned_dot(logit_grad, router_ref[...])
    own_load.wait()
    router_grad = jnp.dot(logit_grad, pair_rows[0, 0:tok_rows, :], preferred_element_type=f32)
    for device in range(size):
        router_grad_ref[device * experts_local : (device + 1) * experts_local, :] = router_grad[
            device * 8 : device * 8 + experts_local
        ]
    residual = residual_ref[...]
    inverse = lax.rsqrt(jnp.mean(residual * residual, -1, keepdims=True) + EPSILON)
    unit = residual * inverse
    gain_ref[...] = jnp.broadcast_to(
        jnp.sum(routed_grad * unit, 0, keepdims=True), gain_ref.shape
    )
    routed_grad = routed_grad * gains_ref[1:2, :]
    routed_grad = inverse * (
        routed_grad - unit * jnp.mean(routed_grad * unit, -1, keepdims=True)
    )
    residual_grad = cotangent_ref[...].astype(f32) + routed_grad
    residual_grad_ref[...] = residual_grad
    out_grad_ref[...] = residual_grad.astype(half)
    reduce.sent()
    hidden_keep.wait()
    for keep in grad_keeps:
        keep.wait()
    down_send_all.wait()


def experts(
    sizes,
    routed_seq,
    routed_cross,
    choices,
    onehot,
    mate_onehot,
    placed,
    router_rows,
    gain_rows,
    residual,
    cotangent,
    weights,
    which,
):
    size, split, chips, experts_local = sizes
    gate_full, up_full, down_full = weights
    model_width, hidden_width = gate_full.shape
    tok_rows = residual.shape[0]
    pairs, double = size // 2, 2 * CAP
    f32, half = jnp.float32, jnp.bfloat16
    vmem = pl.BlockSpec(memory_space=pltpu.VMEM)
    anywhere = pl.BlockSpec(memory_space=pl.ANY)
    kind = pltpu.SemaphoreType.DMA
    shape = jax.ShapeDtypeStruct
    few = kind((experts_local,))
    crossed = split == experts_local == 4
    wide_rows = (experts_local, pairs, double, model_width)
    narrow_rows = (experts_local, pairs, double, hidden_width)
    flags = (experts_local, pairs, 8, double)
    return pl.pallas_call(
        functools.partial(experts_kernel, sizes),
        out_shape=(
            shape((tok_rows, model_width), f32),
            shape((tok_rows, model_width), half),
            shape((8, model_width), f32),
            shape((size * experts_local, model_width), f32),
            shape(narrow_rows, half),
            shape(gate_full.shape, half),
            shape(up_full.shape, half),
            shape((split, hidden_width, model_width // split), half),
            shape(routed_seq.shape if crossed else (16, model_width), half),
        ),
        in_specs=[anywhere] * 2 + [vmem] * 3 + [anywhere] + [vmem] * 4 + [anywhere] * 3,
        out_specs=tuple([vmem] * 4 + [anywhere] * 5),
        scratch_shapes=[
            pltpu.VMEM(gate_full.shape, half),
            pltpu.VMEM(up_full.shape, half),
            pltpu.VMEM(down_full.shape, half),
            pltpu.VMEM(wide_rows, half),
            pltpu.VMEM((2 if chips < 8 else 1, 2 * tok_rows, model_width), half),
            pltpu.VMEM((max(experts_local - 1, 1), *wide_rows[1:]), half),
            pltpu.VMEM(wide_rows, half),
            pltpu.VMEM(narrow_rows, half),
            pltpu.VMEM(narrow_rows, half),
            pltpu.VMEM(narrow_rows, half),
            pltpu.VMEM((pairs, experts_local * double, model_width), half),
            pltpu.VMEM((size, size * 8, tok_rows), f32),
            pltpu.VMEM(flags, f32),
            pltpu.VMEM(flags, f32),
            pltpu.VMEM(flags, f32),
            pltpu.VMEM(flags, f32),
            pltpu.VMEM((size, 8, tok_rows), f32),
            pltpu.VMEM((size, 8, tok_rows), f32),
            pltpu.VMEM((pairs * double, 128), f32),
            kind((6,)),
            kind((2,)),
            kind,
            kind,
            kind((3, chips)),
            kind((2, chips)),
            few,
            few,
            few,
            few,
            few,
            few,
            few,
            few,
            few,
            few,
            kind((size,)),
            kind((size,)),
            kind((split,)),
            kind((split,)),
            *ChainReduce.scratch(chips, tok_rows, model_width),
        ],
        compiler_params=pltpu.CompilerParams(
            collective_id=which, has_side_effects=True, vmem_limit_bytes=63 * 2**20
        ),
        cost_estimate=pl.CostEstimate(
            flops=2 * experts_local * pairs * double * model_width * hidden_width * 8,
            bytes_accessed=500 * 2**20,
            transcendentals=0,
        ),
    )(
        routed_seq,
        routed_cross,
        choices,
        onehot,
        mate_onehot,
        placed,
        router_rows,
        gain_rows,
        residual,
        cotangent,
        gate_full,
        up_full,
        down_full,
    )

def back_kernel(
    sizes,
    out_grad_ref,
    gains_ref,
    second_gain_ref,
    seg_row_ref,
    sums_ref,
    *refs,
):
    kept_count = 13
    kept, refs = refs[:kept_count], refs[kept_count:]
    back_body(sizes, out_grad_ref, gains_ref, second_gain_ref, seg_row_ref, sums_ref, kept, *refs)


def back_body(
    sizes,
    out_grad_ref,
    gains_ref,
    second_gain_ref,
    seg_row_ref,
    sums_ref,
    kept,
    normed_ref,
    hidden_ref,
    down_ref,
    grad_gate_ref,
    input_grad_ref,
    gains_out_ref,
    out_w_grad_ref,
    mixed_rows,
    gate_landing,
    qkv_out,
    rows_full_ref,
    attended_ref,
    q_ref,
    k_ref,
    v_ref,
    seg_col_ref,
    log_ref,
    cos_ref,
    sin_ref,
    unit_ref,
    qkv_ref,
    tokens_ref,
    residual_grad_ref,
    down_full,
    out_grads,
    attended_grad,
    hidden,
    returned,
    key_total,
    value_total,
    scaled,
    raw_grads,
    centers_own,
    centers_in,
    qkv_stage,
    out_stage,
    out_landing,
    load_sem,
    gather_local,
    gather_send,
    gather_recv,
    gate_local,
    gate_send,
    gate_recv,
    rows_local,
    rows_send,
    rows_recv,
    centers_send,
    centers_recv,
    kept_sem,
    out_local,
    out_send,
    out_recv,
    *reduce_buffers,
):
    size, split, chips, experts_local = sizes
    f32, half = jnp.float32, jnp.bfloat16
    me, mine = lax.axis_index("seq"), lax.axis_index("fsdp")
    tok_rows, model_width = out_grad_ref.shape
    length, local_width = q_ref.shape
    hidden_width = down_ref.shape[0]
    part = model_width // split
    head = HEAD_DIM
    heads = local_width // head
    double = 2 * CAP
    pairs = size // 2
    rows_of = pairs * double

    down_load = pltpu.make_async_copy(down_ref, down_full, load_sem.at[0])
    hidden_load = pltpu.make_async_copy(hidden_ref, hidden, load_sem.at[1])
    down_load.start()
    hidden_load.start()
    targets = (
        rows_full_ref,
        attended_ref,
        q_ref,
        k_ref,
        v_ref,
        seg_col_ref,
        log_ref,
        cos_ref,
        sin_ref,
        unit_ref,
        qkv_ref,
        tokens_ref,
        residual_grad_ref,
    )
    kept_loads = [
        pltpu.make_async_copy(source, target, kept_sem.at[index])
        for index, (source, target) in enumerate(zip(kept, targets))
    ]
    greet_all(size, split)
    gather = ChainGather(chips, out_grad_ref, out_grads, gather_local, gather_send, gather_recv)
    gather.start()
    gate_send_all = ShardSend(
        split,
        lambda dest: grad_gate_ref.at[pl.ds(pl.multiple_of(dest * part, part), part)],
        gate_landing,
        gate_local,
        gate_send,
        gate_recv,
    )

    gate_send_all.start()
    for load in kept_loads:
        load.start()

    down_load.wait()
    hidden_load.wait()
    width_step = min(512, model_width)

    def rows_target(move):
        return mixed_rows.at[:, pl.ds(move * double, double), :]

    def rows_copy(move):
        return pltpu.make_async_remote_copy(
            src_ref=returned.at[move],
            dst_ref=rows_target(move),
            send_sem=rows_send.at[move],
            recv_sem=rows_recv.at[move],
            device_id={"fsdp": partner_of(mine, move)},
        )

    own_rows = pltpu.make_async_copy(returned.at[0], rows_target(0), rows_local)
    for move in range(experts_local - 1, -1, -1):

        @pl.loop(0, model_width // width_step)
        def _(index):
            cols = pl.ds(pl.multiple_of(index * width_step, width_step), width_step)
            made = jnp.dot(
                hidden[move].reshape(rows_of, hidden_width),
                down_full[:, cols],
                preferred_element_type=f32,
            )
            returned[move, :, :, cols] = made.astype(half).reshape(pairs, double, width_step)

        if move:
            rows_copy(move).start()
    own_rows.start()
    gather.steps()
    for load in kept_loads:
        load.wait()
    gather.landed()

    block = min(512, length)

    @pl.loop(0, length // block)
    def _(step):
        rows = pl.ds(pl.multiple_of(step * block, block), block)
        total = cross_dot(out_grads[rows, 0:part], rows_full_ref[0])
        for piece in range(1, split):
            total += cross_dot(
                out_grads[rows, piece * part : (piece + 1) * part], rows_full_ref[piece]
            )
        attended_grad[rows, :] = total.astype(half)

    @pl.loop(0, split)
    def _(piece):
        cols = pl.ds(pl.multiple_of(piece * part, part), part)
        out_stage[piece] = turned_dot(attended_ref[...], out_grads[:, cols]).astype(half)

    out_send_all = ShardSend(
        split, lambda dest: out_stage.at[dest], out_landing, out_local, out_send, out_recv
    )
    out_send_all.start()
    gather.sent()
    normed_load = pltpu.make_async_copy(normed_ref, out_grads, load_sem.at[0])
    normed_load.start()

    wide = min(256, length) if length <= 1024 else 128
    scale = head**-0.5
    segments = seg_row_ref[...].astype(f32)
    for number in range(heads):
        cols = slice(number * head, (number + 1) * head)
        key_total[...] = jnp.zeros_like(key_total)
        value_total[...] = jnp.zeros_like(value_total)

        @pl.loop(0, length // wide)
        def _(step):
            rows = pl.ds(pl.multiple_of(step * wide, wide), wide)
            scores = cross_dot(q_ref[rows, cols], k_ref[:, cols]) * scale
            scores = jnp.where(seg_col_ref[rows, 0:1] == segments, scores, MASKED)
            probs = jnp.exp(scores - log_ref[rows, cols][:, 0:1])
            grads = attended_grad[rows, cols]
            prob_grad = cross_dot(grads, v_ref[:, cols])
            center = jnp.sum(probs * prob_grad, -1, keepdims=True)
            score_grad = (probs * (prob_grad - center)).astype(half)
            query_grad = jnp.dot(score_grad, k_ref[:, cols], preferred_element_type=f32) * scale
            raw_grads[0, rows, cols] = query_grad.astype(half)
            key_total[...] += turned_dot(score_grad, q_ref[rows, cols])
            value_total[...] += turned_dot(probs.astype(half), grads)

        raw_grads[1, :, cols] = (key_total[...] * scale).astype(half)
        raw_grads[2, :, cols] = value_total[...].astype(half)

    lanes = lax.broadcasted_iota(jnp.int32, (8, local_width), 0)
    first_row, second_row = (lanes == 0).astype(f32), (lanes == 1).astype(f32)
    gains_out_ref[...] = jnp.zeros_like(gains_out_ref)
    own_cols = pl.ds(pl.multiple_of(me * local_width, local_width), local_width)
    gains_out_ref[1:2, :] = second_gain_ref[0:1, :]

    @pl.loop(0, length // block)
    def _(step):
        rows = pl.ds(pl.multiple_of(step * block, block), block)
        found = jnp.zeros((8, block), f32)
        for index, pick in ((0, first_row), (1, second_row)):
            unit = unit_ref[index, rows, :]
            pieces = []
            for number in range(heads):
                cols = slice(number * head, (number + 1) * head)
                piece = raw_grads[index, rows, cols].astype(f32)
                pieces.append(piece * cos_ref[rows, :] - turned_halves(piece) * sin_ref[rows, :])
            unit_grad = pieces[0] if heads == 1 else jnp.concatenate(pieces, 1)
            gains_out_ref[2 + index : 3 + index, own_cols] += jnp.sum(
                unit_grad * unit, 0, keepdims=True
            )
            grown = unit_grad * gains_ref[2 + index : 3 + index, own_cols]
            scaled[index, rows, :] = grown
            found += row_sums(grown * unit, pick)
        centers_own[:, rows] = found

    def centers_copy(shift):
        return pltpu.make_async_remote_copy(
            src_ref=centers_own,
            dst_ref=centers_in.at[me],
            send_sem=centers_send.at[shift],
            recv_sem=centers_recv.at[shift],
            device_id={"seq": lax.rem(me + shift, size)},
        )

    for shift in range(1, size):
        centers_copy(shift).start()
    centers_in[me] = centers_own[...]
    for shift in range(1, size):
        centers_copy(shift).wait()
    centers_own[...] = jnp.sum(centers_in[...], 0) * (1.0 / model_width)

    @pl.loop(0, length // block)
    def _(step):
        rows = pl.ds(pl.multiple_of(step * block, block), block)
        for index, pick in ((0, first_row), (1, second_row)):
            inverse = lax.rsqrt(column_of(sums_ref[:, rows], pick) / model_width + EPSILON)
            center = column_of(centers_own[:, rows], pick)
            raw_grads[index, rows, :] = (
                inverse * (scaled[index, rows, :] - unit_ref[index, rows, :] * center)
            ).astype(half)

    reduce = ChainReduce(chips, input_grad_ref, reduce_buffers)

    def product(index, store):
        rows = pl.ds(pl.multiple_of(index * tok_rows, tok_rows), tok_rows)

        @pl.loop(0, model_width // width_step)
        def _(step):
            cols = pl.ds(pl.multiple_of(step * width_step, width_step), width_step)
            total = cross_dot(raw_grads[0, rows, :], qkv_ref[0, cols, :])
            total += cross_dot(raw_grads[1, rows, :], qkv_ref[1, cols, :])
            total += cross_dot(raw_grads[2, rows, :], qkv_ref[2, cols, :])
            store(cols, total)

    qkv_keep = pltpu.make_async_copy(qkv_stage, qkv_out, load_sem.at[1])

    def between():
        normed_load.wait()

        @pl.loop(0, split)
        def _(piece):
            cols = pl.ds(pl.multiple_of(piece * part, part), part)
            left = out_grads[:, cols]
            for index in range(3):
                qkv_stage[piece, index] = turned_dot(left, raw_grads[index]).astype(half)

        qkv_keep.start()

    reduce.run(product, between)

    inputs = tokens_ref[...].astype(f32)
    inverse = lax.rsqrt(jnp.mean(inputs * inputs, -1, keepdims=True) + EPSILON)
    unit = inputs * inverse
    grads = input_grad_ref[...]
    gains_out_ref[0:1, :] = jnp.sum(grads * unit, 0, keepdims=True)
    grads = grads * gains_ref[0:1, :]
    input_grad_ref[...] = residual_grad_ref[...] + inverse * (
        grads - unit * jnp.mean(grads * unit, -1, keepdims=True)
    )

    out_send_all.wait()
    total = out_landing[0].astype(f32)
    for index in range(1, split):
        total += out_landing[index].astype(f32)
    out_w_grad_ref[...] = total
    qkv_keep.wait()
    reduce.sent()
    own_rows.wait()
    for move in range(1, experts_local):
        rows_copy(move).wait()
    gate_send_all.wait()


def back(sizes, out_grad, small, kept, big_ones, which):
    size, split, chips, experts_local = sizes
    f32, half = jnp.float32, jnp.bfloat16
    tok_rows, model_width = out_grad.shape
    length, local_width = kept[1].shape
    normed_seq, hidden, down_full, grad_gate = big_ones
    hidden_width = down_full.shape[0]
    part = model_width // split
    vmem = pl.BlockSpec(memory_space=pltpu.VMEM)
    anywhere = pl.BlockSpec(memory_space=pl.ANY)
    kind = pltpu.SemaphoreType.DMA
    shape = jax.ShapeDtypeStruct
    few, fsdp = kind((experts_local,)), kind((split,))
    return pl.pallas_call(
        functools.partial(back_kernel, sizes),
        out_shape=(
            shape((tok_rows, model_width), f32),
            shape((8, model_width), f32),
            shape((local_width, part), f32),
            shape((size // 2, experts_local * 2 * CAP, model_width), half),
            shape((split, part, hidden_width), half),
            shape((split, 3, part, local_width), half),
        ),
        in_specs=[vmem] * 5 + [anywhere] * (len(kept) + 4),
        out_specs=tuple([vmem] * 3 + [anywhere] * 3),
        scratch_shapes=[
            *[pltpu.VMEM(one.shape, one.dtype) for one in kept],
            pltpu.VMEM(down_full.shape, half),
            pltpu.VMEM((length, model_width), half),
            pltpu.VMEM((length, local_width), half),
            pltpu.VMEM(hidden.shape, half),
            pltpu.VMEM((experts_local, size // 2, 2 * CAP, model_width), half),
            pltpu.VMEM((length, HEAD_DIM), f32),
            pltpu.VMEM((length, HEAD_DIM), f32),
            pltpu.VMEM((2, length, local_width), f32),
            pltpu.VMEM((3, length, local_width), half),
            pltpu.VMEM((8, length), f32),
            pltpu.VMEM((size, 8, length), f32),
            pltpu.VMEM((split, 3, part, local_width), half),
            pltpu.VMEM((split, local_width, part), half),
            pltpu.VMEM((split, local_width, part), half),
            kind((2,)),
            kind,
            kind((3, chips)),
            kind((2, chips)),
            kind,
            fsdp,
            fsdp,
            kind,
            few,
            few,
            kind((size,)),
            kind((size,)),
            kind((len(kept),)),
            kind,
            fsdp,
            fsdp,
            *ChainReduce.scratch(chips, tok_rows, model_width),
        ],
        compiler_params=pltpu.CompilerParams(
            collective_id=which, has_side_effects=True, vmem_limit_bytes=63 * 2**20
        ),
        cost_estimate=pl.CostEstimate(
            flops=2 * length * model_width * local_width * 8,
            bytes_accessed=500 * 2**20,
            transcendentals=0,
        ),
    )(out_grad, *small, *kept, *big_ones)


def close_kernel(
    sizes,
    onehot_ref,
    gains_ref,
    router_ref,
    mixed_rows_any,
    residual_any,
    qkv_any,
    grad_up_ref,
    output_ref,
    gains_out_ref,
    router_out_ref,
    query_w_grad_ref,
    key_w_grad_ref,
    value_w_grad_ref,
    up_landing,
    mixed_rows_ref,
    residual_ref,
    qkv_ref,
    qkv_in,
    qkv_sum,
    load_sem,
    qkv_send,
    qkv_recv,
    total,
    small,
    first,
    second,
    final,
    up_local,
    up_send,
    up_recv,
    send_one,
    recv_one,
    send_two,
    recv_two,
    send_three,
    recv_three,
    *reduce_buffers,
):
    size, split, chips, experts_local = sizes
    f32 = jnp.float32
    me, mine = lax.axis_index("seq"), lax.axis_index("fsdp")
    tok_rows, model_width = residual_ref.shape
    part = model_width // split
    slice_width = model_width // size
    experts_all = router_ref.shape[0]
    loads = [
        pltpu.make_async_copy(source, target, load_sem.at[index])
        for index, (source, target) in enumerate(
            ((qkv_any, qkv_ref), (mixed_rows_any, mixed_rows_ref), (residual_any, residual_ref))
        )
    ]
    for load in loads:
        load.start()
    small[0:8, :] = gains_ref[...]
    small[8 : 8 + experts_all, :] = router_ref[...]
    greet_all(size, split)
    up_send_all = ShardSend(
        split,
        lambda dest: grad_up_ref.at[pl.ds(pl.multiple_of(dest * part, part), part)],
        up_landing,
        up_local,
        up_send,
        up_recv,
    )
    loads[0].wait()

    half_part = qkv_ref.shape[2] // 2
    lower, upper = pl.ds(0, half_part), pl.ds(half_part, half_part)
    mates = (partner_of(mine, 1), partner_of(mine, 2), partner_of(mine, 3)) if split == 4 else ()

    def qkv_copy(index):
        side = index % 2
        rows = (lower, upper)[side]
        if index < 4:
            dest = mates[side] if index < 2 else mates[2]
            source, mate = qkv_ref.at[dest, :, rows], mates[side]
        else:
            source, mate = qkv_sum.at[side], mates[1 - side]
        return pltpu.make_async_remote_copy(
            src_ref=source,
            dst_ref=qkv_in.at[index],
            send_sem=qkv_send.at[index],
            recv_sem=qkv_recv.at[index],
            device_id={"fsdp": mate},
        )

    def qkv_shift(shift):
        dest = lax.rem(mine + shift, split)
        return pltpu.make_async_remote_copy(
            src_ref=qkv_ref.at[dest],
            dst_ref=qkv_in.at[shift],
            send_sem=qkv_send.at[shift],
            recv_sem=qkv_recv.at[shift],
            device_id={"fsdp": dest},
        )

    if split == 4:
        for index in range(4):
            qkv_copy(index).start()
    else:
        for shift in range(1, split):
            qkv_shift(shift).start()
    up_send_all.start()

    def columns(index):
        return pl.ds(pl.multiple_of(index * slice_width, slice_width), slice_width)

    def scatter(shift):
        peer = lax.rem(me + shift, size)
        return pltpu.make_async_remote_copy(
            src_ref=small.at[:, columns(peer)],
            dst_ref=first.at[me],
            send_sem=send_one.at[shift],
            recv_sem=recv_one.at[shift],
            device_id={"seq": peer},
        )

    def share(shift):
        return pltpu.make_async_remote_copy(
            src_ref=second.at[mine],
            dst_ref=second.at[mine],
            send_sem=send_two.at[shift],
            recv_sem=recv_two.at[shift],
            device_id={"fsdp": lax.rem(mine + shift, split)},
        )

    def collect(shift):
        return pltpu.make_async_remote_copy(
            src_ref=final.at[me],
            dst_ref=final.at[me],
            send_sem=send_three.at[shift],
            recv_sem=recv_three.at[shift],
            device_id={"seq": lax.rem(me + shift, size)},
        )

    for shift in range(1, size):
        scatter(shift).start()
    first[me] = small[:, columns(me)]

    reduce = ChainReduce(chips, total, reduce_buffers)
    width_step = min(512, model_width)

    def product(index, store):
        side = pl.ds(pl.multiple_of(lax.rem(index, 2) * tok_rows, tok_rows), tok_rows)
        left = onehot_ref[index // 2, :, side]

        @pl.loop(0, model_width // width_step)
        def _(step):
            cols = pl.ds(pl.multiple_of(step * width_step, width_step), width_step)
            store(cols, turned_dot(left, mixed_rows_ref[index // 2, :, cols]))

    def between():
        for shift in range(1, size):
            scatter(shift).wait_recv()
        second[mine] = jnp.sum(first[...], 0)
        for shift in range(1, split):
            share(shift).start()

    loads[1].wait()
    reduce.run(product, between)
    if split == 4:
        for side in range(2):
            qkv_copy(2 + side).wait_recv()
            rows = (lower, upper)[side]
            qkv_sum[side] = (
                qkv_ref[mates[1 - side], :, rows].astype(f32) + qkv_in[2 + side].astype(f32)
            ).astype(qkv_sum.dtype)
            qkv_copy(4 + side).start()
    loads[2].wait()
    for shift in range(1, split):
        share(shift).wait_recv()
    final[me] = jnp.sum(second[...], 0)
    for shift in range(1, size):
        collect(shift).start()
    output_ref[...] = (residual_ref[...] + total[...]).astype(output_ref.dtype)
    for shift in range(1, size):
        scatter(shift).wait_send()
    for shift in range(1, split):
        share(shift).wait_send()
    for shift in range(1, size):
        collect(shift).wait()
    for index in range(size):
        cols = slice(index * slice_width, (index + 1) * slice_width)
        gains_out_ref[:, cols] = final[index, 0:4]
        router_out_ref[:, cols] = final[index, 8:]
    targets = (query_w_grad_ref, key_w_grad_ref, value_w_grad_ref)
    if split == 4:
        for side in range(2):
            for index in (side, 2 + side, 5 - side):
                copy = qkv_copy(index)
                copy.wait() if index < 2 or index > 3 else copy.wait_send()
        for side in range(2):
            rows = (lower, upper)[side]
            for index, target in enumerate(targets):
                target[rows, :] = (
                    qkv_ref[mine, index, rows].astype(f32)
                    + qkv_in[side, index].astype(f32)
                    + qkv_in[4 + side, index].astype(f32)
                )
    else:
        for shift in range(1, split):
            qkv_shift(shift).wait()
        for index, target in enumerate(targets):
            sums = qkv_ref[mine, index].astype(f32)
            for shift in range(1, split):
                sums += qkv_in[shift, index].astype(f32)
            target[...] = sums
    reduce.sent()
    up_send_all.wait()


def close(sizes, onehot, gains, router_grad, mixed_rows, residual, qkv_parts, grad_up, which):
    size, split, chips, experts_local = sizes
    f32, half = jnp.float32, jnp.bfloat16
    tok_rows, model_width = residual.shape
    hidden_width = grad_up.shape[1]
    part, slice_width = model_width // split, model_width // size
    rows = 8 + router_grad.shape[0]
    vmem = pl.BlockSpec(memory_space=pltpu.VMEM)
    anywhere = pl.BlockSpec(memory_space=pl.ANY)
    kind = pltpu.SemaphoreType.DMA
    shape = jax.ShapeDtypeStruct
    seq, fsdp = kind((size,)), kind((split,))
    share = qkv_parts.shape[2:]
    return pl.pallas_call(
        functools.partial(close_kernel, sizes),
        out_shape=(
            shape((tok_rows, model_width), half),
            shape((4, model_width), f32),
            shape(router_grad.shape, f32),
            shape(share, f32),
            shape(share, f32),
            shape(share, f32),
            shape((split, part, hidden_width), half),
        ),
        in_specs=[vmem] * 3 + [anywhere] * 4,
        out_specs=tuple([vmem] * 6 + [anywhere]),
        scratch_shapes=[
            pltpu.VMEM(mixed_rows.shape, half),
            pltpu.VMEM(residual.shape, f32),
            pltpu.VMEM(qkv_parts.shape, half),
            pltpu.VMEM((6, 3, share[0] // 2, share[1]) if split == 4 else qkv_parts.shape, half),
            pltpu.VMEM((2, 3, share[0] // 2, share[1]), half),
            kind((3,)),
            kind((max(6, split),)),
            kind((max(6, split),)),
            pltpu.VMEM((tok_rows, model_width), f32),
            pltpu.VMEM((rows, model_width), f32),
            pltpu.VMEM((size, rows, slice_width), f32),
            pltpu.VMEM((split, rows, slice_width), f32),
            pltpu.VMEM((size, rows, slice_width), f32),
            kind,
            fsdp,
            fsdp,
            seq,
            seq,
            fsdp,
            fsdp,
            seq,
            seq,
            *ChainReduce.scratch(chips, tok_rows, model_width),
        ],
        compiler_params=pltpu.CompilerParams(
            collective_id=which, has_side_effects=True, vmem_limit_bytes=56 * 2**20
        ),
    )(onehot, gains, router_grad, mixed_rows, residual, qkv_parts, grad_up)


def finish_kernel(count, *refs):
    sources, targets = refs[: len(refs) // 2], refs[len(refs) // 2 :]
    for source, target in zip(sources[:count], targets[:count]):
        target[...] = source[...]
    for source, target in zip(sources[count:], targets[count:]):
        total = source[0].astype(target.dtype)
        for index in range(1, source.shape[0]):
            total += source[index].astype(target.dtype)
        target[...] = total


def finish(results, landings, experts_local):
    halves = 1
    steps = experts_local * halves
    in_specs, out_specs, shapes = [], [], []
    for one in results:
        rows = one.shape[0] // steps
        spec = pl.BlockSpec((rows, one.shape[1]), lambda step: (step, 0))
        if one.shape[0] % (steps * 16):
            spec = pl.BlockSpec(one.shape, lambda step: (0, 0))
        in_specs.append(spec)
        out_specs.append(spec)
        shapes.append(jax.ShapeDtypeStruct(one.shape, one.dtype))
    grouped = []
    for one in landings:
        groups = one.shape[0] // experts_local
        grouped.append(one.reshape(groups, experts_local, *one.shape[1:]))
        block = (one.shape[1] // halves, one.shape[2])
        in_specs.append(
            pl.BlockSpec(
                (groups, 1, *block), lambda step: (0, step // halves, step % halves, 0)
            )
        )
        out_specs.append(
            pl.BlockSpec((1, *block), lambda step: (step // halves, step % halves, 0))
        )
        shapes.append(jax.ShapeDtypeStruct((experts_local, *one.shape[1:]), jnp.float32))
    return pl.pallas_call(
        functools.partial(finish_kernel, len(results)),
        grid=(steps,),
        in_specs=in_specs,
        out_specs=out_specs,
        out_shape=shapes,
        compiler_params=pltpu.CompilerParams(vmem_limit_bytes=63 * 2**20),
    )(*results, *grouped)


def shards(
    tokens,
    norm_gains,
    w_query,
    w_key,
    w_value,
    w_out,
    w_router,
    w_gate,
    w_up,
    w_down,
    segment_ids,
    expert_ids,
    expert_slots,
    cotangent,
):
    half_type = jnp.bfloat16
    model_width = tokens.shape[1]
    experts_local = w_gate.shape[0]
    seq_size = lax.axis_size("seq")
    split = lax.axis_size("fsdp")
    length = seq_size * tokens.shape[0]
    sizes = (seq_size, split, seq_size // 2, experts_local)
    cosine_wide, sine_wide = rope_tables(length, HEAD_DIM)
    segment_row = segment_ids.reshape(1, -1)
    (
        normed_seq,
        qkv_stack,
        out_stack,
        query_heads,
        key_heads,
        value_heads,
        unit_pair,
        log_wide,
        attended_heads,
        square_sums,
        residual,
        gain_rows,
        segment_cols,
        routed_seq,
        routed_cross,
        placed,
        gate_full,
        up_full,
        down_full,
        choices,
        onehot,
        mate_onehot,
    ) = front(
        sizes,
        tokens,
        norm_gains,
        cosine_wide,
        sine_wide,
        segment_row,
        expert_ids.T,
        expert_slots.T,
        cotangent,
        (w_query, w_key, w_value, w_out, w_gate, w_up, w_down),
        0,
    )
    router_rows = jnp.zeros((seq_size, 8, model_width), half_type)
    router_rows = router_rows.at[:, :experts_local].set(
        w_router.T.reshape(seq_size, experts_local, model_width)
    )
    router_rows = router_rows.reshape(seq_size * 8, model_width)
    (
        residual_grad,
        out_grad,
        gain_second_grad,
        router_grad,
        hidden,
        grad_gate_full,
        grad_up_full,
        down_landing,
        _,
    ) = experts(
        sizes,
        routed_seq,
        routed_cross,
        choices,
        onehot,
        mate_onehot,
        placed,
        router_rows,
        gain_rows,
        residual,
        cotangent,
        (gate_full, up_full, down_full),
        1,
    )
    input_grad, gain_grads, out_owned, mixed_rows, gate_landing, qkv_parts = back(
        sizes,
        out_grad,
        (gain_rows, gain_second_grad, segment_row, square_sums),
        (
            out_stack,
            attended_heads,
            query_heads,
            key_heads,
            value_heads,
            segment_cols,
            log_wide,
            cosine_wide,
            sine_wide,
            unit_pair,
            qkv_stack,
            tokens,
            residual_grad,
        ),
        (normed_seq, hidden, down_full, grad_gate_full),
        2,
    )
    output, gain_sums, router_sums, query_owned, key_owned, value_owned, up_landing = close(
        sizes, onehot, gain_grads, router_grad, mixed_rows, residual, qkv_parts, grad_up_full, 3
    )
    (
        output,
        input_grad,
        gain_sums,
        query_owned,
        key_owned,
        value_owned,
        out_owned,
        router_sums,
        gate_owned,
        up_owned,
        down_owned,
    ) = finish(
        (
            output,
            input_grad,
            gain_sums,
            query_owned,
            key_owned,
            value_owned,
            out_owned,
            router_sums,
        ),
        (gate_landing, up_landing, down_landing),
        experts_local,
    )
    return (
        output,
        input_grad,
        gain_sums,
        query_owned,
        key_owned,
        value_owned,
        out_owned,
        router_sums.T,
        gate_owned,
        up_owned,
        down_owned,
    )


def solution(mesh):
    in_specs = (
        P(("fsdp", "seq"), None),
        P(),
        P("fsdp", "seq"),
        P("fsdp", "seq"),
        P("fsdp", "seq"),
        P("seq", "fsdp"),
        P(),
        P("seq", "fsdp", None),
        P("seq", "fsdp", None),
        P("seq", None, "fsdp"),
        P("fsdp"),
        P(("fsdp", "seq"), None),
        P(("fsdp", "seq"), None),
        P(("fsdp", "seq"), None),
    )
    out_specs = (
        P(("fsdp", "seq"), None),
        P(("fsdp", "seq"), None),
        P(),
        P("fsdp", "seq"),
        P("fsdp", "seq"),
        P("fsdp", "seq"),
        P("seq", "fsdp"),
        P(),
        P("seq", "fsdp", None),
        P("seq", "fsdp", None),
        P("seq", None, "fsdp"),
    )
    return jax.shard_map(shards, mesh=mesh, in_specs=in_specs, out_specs=out_specs, check_vma=False)
```

```python
import functools

import jax
import jax.numpy as jnp
import numpy as np
from jax import lax
from jax.experimental import pallas as pl
from jax.experimental.pallas import tpu as pltpu
from jax.sharding import PartitionSpec as P

HEAD_DIM = 128
CAP = 40


EPSILON = 1e-06
THETA = 10000.0
MASKED = -1e30
HIGHEST = lax.Precision.HIGHEST


def rope_tables(length, head_size):
    half_dim = head_size // 2
    frequency = THETA ** (-np.arange(half_dim, dtype=np.float64) / half_dim)
    angles = np.arange(length, dtype=np.float64)[:, None] * frequency.astype(np.float32)
    cosine, sine = np.cos(angles), np.sin(angles)
    return (
        jnp.asarray(np.concatenate([cosine, cosine], 1), jnp.float32),
        jnp.asarray(np.concatenate([-sine, sine], 1), jnp.float32),
    )


class ChainGather:
    def __init__(self, chips, x_ref, out_ref, local_sem, sends, arrivals):
        self.chips, self.x_ref, self.out_ref = chips, x_ref, out_ref
        self.local_sem, self.sends, self.arrivals = local_sem, sends, arrivals
        me = lax.axis_index("seq")
        self.chip, self.core = me // 2, lax.rem(me, 2)
        self.rows = x_ref.shape[0]

    def block(self, source, core):
        start = pl.multiple_of((source * 2 + core) * self.rows, self.rows)
        return self.out_ref.at[pl.ds(start, self.rows)]

    def hop(self, source, ref, target, way, lane):
        return pltpu.make_async_remote_copy(
            src_ref=ref,
            dst_ref=self.block(source, self.core),
            send_sem=self.sends.at[way, source],
            recv_sem=self.arrivals.at[lane, source],
            device_id={"seq": target},
        )

    def upward(self, source, ref):
        return self.hop(source, ref, self.chip * 2 + 2 + self.core, 0, 0)

    def downward(self, source, ref):
        return self.hop(source, ref, self.chip * 2 - 2 + self.core, 1, 0)

    def sideways(self, source, ref):
        return self.hop(source, ref, self.chip * 2 + 1 - self.core, 2, 1)

    def own(self):
        return pltpu.make_async_copy(
            self.x_ref, self.block(self.chip, self.core), self.local_sem
        )

    def start(self):
        @pl.when(self.chip < self.chips - 1)
        def _():
            self.upward(self.chip, self.x_ref).start()

        @pl.when(self.chip > 0)
        def _():
            self.downward(self.chip, self.x_ref).start()

        self.sideways(self.chip, self.x_ref).start()
        self.own().start()

    def step(self, distance):
        below, above = self.chip - distance, self.chip + distance

        @pl.when(below >= 0)
        def _():
            landed = self.block(below, self.core)
            self.upward(below, landed).wait_recv()

            @pl.when(self.chip < self.chips - 1)
            def _():
                self.upward(below, landed).start()

            self.sideways(below, landed).start()

        @pl.when(above < self.chips)
        def _():
            landed = self.block(above, self.core)
            self.downward(above, landed).wait_recv()

            @pl.when(self.chip > 0)
            def _():
                self.downward(above, landed).start()

            self.sideways(above, landed).start()

    def steps(self):
        for distance in range(1, self.chips):
            self.step(distance)

    def landed(self):
        self.own().wait()
        for source in range(self.chips):
            self.sideways(source, self.block(source, self.core)).wait_recv()

    def sent(self):
        for source in range(self.chips):
            ref = self.block(source, self.core)
            self.sideways(source, ref).wait_send()

            @pl.when((self.chip < self.chips - 1) & (source <= self.chip))
            def _():
                self.upward(source, ref).wait_send()

            @pl.when((self.chip > 0) & (source >= self.chip))
            def _():
                self.downward(source, ref).wait_send()


class ChainReduce:
    def __init__(self, chips, total, buffers):
        self.total = total
        (
            self.side_out,
            self.side_in,
            self.chain_in,
            self.side_send,
            self.side_recv,
            self.chain_send,
            self.chain_recv,
        ) = buffers
        self.chips = chips
        me = lax.axis_index("seq")
        self.chip, self.core = me // 2, lax.rem(me, 2)

    @staticmethod
    def scratch(chips, rows, width):
        half = jnp.bfloat16
        return [
            pltpu.VMEM((chips, rows, width), half),
            pltpu.VMEM((chips, rows, width), half),
            pltpu.VMEM((chips + 1, rows, width), half),
            pltpu.SemaphoreType.DMA((chips,)),
            pltpu.SemaphoreType.DMA((chips,)),
            pltpu.SemaphoreType.DMA((chips,)),
            pltpu.SemaphoreType.DMA((2, chips)),
        ]

    def side_copy(self, dest):
        return pltpu.make_async_remote_copy(
            src_ref=self.side_out.at[dest],
            dst_ref=self.side_in.at[dest],
            send_sem=self.side_send.at[dest],
            recv_sem=self.side_recv.at[dest],
            device_id={"seq": self.chip * 2 + 1 - self.core},
        )

    def chain_copy(self, way, dest, target):
        return pltpu.make_async_remote_copy(
            src_ref=self.side_out.at[dest],
            dst_ref=self.chain_in.at[self.slot(way, dest, target // 2)],
            send_sem=self.chain_send.at[dest],
            recv_sem=self.chain_recv.at[way, dest],
            device_id={"seq": target},
        )

    def slot(self, way, dest, holder):
        return jnp.where(dest == holder, self.chips, dest) if way else dest

    def place(self, index):
        distance = self.chips - 1 - index // 2
        dest = self.chip + (1 - 2 * lax.rem(index, 2)) * distance
        return dest, (dest >= 0) & (dest < self.chips)

    def run(self, product, between=None, hook=None):
        chips, chip, core, total = self.chips, self.chip, self.core, self.total
        sibling = chip * 2 + 1 - core

        @pl.loop(0, 2 * chips - 1)
        def _(index):
            dest, inside = self.place(index)

            @pl.when(inside)
            def _():
                def store(cols, part):
                    self.side_out[dest, :, cols] = part.astype(self.side_out.dtype)

                product(dest * 2 + 1 - core, store)
                self.side_copy(dest).start()

        if between:
            between()

        @pl.loop(0, 2 * chips - 1)
        def _(index):
            dest, inside = self.place(index)
            if hook:
                hook(index)

            @pl.when(inside)
            def _():
                def store(cols, part):
                    total[:, cols] = part

                product(dest * 2 + core, store)
                self.side_copy(dest).wait_recv()
                total[...] += self.side_in[dest].astype(jnp.float32)

                @pl.when((dest >= chip) & (chip > 0))
                def _():
                    self.chain_copy(0, dest, sibling).wait_recv()
                    total[...] += self.chain_in[dest].astype(jnp.float32)

                @pl.when((dest <= chip) & (chip < chips - 1))
                def _():
                    self.chain_copy(1, dest, sibling).wait_recv()
                    total[...] += self.chain_in[self.slot(1, dest, chip)].astype(jnp.float32)

                self.side_copy(dest).wait_send()

                @pl.when(dest != chip)
                def _():
                    self.side_out[dest] = total[...].astype(self.side_out.dtype)

                @pl.when(dest > chip)
                def _():
                    self.chain_copy(0, dest, chip * 2 + 2 + core).start()

                @pl.when(dest < chip)
                def _():
                    self.chain_copy(1, dest, chip * 2 - 2 + core).start()

    def sent(self):
        sibling = self.chip * 2 + 1 - self.core

        @pl.loop(0, self.chips)
        def _(dest):
            @pl.when(dest != self.chip)
            def _():
                self.chain_copy(0, dest, sibling).wait_send()


def partner_of(index, move):
    turned, bit = index, 1
    while bit <= move:
        if move // bit % 2:
            turned = turned + bit - 2 * bit * lax.rem(index // bit, 2)
        bit *= 2
    return turned


def greet_all(size, split):
    me, mine = lax.axis_index("seq"), lax.axis_index("fsdp")
    barrier = pltpu.get_barrier_semaphore()
    for shift in range(1, size):
        pl.semaphore_signal(barrier, inc=1, device_id={"seq": lax.rem(me + shift, size)})
    for shift in range(1, split):
        pl.semaphore_signal(barrier, inc=1, device_id={"fsdp": lax.rem(mine + shift, split)})
    pl.semaphore_wait(barrier, size + split - 2)


def turned_halves(head):
    return pltpu.roll(head, head.shape[-1] // 2, 1)


def row_sums(values, pick):
    return lax.dot_general(
        pick, values, (((1,), (1,)), ((), ())), precision=HIGHEST, preferred_element_type=jnp.float32
    )


def column_of(row_form, pick):
    return lax.dot_general(
        row_form, pick, (((0,), (0,)), ((), ())), precision=HIGHEST, preferred_element_type=jnp.float32
    )


def front_kernel(
    sizes,
    tokens_ref,
    gains_in_ref,
    cos_ref,
    sin_ref,
    seg_row_ref,
    ids_ref,
    slots_ref,
    cotangent_ref,
    wq_ref,
    wk_ref,
    wv_ref,
    wo_ref,
    w_gate_ref,
    w_up_ref,
    w_down_ref,
    normed_out,
    qkv_out,
    rows_out,
    q_out,
    k_out,
    v_out,
    unit_out,
    log_out,
    attended_out,
    sums_ref,
    residual_out,
    gains_ref,
    seg_col_ref,
    routed_out,
    routed_cross,
    placed_out,
    gate_full,
    up_full,
    down_full,
    choices,
    onehot_ref,
    mate_onehot,
    residual_ref,
    q_ref,
    k_ref,
    v_ref,
    unit_ref,
    log_ref,
    attended_ref,
    normed,
    qkv,
    rows_full,
    routed_own,
    choice_own,
    cotangent_pair,
    cotangent_all,
    mate_choices,
    placed,
    raw,
    sums_own,
    sums_in,
    gather_local,
    gather_send,
    gather_recv,
    sums_send,
    sums_recv,
    choice_send,
    choice_recv,
    mate_send,
    mate_recv,
    cross_local,
    cross_send,
    cross_recv,
    placed_local,
    shard_local,
    shard_send,
    shard_recv,
    expert_local,
    expert_send,
    expert_recv,
    out_sem,
    *reduce_buffers,
):
    size, split, chips, experts_local = sizes
    f32, half = jnp.float32, jnp.bfloat16
    me, mine = lax.axis_index("seq"), lax.axis_index("fsdp")
    tok_rows, model_width = tokens_ref.shape
    length, local_width = q_ref.shape
    part = model_width // split
    head = HEAD_DIM
    heads = local_width // head

    inputs = tokens_ref[...].astype(f32)
    inverse = lax.rsqrt(jnp.mean(inputs * inputs, -1, keepdims=True) + EPSILON)
    gains_ref[...] = gains_in_ref[...].astype(f32)
    routed_half = routed_own.at[pl.ds(0, tok_rows)]
    routed_half[...] = (inputs * inverse * gains_ref[0:1, :]).astype(half)
    crossed = split == experts_local == 4
    half_width = model_width // 2
    x_mate, y_mate = {"fsdp": partner_of(mine, 1)}, {"fsdp": partner_of(mine, 2)}
    greet_all(size, split)

    def gather(index, x_ref, out_ref):
        return ChainGather(
            chips,
            x_ref,
            out_ref,
            gather_local.at[index],
            gather_send.at[index],
            gather_recv.at[index],
        )

    first = gather(0, routed_half, normed)
    first.start()

    cross_rows = pl.ds(tok_rows, tok_rows)
    lower, upper = pl.ds(0, half_width), pl.ds(half_width, half_width)

    def cross_copy(index):
        cols = (lower, upper)[index % 2]
        source, target = (
            (cotangent_ref, cotangent_pair) if index < 2 else (routed_half, routed_own)
        )
        return pltpu.make_async_remote_copy(
            src_ref=source.at[:, cols],
            dst_ref=target.at[cross_rows, cols],
            send_sem=cross_send.at[index],
            recv_sem=cross_recv.at[index],
            device_id=(x_mate, y_mate)[index % 2],
        )

    if crossed:
        cross_own = pltpu.make_async_copy(
            cotangent_ref, cotangent_pair.at[pl.ds(0, tok_rows)], cross_local
        )
        cross_copy(0).start()
        cross_copy(1).start()
        cross_own.start()

    top_count = ids_ref.shape[0]
    ids_row, slots_row = ids_ref[...], slots_ref[...]
    choice_own[0:top_count, :] = ids_row
    choice_own[top_count : 2 * top_count, :] = jnp.where(
        slots_row < CAP, ids_row * CAP + slots_row, -(10**6)
    )

    def choice_copy(shift):
        return pltpu.make_async_remote_copy(
            src_ref=choice_own,
            dst_ref=choices.at[me],
            send_sem=choice_send.at[shift],
            recv_sem=choice_recv.at[shift],
            device_id={"seq": lax.rem(me + shift, size)},
        )

    own_part = pl.ds(pl.multiple_of(mine * part, part), part)
    shard_pairs = (
        (wq_ref, qkv.at[0, own_part]),
        (wk_ref, qkv.at[1, own_part]),
        (wv_ref, qkv.at[2, own_part]),
        (wo_ref, rows_full.at[mine]),
    )

    def shard_copy(index, shift):
        source, target = shard_pairs[index]
        return pltpu.make_async_remote_copy(
            src_ref=source,
            dst_ref=target,
            send_sem=shard_send.at[index, shift],
            recv_sem=shard_recv.at[index, shift],
            device_id={"fsdp": lax.rem(mine + shift, split)},
        )

    def landed_half(index, owner, side):
        if index == 3:
            rows = local_width // 2
            return rows_full.at[owner, pl.ds(side * rows, rows)]
        rows = part // 2
        start = pl.multiple_of(owner * part + side * rows, rows)
        return qkv.at[index, pl.ds(start, rows)]

    def relay_copy(index, step):
        if step < 2:
            source, target = shard_pairs[index]
        else:
            source = target = landed_half(index, partner_of(mine, step - 1), step - 2)
        return pltpu.make_async_remote_copy(
            src_ref=source,
            dst_ref=target,
            send_sem=shard_send.at[index, step],
            recv_sem=shard_recv.at[index, step],
            device_id=(x_mate, y_mate, y_mate, x_mate)[step],
        )

    def shard_own(index):
        source, target = shard_pairs[index]
        return pltpu.make_async_copy(source, target, shard_local.at[index])

    for index in range(4):
        if split == 4:
            relay_copy(index, 0).start()
            relay_copy(index, 1).start()
        else:
            for shift in range(1, split):
                shard_copy(index, shift).start()
        shard_own(index).start()

    def expert_pair(index, dest):
        expert = lax.rem(dest, experts_local)
        if index == 2:
            return w_down_ref.at[expert], down_full.at[:, own_part]
        source, target = ((w_gate_ref, gate_full), (w_up_ref, up_full))[index]
        return source.at[expert], target.at[own_part]

    def expert_copy(index, shift):
        dest = lax.rem(mine + shift, split)
        source, target = expert_pair(index, dest)
        return pltpu.make_async_remote_copy(
            src_ref=source,
            dst_ref=target,
            send_sem=expert_send.at[index, shift],
            recv_sem=expert_recv.at[index, shift],
            device_id={"fsdp": dest},
        )

    def expert_own(index):
        source, target = expert_pair(index, mine)
        return pltpu.make_async_copy(source, target, expert_local.at[index])

    for distance in range(1, chips):
        first.step(distance)
        if split == 4 and distance == min(2, chips - 1):
            for index in range(4):
                for step in range(2):
                    relay_copy(index, step).wait_recv()
                    relay_copy(index, step + 2).start()
    for index in range(4):
        shard_own(index).wait()
        if split == 4:
            relay_copy(index, 2).wait_recv()
            relay_copy(index, 3).wait_recv()
        else:
            for shift in range(1, split):
                shard_copy(index, shift).wait_recv()

    def expert_start(index):
        for shift in range(1, split):
            expert_copy(index, shift).start()
        expert_own(index).start()

    expert_start(0)
    first.landed()
    for shift in range(1, size):
        choice_copy(shift).start()
    choices[me] = choice_own[...]
    if crossed:
        cross_own.wait()
        cross_copy(0).wait()
        cross_copy(1).wait()
        second = gather(1, cotangent_pair, cotangent_all)
    else:
        second = gather(1, cotangent_ref, cotangent_all)
    second.start()
    keeps = [
        pltpu.make_async_copy(normed, normed_out, out_sem.at[0]),
        pltpu.make_async_copy(qkv, qkv_out, out_sem.at[1]),
        pltpu.make_async_copy(rows_full, rows_out, out_sem.at[2]),
    ]
    for keep in keeps:
        keep.start()

    own_cols = pl.ds(pl.multiple_of(me * local_width, local_width), local_width)
    block = min(512, length)
    lanes = lax.broadcasted_iota(jnp.int32, (8, local_width), 0)
    first_row, second_row = (lanes == 0).astype(f32), (lanes == 1).astype(f32)

    @pl.loop(0, length // block)
    def _(step):
        rows = pl.ds(pl.multiple_of(step * block, block), block)
        left = normed[rows, :]
        query = jnp.dot(left, qkv[0], preferred_element_type=f32)
        raw[0, rows, :] = query
        keys = jnp.dot(left, qkv[1], preferred_element_type=f32)
        raw[1, rows, :] = keys
        sums_own[:, rows] = row_sums(query * query, first_row) + row_sums(keys * keys, second_row)
        v_ref[rows, :] = jnp.dot(left, qkv[2], preferred_element_type=f32).astype(half)

    def sums_copy(shift):
        return pltpu.make_async_remote_copy(
            src_ref=sums_own,
            dst_ref=sums_in.at[me],
            send_sem=sums_send.at[shift],
            recv_sem=sums_recv.at[shift],
            device_id={"seq": lax.rem(me + shift, size)},
        )

    for shift in range(1, size):
        sums_copy(shift).start()
    sums_in[me] = sums_own[...]
    for shift in range(1, size):
        sums_copy(shift).wait()
    sums_ref[...] = jnp.sum(sums_in[...], 0)
    for shift in range(1, size):
        choice_copy(shift).wait()

    def mate_copy(index):
        return pltpu.make_async_remote_copy(
            src_ref=choices,
            dst_ref=mate_choices.at[index],
            send_sem=mate_send.at[index],
            recv_sem=mate_recv.at[index],
            device_id=(x_mate, y_mate)[index],
        )

    if crossed:
        mate_copy(0).start()
        mate_copy(1).start()
    segments = seg_row_ref[...].astype(f32)
    narrow = first_row[:, 0:128]

    @pl.loop(0, length // block)
    def _(step):
        rows = pl.ds(pl.multiple_of(step * block, block), block)
        square_sums = sums_ref[:, rows]
        seg_col_ref[rows, :] = column_of(
            jnp.broadcast_to(seg_row_ref[:, rows].astype(f32), (8, block)), narrow
        )
        for index, pick, target in ((0, first_row, q_ref), (1, second_row, k_ref)):
            scale = lax.rsqrt(column_of(square_sums, pick) / model_width + EPSILON)
            unit = raw[index, rows, :] * scale
            unit_ref[index, rows, :] = unit
            scaled = unit * gains_ref[2 + index : 3 + index, own_cols]
            for number in range(heads):
                cols = slice(number * head, (number + 1) * head)
                piece = scaled[:, cols]
                target[rows, cols] = (
                    piece * cos_ref[rows, :] + turned_halves(piece) * sin_ref[rows, :]
                ).astype(half)

    second.step(1)

    wide = min(256, length)
    for number in range(heads):
        cols = slice(number * head, (number + 1) * head)

        @pl.loop(0, length // wide)
        def _(step):
            rows = pl.ds(pl.multiple_of(step * wide, wide), wide)
            scores = lax.dot_general(
                q_ref[rows, cols],
                k_ref[:, cols],
                (((1,), (1,)), ((), ())),
                preferred_element_type=f32,
            )
            scores = scores * (head**-0.5)
            scores = jnp.where(seg_col_ref[rows, 0:1] == segments, scores, MASKED)
            peak = jnp.max(scores, -1, keepdims=True)
            grown = jnp.exp(scores - peak)
            weight = jnp.sum(grown, -1, keepdims=True)
            probs = (grown * (1.0 / weight)).astype(half)
            attended_ref[rows, cols] = jnp.dot(
                probs, v_ref[:, cols], preferred_element_type=f32
            ).astype(half)
            log_ref[rows, cols] = jnp.broadcast_to(peak + jnp.log(weight), (wide, head))

    expert_start(1)
    for index, (source, target) in enumerate(
        (
            (q_ref, q_out),
            (k_ref, k_out),
            (v_ref, v_out),
            (unit_ref, unit_out),
            (log_ref, log_out),
            (attended_ref, attended_out),
        )
    ):
        keeps.append(pltpu.make_async_copy(source, target, out_sem.at[3 + index]))
        keeps[-1].start()

    reduce = ChainReduce(chips, residual_ref, reduce_buffers)

    def product(index, store):
        left = attended_ref[pl.ds(pl.multiple_of(index * tok_rows, tok_rows), tok_rows), :]
        for piece in range(split):
            cols = pl.ds(piece * part, part)
            store(cols, jnp.dot(left, rows_full[piece], preferred_element_type=f32))

    def hook(index):
        for distance in range(2, chips - 1):

            @pl.when(index == 2 * distance)
            def _():
                second.step(distance)

    reduce.run(product, hook=hook)
    residual = tokens_ref[...].astype(f32) + reduce.total[...]
    residual_ref[...] = residual
    keeps.append(pltpu.make_async_copy(residual_ref, residual_out, out_sem.at[9]))
    keeps[-1].start()
    inverse = lax.rsqrt(jnp.mean(residual * residual, -1, keepdims=True) + EPSILON)
    first.sent()
    routed_half[...] = (residual * inverse * gains_ref[1:2, :]).astype(half)
    if crossed:
        cross_copy(2).start()
        cross_copy(3).start()
    third = gather(2, routed_half, routed_out)
    third.start()
    if chips > 2:
        second.step(chips - 1)
    expert_start(2)

    second.landed()
    double = 2 * CAP
    member = lax.rem(mine, experts_local)
    slot_row = lax.broadcasted_iota(jnp.int32, (double, tok_rows), 0)
    if crossed:
        mate_copy(0).wait()
        mate_copy(1).wait()

    def one_hot(places, target, rows, expert):
        base = (me * experts_local + expert) * CAP
        for side in range(2):
            want = jnp.where(slot_row // CAP == side, slot_row - side * CAP + base, -1)
            hit = want == places(side)[top_count : top_count + 1, :]
            for choice in range(1, top_count):
                hit = hit | (want == places(side)[top_count + choice : top_count + choice + 1, :])
            cols = slice(side * tok_rows, (side + 1) * tok_rows)
            target[rows, cols] = jnp.where(hit, 1.0, 0.0).astype(half)

    def slot_range(move):
        return slice(move * double, (move + 1) * double)

    @pl.loop(0, size // 2)
    def _(pair):
        for move in range(experts_local):
            one_hot(
                lambda side: choices[pair * 2 + side],
                onehot_ref.at[pair],
                slot_range(move),
                partner_of(member, move),
            )
        if crossed:
            start = pl.multiple_of(pair * 4 * tok_rows, 4 * tok_rows)
            four = cotangent_all[pl.ds(start, 4 * tok_rows), :]
            own = jnp.concatenate(
                [four[0:tok_rows], four[2 * tok_rows : 3 * tok_rows]], 0
            )
            mates = jnp.concatenate(
                [four[tok_rows : 2 * tok_rows], four[3 * tok_rows : 4 * tok_rows]], 0
            )
            made = jnp.dot(onehot_ref[pair], own, preferred_element_type=f32).astype(half)
            placed[0, pair] = made[slot_range(0)]
            placed[1, pair, :, upper] = made[slot_range(1), half_width:]
            placed[2, pair, :, lower] = made[slot_range(2), :half_width]
            for index in range(2):
                for row, expert in enumerate((member, partner_of(member, 2 - index))):
                    one_hot(
                        lambda side: mate_choices[index, pair * 2 + side],
                        mate_onehot.at[pair, index],
                        slot_range(row),
                        expert,
                    )
                cols = (lower, upper)[index]
                taken = mates[:, :half_width] if index == 0 else mates[:, half_width:]
                made = jnp.dot(
                    mate_onehot[pair, index], taken, preferred_element_type=f32
                ).astype(half)
                placed[index + 1, pair, :, cols] = made[slot_range(0)]
                placed[3, pair, :, cols] = made[slot_range(1)]
        else:
            start = pl.multiple_of(pair * 2 * tok_rows, 2 * tok_rows)
            made = jnp.dot(
                onehot_ref[pair],
                cotangent_all[pl.ds(start, 2 * tok_rows), :],
                preferred_element_type=f32,
            ).astype(half)
            for move in range(experts_local):
                placed[move, pair] = made[slot_range(move)]

    placed_keep = pltpu.make_async_copy(placed, placed_out, placed_local.at[0])
    placed_keep.start()
    third.steps()
    third.landed()
    if crossed:
        cross_copy(2).wait()
        cross_copy(3).wait()
        cross_keep = pltpu.make_async_copy(
            routed_own.at[cross_rows], routed_cross, placed_local.at[1]
        )
        cross_keep.start()
    reduce.sent()
    second.sent()
    third.sent()
    for index in range(4):
        if split == 4:
            for step in range(4):
                relay_copy(index, step).wait_send()
        else:
            for shift in range(1, split):
                shard_copy(index, shift).wait_send()
    for keep in keeps:
        keep.wait()
    placed_keep.wait()
    if crossed:
        cross_keep.wait()
    for index in range(3):
        expert_own(index).wait()
        for shift in range(1, split):
            expert_copy(index, shift).wait()


def front(sizes, tokens, gains, cos, sin, segment_row, ids, slots, cotangent, weights, which):
    size, split, chips, experts_local = sizes
    w_query, w_key, w_value, w_out, w_gate, w_up, w_down = weights
    tok_rows, model_width = tokens.shape
    length = size * tok_rows
    local_width = w_query.shape[1]
    hidden_width = w_gate.shape[2]
    f32, half = jnp.float32, jnp.bfloat16
    vmem = pl.BlockSpec(memory_space=pltpu.VMEM)
    anywhere = pl.BlockSpec(memory_space=pl.ANY)
    kind = pltpu.SemaphoreType.DMA
    shape = jax.ShapeDtypeStruct
    crossed = split == experts_local == 4
    choices = (size, 2 * ids.shape[0], tok_rows)
    return pl.pallas_call(
        functools.partial(front_kernel, sizes),
        out_shape=(
            shape((length, model_width), half),
            shape((3, model_width, local_width), half),
            shape((split, *w_out.shape), half),
            shape((length, local_width), half),
            shape((length, local_width), half),
            shape((length, local_width), half),
            shape((2, length, local_width), f32),
            shape((length, local_width), f32),
            shape((length, local_width), half),
            shape((8, length), f32),
            shape((tok_rows, model_width), f32),
            shape(gains.shape, f32),
            shape((length, 128), f32),
            shape((length, model_width), half),
            shape((tok_rows, model_width), half),
            shape((experts_local, size // 2, 2 * CAP, model_width), half),
            shape((model_width, hidden_width), half),
            shape((model_width, hidden_width), half),
            shape((hidden_width, model_width), half),
            shape((size, 2 * ids.shape[0], tok_rows), jnp.int32),
            shape((size // 2, experts_local * 2 * CAP, 2 * tok_rows), half),
            shape((size // 2 if crossed else 1, 2, 4 * CAP, 2 * tok_rows), half),
        ),
        in_specs=[vmem] * 7 + [anywhere] * 8,
        out_specs=tuple(
            [anywhere] * 9 + [vmem, anywhere, vmem, vmem] + [anywhere] * 6 + [vmem] * 3
        ),
        scratch_shapes=[
            pltpu.VMEM((tok_rows, model_width), f32),
            pltpu.VMEM((length, local_width), half),
            pltpu.VMEM((length, local_width), half),
            pltpu.VMEM((length, local_width), half),
            pltpu.VMEM((2, length, local_width), f32),
            pltpu.VMEM((length, local_width), f32),
            pltpu.VMEM((length, local_width), half),
            pltpu.VMEM((length, model_width), half),
            pltpu.VMEM((3, model_width, local_width), half),
            pltpu.VMEM((split, *w_out.shape), half),
            pltpu.VMEM((2 * tok_rows, model_width), half),
            pltpu.VMEM((2 * ids.shape[0], tok_rows), jnp.int32),
            pltpu.VMEM((2 * tok_rows if crossed else 16, model_width), half),
            pltpu.VMEM(((2 if crossed else 1) * length, model_width), half),
            pltpu.VMEM((2, *(choices if crossed else (1, 8, 128))), jnp.int32),
            pltpu.VMEM((experts_local, size // 2, 2 * CAP, model_width), half),
            pltpu.VMEM((2, length, local_width), f32),
            pltpu.VMEM((8, length), f32),
            pltpu.VMEM((size, 8, length), f32),
            kind((3,)),
            kind((3, 3, chips)),
            kind((3, 2, chips)),
            kind((size,)),
            kind((size,)),
            kind((size,)),
            kind((size,)),
            kind((2,)),
            kind((2,)),
            kind,
            kind((4,)),
            kind((4,)),
            kind((2,)),
            kind((4,)),
            kind((4, split)),
            kind((4, split)),
            kind((3,)),
            kind((3, split)),
            kind((3, split)),
            kind((10,)),
            *ChainReduce.scratch(chips, tok_rows, model_width),
        ],
        compiler_params=pltpu.CompilerParams(
            collective_id=which, has_side_effects=True, vmem_limit_bytes=58 * 2**20
        ),
        cost_estimate=pl.CostEstimate(
            flops=2 * length * model_width * local_width * 4,
            bytes_accessed=500 * 2**20,
            transcendentals=0,
        ),
    )(
        tokens, gains, cos, sin, segment_row, ids, slots, cotangent, *weights
    )


class ShardSend:
    def __init__(self, split, source, landing, local_sem, sends, arrivals):
        self.split, self.source, self.landing = split, source, landing
        self.local_sem, self.sends, self.arrivals = local_sem, sends, arrivals
        self.mine = lax.axis_index("fsdp")

    def copy(self, shift):
        dest = lax.rem(self.mine + shift, self.split)
        return pltpu.make_async_remote_copy(
            src_ref=self.source(dest),
            dst_ref=self.landing.at[self.mine],
            send_sem=self.sends.at[shift],
            recv_sem=self.arrivals.at[shift],
            device_id={"fsdp": dest},
        )

    def own(self):
        return pltpu.make_async_copy(
            self.source(self.mine), self.landing.at[self.mine], self.local_sem
        )

    def start(self):
        for shift in range(1, self.split):
            self.copy(shift).start()
        self.own().start()

    def wait(self):
        for shift in range(1, self.split):
            self.copy(shift).wait()
        self.own().wait()


def turned_dot(left, right):
    return lax.dot_general(
        left, right, (((0,), (0,)), ((), ())), preferred_element_type=jnp.float32
    )


def cross_dot(left, right):
    return lax.dot_general(
        left, right, (((1,), (1,)), ((), ())), preferred_element_type=jnp.float32
    )


def experts_kernel(
    sizes,
    routed_ref,
    routed_cross_ref,
    choices_ref,
    onehot_ref,
    mate_onehot_any,
    placed_ref,
    router_ref,
    gains_ref,
    residual_any,
    cotangent_any,
    gate_ref,
    up_ref,
    down_ref,
    residual_grad_ref,
    out_grad_ref,
    gain_ref,
    router_grad_ref,
    hidden_out,
    grad_gate_ref,
    grad_up_ref,
    down_landing,
    routed_mates,
    mate_onehot_ref,
    residual_ref,
    cotangent_ref,
    late_sem,
    gate_full,
    up_full,
    down_full,
    upstream,
    pair_rows,
    outgoing,
    arrived,
    hidden,
    gate_grad,
    up_grad,
    back,
    gates,
    gates_out,
    gates_in,
    dots_out,
    dots_in,
    token_out,
    token_in,
    scales,
    load_sem,
    pair_sem,
    keep_sem,
    gather_local,
    gather_send,
    gather_recv,
    upstream_send,
    upstream_recv,
    rows_send,
    rows_recv,
    gates_send,
    gates_recv,
    back_send,
    back_recv,
    dots_send,
    dots_recv,
    token_send,
    token_recv,
    down_send,
    down_recv,
    *reduce_buffers,
):
    size, split, chips, experts_local = sizes
    f32, half = jnp.float32, jnp.bfloat16
    me, mine = lax.axis_index("seq"), lax.axis_index("fsdp")
    tok_rows, model_width = residual_ref.shape
    pairs = size // 2
    double = 2 * CAP
    wide = 2 * tok_rows
    hidden_width = gate_full.shape[1]
    rows_of = pairs * double
    part = model_width // split
    member = lax.rem(mine, experts_local)
    crossed = split == experts_local == 4
    half_width = model_width // 2
    lower, upper = pl.ds(0, half_width), pl.ds(half_width, half_width)

    loads = [
        pltpu.make_async_copy(source, target, load_sem.at[index])
        for index, (source, target) in enumerate(
            (
                (gate_ref, gate_full),
                (up_ref, up_full),
                (down_ref, down_full),
            )
        )
    ]
    if crossed:
        pieces = (
            (placed_ref.at[0], upstream.at[0]),
            (placed_ref.at[1, :, :, lower], upstream.at[1, :, :, lower]),
            (placed_ref.at[2, :, :, upper], upstream.at[2, :, :, upper]),
        )
    else:
        pieces = ((placed_ref.at[0], upstream.at[0]),)
    loads += [
        pltpu.make_async_copy(source, target, load_sem.at[3 + index])
        for index, (source, target) in enumerate(pieces)
    ]

    slots = pair_rows.shape[0]

    def pair_load(source, pair):
        slot = lax.rem(pair, slots)
        start = pl.multiple_of(pair * wide, wide)
        return pltpu.make_async_copy(
            source.at[pl.ds(start, wide)], pair_rows.at[slot], pair_sem.at[slot]
        )

    pair_load(routed_ref, 0).start()
    for load in loads:
        load.start()
    late_loads = [
        pltpu.make_async_copy(source, target, late_sem.at[index])
        for index, (source, target) in enumerate(
            (
                (mate_onehot_any, mate_onehot_ref),
                (residual_any, residual_ref),
                (cotangent_any, cotangent_ref),
            )
        )
    ]
    for load in late_loads:
        load.start()
    greet_all(size, split)

    def mate(move):
        return {"fsdp": partner_of(mine, move)}

    def upstream_piece(move, index, cols, target):
        return pltpu.make_async_remote_copy(
            src_ref=placed_ref.at[move, :, :, cols],
            dst_ref=upstream.at[move, :, :, cols],
            send_sem=upstream_send.at[index],
            recv_sem=upstream_recv.at[index],
            device_id=mate(target),
        )

    def halves_of(piece, move):
        if not crossed:
            return [piece(move, move, pl.ds(0, model_width), move)]
        if move == 3:
            return [piece(3, 3, upper, 1), piece(3, 0, lower, 2)]
        return [piece(move, move, (upper, lower)[move - 1], move)]

    order = [1, 2, 3] if crossed else list(range(experts_local - 1, 0, -1))
    if crossed:
        gather = ChainGather(
            chips, routed_cross_ref, routed_mates, gather_local, gather_send, gather_recv
        )
        gather.start()
    for move in order:
        if not crossed or move < 3:
            for copy in halves_of(upstream_piece, move):
                copy.start()

    padded = size * 8
    expert_row = lax.broadcasted_iota(jnp.int32, (padded, tok_rows), 0)
    inner = lax.rem(expert_row, 8)
    expert_row = jnp.where(inner < experts_local, expert_row // 8 * experts_local + inner, -1)
    ones = jnp.ones((8, wide), f32)
    top_count = choices_ref.shape[1] // 2

    @pl.loop(0, pairs)
    def _(pair):
        pair_load(routed_ref, pair).wait()

        @pl.when((pair + 1 < pairs) & (slots > 1))
        def _():
            pair_load(routed_ref, pair + 1).start()

        rows = pair_rows[lax.rem(pair, slots)]
        logits = lax.dot_general(
            router_ref[...], rows, (((1,), (1,)), ((), ())), preferred_element_type=f32
        )
        for side in range(2):
            ids = choices_ref[pair * 2 + side]
            chosen = expert_row == ids[0:1, :]
            for choice in range(1, top_count):
                chosen = chosen | (expert_row == ids[choice : choice + 1, :])
            own = jnp.where(chosen, logits[:, side * tok_rows : (side + 1) * tok_rows], MASKED)
            grown = jnp.where(chosen, jnp.exp(own - jnp.max(own, 0, keepdims=True)), 0.0)
            gates[pair * 2 + side] = grown / jnp.sum(grown, 0, keepdims=True)
        placed = jnp.dot(onehot_ref[pair], rows, preferred_element_type=f32).astype(half)
        for move in range(experts_local):
            piece = placed[move * double : (move + 1) * double]
            if move == 0:
                arrived[0, pair] = piece
            elif not crossed:
                outgoing[move - 1, pair] = piece
            elif move < 3:
                cols = (upper, lower)[move - 1]
                outgoing[move - 1, pair, :, cols] = (
                    piece[:, half_width:] if move == 1 else piece[:, :half_width]
                )
            row = me * 8 + partner_of(member, move)
            weights = jnp.concatenate(
                [gates[pair * 2, pl.ds(row, 1), :], gates[pair * 2 + 1, pl.ds(row, 1), :]], 1
            )
            slot_rows = pl.ds(move * double, double)
            weighted = onehot_ref[pair, slot_rows, :].astype(f32) * weights
            gates_out[move, pair] = row_sums(weighted, ones)

        @pl.when((pair + 1 < pairs) & (slots == 1))
        def _():
            pair_load(routed_ref, pair + 1).start()

    def rows_piece(move, index, cols, target):
        return pltpu.make_async_remote_copy(
            src_ref=outgoing.at[move - 1, :, :, cols],
            dst_ref=arrived.at[move, :, :, cols],
            send_sem=rows_send.at[index],
            recv_sem=rows_recv.at[index],
            device_id=mate(target),
        )

    def gates_copy(move):
        return pltpu.make_async_remote_copy(
            src_ref=gates_out.at[move],
            dst_ref=gates_in.at[move],
            send_sem=gates_send.at[move],
            recv_sem=gates_recv.at[move],
            device_id=mate(move),
        )

    def back_rows(move):
        return back.at[:, pl.ds(move * double, double), :]

    def back_copy(move):
        return pltpu.make_async_remote_copy(
            src_ref=outgoing.at[move - 1],
            dst_ref=back_rows(move),
            send_sem=back_send.at[move],
            recv_sem=back_recv.at[move],
            device_id=mate(move),
        )

    def dots_copy(move):
        return pltpu.make_async_remote_copy(
            src_ref=dots_out.at[move],
            dst_ref=dots_in.at[move],
            send_sem=dots_send.at[move],
            recv_sem=dots_recv.at[move],
            device_id=mate(move),
        )

    for move in order:
        gates_copy(move).start()
        if not crossed or move < 3:
            for copy in halves_of(rows_piece, move):
                copy.start()
    if crossed:
        for copy in halves_of(upstream_piece, 3):
            copy.start()
    gates_in[0] = gates_out[0]
    for load in loads + late_loads:
        load.wait()
    if crossed:
        gather.step(1)

    def mates_rows():
        for distance in range(3, chips):
            gather.step(distance)
        gather.landed()
        pair_load(routed_mates, 0).start()

        @pl.loop(0, pairs)
        def _(pair):
            pair_load(routed_mates, pair).wait()

            @pl.when(pair + 1 < pairs)
            def _():
                pair_load(routed_mates, pair + 1).start()

            for index, cols in enumerate((lower, upper)):
                made = jnp.dot(
                    mate_onehot_ref[pair, index],
                    pair_rows[lax.rem(pair, slots), :, cols],
                    preferred_element_type=f32,
                ).astype(half)
                arrived[index + 1, pair, :, cols] = made[0:double]
                outgoing[2, pair, :, cols] = made[double:]

        for copy in halves_of(rows_piece, 3):
            copy.start()
        gather.sent()

    cols_step = min(256, hidden_width)
    width_step = min(512, model_width)
    spread = (lax.broadcasted_iota(jnp.int32, (8, 128), 0) == 0).astype(f32)
    for move in [0] + order:
        if move:
            gates_copy(move).wait()
            for copy in halves_of(rows_piece, move) + halves_of(upstream_piece, move):
                copy.wait()
        for pair in range(pairs):
            scales[pair * double : (pair + 1) * double, :] = column_of(
                gates_in[move, pair], spread
            )
        dots_out[move] = jnp.zeros_like(dots_out[move])

        @pl.loop(0, hidden_width // cols_step)
        def _(index):
            cols = pl.ds(pl.multiple_of(index * cols_step, cols_step), cols_step)
            rows = arrived[move].reshape(rows_of, model_width)
            pre = jnp.dot(rows, gate_full[:, cols], preferred_element_type=f32)
            up = jnp.dot(rows, up_full[:, cols], preferred_element_type=f32)
            plain = lax.dot_general(
                upstream[move].reshape(rows_of, model_width),
                down_full[cols, :],
                (((1,), (1,)), ((), ())),
                preferred_element_type=f32,
            )
            sigmoid = 1.0 / (1.0 + jnp.exp(-pre))
            active = pre * sigmoid
            made = (active * up).astype(half)
            weighted = made.astype(f32) * scales[:, 0:1]
            hidden[move, :, :, cols] = weighted.astype(half).reshape(pairs, double, cols_step)
            dots = made.astype(f32) * plain
            for pair in range(pairs):
                dots_out[move, pair] += row_sums(
                    dots[pair * double : (pair + 1) * double], jnp.ones((8, cols_step), f32)
                )
            scaled = plain * scales[:, 0:1]
            gate_back = scaled * up * sigmoid * (1.0 + pre * (1.0 - sigmoid))
            gate_grad[move, :, :, cols] = gate_back.astype(half).reshape(pairs, double, cols_step)
            up_grad[move, :, :, cols] = (
                (scaled * active).astype(half).reshape(pairs, double, cols_step)
            )

        if move:
            dots_copy(move).start()
        else:
            dots_in[0] = dots_out[0]
            if crossed and chips > 2:
                gather.step(2)

        @pl.loop(0, model_width // width_step)
        def _(index):
            cols = pl.ds(pl.multiple_of(index * width_step, width_step), width_step)
            rows_grad = lax.dot_general(
                gate_grad[move].reshape(rows_of, hidden_width),
                gate_full[cols, :],
                (((1,), (1,)), ((), ())),
                preferred_element_type=f32,
            )
            rows_grad = rows_grad + lax.dot_general(
                up_grad[move].reshape(rows_of, hidden_width),
                up_full[cols, :],
                (((1,), (1,)), ((), ())),
                preferred_element_type=f32,
            )
            rows_grad = rows_grad.astype(half).reshape(pairs, double, width_step)
            if move:
                outgoing[move - 1, :, :, cols] = rows_grad
            else:
                back[:, 0:double, cols] = rows_grad

        if move:
            back_copy(move).start()
        elif crossed:
            mates_rows()

    own_rows = pl.ds(pl.multiple_of(me * tok_rows, tok_rows), tok_rows)
    own_load = pltpu.make_async_copy(
        routed_ref.at[own_rows], pair_rows.at[0, pl.ds(0, tok_rows)], pair_sem.at[0]
    )
    own_load.start()
    hidden_keep = pltpu.make_async_copy(hidden, hidden_out, keep_sem)
    hidden_keep.start()

    total_rows = experts_local * rows_of

    def flat(ref, cols):
        return ref[:, :, :, cols].reshape(total_rows, -1)

    every = pl.ds(0, hidden_width)

    @pl.loop(0, split)
    def _(piece):
        cols = pl.ds(pl.multiple_of(piece * part, part), part)
        gate_full[cols, :] = turned_dot(flat(arrived, cols), flat(gate_grad, every)).astype(half)
        up_full[cols, :] = turned_dot(flat(arrived, cols), flat(up_grad, every)).astype(half)
        down_full[:, cols] = turned_dot(flat(hidden, every), flat(upstream, cols)).astype(half)

    grad_keeps = [
        pltpu.make_async_copy(source, target, load_sem.at[index])
        for index, (source, target) in enumerate(
            ((gate_full, grad_gate_ref), (up_full, grad_up_ref))
        )
    ]
    for keep in grad_keeps:
        keep.start()
    down_send_all = ShardSend(
        split,
        lambda dest: down_full.at[:, pl.ds(pl.multiple_of(dest * part, part), part)],
        down_landing,
        load_sem.at[2],
        down_send,
        down_recv,
    )

    for move in order:
        dots_copy(move).wait()
    token_out[...] = jnp.zeros_like(token_out)

    @pl.loop(0, pairs)
    def _(pair):
        for move in range(experts_local):
            found = jnp.dot(
                dots_in[move, pair],
                onehot_ref[pair, pl.ds(move * double, double), :].astype(f32),
                precision=HIGHEST,
                preferred_element_type=f32,
            )
            row = partner_of(member, move)
            for side in range(2):
                token_out[pair * 2 + side, pl.ds(row, 1), :] = found[
                    0:1, side * tok_rows : (side + 1) * tok_rows
                ]

    def token_copy(shift):
        peer = lax.rem(me + shift, size)
        return pltpu.make_async_remote_copy(
            src_ref=token_out.at[peer],
            dst_ref=token_in.at[me],
            send_sem=token_send.at[shift],
            recv_sem=token_recv.at[shift],
            device_id={"seq": peer},
        )

    for shift in range(1, size):
        token_copy(shift).start()
    token_in[me] = token_out[me]
    for move in order:
        back_copy(move).wait()
    down_send_all.start()

    reduce = ChainReduce(chips, residual_grad_ref, reduce_buffers)

    def product(index, store):
        side = pl.ds(pl.multiple_of(lax.rem(index, 2) * tok_rows, tok_rows), tok_rows)
        left = onehot_ref[index // 2, :, side]

        @pl.loop(0, model_width // width_step)
        def _(step):
            cols = pl.ds(pl.multiple_of(step * width_step, width_step), width_step)
            store(cols, turned_dot(left, back[index // 2, :, cols]))

    reduce.run(product)

    for shift in range(1, size):
        token_copy(shift).wait()
    own_gates = gates[me]
    grads = token_in[...].reshape(padded, tok_rows)
    mean = jnp.sum(own_gates * grads, 0, keepdims=True)
    logit_grad = (own_gates * (grads - mean)).astype(half)
    routed_grad = reduce.total[...] + turned_dot(logit_grad, router_ref[...])
    own_load.wait()
    router_grad = jnp.dot(logit_grad, pair_rows[0, 0:tok_rows, :], preferred_element_type=f32)
    for device in range(size):
        router_grad_ref[device * experts_local : (device + 1) * experts_local, :] = router_grad[
            device * 8 : device * 8 + experts_local
        ]
    residual = residual_ref[...]
    inverse = lax.rsqrt(jnp.mean(residual * residual, -1, keepdims=True) + EPSILON)
    unit = residual * inverse
    gain_ref[...] = jnp.broadcast_to(
        jnp.sum(routed_grad * unit, 0, keepdims=True), gain_ref.shape
    )
    routed_grad = routed_grad * gains_ref[1:2, :]
    routed_grad = inverse * (
        routed_grad - unit * jnp.mean(routed_grad * unit, -1, keepdims=True)
    )
    residual_grad = cotangent_ref[...].astype(f32) + routed_grad
    residual_grad_ref[...] = residual_grad
    out_grad_ref[...] = residual_grad.astype(half)
    reduce.sent()
    hidden_keep.wait()
    for keep in grad_keeps:
        keep.wait()
    down_send_all.wait()


def experts(
    sizes,
    routed_seq,
    routed_cross,
    choices,
    onehot,
    mate_onehot,
    placed,
    router_rows,
    gain_rows,
    residual,
    cotangent,
    weights,
    which,
):
    size, split, chips, experts_local = sizes
    gate_full, up_full, down_full = weights
    model_width, hidden_width = gate_full.shape
    tok_rows = residual.shape[0]
    pairs, double = size // 2, 2 * CAP
    f32, half = jnp.float32, jnp.bfloat16
    vmem = pl.BlockSpec(memory_space=pltpu.VMEM)
    anywhere = pl.BlockSpec(memory_space=pl.ANY)
    kind = pltpu.SemaphoreType.DMA
    shape = jax.ShapeDtypeStruct
    few = kind((experts_local,))
    crossed = split == experts_local == 4
    wide_rows = (experts_local, pairs, double, model_width)
    narrow_rows = (experts_local, pairs, double, hidden_width)
    flags = (experts_local, pairs, 8, double)
    return pl.pallas_call(
        functools.partial(experts_kernel, sizes),
        out_shape=(
            shape((tok_rows, model_width), f32),
            shape((tok_rows, model_width), half),
            shape((8, model_width), f32),
            shape((size * experts_local, model_width), f32),
            shape(narrow_rows, half),
            shape(gate_full.shape, half),
            shape(up_full.shape, half),
            shape((split, hidden_width, model_width // split), half),
            shape(routed_seq.shape if crossed else (16, model_width), half),
        ),
        in_specs=[anywhere] * 2 + [vmem] * 2 + [anywhere] * 2 + [vmem] * 2 + [anywhere] * 5,
        out_specs=tuple([vmem] * 4 + [anywhere] * 5),
        scratch_shapes=[
            pltpu.VMEM(mate_onehot.shape, half),
            pltpu.VMEM(residual.shape, f32),
            pltpu.VMEM(cotangent.shape, half),
            kind((3,)),
            pltpu.VMEM(gate_full.shape, half),
            pltpu.VMEM(up_full.shape, half),
            pltpu.VMEM(down_full.shape, half),
            pltpu.VMEM(wide_rows, half),
            pltpu.VMEM((2 if chips < 8 else 1, 2 * tok_rows, model_width), half),
            pltpu.VMEM((max(experts_local - 1, 1), *wide_rows[1:]), half),
            pltpu.VMEM(wide_rows, half),
            pltpu.VMEM(narrow_rows, half),
            pltpu.VMEM(narrow_rows, half),
            pltpu.VMEM(narrow_rows, half),
            pltpu.VMEM((pairs, experts_local * double, model_width), half),
            pltpu.VMEM((size, size * 8, tok_rows), f32),
            pltpu.VMEM(flags, f32),
            pltpu.VMEM(flags, f32),
            pltpu.VMEM(flags, f32),
            pltpu.VMEM(flags, f32),
            pltpu.VMEM((size, 8, tok_rows), f32),
            pltpu.VMEM((size, 8, tok_rows), f32),
            pltpu.VMEM((pairs * double, 128), f32),
            kind((6,)),
            kind((2,)),
            kind,
            kind,
            kind((3, chips)),
            kind((2, chips)),
            few,
            few,
            few,
            few,
            few,
            few,
            few,
            few,
            few,
            few,
            kind((size,)),
            kind((size,)),
            kind((split,)),
            kind((split,)),
            *ChainReduce.scratch(chips, tok_rows, model_width),
        ],
        compiler_params=pltpu.CompilerParams(
            collective_id=which, has_side_effects=True, vmem_limit_bytes=63 * 2**20
        ),
        cost_estimate=pl.CostEstimate(
            flops=2 * experts_local * pairs * double * model_width * hidden_width * 8,
            bytes_accessed=500 * 2**20,
            transcendentals=0,
        ),
    )(
        routed_seq,
        routed_cross,
        choices,
        onehot,
        mate_onehot,
        placed,
        router_rows,
        gain_rows,
        residual,
        cotangent,
        gate_full,
        up_full,
        down_full,
    )

def back_kernel(
    sizes,
    out_grad_ref,
    gains_ref,
    second_gain_ref,
    seg_row_ref,
    sums_ref,
    *refs,
):
    kept_count = 13
    kept, refs = refs[:kept_count], refs[kept_count:]
    back_body(sizes, out_grad_ref, gains_ref, second_gain_ref, seg_row_ref, sums_ref, kept, *refs)


def back_body(
    sizes,
    out_grad_ref,
    gains_ref,
    second_gain_ref,
    seg_row_ref,
    sums_ref,
    kept,
    normed_ref,
    hidden_ref,
    down_ref,
    grad_gate_ref,
    input_grad_ref,
    gains_out_ref,
    out_w_grad_ref,
    mixed_rows,
    gate_landing,
    qkv_out,
    rows_full_ref,
    attended_ref,
    q_ref,
    k_ref,
    v_ref,
    seg_col_ref,
    log_ref,
    cos_ref,
    sin_ref,
    unit_ref,
    qkv_ref,
    tokens_ref,
    residual_grad_ref,
    down_full,
    out_grads,
    attended_grad,
    hidden,
    returned,
    key_total,
    value_total,
    scaled,
    raw_grads,
    centers_own,
    centers_in,
    qkv_stage,
    out_stage,
    out_landing,
    load_sem,
    gather_local,
    gather_send,
    gather_recv,
    gate_local,
    gate_send,
    gate_recv,
    rows_local,
    rows_send,
    rows_recv,
    centers_send,
    centers_recv,
    kept_sem,
    out_local,
    out_send,
    out_recv,
    *reduce_buffers,
):
    size, split, chips, experts_local = sizes
    f32, half = jnp.float32, jnp.bfloat16
    me, mine = lax.axis_index("seq"), lax.axis_index("fsdp")
    tok_rows, model_width = out_grad_ref.shape
    length, local_width = q_ref.shape
    hidden_width = down_ref.shape[0]
    part = model_width // split
    head = HEAD_DIM
    heads = local_width // head
    double = 2 * CAP
    pairs = size // 2
    rows_of = pairs * double

    down_load = pltpu.make_async_copy(down_ref, down_full, load_sem.at[0])
    hidden_load = pltpu.make_async_copy(hidden_ref, hidden, load_sem.at[1])
    down_load.start()
    hidden_load.start()
    targets = (
        rows_full_ref,
        attended_ref,
        q_ref,
        k_ref,
        v_ref,
        seg_col_ref,
        log_ref,
        cos_ref,
        sin_ref,
        unit_ref,
        qkv_ref,
        tokens_ref,
        residual_grad_ref,
    )
    kept_loads = [
        pltpu.make_async_copy(source, target, kept_sem.at[index])
        for index, (source, target) in enumerate(zip(kept, targets))
    ]
    greet_all(size, split)
    gather = ChainGather(chips, out_grad_ref, out_grads, gather_local, gather_send, gather_recv)
    gather.start()
    gate_send_all = ShardSend(
        split,
        lambda dest: grad_gate_ref.at[pl.ds(pl.multiple_of(dest * part, part), part)],
        gate_landing,
        gate_local,
        gate_send,
        gate_recv,
    )

    gate_send_all.start()
    for load in kept_loads:
        load.start()

    down_load.wait()
    hidden_load.wait()
    width_step = min(512, model_width)

    def rows_target(move):
        return mixed_rows.at[:, pl.ds(move * double, double), :]

    def rows_copy(move):
        return pltpu.make_async_remote_copy(
            src_ref=returned.at[move],
            dst_ref=rows_target(move),
            send_sem=rows_send.at[move],
            recv_sem=rows_recv.at[move],
            device_id={"fsdp": partner_of(mine, move)},
        )

    own_rows = pltpu.make_async_copy(returned.at[0], rows_target(0), rows_local)
    for move in range(experts_local - 1, -1, -1):

        @pl.loop(0, model_width // width_step)
        def _(index):
            cols = pl.ds(pl.multiple_of(index * width_step, width_step), width_step)
            made = jnp.dot(
                hidden[move].reshape(rows_of, hidden_width),
                down_full[:, cols],
                preferred_element_type=f32,
            )
            returned[move, :, :, cols] = made.astype(half).reshape(pairs, double, width_step)

        if move:
            rows_copy(move).start()
    own_rows.start()
    gather.steps()
    for load in kept_loads:
        load.wait()
    gather.landed()

    block = min(512, length)

    @pl.loop(0, length // block)
    def _(step):
        rows = pl.ds(pl.multiple_of(step * block, block), block)
        total = cross_dot(out_grads[rows, 0:part], rows_full_ref[0])
        for piece in range(1, split):
            total += cross_dot(
                out_grads[rows, piece * part : (piece + 1) * part], rows_full_ref[piece]
            )
        attended_grad[rows, :] = total.astype(half)

    @pl.loop(0, split)
    def _(piece):
        cols = pl.ds(pl.multiple_of(piece * part, part), part)
        out_stage[piece] = turned_dot(attended_ref[...], out_grads[:, cols]).astype(half)

    out_send_all = ShardSend(
        split, lambda dest: out_stage.at[dest], out_landing, out_local, out_send, out_recv
    )
    out_send_all.start()
    gather.sent()
    normed_load = pltpu.make_async_copy(normed_ref, out_grads, load_sem.at[0])
    normed_load.start()

    wide = min(256, length) if length <= 1024 else 128
    scale = head**-0.5
    segments = seg_row_ref[...].astype(f32)
    for number in range(heads):
        cols = slice(number * head, (number + 1) * head)
        key_total[...] = jnp.zeros_like(key_total)
        value_total[...] = jnp.zeros_like(value_total)

        @pl.loop(0, length // wide)
        def _(step):
            rows = pl.ds(pl.multiple_of(step * wide, wide), wide)
            scores = cross_dot(q_ref[rows, cols], k_ref[:, cols]) * scale
            scores = jnp.where(seg_col_ref[rows, 0:1] == segments, scores, MASKED)
            probs = jnp.exp(scores - log_ref[rows, cols][:, 0:1])
            grads = attended_grad[rows, cols]
            prob_grad = cross_dot(grads, v_ref[:, cols])
            center = jnp.sum(probs * prob_grad, -1, keepdims=True)
            score_grad = (probs * (prob_grad - center)).astype(half)
            query_grad = jnp.dot(score_grad, k_ref[:, cols], preferred_element_type=f32) * scale
            raw_grads[0, rows, cols] = query_grad.astype(half)
            key_total[...] += turned_dot(score_grad, q_ref[rows, cols])
            value_total[...] += turned_dot(probs.astype(half), grads)

        raw_grads[1, :, cols] = (key_total[...] * scale).astype(half)
        raw_grads[2, :, cols] = value_total[...].astype(half)

    lanes = lax.broadcasted_iota(jnp.int32, (8, local_width), 0)
    first_row, second_row = (lanes == 0).astype(f32), (lanes == 1).astype(f32)
    gains_out_ref[...] = jnp.zeros_like(gains_out_ref)
    own_cols = pl.ds(pl.multiple_of(me * local_width, local_width), local_width)
    gains_out_ref[1:2, :] = second_gain_ref[0:1, :]

    @pl.loop(0, length // block)
    def _(step):
        rows = pl.ds(pl.multiple_of(step * block, block), block)
        found = jnp.zeros((8, block), f32)
        for index, pick in ((0, first_row), (1, second_row)):
            unit = unit_ref[index, rows, :]
            pieces = []
            for number in range(heads):
                cols = slice(number * head, (number + 1) * head)
                piece = raw_grads[index, rows, cols].astype(f32)
                pieces.append(piece * cos_ref[rows, :] - turned_halves(piece) * sin_ref[rows, :])
            unit_grad = pieces[0] if heads == 1 else jnp.concatenate(pieces, 1)
            gains_out_ref[2 + index : 3 + index, own_cols] += jnp.sum(
                unit_grad * unit, 0, keepdims=True
            )
            grown = unit_grad * gains_ref[2 + index : 3 + index, own_cols]
            scaled[index, rows, :] = grown
            found += row_sums(grown * unit, pick)
        centers_own[:, rows] = found

    def centers_copy(shift):
        return pltpu.make_async_remote_copy(
            src_ref=centers_own,
            dst_ref=centers_in.at[me],
            send_sem=centers_send.at[shift],
            recv_sem=centers_recv.at[shift],
            device_id={"seq": lax.rem(me + shift, size)},
        )

    for shift in range(1, size):
        centers_copy(shift).start()
    centers_in[me] = centers_own[...]
    for shift in range(1, size):
        centers_copy(shift).wait()
    centers_own[...] = jnp.sum(centers_in[...], 0) * (1.0 / model_width)

    @pl.loop(0, length // block)
    def _(step):
        rows = pl.ds(pl.multiple_of(step * block, block), block)
        for index, pick in ((0, first_row), (1, second_row)):
            inverse = lax.rsqrt(column_of(sums_ref[:, rows], pick) / model_width + EPSILON)
            center = column_of(centers_own[:, rows], pick)
            raw_grads[index, rows, :] = (
                inverse * (scaled[index, rows, :] - unit_ref[index, rows, :] * center)
            ).astype(half)

    reduce = ChainReduce(chips, input_grad_ref, reduce_buffers)

    def product(index, store):
        rows = pl.ds(pl.multiple_of(index * tok_rows, tok_rows), tok_rows)

        @pl.loop(0, model_width // width_step)
        def _(step):
            cols = pl.ds(pl.multiple_of(step * width_step, width_step), width_step)
            total = cross_dot(raw_grads[0, rows, :], qkv_ref[0, cols, :])
            total += cross_dot(raw_grads[1, rows, :], qkv_ref[1, cols, :])
            total += cross_dot(raw_grads[2, rows, :], qkv_ref[2, cols, :])
            store(cols, total)

    qkv_keep = pltpu.make_async_copy(qkv_stage, qkv_out, load_sem.at[1])

    def between():
        normed_load.wait()

        @pl.loop(0, split)
        def _(piece):
            cols = pl.ds(pl.multiple_of(piece * part, part), part)
            left = out_grads[:, cols]
            for index in range(3):
                qkv_stage[piece, index] = turned_dot(left, raw_grads[index]).astype(half)

        qkv_keep.start()

    reduce.run(product, between)

    inputs = tokens_ref[...].astype(f32)
    inverse = lax.rsqrt(jnp.mean(inputs * inputs, -1, keepdims=True) + EPSILON)
    unit = inputs * inverse
    grads = input_grad_ref[...]
    gains_out_ref[0:1, :] = jnp.sum(grads * unit, 0, keepdims=True)
    grads = grads * gains_ref[0:1, :]
    input_grad_ref[...] = residual_grad_ref[...] + inverse * (
        grads - unit * jnp.mean(grads * unit, -1, keepdims=True)
    )

    out_send_all.wait()
    total = out_landing[0].astype(f32)
    for index in range(1, split):
        total += out_landing[index].astype(f32)
    out_w_grad_ref[...] = total
    qkv_keep.wait()
    reduce.sent()
    own_rows.wait()
    for move in range(1, experts_local):
        rows_copy(move).wait()
    gate_send_all.wait()


def back(sizes, out_grad, small, kept, big_ones, which):
    size, split, chips, experts_local = sizes
    f32, half = jnp.float32, jnp.bfloat16
    tok_rows, model_width = out_grad.shape
    length, local_width = kept[1].shape
    normed_seq, hidden, down_full, grad_gate = big_ones
    hidden_width = down_full.shape[0]
    part = model_width // split
    vmem = pl.BlockSpec(memory_space=pltpu.VMEM)
    anywhere = pl.BlockSpec(memory_space=pl.ANY)
    kind = pltpu.SemaphoreType.DMA
    shape = jax.ShapeDtypeStruct
    few, fsdp = kind((experts_local,)), kind((split,))
    return pl.pallas_call(
        functools.partial(back_kernel, sizes),
        out_shape=(
            shape((tok_rows, model_width), f32),
            shape((8, model_width), f32),
            shape((local_width, part), f32),
            shape((size // 2, experts_local * 2 * CAP, model_width), half),
            shape((split, part, hidden_width), half),
            shape((split, 3, part, local_width), half),
        ),
        in_specs=[vmem] * 5 + [anywhere] * (len(kept) + 4),
        out_specs=tuple([vmem] * 3 + [anywhere] * 3),
        scratch_shapes=[
            *[pltpu.VMEM(one.shape, one.dtype) for one in kept],
            pltpu.VMEM(down_full.shape, half),
            pltpu.VMEM((length, model_width), half),
            pltpu.VMEM((length, local_width), half),
            pltpu.VMEM(hidden.shape, half),
            pltpu.VMEM((experts_local, size // 2, 2 * CAP, model_width), half),
            pltpu.VMEM((length, HEAD_DIM), f32),
            pltpu.VMEM((length, HEAD_DIM), f32),
            pltpu.VMEM((2, length, local_width), f32),
            pltpu.VMEM((3, length, local_width), half),
            pltpu.VMEM((8, length), f32),
            pltpu.VMEM((size, 8, length), f32),
            pltpu.VMEM((split, 3, part, local_width), half),
            pltpu.VMEM((split, local_width, part), half),
            pltpu.VMEM((split, local_width, part), half),
            kind((2,)),
            kind,
            kind((3, chips)),
            kind((2, chips)),
            kind,
            fsdp,
            fsdp,
            kind,
            few,
            few,
            kind((size,)),
            kind((size,)),
            kind((len(kept),)),
            kind,
            fsdp,
            fsdp,
            *ChainReduce.scratch(chips, tok_rows, model_width),
        ],
        compiler_params=pltpu.CompilerParams(
            collective_id=which, has_side_effects=True, vmem_limit_bytes=63 * 2**20
        ),
        cost_estimate=pl.CostEstimate(
            flops=2 * length * model_width * local_width * 8,
            bytes_accessed=500 * 2**20,
            transcendentals=0,
        ),
    )(out_grad, *small, *kept, *big_ones)


def close_kernel(
    sizes,
    onehot_ref,
    gains_ref,
    router_ref,
    mixed_rows_any,
    residual_any,
    qkv_any,
    grad_up_ref,
    output_ref,
    gains_out_ref,
    router_out_ref,
    query_w_grad_ref,
    key_w_grad_ref,
    value_w_grad_ref,
    up_landing,
    mixed_rows_ref,
    residual_ref,
    qkv_ref,
    qkv_in,
    qkv_sum,
    load_sem,
    qkv_send,
    qkv_recv,
    total,
    small,
    first,
    second,
    final,
    up_local,
    up_send,
    up_recv,
    send_one,
    recv_one,
    send_two,
    recv_two,
    send_three,
    recv_three,
    *reduce_buffers,
):
    size, split, chips, experts_local = sizes
    f32 = jnp.float32
    me, mine = lax.axis_index("seq"), lax.axis_index("fsdp")
    tok_rows, model_width = residual_ref.shape
    part = model_width // split
    slice_width = model_width // size
    experts_all = router_ref.shape[0]
    loads = [
        pltpu.make_async_copy(source, target, load_sem.at[index])
        for index, (source, target) in enumerate(
            ((qkv_any, qkv_ref), (mixed_rows_any, mixed_rows_ref), (residual_any, residual_ref))
        )
    ]
    for load in loads:
        load.start()
    small[0:8, :] = gains_ref[...]
    small[8 : 8 + experts_all, :] = router_ref[...]
    greet_all(size, split)
    up_send_all = ShardSend(
        split,
        lambda dest: grad_up_ref.at[pl.ds(pl.multiple_of(dest * part, part), part)],
        up_landing,
        up_local,
        up_send,
        up_recv,
    )
    loads[0].wait()

    half_part = qkv_ref.shape[2] // 2
    lower, upper = pl.ds(0, half_part), pl.ds(half_part, half_part)
    mates = (partner_of(mine, 1), partner_of(mine, 2), partner_of(mine, 3)) if split == 4 else ()

    def qkv_copy(index):
        side = index % 2
        rows = (lower, upper)[side]
        if index < 4:
            dest = mates[side] if index < 2 else mates[2]
            source, mate = qkv_ref.at[dest, :, rows], mates[side]
        else:
            source, mate = qkv_sum.at[side], mates[1 - side]
        return pltpu.make_async_remote_copy(
            src_ref=source,
            dst_ref=qkv_in.at[index],
            send_sem=qkv_send.at[index],
            recv_sem=qkv_recv.at[index],
            device_id={"fsdp": mate},
        )

    def qkv_shift(shift):
        dest = lax.rem(mine + shift, split)
        return pltpu.make_async_remote_copy(
            src_ref=qkv_ref.at[dest],
            dst_ref=qkv_in.at[shift],
            send_sem=qkv_send.at[shift],
            recv_sem=qkv_recv.at[shift],
            device_id={"fsdp": dest},
        )

    if split == 4:
        for index in range(4):
            qkv_copy(index).start()
    else:
        for shift in range(1, split):
            qkv_shift(shift).start()
    up_send_all.start()

    def columns(index):
        return pl.ds(pl.multiple_of(index * slice_width, slice_width), slice_width)

    def scatter(shift):
        peer = lax.rem(me + shift, size)
        return pltpu.make_async_remote_copy(
            src_ref=small.at[:, columns(peer)],
            dst_ref=first.at[me],
            send_sem=send_one.at[shift],
            recv_sem=recv_one.at[shift],
            device_id={"seq": peer},
        )

    def share(shift):
        return pltpu.make_async_remote_copy(
            src_ref=second.at[mine],
            dst_ref=second.at[mine],
            send_sem=send_two.at[shift],
            recv_sem=recv_two.at[shift],
            device_id={"fsdp": lax.rem(mine + shift, split)},
        )

    def collect(shift):
        return pltpu.make_async_remote_copy(
            src_ref=final.at[me],
            dst_ref=final.at[me],
            send_sem=send_three.at[shift],
            recv_sem=recv_three.at[shift],
            device_id={"seq": lax.rem(me + shift, size)},
        )

    for shift in range(1, size):
        scatter(shift).start()
    first[me] = small[:, columns(me)]

    reduce = ChainReduce(chips, total, reduce_buffers)
    width_step = min(512, model_width)

    def product(index, store):
        side = pl.ds(pl.multiple_of(lax.rem(index, 2) * tok_rows, tok_rows), tok_rows)
        left = onehot_ref[index // 2, :, side]

        @pl.loop(0, model_width // width_step)
        def _(step):
            cols = pl.ds(pl.multiple_of(step * width_step, width_step), width_step)
            store(cols, turned_dot(left, mixed_rows_ref[index // 2, :, cols]))

    def between():
        for shift in range(1, size):
            scatter(shift).wait_recv()
        second[mine] = jnp.sum(first[...], 0)
        for shift in range(1, split):
            share(shift).start()

    loads[1].wait()
    reduce.run(product, between)
    if split == 4:
        for side in range(2):
            qkv_copy(2 + side).wait_recv()
            rows = (lower, upper)[side]
            qkv_sum[side] = (
                qkv_ref[mates[1 - side], :, rows].astype(f32) + qkv_in[2 + side].astype(f32)
            ).astype(qkv_sum.dtype)
            qkv_copy(4 + side).start()
    loads[2].wait()
    for shift in range(1, split):
        share(shift).wait_recv()
    final[me] = jnp.sum(second[...], 0)
    for shift in range(1, size):
        collect(shift).start()
    output_ref[...] = (residual_ref[...] + total[...]).astype(output_ref.dtype)
    for shift in range(1, size):
        scatter(shift).wait_send()
    for shift in range(1, split):
        share(shift).wait_send()
    for shift in range(1, size):
        collect(shift).wait()
    for index in range(size):
        cols = slice(index * slice_width, (index + 1) * slice_width)
        gains_out_ref[:, cols] = final[index, 0:4]
        router_out_ref[:, cols] = final[index, 8:]
    targets = (query_w_grad_ref, key_w_grad_ref, value_w_grad_ref)
    if split == 4:
        for side in range(2):
            for index in (side, 2 + side, 5 - side):
                copy = qkv_copy(index)
                copy.wait() if index < 2 or index > 3 else copy.wait_send()
        for side in range(2):
            rows = (lower, upper)[side]
            for index, target in enumerate(targets):
                target[rows, :] = (
                    qkv_ref[mine, index, rows].astype(f32)
                    + qkv_in[side, index].astype(f32)
                    + qkv_in[4 + side, index].astype(f32)
                )
    else:
        for shift in range(1, split):
            qkv_shift(shift).wait()
        for index, target in enumerate(targets):
            sums = qkv_ref[mine, index].astype(f32)
            for shift in range(1, split):
                sums += qkv_in[shift, index].astype(f32)
            target[...] = sums
    reduce.sent()
    up_send_all.wait()


def close(sizes, onehot, gains, router_grad, mixed_rows, residual, qkv_parts, grad_up, which):
    size, split, chips, experts_local = sizes
    f32, half = jnp.float32, jnp.bfloat16
    tok_rows, model_width = residual.shape
    hidden_width = grad_up.shape[1]
    part, slice_width = model_width // split, model_width // size
    rows = 8 + router_grad.shape[0]
    vmem = pl.BlockSpec(memory_space=pltpu.VMEM)
    anywhere = pl.BlockSpec(memory_space=pl.ANY)
    kind = pltpu.SemaphoreType.DMA
    shape = jax.ShapeDtypeStruct
    seq, fsdp = kind((size,)), kind((split,))
    share = qkv_parts.shape[2:]
    return pl.pallas_call(
        functools.partial(close_kernel, sizes),
        out_shape=(
            shape((tok_rows, model_width), half),
            shape((4, model_width), f32),
            shape(router_grad.shape, f32),
            shape(share, f32),
            shape(share, f32),
            shape(share, f32),
            shape((split, part, hidden_width), half),
        ),
        in_specs=[vmem] * 3 + [anywhere] * 4,
        out_specs=tuple([vmem] * 6 + [anywhere]),
        scratch_shapes=[
            pltpu.VMEM(mixed_rows.shape, half),
            pltpu.VMEM(residual.shape, f32),
            pltpu.VMEM(qkv_parts.shape, half),
            pltpu.VMEM((6, 3, share[0] // 2, share[1]) if split == 4 else qkv_parts.shape, half),
            pltpu.VMEM((2, 3, share[0] // 2, share[1]), half),
            kind((3,)),
            kind((max(6, split),)),
            kind((max(6, split),)),
            pltpu.VMEM((tok_rows, model_width), f32),
            pltpu.VMEM((rows, model_width), f32),
            pltpu.VMEM((size, rows, slice_width), f32),
            pltpu.VMEM((split, rows, slice_width), f32),
            pltpu.VMEM((size, rows, slice_width), f32),
            kind,
            fsdp,
            fsdp,
            seq,
            seq,
            fsdp,
            fsdp,
            seq,
            seq,
            *ChainReduce.scratch(chips, tok_rows, model_width),
        ],
        compiler_params=pltpu.CompilerParams(
            collective_id=which, has_side_effects=True, vmem_limit_bytes=56 * 2**20
        ),
    )(onehot, gains, router_grad, mixed_rows, residual, qkv_parts, grad_up)


def finish_kernel(count, *refs):
    sources, targets = refs[: len(refs) // 2], refs[len(refs) // 2 :]
    for source, target in zip(sources[:count], targets[:count]):
        target[...] = source[...]
    for source, target in zip(sources[count:], targets[count:]):
        total = source[0].astype(target.dtype)
        for index in range(1, source.shape[0]):
            total += source[index].astype(target.dtype)
        target[...] = total


def finish(results, landings, experts_local):
    halves = 1
    steps = experts_local * halves
    in_specs, out_specs, shapes = [], [], []
    for one in results:
        rows = one.shape[0] // steps
        spec = pl.BlockSpec((rows, one.shape[1]), lambda step: (step, 0))
        if one.shape[0] % (steps * 16):
            spec = pl.BlockSpec(one.shape, lambda step: (0, 0))
        in_specs.append(spec)
        out_specs.append(spec)
        shapes.append(jax.ShapeDtypeStruct(one.shape, one.dtype))
    grouped = []
    for one in landings:
        groups = one.shape[0] // experts_local
        grouped.append(one.reshape(groups, experts_local, *one.shape[1:]))
        block = (one.shape[1] // halves, one.shape[2])
        in_specs.append(
            pl.BlockSpec(
                (groups, 1, *block), lambda step: (0, step // halves, step % halves, 0)
            )
        )
        out_specs.append(
            pl.BlockSpec((1, *block), lambda step: (step // halves, step % halves, 0))
        )
        shapes.append(jax.ShapeDtypeStruct((experts_local, *one.shape[1:]), jnp.float32))
    return pl.pallas_call(
        functools.partial(finish_kernel, len(results)),
        grid=(steps,),
        in_specs=in_specs,
        out_specs=out_specs,
        out_shape=shapes,
        compiler_params=pltpu.CompilerParams(vmem_limit_bytes=63 * 2**20),
    )(*results, *grouped)


def shards(
    tokens,
    norm_gains,
    w_query,
    w_key,
    w_value,
    w_out,
    w_router,
    w_gate,
    w_up,
    w_down,
    segment_ids,
    expert_ids,
    expert_slots,
    cotangent,
):
    half_type = jnp.bfloat16
    model_width = tokens.shape[1]
    experts_local = w_gate.shape[0]
    seq_size = lax.axis_size("seq")
    split = lax.axis_size("fsdp")
    length = seq_size * tokens.shape[0]
    sizes = (seq_size, split, seq_size // 2, experts_local)
    cosine_wide, sine_wide = rope_tables(length, HEAD_DIM)
    segment_row = segment_ids.reshape(1, -1)
    (
        normed_seq,
        qkv_stack,
        out_stack,
        query_heads,
        key_heads,
        value_heads,
        unit_pair,
        log_wide,
        attended_heads,
        square_sums,
        residual,
        gain_rows,
        segment_cols,
        routed_seq,
        routed_cross,
        placed,
        gate_full,
        up_full,
        down_full,
        choices,
        onehot,
        mate_onehot,
    ) = front(
        sizes,
        tokens,
        norm_gains,
        cosine_wide,
        sine_wide,
        segment_row,
        expert_ids.T,
        expert_slots.T,
        cotangent,
        (w_query, w_key, w_value, w_out, w_gate, w_up, w_down),
        0,
    )
    router_rows = jnp.zeros((seq_size, 8, model_width), half_type)
    router_rows = router_rows.at[:, :experts_local].set(
        w_router.T.reshape(seq_size, experts_local, model_width)
    )
    router_rows = router_rows.reshape(seq_size * 8, model_width)
    (
        residual_grad,
        out_grad,
        gain_second_grad,
        router_grad,
        hidden,
        grad_gate_full,
        grad_up_full,
        down_landing,
        _,
    ) = experts(
        sizes,
        routed_seq,
        routed_cross,
        choices,
        onehot,
        mate_onehot,
        placed,
        router_rows,
        gain_rows,
        residual,
        cotangent,
        (gate_full, up_full, down_full),
        1,
    )
    input_grad, gain_grads, out_owned, mixed_rows, gate_landing, qkv_parts = back(
        sizes,
        out_grad,
        (gain_rows, gain_second_grad, segment_row, square_sums),
        (
            out_stack,
            attended_heads,
            query_heads,
            key_heads,
            value_heads,
            segment_cols,
            log_wide,
            cosine_wide,
            sine_wide,
            unit_pair,
            qkv_stack,
            tokens,
            residual_grad,
        ),
        (normed_seq, hidden, down_full, grad_gate_full),
        2,
    )
    output, gain_sums, router_sums, query_owned, key_owned, value_owned, up_landing = close(
        sizes, onehot, gain_grads, router_grad, mixed_rows, residual, qkv_parts, grad_up_full, 3
    )
    (
        output,
        input_grad,
        gain_sums,
        query_owned,
        key_owned,
        value_owned,
        out_owned,
        router_sums,
        gate_owned,
        up_owned,
        down_owned,
    ) = finish(
        (
            output,
            input_grad,
            gain_sums,
            query_owned,
            key_owned,
            value_owned,
            out_owned,
            router_sums,
        ),
        (gate_landing, up_landing, down_landing),
        experts_local,
    )
    return (
        output,
        input_grad,
        gain_sums,
        query_owned,
        key_owned,
        value_owned,
        out_owned,
        router_sums.T,
        gate_owned,
        up_owned,
        down_owned,
    )


def solution(mesh):
    in_specs = (
        P(("fsdp", "seq"), None),
        P(),
        P("fsdp", "seq"),
        P("fsdp", "seq"),
        P("fsdp", "seq"),
        P("seq", "fsdp"),
        P(),
        P("seq", "fsdp", None),
        P("seq", "fsdp", None),
        P("seq", None, "fsdp"),
        P("fsdp"),
        P(("fsdp", "seq"), None),
        P(("fsdp", "seq"), None),
        P(("fsdp", "seq"), None),
    )
    out_specs = (
        P(("fsdp", "seq"), None),
        P(("fsdp", "seq"), None),
        P(),
        P("fsdp", "seq"),
        P("fsdp", "seq"),
        P("fsdp", "seq"),
        P("seq", "fsdp"),
        P(),
        P("seq", "fsdp", None),
        P("seq", "fsdp", None),
        P("seq", None, "fsdp"),
    )
    return jax.shard_map(shards, mesh=mesh, in_specs=in_specs, out_specs=out_specs, check_vma=False)
```

```python
import functools

import jax
import jax.numpy as jnp
import numpy as np
from jax import lax
from jax.experimental import pallas as pl
from jax.experimental.pallas import tpu as pltpu
from jax.sharding import PartitionSpec as P

HEAD_DIM = 128
CAP = 40


EPSILON = 1e-06
THETA = 10000.0
MASKED = -1e30
HIGHEST = lax.Precision.HIGHEST


def rope_tables(length, head_size):
    half_dim = head_size // 2
    frequency = THETA ** (-np.arange(half_dim, dtype=np.float64) / half_dim)
    angles = np.arange(length, dtype=np.float64)[:, None] * frequency.astype(np.float32)
    cosine, sine = np.cos(angles), np.sin(angles)
    return (
        jnp.asarray(np.concatenate([cosine, cosine], 1), jnp.float32),
        jnp.asarray(np.concatenate([-sine, sine], 1), jnp.float32),
    )


class ChainGather:
    def __init__(self, chips, x_ref, out_ref, local_sem, sends, arrivals):
        self.chips, self.x_ref, self.out_ref = chips, x_ref, out_ref
        self.local_sem, self.sends, self.arrivals = local_sem, sends, arrivals
        me = lax.axis_index("seq")
        self.chip, self.core = me // 2, lax.rem(me, 2)
        self.rows = x_ref.shape[0]

    def block(self, source, core):
        start = pl.multiple_of((source * 2 + core) * self.rows, self.rows)
        return self.out_ref.at[pl.ds(start, self.rows)]

    def hop(self, source, ref, target, way, lane):
        return pltpu.make_async_remote_copy(
            src_ref=ref,
            dst_ref=self.block(source, self.core),
            send_sem=self.sends.at[way, source],
            recv_sem=self.arrivals.at[lane, source],
            device_id={"seq": target},
        )

    def upward(self, source, ref):
        return self.hop(source, ref, self.chip * 2 + 2 + self.core, 0, 0)

    def downward(self, source, ref):
        return self.hop(source, ref, self.chip * 2 - 2 + self.core, 1, 0)

    def sideways(self, source, ref):
        return self.hop(source, ref, self.chip * 2 + 1 - self.core, 2, 1)

    def own(self):
        return pltpu.make_async_copy(
            self.x_ref, self.block(self.chip, self.core), self.local_sem
        )

    def start(self):
        @pl.when(self.chip < self.chips - 1)
        def _():
            self.upward(self.chip, self.x_ref).start()

        @pl.when(self.chip > 0)
        def _():
            self.downward(self.chip, self.x_ref).start()

        self.sideways(self.chip, self.x_ref).start()
        self.own().start()

    def step(self, distance):
        below, above = self.chip - distance, self.chip + distance

        @pl.when(below >= 0)
        def _():
            landed = self.block(below, self.core)
            self.upward(below, landed).wait_recv()

            @pl.when(self.chip < self.chips - 1)
            def _():
                self.upward(below, landed).start()

            self.sideways(below, landed).start()

        @pl.when(above < self.chips)
        def _():
            landed = self.block(above, self.core)
            self.downward(above, landed).wait_recv()

            @pl.when(self.chip > 0)
            def _():
                self.downward(above, landed).start()

            self.sideways(above, landed).start()

    def steps(self):
        for distance in range(1, self.chips):
            self.step(distance)

    def landed(self):
        self.own().wait()
        for source in range(self.chips):
            self.sideways(source, self.block(source, self.core)).wait_recv()

    def sent(self):
        for source in range(self.chips):
            ref = self.block(source, self.core)
            self.sideways(source, ref).wait_send()

            @pl.when((self.chip < self.chips - 1) & (source <= self.chip))
            def _():
                self.upward(source, ref).wait_send()

            @pl.when((self.chip > 0) & (source >= self.chip))
            def _():
                self.downward(source, ref).wait_send()


class ChainReduce:
    def __init__(self, chips, total, buffers):
        self.total = total
        (
            self.side_out,
            self.side_in,
            self.chain_in,
            self.side_send,
            self.side_recv,
            self.chain_send,
            self.chain_recv,
        ) = buffers
        self.chips = chips
        me = lax.axis_index("seq")
        self.chip, self.core = me // 2, lax.rem(me, 2)

    @staticmethod
    def scratch(chips, rows, width):
        half = jnp.bfloat16
        return [
            pltpu.VMEM((chips, rows, width), half),
            pltpu.VMEM((chips, rows, width), half),
            pltpu.VMEM((chips + 1, rows, width), half),
            pltpu.SemaphoreType.DMA((chips,)),
            pltpu.SemaphoreType.DMA((chips,)),
            pltpu.SemaphoreType.DMA((chips,)),
            pltpu.SemaphoreType.DMA((2, chips)),
        ]

    def side_copy(self, dest):
        return pltpu.make_async_remote_copy(
            src_ref=self.side_out.at[dest],
            dst_ref=self.side_in.at[dest],
            send_sem=self.side_send.at[dest],
            recv_sem=self.side_recv.at[dest],
            device_id={"seq": self.chip * 2 + 1 - self.core},
        )

    def chain_copy(self, way, dest, target):
        return pltpu.make_async_remote_copy(
            src_ref=self.side_out.at[dest],
            dst_ref=self.chain_in.at[self.slot(way, dest, target // 2)],
            send_sem=self.chain_send.at[dest],
            recv_sem=self.chain_recv.at[way, dest],
            device_id={"seq": target},
        )

    def slot(self, way, dest, holder):
        return jnp.where(dest == holder, self.chips, dest) if way else dest

    def place(self, index):
        distance = self.chips - 1 - index // 2
        dest = self.chip + (1 - 2 * lax.rem(index, 2)) * distance
        return dest, (dest >= 0) & (dest < self.chips)

    def run(self, product, between=None, hook=None):
        chips, chip, core, total = self.chips, self.chip, self.core, self.total
        sibling = chip * 2 + 1 - core

        @pl.loop(0, 2 * chips - 1)
        def _(index):
            dest, inside = self.place(index)

            @pl.when(inside)
            def _():
                def store(cols, part):
                    self.side_out[dest, :, cols] = part.astype(self.side_out.dtype)

                product(dest * 2 + 1 - core, store)
                self.side_copy(dest).start()

        if between:
            between()

        @pl.loop(0, 2 * chips - 1)
        def _(index):
            dest, inside = self.place(index)
            if hook:
                hook(index)

            @pl.when(inside)
            def _():
                def store(cols, part):
                    total[:, cols] = part

                product(dest * 2 + core, store)
                self.side_copy(dest).wait_recv()
                total[...] += self.side_in[dest].astype(jnp.float32)

                @pl.when((dest >= chip) & (chip > 0))
                def _():
                    self.chain_copy(0, dest, sibling).wait_recv()
                    total[...] += self.chain_in[dest].astype(jnp.float32)

                @pl.when((dest <= chip) & (chip < chips - 1))
                def _():
                    self.chain_copy(1, dest, sibling).wait_recv()
                    total[...] += self.chain_in[self.slot(1, dest, chip)].astype(jnp.float32)

                self.side_copy(dest).wait_send()

                @pl.when(dest != chip)
                def _():
                    self.side_out[dest] = total[...].astype(self.side_out.dtype)

                @pl.when(dest > chip)
                def _():
                    self.chain_copy(0, dest, chip * 2 + 2 + core).start()

                @pl.when(dest < chip)
                def _():
                    self.chain_copy(1, dest, chip * 2 - 2 + core).start()

    def sent(self):
        sibling = self.chip * 2 + 1 - self.core

        @pl.loop(0, self.chips)
        def _(dest):
            @pl.when(dest != self.chip)
            def _():
                self.chain_copy(0, dest, sibling).wait_send()


def partner_of(index, move):
    turned, bit = index, 1
    while bit <= move:
        if move // bit % 2:
            turned = turned + bit - 2 * bit * lax.rem(index // bit, 2)
        bit *= 2
    return turned


def greet_all(size, split):
    me, mine = lax.axis_index("seq"), lax.axis_index("fsdp")
    barrier = pltpu.get_barrier_semaphore()
    for shift in range(1, size):
        pl.semaphore_signal(barrier, inc=1, device_id={"seq": lax.rem(me + shift, size)})
    for shift in range(1, split):
        pl.semaphore_signal(barrier, inc=1, device_id={"fsdp": lax.rem(mine + shift, split)})
    pl.semaphore_wait(barrier, size + split - 2)


def turned_halves(head):
    return pltpu.roll(head, head.shape[-1] // 2, 1)


def row_sums(values, pick):
    return lax.dot_general(
        pick, values, (((1,), (1,)), ((), ())), precision=HIGHEST, preferred_element_type=jnp.float32
    )


def column_of(row_form, pick):
    return lax.dot_general(
        row_form, pick, (((0,), (0,)), ((), ())), precision=HIGHEST, preferred_element_type=jnp.float32
    )


def front_kernel(
    sizes,
    tokens_ref,
    gains_in_ref,
    cos_ref,
    sin_ref,
    seg_row_ref,
    ids_ref,
    slots_ref,
    cotangent_ref,
    wq_ref,
    wk_ref,
    wv_ref,
    wo_ref,
    w_gate_ref,
    w_up_ref,
    w_down_ref,
    normed_out,
    qkv_out,
    rows_out,
    q_out,
    k_out,
    v_out,
    unit_out,
    log_out,
    attended_out,
    sums_ref,
    residual_out,
    gains_ref,
    seg_col_out,
    routed_out,
    routed_cross,
    placed_out,
    gate_full,
    up_full,
    down_full,
    choices,
    onehot_out,
    mate_out,
    seg_col_ref,
    onehot_ref,
    mate_onehot,
    residual_ref,
    q_ref,
    k_ref,
    v_ref,
    unit_ref,
    log_ref,
    attended_ref,
    normed,
    qkv,
    rows_full,
    routed_own,
    choice_own,
    cotangent_pair,
    cotangent_all,
    mate_choices,
    placed,
    raw,
    sums_own,
    sums_in,
    gather_local,
    gather_send,
    gather_recv,
    sums_send,
    sums_recv,
    choice_send,
    choice_recv,
    mate_send,
    mate_recv,
    cross_local,
    cross_send,
    cross_recv,
    placed_local,
    shard_local,
    shard_send,
    shard_recv,
    expert_local,
    expert_send,
    expert_recv,
    out_sem,
    *reduce_buffers,
):
    size, split, chips, experts_local = sizes
    f32, half = jnp.float32, jnp.bfloat16
    me, mine = lax.axis_index("seq"), lax.axis_index("fsdp")
    tok_rows, model_width = tokens_ref.shape
    length, local_width = q_ref.shape
    part = model_width // split
    head = HEAD_DIM
    heads = local_width // head

    inputs = tokens_ref[...].astype(f32)
    inverse = lax.rsqrt(jnp.mean(inputs * inputs, -1, keepdims=True) + EPSILON)
    gains_ref[...] = gains_in_ref[...].astype(f32)
    routed_half = routed_own.at[pl.ds(0, tok_rows)]
    routed_half[...] = (inputs * inverse * gains_ref[0:1, :]).astype(half)
    crossed = split == experts_local == 4
    half_width = model_width // 2
    x_mate, y_mate = {"fsdp": partner_of(mine, 1)}, {"fsdp": partner_of(mine, 2)}
    greet_all(size, split)

    def gather(index, x_ref, out_ref):
        return ChainGather(
            chips,
            x_ref,
            out_ref,
            gather_local.at[index],
            gather_send.at[index],
            gather_recv.at[index],
        )

    first = gather(0, routed_half, normed)
    first.start()

    cross_rows = pl.ds(tok_rows, tok_rows)
    lower, upper = pl.ds(0, half_width), pl.ds(half_width, half_width)

    def cross_copy(index):
        cols = (lower, upper)[index % 2]
        source, target = (
            (cotangent_ref, cotangent_pair) if index < 2 else (routed_half, routed_own)
        )
        return pltpu.make_async_remote_copy(
            src_ref=source.at[:, cols],
            dst_ref=target.at[cross_rows, cols],
            send_sem=cross_send.at[index],
            recv_sem=cross_recv.at[index],
            device_id=(x_mate, y_mate)[index % 2],
        )

    if crossed:
        cross_own = pltpu.make_async_copy(
            cotangent_ref, cotangent_pair.at[pl.ds(0, tok_rows)], cross_local
        )
        cross_copy(0).start()
        cross_copy(1).start()
        cross_own.start()

    top_count = ids_ref.shape[0]
    ids_row, slots_row = ids_ref[...], slots_ref[...]
    choice_own[0:top_count, :] = ids_row
    choice_own[top_count : 2 * top_count, :] = jnp.where(
        slots_row < CAP, ids_row * CAP + slots_row, -(10**6)
    )

    def choice_copy(shift):
        return pltpu.make_async_remote_copy(
            src_ref=choice_own,
            dst_ref=choices.at[me],
            send_sem=choice_send.at[shift],
            recv_sem=choice_recv.at[shift],
            device_id={"seq": lax.rem(me + shift, size)},
        )

    own_part = pl.ds(pl.multiple_of(mine * part, part), part)
    shard_pairs = (
        (wq_ref, qkv.at[0, own_part]),
        (wk_ref, qkv.at[1, own_part]),
        (wv_ref, qkv.at[2, own_part]),
        (wo_ref, rows_full.at[mine]),
    )

    def shard_copy(index, shift):
        source, target = shard_pairs[index]
        return pltpu.make_async_remote_copy(
            src_ref=source,
            dst_ref=target,
            send_sem=shard_send.at[index, shift],
            recv_sem=shard_recv.at[index, shift],
            device_id={"fsdp": lax.rem(mine + shift, split)},
        )

    def landed_half(index, owner, side):
        if index == 3:
            rows = local_width // 2
            return rows_full.at[owner, pl.ds(side * rows, rows)]
        rows = part // 2
        start = pl.multiple_of(owner * part + side * rows, rows)
        return qkv.at[index, pl.ds(start, rows)]

    def relay_copy(index, step):
        if step < 2:
            source, target = shard_pairs[index]
        else:
            source = target = landed_half(index, partner_of(mine, step - 1), step - 2)
        return pltpu.make_async_remote_copy(
            src_ref=source,
            dst_ref=target,
            send_sem=shard_send.at[index, step],
            recv_sem=shard_recv.at[index, step],
            device_id=(x_mate, y_mate, y_mate, x_mate)[step],
        )

    def shard_own(index):
        source, target = shard_pairs[index]
        return pltpu.make_async_copy(source, target, shard_local.at[index])

    for index in range(4):
        if split == 4:
            relay_copy(index, 0).start()
            relay_copy(index, 1).start()
        else:
            for shift in range(1, split):
                shard_copy(index, shift).start()
        shard_own(index).start()

    def expert_pair(index, dest):
        expert = lax.rem(dest, experts_local)
        if index == 2:
            return w_down_ref.at[expert], down_full.at[:, own_part]
        source, target = ((w_gate_ref, gate_full), (w_up_ref, up_full))[index]
        return source.at[expert], target.at[own_part]

    def expert_copy(index, shift):
        dest = lax.rem(mine + shift, split)
        source, target = expert_pair(index, dest)
        return pltpu.make_async_remote_copy(
            src_ref=source,
            dst_ref=target,
            send_sem=expert_send.at[index, shift],
            recv_sem=expert_recv.at[index, shift],
            device_id={"fsdp": dest},
        )

    def expert_own(index):
        source, target = expert_pair(index, mine)
        return pltpu.make_async_copy(source, target, expert_local.at[index])

    for distance in range(1, chips):
        first.step(distance)
        if split == 4 and distance == min(2, chips - 1):
            for index in range(4):
                for step in range(2):
                    relay_copy(index, step).wait_recv()
                    relay_copy(index, step + 2).start()
    for index in range(4):
        shard_own(index).wait()
        if split == 4:
            relay_copy(index, 2).wait_recv()
            relay_copy(index, 3).wait_recv()
        else:
            for shift in range(1, split):
                shard_copy(index, shift).wait_recv()

    def expert_start(index):
        for shift in range(1, split):
            expert_copy(index, shift).start()
        expert_own(index).start()

    expert_start(0)
    first.landed()
    for shift in range(1, size):
        choice_copy(shift).start()
    choices[me] = choice_own[...]
    if crossed:
        cross_own.wait()
        cross_copy(0).wait()
        cross_copy(1).wait()
        second = gather(1, cotangent_pair, cotangent_all)
    else:
        second = gather(1, cotangent_ref, cotangent_all)
    second.start()
    keeps = [
        pltpu.make_async_copy(normed, normed_out, out_sem.at[0]),
        pltpu.make_async_copy(qkv, qkv_out, out_sem.at[1]),
        pltpu.make_async_copy(rows_full, rows_out, out_sem.at[2]),
    ]
    for keep in keeps:
        keep.start()

    own_cols = pl.ds(pl.multiple_of(me * local_width, local_width), local_width)
    block = min(512, length)
    lanes = lax.broadcasted_iota(jnp.int32, (8, local_width), 0)
    first_row, second_row = (lanes == 0).astype(f32), (lanes == 1).astype(f32)

    @pl.loop(0, length // block)
    def _(step):
        rows = pl.ds(pl.multiple_of(step * block, block), block)
        left = normed[rows, :]
        query = jnp.dot(left, qkv[0], preferred_element_type=f32)
        raw[0, rows, :] = query
        keys = jnp.dot(left, qkv[1], preferred_element_type=f32)
        raw[1, rows, :] = keys
        sums_own[:, rows] = row_sums(query * query, first_row) + row_sums(keys * keys, second_row)
        v_ref[rows, :] = jnp.dot(left, qkv[2], preferred_element_type=f32).astype(half)

    def sums_copy(shift):
        return pltpu.make_async_remote_copy(
            src_ref=sums_own,
            dst_ref=sums_in.at[me],
            send_sem=sums_send.at[shift],
            recv_sem=sums_recv.at[shift],
            device_id={"seq": lax.rem(me + shift, size)},
        )

    for shift in range(1, size):
        sums_copy(shift).start()
    sums_in[me] = sums_own[...]
    for shift in range(1, size):
        sums_copy(shift).wait()
    sums_ref[...] = jnp.sum(sums_in[...], 0)
    for shift in range(1, size):
        choice_copy(shift).wait()

    def mate_copy(index):
        return pltpu.make_async_remote_copy(
            src_ref=choices,
            dst_ref=mate_choices.at[index],
            send_sem=mate_send.at[index],
            recv_sem=mate_recv.at[index],
            device_id=(x_mate, y_mate)[index],
        )

    if crossed:
        mate_copy(0).start()
        mate_copy(1).start()
    segments = seg_row_ref[...].astype(f32)
    narrow = first_row[:, 0:128]

    @pl.loop(0, length // block)
    def _(step):
        rows = pl.ds(pl.multiple_of(step * block, block), block)
        square_sums = sums_ref[:, rows]
        seg_col_ref[rows, :] = column_of(
            jnp.broadcast_to(seg_row_ref[:, rows].astype(f32), (8, block)), narrow
        )
        for index, pick, target in ((0, first_row, q_ref), (1, second_row, k_ref)):
            scale = lax.rsqrt(column_of(square_sums, pick) / model_width + EPSILON)
            unit = raw[index, rows, :] * scale
            unit_ref[index, rows, :] = unit
            scaled = unit * gains_ref[2 + index : 3 + index, own_cols]
            for number in range(heads):
                cols = slice(number * head, (number + 1) * head)
                piece = scaled[:, cols]
                target[rows, cols] = (
                    piece * cos_ref[rows, :] + turned_halves(piece) * sin_ref[rows, :]
                ).astype(half)

    second.step(1)

    wide = min(256, length)
    for number in range(heads):
        cols = slice(number * head, (number + 1) * head)

        @pl.loop(0, length // wide)
        def _(step):
            rows = pl.ds(pl.multiple_of(step * wide, wide), wide)
            scores = lax.dot_general(
                q_ref[rows, cols],
                k_ref[:, cols],
                (((1,), (1,)), ((), ())),
                preferred_element_type=f32,
            )
            scores = scores * (head**-0.5)
            scores = jnp.where(seg_col_ref[rows, 0:1] == segments, scores, MASKED)
            peak = jnp.max(scores, -1, keepdims=True)
            grown = jnp.exp(scores - peak)
            weight = jnp.sum(grown, -1, keepdims=True)
            probs = (grown * (1.0 / weight)).astype(half)
            attended_ref[rows, cols] = jnp.dot(
                probs, v_ref[:, cols], preferred_element_type=f32
            ).astype(half)
            log_ref[rows, cols] = jnp.broadcast_to(peak + jnp.log(weight), (wide, head))

    expert_start(1)
    for index, (source, target) in enumerate(
        (
            (q_ref, q_out),
            (k_ref, k_out),
            (v_ref, v_out),
            (unit_ref, unit_out),
            (log_ref, log_out),
            (attended_ref, attended_out),
            (seg_col_ref, seg_col_out),
        )
    ):
        keeps.append(pltpu.make_async_copy(source, target, out_sem.at[3 + index]))
        keeps[-1].start()

    reduce = ChainReduce(chips, residual_ref, reduce_buffers)

    def product(index, store):
        left = attended_ref[pl.ds(pl.multiple_of(index * tok_rows, tok_rows), tok_rows), :]
        for piece in range(split):
            cols = pl.ds(piece * part, part)
            store(cols, jnp.dot(left, rows_full[piece], preferred_element_type=f32))

    def hook(index):
        for distance in range(2, chips - 1):

            @pl.when(index == 2 * distance)
            def _():
                second.step(distance)

    reduce.run(product, hook=hook)
    residual = tokens_ref[...].astype(f32) + reduce.total[...]
    residual_ref[...] = residual
    keeps.append(pltpu.make_async_copy(residual_ref, residual_out, out_sem.at[10]))
    keeps[-1].start()
    inverse = lax.rsqrt(jnp.mean(residual * residual, -1, keepdims=True) + EPSILON)
    first.sent()
    routed_half[...] = (residual * inverse * gains_ref[1:2, :]).astype(half)
    if crossed:
        cross_copy(2).start()
        cross_copy(3).start()
    third = gather(2, routed_half, routed_out)
    third.start()
    if chips > 2:
        second.step(chips - 1)
    expert_start(2)

    second.landed()
    double = 2 * CAP
    member = lax.rem(mine, experts_local)
    slot_row = lax.broadcasted_iota(jnp.int32, (double, tok_rows), 0)
    if crossed:
        mate_copy(0).wait()
        mate_copy(1).wait()

    def one_hot(places, target, rows, expert):
        base = (me * experts_local + expert) * CAP
        for side in range(2):
            want = jnp.where(slot_row // CAP == side, slot_row - side * CAP + base, -1)
            hit = want == places(side)[top_count : top_count + 1, :]
            for choice in range(1, top_count):
                hit = hit | (want == places(side)[top_count + choice : top_count + choice + 1, :])
            cols = slice(side * tok_rows, (side + 1) * tok_rows)
            target[rows, cols] = jnp.where(hit, 1.0, 0.0).astype(half)

    def slot_range(move):
        return slice(move * double, (move + 1) * double)

    @pl.loop(0, size // 2)
    def _(pair):
        for move in range(experts_local):
            one_hot(
                lambda side: choices[pair * 2 + side],
                onehot_ref.at[pair],
                slot_range(move),
                partner_of(member, move),
            )
        if crossed:
            start = pl.multiple_of(pair * 4 * tok_rows, 4 * tok_rows)
            four = cotangent_all[pl.ds(start, 4 * tok_rows), :]
            own = jnp.concatenate(
                [four[0:tok_rows], four[2 * tok_rows : 3 * tok_rows]], 0
            )
            mates = jnp.concatenate(
                [four[tok_rows : 2 * tok_rows], four[3 * tok_rows : 4 * tok_rows]], 0
            )
            made = jnp.dot(onehot_ref[pair], own, preferred_element_type=f32).astype(half)
            placed[0, pair] = made[slot_range(0)]
            placed[1, pair, :, upper] = made[slot_range(1), half_width:]
            placed[2, pair, :, lower] = made[slot_range(2), :half_width]
            for index in range(2):
                for row, expert in enumerate((member, partner_of(member, 2 - index))):
                    one_hot(
                        lambda side: mate_choices[index, pair * 2 + side],
                        mate_onehot.at[pair, index],
                        slot_range(row),
                        expert,
                    )
                cols = (lower, upper)[index]
                taken = mates[:, :half_width] if index == 0 else mates[:, half_width:]
                made = jnp.dot(
                    mate_onehot[pair, index], taken, preferred_element_type=f32
                ).astype(half)
                placed[index + 1, pair, :, cols] = made[slot_range(0)]
                placed[3, pair, :, cols] = made[slot_range(1)]
        else:
            start = pl.multiple_of(pair * 2 * tok_rows, 2 * tok_rows)
            made = jnp.dot(
                onehot_ref[pair],
                cotangent_all[pl.ds(start, 2 * tok_rows), :],
                preferred_element_type=f32,
            ).astype(half)
            for move in range(experts_local):
                placed[move, pair] = made[slot_range(move)]

    placed_keep = pltpu.make_async_copy(placed, placed_out, placed_local.at[0])
    placed_keep.start()
    for index, (source, target) in enumerate(((onehot_ref, onehot_out), (mate_onehot, mate_out))):
        keeps.append(pltpu.make_async_copy(source, target, out_sem.at[11 + index]))
        keeps[-1].start()
    third.steps()
    third.landed()
    if crossed:
        cross_copy(2).wait()
        cross_copy(3).wait()
        cross_keep = pltpu.make_async_copy(
            routed_own.at[cross_rows], routed_cross, placed_local.at[1]
        )
        cross_keep.start()
    reduce.sent()
    second.sent()
    third.sent()
    for index in range(4):
        if split == 4:
            for step in range(4):
                relay_copy(index, step).wait_send()
        else:
            for shift in range(1, split):
                shard_copy(index, shift).wait_send()
    for keep in keeps:
        keep.wait()
    placed_keep.wait()
    if crossed:
        cross_keep.wait()
    for index in range(3):
        expert_own(index).wait()
        for shift in range(1, split):
            expert_copy(index, shift).wait()


def front(sizes, tokens, gains, cos, sin, segment_row, ids, slots, cotangent, weights, which):
    size, split, chips, experts_local = sizes
    w_query, w_key, w_value, w_out, w_gate, w_up, w_down = weights
    tok_rows, model_width = tokens.shape
    length = size * tok_rows
    local_width = w_query.shape[1]
    hidden_width = w_gate.shape[2]
    f32, half = jnp.float32, jnp.bfloat16
    vmem = pl.BlockSpec(memory_space=pltpu.VMEM)
    anywhere = pl.BlockSpec(memory_space=pl.ANY)
    kind = pltpu.SemaphoreType.DMA
    shape = jax.ShapeDtypeStruct
    crossed = split == experts_local == 4
    choices = (size, 2 * ids.shape[0], tok_rows)
    return pl.pallas_call(
        functools.partial(front_kernel, sizes),
        out_shape=(
            shape((length, model_width), half),
            shape((3, model_width, local_width), half),
            shape((split, *w_out.shape), half),
            shape((length, local_width), half),
            shape((length, local_width), half),
            shape((length, local_width), half),
            shape((2, length, local_width), f32),
            shape((length, local_width), f32),
            shape((length, local_width), half),
            shape((8, length), f32),
            shape((tok_rows, model_width), f32),
            shape(gains.shape, f32),
            shape((length, 128), f32),
            shape((length, model_width), half),
            shape((tok_rows, model_width), half),
            shape((experts_local, size // 2, 2 * CAP, model_width), half),
            shape((model_width, hidden_width), half),
            shape((model_width, hidden_width), half),
            shape((hidden_width, model_width), half),
            shape((size, 2 * ids.shape[0], tok_rows), jnp.int32),
            shape((size // 2, experts_local * 2 * CAP, 2 * tok_rows), half),
            shape((size // 2 if crossed else 1, 2, 4 * CAP, 2 * tok_rows), half),
        ),
        in_specs=[vmem] * 7 + [anywhere] * 8,
        out_specs=tuple(
            [anywhere] * 9 + [vmem, anywhere, vmem, anywhere] + [anywhere] * 6 + [vmem, anywhere, anywhere]
        ),
        scratch_shapes=[
            pltpu.VMEM((length, 128), f32),
            pltpu.VMEM((size // 2, experts_local * 2 * CAP, 2 * tok_rows), half),
            pltpu.VMEM((size // 2 if crossed else 1, 2, 4 * CAP, 2 * tok_rows), half),
            pltpu.VMEM((tok_rows, model_width), f32),
            pltpu.VMEM((length, local_width), half),
            pltpu.VMEM((length, local_width), half),
            pltpu.VMEM((length, local_width), half),
            pltpu.VMEM((2, length, local_width), f32),
            pltpu.VMEM((length, local_width), f32),
            pltpu.VMEM((length, local_width), half),
            pltpu.VMEM((length, model_width), half),
            pltpu.VMEM((3, model_width, local_width), half),
            pltpu.VMEM((split, *w_out.shape), half),
            pltpu.VMEM((2 * tok_rows, model_width), half),
            pltpu.VMEM((2 * ids.shape[0], tok_rows), jnp.int32),
            pltpu.VMEM((2 * tok_rows if crossed else 16, model_width), half),
            pltpu.VMEM(((2 if crossed else 1) * length, model_width), half),
            pltpu.VMEM((2, *(choices if crossed else (1, 8, 128))), jnp.int32),
            pltpu.VMEM((experts_local, size // 2, 2 * CAP, model_width), half),
            pltpu.VMEM((2, length, local_width), f32),
            pltpu.VMEM((8, length), f32),
            pltpu.VMEM((size, 8, length), f32),
            kind((3,)),
            kind((3, 3, chips)),
            kind((3, 2, chips)),
            kind((size,)),
            kind((size,)),
            kind((size,)),
            kind((size,)),
            kind((2,)),
            kind((2,)),
            kind,
            kind((4,)),
            kind((4,)),
            kind((2,)),
            kind((4,)),
            kind((4, split)),
            kind((4, split)),
            kind((3,)),
            kind((3, split)),
            kind((3, split)),
            kind((13,)),
            *ChainReduce.scratch(chips, tok_rows, model_width),
        ],
        compiler_params=pltpu.CompilerParams(
            collective_id=which, has_side_effects=True, vmem_limit_bytes=58 * 2**20
        ),
        cost_estimate=pl.CostEstimate(
            flops=2 * length * model_width * local_width * 4,
            bytes_accessed=500 * 2**20,
            transcendentals=0,
        ),
    )(
        tokens, gains, cos, sin, segment_row, ids, slots, cotangent, *weights
    )


class ShardSend:
    def __init__(self, split, source, landing, local_sem, sends, arrivals):
        self.split, self.source, self.landing = split, source, landing
        self.local_sem, self.sends, self.arrivals = local_sem, sends, arrivals
        self.mine = lax.axis_index("fsdp")

    def copy(self, shift):
        dest = lax.rem(self.mine + shift, self.split)
        return pltpu.make_async_remote_copy(
            src_ref=self.source(dest),
            dst_ref=self.landing.at[self.mine],
            send_sem=self.sends.at[shift],
            recv_sem=self.arrivals.at[shift],
            device_id={"fsdp": dest},
        )

    def own(self):
        return pltpu.make_async_copy(
            self.source(self.mine), self.landing.at[self.mine], self.local_sem
        )

    def start(self):
        for shift in range(1, self.split):
            self.copy(shift).start()
        self.own().start()

    def wait(self):
        for shift in range(1, self.split):
            self.copy(shift).wait()
        self.own().wait()


def turned_dot(left, right):
    return lax.dot_general(
        left, right, (((0,), (0,)), ((), ())), preferred_element_type=jnp.float32
    )


def cross_dot(left, right):
    return lax.dot_general(
        left, right, (((1,), (1,)), ((), ())), preferred_element_type=jnp.float32
    )


def experts_kernel(
    sizes,
    routed_ref,
    routed_cross_ref,
    choices_ref,
    onehot_ref,
    mate_onehot_any,
    placed_ref,
    router_ref,
    gains_ref,
    residual_any,
    cotangent_any,
    gate_ref,
    up_ref,
    down_ref,
    residual_grad_ref,
    out_grad_ref,
    gain_ref,
    router_grad_ref,
    hidden_out,
    grad_gate_ref,
    grad_up_ref,
    down_landing,
    routed_mates,
    mate_onehot_ref,
    residual_ref,
    cotangent_ref,
    late_sem,
    gate_full,
    up_full,
    down_full,
    upstream,
    pair_rows,
    outgoing,
    arrived,
    hidden,
    gate_grad,
    up_grad,
    back,
    gates,
    gates_out,
    gates_in,
    dots_out,
    dots_in,
    token_out,
    token_in,
    scales,
    load_sem,
    pair_sem,
    keep_sem,
    gather_local,
    gather_send,
    gather_recv,
    upstream_send,
    upstream_recv,
    rows_send,
    rows_recv,
    gates_send,
    gates_recv,
    back_send,
    back_recv,
    dots_send,
    dots_recv,
    token_send,
    token_recv,
    down_send,
    down_recv,
    *reduce_buffers,
):
    size, split, chips, experts_local = sizes
    f32, half = jnp.float32, jnp.bfloat16
    me, mine = lax.axis_index("seq"), lax.axis_index("fsdp")
    tok_rows, model_width = residual_ref.shape
    pairs = size // 2
    double = 2 * CAP
    wide = 2 * tok_rows
    hidden_width = gate_full.shape[1]
    rows_of = pairs * double
    part = model_width // split
    member = lax.rem(mine, experts_local)
    crossed = split == experts_local == 4
    half_width = model_width // 2
    lower, upper = pl.ds(0, half_width), pl.ds(half_width, half_width)

    loads = [
        pltpu.make_async_copy(source, target, load_sem.at[index])
        for index, (source, target) in enumerate(
            (
                (gate_ref, gate_full),
                (up_ref, up_full),
                (down_ref, down_full),
            )
        )
    ]
    if crossed:
        pieces = (
            (placed_ref.at[0], upstream.at[0]),
            (placed_ref.at[1, :, :, lower], upstream.at[1, :, :, lower]),
            (placed_ref.at[2, :, :, upper], upstream.at[2, :, :, upper]),
        )
    else:
        pieces = ((placed_ref.at[0], upstream.at[0]),)
    loads += [
        pltpu.make_async_copy(source, target, load_sem.at[3 + index])
        for index, (source, target) in enumerate(pieces)
    ]

    slots = pair_rows.shape[0]

    def pair_load(source, pair):
        slot = lax.rem(pair, slots)
        start = pl.multiple_of(pair * wide, wide)
        return pltpu.make_async_copy(
            source.at[pl.ds(start, wide)], pair_rows.at[slot], pair_sem.at[slot]
        )

    pair_load(routed_ref, 0).start()
    for load in loads:
        load.start()
    late_loads = [
        pltpu.make_async_copy(source, target, late_sem.at[index])
        for index, (source, target) in enumerate(
            (
                (mate_onehot_any, mate_onehot_ref),
                (residual_any, residual_ref),
                (cotangent_any, cotangent_ref),
            )
        )
    ]
    for load in late_loads:
        load.start()
    greet_all(size, split)

    def mate(move):
        return {"fsdp": partner_of(mine, move)}

    def upstream_piece(move, index, cols, target):
        return pltpu.make_async_remote_copy(
            src_ref=placed_ref.at[move, :, :, cols],
            dst_ref=upstream.at[move, :, :, cols],
            send_sem=upstream_send.at[index],
            recv_sem=upstream_recv.at[index],
            device_id=mate(target),
        )

    def halves_of(piece, move):
        if not crossed:
            return [piece(move, move, pl.ds(0, model_width), move)]
        if move == 3:
            return [piece(3, 3, upper, 1), piece(3, 0, lower, 2)]
        return [piece(move, move, (upper, lower)[move - 1], move)]

    order = [1, 2, 3] if crossed else list(range(experts_local - 1, 0, -1))
    if crossed:
        gather = ChainGather(
            chips, routed_cross_ref, routed_mates, gather_local, gather_send, gather_recv
        )
        gather.start()
    for move in order:
        if not crossed or move < 3:
            for copy in halves_of(upstream_piece, move):
                copy.start()

    padded = size * 8
    expert_row = lax.broadcasted_iota(jnp.int32, (padded, tok_rows), 0)
    inner = lax.rem(expert_row, 8)
    expert_row = jnp.where(inner < experts_local, expert_row // 8 * experts_local + inner, -1)
    ones = jnp.ones((8, wide), f32)
    top_count = choices_ref.shape[1] // 2

    @pl.loop(0, pairs)
    def _(pair):
        pair_load(routed_ref, pair).wait()

        @pl.when((pair + 1 < pairs) & (slots > 1))
        def _():
            pair_load(routed_ref, pair + 1).start()

        rows = pair_rows[lax.rem(pair, slots)]
        logits = lax.dot_general(
            router_ref[...], rows, (((1,), (1,)), ((), ())), preferred_element_type=f32
        )
        for side in range(2):
            ids = choices_ref[pair * 2 + side]
            chosen = expert_row == ids[0:1, :]
            for choice in range(1, top_count):
                chosen = chosen | (expert_row == ids[choice : choice + 1, :])
            own = jnp.where(chosen, logits[:, side * tok_rows : (side + 1) * tok_rows], MASKED)
            grown = jnp.where(chosen, jnp.exp(own - jnp.max(own, 0, keepdims=True)), 0.0)
            gates[pair * 2 + side] = grown / jnp.sum(grown, 0, keepdims=True)
        placed = jnp.dot(onehot_ref[pair], rows, preferred_element_type=f32).astype(half)
        for move in range(experts_local):
            piece = placed[move * double : (move + 1) * double]
            if move == 0:
                arrived[0, pair] = piece
            elif not crossed:
                outgoing[move - 1, pair] = piece
            elif move < 3:
                cols = (upper, lower)[move - 1]
                outgoing[move - 1, pair, :, cols] = (
                    piece[:, half_width:] if move == 1 else piece[:, :half_width]
                )
            row = me * 8 + partner_of(member, move)
            weights = jnp.concatenate(
                [gates[pair * 2, pl.ds(row, 1), :], gates[pair * 2 + 1, pl.ds(row, 1), :]], 1
            )
            slot_rows = pl.ds(move * double, double)
            weighted = onehot_ref[pair, slot_rows, :].astype(f32) * weights
            gates_out[move, pair] = row_sums(weighted, ones)

        @pl.when((pair + 1 < pairs) & (slots == 1))
        def _():
            pair_load(routed_ref, pair + 1).start()

    def rows_piece(move, index, cols, target):
        return pltpu.make_async_remote_copy(
            src_ref=outgoing.at[move - 1, :, :, cols],
            dst_ref=arrived.at[move, :, :, cols],
            send_sem=rows_send.at[index],
            recv_sem=rows_recv.at[index],
            device_id=mate(target),
        )

    def gates_copy(move):
        return pltpu.make_async_remote_copy(
            src_ref=gates_out.at[move],
            dst_ref=gates_in.at[move],
            send_sem=gates_send.at[move],
            recv_sem=gates_recv.at[move],
            device_id=mate(move),
        )

    def back_rows(move):
        return back.at[:, pl.ds(move * double, double), :]

    def back_copy(move):
        return pltpu.make_async_remote_copy(
            src_ref=outgoing.at[move - 1],
            dst_ref=back_rows(move),
            send_sem=back_send.at[move],
            recv_sem=back_recv.at[move],
            device_id=mate(move),
        )

    def dots_copy(move):
        return pltpu.make_async_remote_copy(
            src_ref=dots_out.at[move],
            dst_ref=dots_in.at[move],
            send_sem=dots_send.at[move],
            recv_sem=dots_recv.at[move],
            device_id=mate(move),
        )

    for move in order:
        gates_copy(move).start()
        if not crossed or move < 3:
            for copy in halves_of(rows_piece, move):
                copy.start()
    if crossed:
        for copy in halves_of(upstream_piece, 3):
            copy.start()
    gates_in[0] = gates_out[0]
    for load in loads + late_loads:
        load.wait()
    if crossed:
        gather.step(1)

    def mates_rows():
        for distance in range(3, chips):
            gather.step(distance)
        gather.landed()
        pair_load(routed_mates, 0).start()

        @pl.loop(0, pairs)
        def _(pair):
            pair_load(routed_mates, pair).wait()

            @pl.when(pair + 1 < pairs)
            def _():
                pair_load(routed_mates, pair + 1).start()

            for index, cols in enumerate((lower, upper)):
                made = jnp.dot(
                    mate_onehot_ref[pair, index],
                    pair_rows[lax.rem(pair, slots), :, cols],
                    preferred_element_type=f32,
                ).astype(half)
                arrived[index + 1, pair, :, cols] = made[0:double]
                outgoing[2, pair, :, cols] = made[double:]

        for copy in halves_of(rows_piece, 3):
            copy.start()
        gather.sent()

    cols_step = min(256, hidden_width)
    width_step = min(512, model_width)
    spread = (lax.broadcasted_iota(jnp.int32, (8, 128), 0) == 0).astype(f32)
    for move in [0] + order:
        if move:
            gates_copy(move).wait()
            for copy in halves_of(rows_piece, move) + halves_of(upstream_piece, move):
                copy.wait()
        for pair in range(pairs):
            scales[pair * double : (pair + 1) * double, :] = column_of(
                gates_in[move, pair], spread
            )
        dots_out[move] = jnp.zeros_like(dots_out[move])

        @pl.loop(0, hidden_width // cols_step)
        def _(index):
            cols = pl.ds(pl.multiple_of(index * cols_step, cols_step), cols_step)
            rows = arrived[move].reshape(rows_of, model_width)
            pre = jnp.dot(rows, gate_full[:, cols], preferred_element_type=f32)
            up = jnp.dot(rows, up_full[:, cols], preferred_element_type=f32)
            plain = lax.dot_general(
                upstream[move].reshape(rows_of, model_width),
                down_full[cols, :],
                (((1,), (1,)), ((), ())),
                preferred_element_type=f32,
            )
            sigmoid = 1.0 / (1.0 + jnp.exp(-pre))
            active = pre * sigmoid
            made = (active * up).astype(half)
            weighted = made.astype(f32) * scales[:, 0:1]
            hidden[move, :, :, cols] = weighted.astype(half).reshape(pairs, double, cols_step)
            dots = made.astype(f32) * plain
            for pair in range(pairs):
                dots_out[move, pair] += row_sums(
                    dots[pair * double : (pair + 1) * double], jnp.ones((8, cols_step), f32)
                )
            scaled = plain * scales[:, 0:1]
            gate_back = scaled * up * sigmoid * (1.0 + pre * (1.0 - sigmoid))
            gate_grad[move, :, :, cols] = gate_back.astype(half).reshape(pairs, double, cols_step)
            up_grad[move, :, :, cols] = (
                (scaled * active).astype(half).reshape(pairs, double, cols_step)
            )

        if move:
            dots_copy(move).start()
        else:
            dots_in[0] = dots_out[0]
            if crossed and chips > 2:
                gather.step(2)

        @pl.loop(0, model_width // width_step)
        def _(index):
            cols = pl.ds(pl.multiple_of(index * width_step, width_step), width_step)
            rows_grad = lax.dot_general(
                gate_grad[move].reshape(rows_of, hidden_width),
                gate_full[cols, :],
                (((1,), (1,)), ((), ())),
                preferred_element_type=f32,
            )
            rows_grad = rows_grad + lax.dot_general(
                up_grad[move].reshape(rows_of, hidden_width),
                up_full[cols, :],
                (((1,), (1,)), ((), ())),
                preferred_element_type=f32,
            )
            rows_grad = rows_grad.astype(half).reshape(pairs, double, width_step)
            if move:
                outgoing[move - 1, :, :, cols] = rows_grad
            else:
                back[:, 0:double, cols] = rows_grad

        if move:
            back_copy(move).start()
        elif crossed:
            mates_rows()

    own_rows = pl.ds(pl.multiple_of(me * tok_rows, tok_rows), tok_rows)
    own_load = pltpu.make_async_copy(
        routed_ref.at[own_rows], pair_rows.at[0, pl.ds(0, tok_rows)], pair_sem.at[0]
    )
    own_load.start()
    hidden_keep = pltpu.make_async_copy(hidden, hidden_out, keep_sem)
    hidden_keep.start()

    total_rows = experts_local * rows_of

    def flat(ref, cols):
        return ref[:, :, :, cols].reshape(total_rows, -1)

    every = pl.ds(0, hidden_width)

    @pl.loop(0, split)
    def _(piece):
        cols = pl.ds(pl.multiple_of(piece * part, part), part)
        gate_full[cols, :] = turned_dot(flat(arrived, cols), flat(gate_grad, every)).astype(half)
        up_full[cols, :] = turned_dot(flat(arrived, cols), flat(up_grad, every)).astype(half)
        down_full[:, cols] = turned_dot(flat(hidden, every), flat(upstream, cols)).astype(half)

    grad_keeps = [
        pltpu.make_async_copy(source, target, load_sem.at[index])
        for index, (source, target) in enumerate(
            ((gate_full, grad_gate_ref), (up_full, grad_up_ref))
        )
    ]
    for keep in grad_keeps:
        keep.start()
    down_send_all = ShardSend(
        split,
        lambda dest: down_full.at[:, pl.ds(pl.multiple_of(dest * part, part), part)],
        down_landing,
        load_sem.at[2],
        down_send,
        down_recv,
    )

    for move in order:
        dots_copy(move).wait()
    token_out[...] = jnp.zeros_like(token_out)

    @pl.loop(0, pairs)
    def _(pair):
        for move in range(experts_local):
            found = jnp.dot(
                dots_in[move, pair],
                onehot_ref[pair, pl.ds(move * double, double), :].astype(f32),
                precision=HIGHEST,
                preferred_element_type=f32,
            )
            row = partner_of(member, move)
            for side in range(2):
                token_out[pair * 2 + side, pl.ds(row, 1), :] = found[
                    0:1, side * tok_rows : (side + 1) * tok_rows
                ]

    def token_copy(shift):
        peer = lax.rem(me + shift, size)
        return pltpu.make_async_remote_copy(
            src_ref=token_out.at[peer],
            dst_ref=token_in.at[me],
            send_sem=token_send.at[shift],
            recv_sem=token_recv.at[shift],
            device_id={"seq": peer},
        )

    for shift in range(1, size):
        token_copy(shift).start()
    token_in[me] = token_out[me]
    for move in order:
        back_copy(move).wait()
    down_send_all.start()

    reduce = ChainReduce(chips, residual_grad_ref, reduce_buffers)

    def product(index, store):
        side = pl.ds(pl.multiple_of(lax.rem(index, 2) * tok_rows, tok_rows), tok_rows)
        left = onehot_ref[index // 2, :, side]

        @pl.loop(0, model_width // width_step)
        def _(step):
            cols = pl.ds(pl.multiple_of(step * width_step, width_step), width_step)
            store(cols, turned_dot(left, back[index // 2, :, cols]))

    reduce.run(product)

    for shift in range(1, size):
        token_copy(shift).wait()
    own_gates = gates[me]
    grads = token_in[...].reshape(padded, tok_rows)
    mean = jnp.sum(own_gates * grads, 0, keepdims=True)
    logit_grad = (own_gates * (grads - mean)).astype(half)
    routed_grad = reduce.total[...] + turned_dot(logit_grad, router_ref[...])
    own_load.wait()
    router_grad = jnp.dot(logit_grad, pair_rows[0, 0:tok_rows, :], preferred_element_type=f32)
    for device in range(size):
        router_grad_ref[device * experts_local : (device + 1) * experts_local, :] = router_grad[
            device * 8 : device * 8 + experts_local
        ]
    residual = residual_ref[...]
    inverse = lax.rsqrt(jnp.mean(residual * residual, -1, keepdims=True) + EPSILON)
    unit = residual * inverse
    gain_ref[...] = jnp.broadcast_to(
        jnp.sum(routed_grad * unit, 0, keepdims=True), gain_ref.shape
    )
    routed_grad = routed_grad * gains_ref[1:2, :]
    routed_grad = inverse * (
        routed_grad - unit * jnp.mean(routed_grad * unit, -1, keepdims=True)
    )
    residual_grad = cotangent_ref[...].astype(f32) + routed_grad
    residual_grad_ref[...] = residual_grad
    out_grad_ref[...] = residual_grad.astype(half)
    reduce.sent()
    hidden_keep.wait()
    for keep in grad_keeps:
        keep.wait()
    down_send_all.wait()


def experts(
    sizes,
    routed_seq,
    routed_cross,
    choices,
    onehot,
    mate_onehot,
    placed,
    router_rows,
    gain_rows,
    residual,
    cotangent,
    weights,
    which,
):
    size, split, chips, experts_local = sizes
    gate_full, up_full, down_full = weights
    model_width, hidden_width = gate_full.shape
    tok_rows = residual.shape[0]
    pairs, double = size // 2, 2 * CAP
    f32, half = jnp.float32, jnp.bfloat16
    vmem = pl.BlockSpec(memory_space=pltpu.VMEM)
    anywhere = pl.BlockSpec(memory_space=pl.ANY)
    kind = pltpu.SemaphoreType.DMA
    shape = jax.ShapeDtypeStruct
    few = kind((experts_local,))
    crossed = split == experts_local == 4
    wide_rows = (experts_local, pairs, double, model_width)
    narrow_rows = (experts_local, pairs, double, hidden_width)
    flags = (experts_local, pairs, 8, double)
    return pl.pallas_call(
        functools.partial(experts_kernel, sizes),
        out_shape=(
            shape((tok_rows, model_width), f32),
            shape((tok_rows, model_width), half),
            shape((8, model_width), f32),
            shape((size * experts_local, model_width), f32),
            shape(narrow_rows, half),
            shape(gate_full.shape, half),
            shape(up_full.shape, half),
            shape((split, hidden_width, model_width // split), half),
            shape(routed_seq.shape if crossed else (16, model_width), half),
        ),
        in_specs=[anywhere] * 2 + [vmem] * 2 + [anywhere] * 2 + [vmem] * 2 + [anywhere] * 5,
        out_specs=tuple([vmem] * 4 + [anywhere] * 5),
        scratch_shapes=[
            pltpu.VMEM(mate_onehot.shape, half),
            pltpu.VMEM(residual.shape, f32),
            pltpu.VMEM(cotangent.shape, half),
            kind((3,)),
            pltpu.VMEM(gate_full.shape, half),
            pltpu.VMEM(up_full.shape, half),
            pltpu.VMEM(down_full.shape, half),
            pltpu.VMEM(wide_rows, half),
            pltpu.VMEM((2 if chips < 8 else 1, 2 * tok_rows, model_width), half),
            pltpu.VMEM((max(experts_local - 1, 1), *wide_rows[1:]), half),
            pltpu.VMEM(wide_rows, half),
            pltpu.VMEM(narrow_rows, half),
            pltpu.VMEM(narrow_rows, half),
            pltpu.VMEM(narrow_rows, half),
            pltpu.VMEM((pairs, experts_local * double, model_width), half),
            pltpu.VMEM((size, size * 8, tok_rows), f32),
            pltpu.VMEM(flags, f32),
            pltpu.VMEM(flags, f32),
            pltpu.VMEM(flags, f32),
            pltpu.VMEM(flags, f32),
            pltpu.VMEM((size, 8, tok_rows), f32),
            pltpu.VMEM((size, 8, tok_rows), f32),
            pltpu.VMEM((pairs * double, 128), f32),
            kind((6,)),
            kind((2,)),
            kind,
            kind,
            kind((3, chips)),
            kind((2, chips)),
            few,
            few,
            few,
            few,
            few,
            few,
            few,
            few,
            few,
            few,
            kind((size,)),
            kind((size,)),
            kind((split,)),
            kind((split,)),
            *ChainReduce.scratch(chips, tok_rows, model_width),
        ],
        compiler_params=pltpu.CompilerParams(
            collective_id=which, has_side_effects=True, vmem_limit_bytes=63 * 2**20
        ),
        cost_estimate=pl.CostEstimate(
            flops=2 * experts_local * pairs * double * model_width * hidden_width * 8,
            bytes_accessed=500 * 2**20,
            transcendentals=0,
        ),
    )(
        routed_seq,
        routed_cross,
        choices,
        onehot,
        mate_onehot,
        placed,
        router_rows,
        gain_rows,
        residual,
        cotangent,
        gate_full,
        up_full,
        down_full,
    )

def back_kernel(
    sizes,
    out_grad_ref,
    gains_ref,
    second_gain_ref,
    seg_row_ref,
    sums_ref,
    *refs,
):
    kept_count = 13
    kept, refs = refs[:kept_count], refs[kept_count:]
    back_body(sizes, out_grad_ref, gains_ref, second_gain_ref, seg_row_ref, sums_ref, kept, *refs)


def back_body(
    sizes,
    out_grad_ref,
    gains_ref,
    second_gain_ref,
    seg_row_ref,
    sums_ref,
    kept,
    normed_ref,
    hidden_ref,
    down_ref,
    grad_gate_ref,
    input_grad_ref,
    gains_out_ref,
    out_w_grad_ref,
    mixed_rows,
    gate_landing,
    qkv_out,
    rows_full_ref,
    attended_ref,
    q_ref,
    k_ref,
    v_ref,
    seg_col_ref,
    log_ref,
    cos_ref,
    sin_ref,
    unit_ref,
    qkv_ref,
    tokens_ref,
    residual_grad_ref,
    down_full,
    out_grads,
    attended_grad,
    hidden,
    returned,
    key_total,
    value_total,
    scaled,
    raw_grads,
    centers_own,
    centers_in,
    qkv_stage,
    out_stage,
    out_landing,
    load_sem,
    gather_local,
    gather_send,
    gather_recv,
    gate_local,
    gate_send,
    gate_recv,
    rows_local,
    rows_send,
    rows_recv,
    centers_send,
    centers_recv,
    kept_sem,
    out_local,
    out_send,
    out_recv,
    *reduce_buffers,
):
    size, split, chips, experts_local = sizes
    f32, half = jnp.float32, jnp.bfloat16
    me, mine = lax.axis_index("seq"), lax.axis_index("fsdp")
    tok_rows, model_width = out_grad_ref.shape
    length, local_width = q_ref.shape
    hidden_width = down_ref.shape[0]
    part = model_width // split
    head = HEAD_DIM
    heads = local_width // head
    double = 2 * CAP
    pairs = size // 2
    rows_of = pairs * double

    down_load = pltpu.make_async_copy(down_ref, down_full, load_sem.at[0])
    hidden_load = pltpu.make_async_copy(hidden_ref, hidden, load_sem.at[1])
    down_load.start()
    hidden_load.start()
    targets = (
        rows_full_ref,
        attended_ref,
        q_ref,
        k_ref,
        v_ref,
        seg_col_ref,
        log_ref,
        cos_ref,
        sin_ref,
        unit_ref,
        qkv_ref,
        tokens_ref,
        residual_grad_ref,
    )
    kept_loads = [
        pltpu.make_async_copy(source, target, kept_sem.at[index])
        for index, (source, target) in enumerate(zip(kept, targets))
    ]
    greet_all(size, split)
    gather = ChainGather(chips, out_grad_ref, out_grads, gather_local, gather_send, gather_recv)
    gather.start()
    gate_send_all = ShardSend(
        split,
        lambda dest: grad_gate_ref.at[pl.ds(pl.multiple_of(dest * part, part), part)],
        gate_landing,
        gate_local,
        gate_send,
        gate_recv,
    )

    gate_send_all.start()
    for load in kept_loads:
        load.start()

    down_load.wait()
    hidden_load.wait()
    width_step = min(512, model_width)

    def rows_target(move):
        return mixed_rows.at[:, pl.ds(move * double, double), :]

    def rows_copy(move):
        return pltpu.make_async_remote_copy(
            src_ref=returned.at[move],
            dst_ref=rows_target(move),
            send_sem=rows_send.at[move],
            recv_sem=rows_recv.at[move],
            device_id={"fsdp": partner_of(mine, move)},
        )

    own_rows = pltpu.make_async_copy(returned.at[0], rows_target(0), rows_local)
    for move in range(experts_local - 1, -1, -1):

        @pl.loop(0, model_width // width_step)
        def _(index):
            cols = pl.ds(pl.multiple_of(index * width_step, width_step), width_step)
            made = jnp.dot(
                hidden[move].reshape(rows_of, hidden_width),
                down_full[:, cols],
                preferred_element_type=f32,
            )
            returned[move, :, :, cols] = made.astype(half).reshape(pairs, double, width_step)

        if move:
            rows_copy(move).start()
    own_rows.start()
    gather.steps()
    for load in kept_loads:
        load.wait()
    gather.landed()

    block = min(512, length)

    @pl.loop(0, length // block)
    def _(step):
        rows = pl.ds(pl.multiple_of(step * block, block), block)
        total = cross_dot(out_grads[rows, 0:part], rows_full_ref[0])
        for piece in range(1, split):
            total += cross_dot(
                out_grads[rows, piece * part : (piece + 1) * part], rows_full_ref[piece]
            )
        attended_grad[rows, :] = total.astype(half)

    @pl.loop(0, split)
    def _(piece):
        cols = pl.ds(pl.multiple_of(piece * part, part), part)
        out_stage[piece] = turned_dot(attended_ref[...], out_grads[:, cols]).astype(half)

    out_send_all = ShardSend(
        split, lambda dest: out_stage.at[dest], out_landing, out_local, out_send, out_recv
    )
    out_send_all.start()
    gather.sent()
    normed_load = pltpu.make_async_copy(normed_ref, out_grads, load_sem.at[0])
    normed_load.start()

    wide = min(256, length) if length <= 1024 else 128
    scale = head**-0.5
    segments = seg_row_ref[...].astype(f32)
    for number in range(heads):
        cols = slice(number * head, (number + 1) * head)
        key_total[...] = jnp.zeros_like(key_total)
        value_total[...] = jnp.zeros_like(value_total)

        @pl.loop(0, length // wide)
        def _(step):
            rows = pl.ds(pl.multiple_of(step * wide, wide), wide)
            scores = cross_dot(q_ref[rows, cols], k_ref[:, cols]) * scale
            scores = jnp.where(seg_col_ref[rows, 0:1] == segments, scores, MASKED)
            probs = jnp.exp(scores - log_ref[rows, cols][:, 0:1])
            grads = attended_grad[rows, cols]
            prob_grad = cross_dot(grads, v_ref[:, cols])
            center = jnp.sum(probs * prob_grad, -1, keepdims=True)
            score_grad = (probs * (prob_grad - center)).astype(half)
            query_grad = jnp.dot(score_grad, k_ref[:, cols], preferred_element_type=f32) * scale
            raw_grads[0, rows, cols] = query_grad.astype(half)
            key_total[...] += turned_dot(score_grad, q_ref[rows, cols])
            value_total[...] += turned_dot(probs.astype(half), grads)

        raw_grads[1, :, cols] = (key_total[...] * scale).astype(half)
        raw_grads[2, :, cols] = value_total[...].astype(half)

    lanes = lax.broadcasted_iota(jnp.int32, (8, local_width), 0)
    first_row, second_row = (lanes == 0).astype(f32), (lanes == 1).astype(f32)
    gains_out_ref[...] = jnp.zeros_like(gains_out_ref)
    own_cols = pl.ds(pl.multiple_of(me * local_width, local_width), local_width)
    gains_out_ref[1:2, :] = second_gain_ref[0:1, :]

    @pl.loop(0, length // block)
    def _(step):
        rows = pl.ds(pl.multiple_of(step * block, block), block)
        found = jnp.zeros((8, block), f32)
        for index, pick in ((0, first_row), (1, second_row)):
            unit = unit_ref[index, rows, :]
            pieces = []
            for number in range(heads):
                cols = slice(number * head, (number + 1) * head)
                piece = raw_grads[index, rows, cols].astype(f32)
                pieces.append(piece * cos_ref[rows, :] - turned_halves(piece) * sin_ref[rows, :])
            unit_grad = pieces[0] if heads == 1 else jnp.concatenate(pieces, 1)
            gains_out_ref[2 + index : 3 + index, own_cols] += jnp.sum(
                unit_grad * unit, 0, keepdims=True
            )
            grown = unit_grad * gains_ref[2 + index : 3 + index, own_cols]
            scaled[index, rows, :] = grown
            found += row_sums(grown * unit, pick)
        centers_own[:, rows] = found

    def centers_copy(shift):
        return pltpu.make_async_remote_copy(
            src_ref=centers_own,
            dst_ref=centers_in.at[me],
            send_sem=centers_send.at[shift],
            recv_sem=centers_recv.at[shift],
            device_id={"seq": lax.rem(me + shift, size)},
        )

    for shift in range(1, size):
        centers_copy(shift).start()
    centers_in[me] = centers_own[...]
    for shift in range(1, size):
        centers_copy(shift).wait()
    centers_own[...] = jnp.sum(centers_in[...], 0) * (1.0 / model_width)

    @pl.loop(0, length // block)
    def _(step):
        rows = pl.ds(pl.multiple_of(step * block, block), block)
        for index, pick in ((0, first_row), (1, second_row)):
            inverse = lax.rsqrt(column_of(sums_ref[:, rows], pick) / model_width + EPSILON)
            center = column_of(centers_own[:, rows], pick)
            raw_grads[index, rows, :] = (
                inverse * (scaled[index, rows, :] - unit_ref[index, rows, :] * center)
            ).astype(half)

    reduce = ChainReduce(chips, input_grad_ref, reduce_buffers)

    def product(index, store):
        rows = pl.ds(pl.multiple_of(index * tok_rows, tok_rows), tok_rows)

        @pl.loop(0, model_width // width_step)
        def _(step):
            cols = pl.ds(pl.multiple_of(step * width_step, width_step), width_step)
            total = cross_dot(raw_grads[0, rows, :], qkv_ref[0, cols, :])
            total += cross_dot(raw_grads[1, rows, :], qkv_ref[1, cols, :])
            total += cross_dot(raw_grads[2, rows, :], qkv_ref[2, cols, :])
            store(cols, total)

    qkv_keep = pltpu.make_async_copy(qkv_stage, qkv_out, load_sem.at[1])

    def between():
        normed_load.wait()

        @pl.loop(0, split)
        def _(piece):
            cols = pl.ds(pl.multiple_of(piece * part, part), part)
            left = out_grads[:, cols]
            for index in range(3):
                qkv_stage[piece, index] = turned_dot(left, raw_grads[index]).astype(half)

        qkv_keep.start()

    reduce.run(product, between)

    inputs = tokens_ref[...].astype(f32)
    inverse = lax.rsqrt(jnp.mean(inputs * inputs, -1, keepdims=True) + EPSILON)
    unit = inputs * inverse
    grads = input_grad_ref[...]
    gains_out_ref[0:1, :] = jnp.sum(grads * unit, 0, keepdims=True)
    grads = grads * gains_ref[0:1, :]
    input_grad_ref[...] = residual_grad_ref[...] + inverse * (
        grads - unit * jnp.mean(grads * unit, -1, keepdims=True)
    )

    out_send_all.wait()
    total = out_landing[0].astype(f32)
    for index in range(1, split):
        total += out_landing[index].astype(f32)
    out_w_grad_ref[...] = total
    qkv_keep.wait()
    reduce.sent()
    own_rows.wait()
    for move in range(1, experts_local):
        rows_copy(move).wait()
    gate_send_all.wait()


def back(sizes, out_grad, small, kept, big_ones, which):
    size, split, chips, experts_local = sizes
    f32, half = jnp.float32, jnp.bfloat16
    tok_rows, model_width = out_grad.shape
    length, local_width = kept[1].shape
    normed_seq, hidden, down_full, grad_gate = big_ones
    hidden_width = down_full.shape[0]
    part = model_width // split
    vmem = pl.BlockSpec(memory_space=pltpu.VMEM)
    anywhere = pl.BlockSpec(memory_space=pl.ANY)
    kind = pltpu.SemaphoreType.DMA
    shape = jax.ShapeDtypeStruct
    few, fsdp = kind((experts_local,)), kind((split,))
    return pl.pallas_call(
        functools.partial(back_kernel, sizes),
        out_shape=(
            shape((tok_rows, model_width), f32),
            shape((8, model_width), f32),
            shape((local_width, part), f32),
            shape((size // 2, experts_local * 2 * CAP, model_width), half),
            shape((split, part, hidden_width), half),
            shape((split, 3, part, local_width), half),
        ),
        in_specs=[vmem] * 5 + [anywhere] * (len(kept) + 4),
        out_specs=tuple([vmem] * 3 + [anywhere] * 3),
        scratch_shapes=[
            *[pltpu.VMEM(one.shape, one.dtype) for one in kept],
            pltpu.VMEM(down_full.shape, half),
            pltpu.VMEM((length, model_width), half),
            pltpu.VMEM((length, local_width), half),
            pltpu.VMEM(hidden.shape, half),
            pltpu.VMEM((experts_local, size // 2, 2 * CAP, model_width), half),
            pltpu.VMEM((length, HEAD_DIM), f32),
            pltpu.VMEM((length, HEAD_DIM), f32),
            pltpu.VMEM((2, length, local_width), f32),
            pltpu.VMEM((3, length, local_width), half),
            pltpu.VMEM((8, length), f32),
            pltpu.VMEM((size, 8, length), f32),
            pltpu.VMEM((split, 3, part, local_width), half),
            pltpu.VMEM((split, local_width, part), half),
            pltpu.VMEM((split, local_width, part), half),
            kind((2,)),
            kind,
            kind((3, chips)),
            kind((2, chips)),
            kind,
            fsdp,
            fsdp,
            kind,
            few,
            few,
            kind((size,)),
            kind((size,)),
            kind((len(kept),)),
            kind,
            fsdp,
            fsdp,
            *ChainReduce.scratch(chips, tok_rows, model_width),
        ],
        compiler_params=pltpu.CompilerParams(
            collective_id=which, has_side_effects=True, vmem_limit_bytes=63 * 2**20
        ),
        cost_estimate=pl.CostEstimate(
            flops=2 * length * model_width * local_width * 8,
            bytes_accessed=500 * 2**20,
            transcendentals=0,
        ),
    )(out_grad, *small, *kept, *big_ones)


def close_kernel(
    sizes,
    onehot_ref,
    gains_ref,
    router_ref,
    mixed_rows_any,
    residual_any,
    qkv_any,
    grad_up_ref,
    output_ref,
    gains_out_ref,
    router_out_ref,
    query_w_grad_ref,
    key_w_grad_ref,
    value_w_grad_ref,
    up_landing,
    mixed_rows_ref,
    residual_ref,
    qkv_ref,
    qkv_in,
    qkv_sum,
    load_sem,
    qkv_send,
    qkv_recv,
    total,
    small,
    first,
    second,
    final,
    up_local,
    up_send,
    up_recv,
    send_one,
    recv_one,
    send_two,
    recv_two,
    send_three,
    recv_three,
    *reduce_buffers,
):
    size, split, chips, experts_local = sizes
    f32 = jnp.float32
    me, mine = lax.axis_index("seq"), lax.axis_index("fsdp")
    tok_rows, model_width = residual_ref.shape
    part = model_width // split
    slice_width = model_width // size
    experts_all = router_ref.shape[0]
    loads = [
        pltpu.make_async_copy(source, target, load_sem.at[index])
        for index, (source, target) in enumerate(
            ((qkv_any, qkv_ref), (mixed_rows_any, mixed_rows_ref), (residual_any, residual_ref))
        )
    ]
    for load in loads:
        load.start()
    small[0:8, :] = gains_ref[...]
    small[8 : 8 + experts_all, :] = router_ref[...]
    greet_all(size, split)
    up_send_all = ShardSend(
        split,
        lambda dest: grad_up_ref.at[pl.ds(pl.multiple_of(dest * part, part), part)],
        up_landing,
        up_local,
        up_send,
        up_recv,
    )
    loads[0].wait()

    half_part = qkv_ref.shape[2] // 2
    lower, upper = pl.ds(0, half_part), pl.ds(half_part, half_part)
    mates = (partner_of(mine, 1), partner_of(mine, 2), partner_of(mine, 3)) if split == 4 else ()

    def qkv_copy(index):
        side = index % 2
        rows = (lower, upper)[side]
        if index < 4:
            dest = mates[side] if index < 2 else mates[2]
            source, mate = qkv_ref.at[dest, :, rows], mates[side]
        else:
            source, mate = qkv_sum.at[side], mates[1 - side]
        return pltpu.make_async_remote_copy(
            src_ref=source,
            dst_ref=qkv_in.at[index],
            send_sem=qkv_send.at[index],
            recv_sem=qkv_recv.at[index],
            device_id={"fsdp": mate},
        )

    def qkv_shift(shift):
        dest = lax.rem(mine + shift, split)
        return pltpu.make_async_remote_copy(
            src_ref=qkv_ref.at[dest],
            dst_ref=qkv_in.at[shift],
            send_sem=qkv_send.at[shift],
            recv_sem=qkv_recv.at[shift],
            device_id={"fsdp": dest},
        )

    if split == 4:
        for index in range(4):
            qkv_copy(index).start()
    else:
        for shift in range(1, split):
            qkv_shift(shift).start()
    up_send_all.start()

    def columns(index):
        return pl.ds(pl.multiple_of(index * slice_width, slice_width), slice_width)

    def scatter(shift):
        peer = lax.rem(me + shift, size)
        return pltpu.make_async_remote_copy(
            src_ref=small.at[:, columns(peer)],
            dst_ref=first.at[me],
            send_sem=send_one.at[shift],
            recv_sem=recv_one.at[shift],
            device_id={"seq": peer},
        )

    def share(shift):
        return pltpu.make_async_remote_copy(
            src_ref=second.at[mine],
            dst_ref=second.at[mine],
            send_sem=send_two.at[shift],
            recv_sem=recv_two.at[shift],
            device_id={"fsdp": lax.rem(mine + shift, split)},
        )

    def collect(shift):
        return pltpu.make_async_remote_copy(
            src_ref=final.at[me],
            dst_ref=final.at[me],
            send_sem=send_three.at[shift],
            recv_sem=recv_three.at[shift],
            device_id={"seq": lax.rem(me + shift, size)},
        )

    for shift in range(1, size):
        scatter(shift).start()
    first[me] = small[:, columns(me)]

    reduce = ChainReduce(chips, total, reduce_buffers)
    width_step = min(512, model_width)

    def product(index, store):
        side = pl.ds(pl.multiple_of(lax.rem(index, 2) * tok_rows, tok_rows), tok_rows)
        left = onehot_ref[index // 2, :, side]

        @pl.loop(0, model_width // width_step)
        def _(step):
            cols = pl.ds(pl.multiple_of(step * width_step, width_step), width_step)
            store(cols, turned_dot(left, mixed_rows_ref[index // 2, :, cols]))

    def between():
        for shift in range(1, size):
            scatter(shift).wait_recv()
        second[mine] = jnp.sum(first[...], 0)
        for shift in range(1, split):
            share(shift).start()

    loads[1].wait()
    reduce.run(product, between)
    if split == 4:
        for side in range(2):
            qkv_copy(2 + side).wait_recv()
            rows = (lower, upper)[side]
            qkv_sum[side] = (
                qkv_ref[mates[1 - side], :, rows].astype(f32) + qkv_in[2 + side].astype(f32)
            ).astype(qkv_sum.dtype)
            qkv_copy(4 + side).start()
    loads[2].wait()
    for shift in range(1, split):
        share(shift).wait_recv()
    final[me] = jnp.sum(second[...], 0)
    for shift in range(1, size):
        collect(shift).start()
    output_ref[...] = (residual_ref[...] + total[...]).astype(output_ref.dtype)
    for shift in range(1, size):
        scatter(shift).wait_send()
    for shift in range(1, split):
        share(shift).wait_send()
    for shift in range(1, size):
        collect(shift).wait()
    for index in range(size):
        cols = slice(index * slice_width, (index + 1) * slice_width)
        gains_out_ref[:, cols] = final[index, 0:4]
        router_out_ref[:, cols] = final[index, 8:]
    targets = (query_w_grad_ref, key_w_grad_ref, value_w_grad_ref)
    if split == 4:
        for side in range(2):
            for index in (side, 2 + side, 5 - side):
                copy = qkv_copy(index)
                copy.wait() if index < 2 or index > 3 else copy.wait_send()
        for side in range(2):
            rows = (lower, upper)[side]
            for index, target in enumerate(targets):
                target[rows, :] = (
                    qkv_ref[mine, index, rows].astype(f32)
                    + qkv_in[side, index].astype(f32)
                    + qkv_in[4 + side, index].astype(f32)
                )
    else:
        for shift in range(1, split):
            qkv_shift(shift).wait()
        for index, target in enumerate(targets):
            sums = qkv_ref[mine, index].astype(f32)
            for shift in range(1, split):
                sums += qkv_in[shift, index].astype(f32)
            target[...] = sums
    reduce.sent()
    up_send_all.wait()


def close(sizes, onehot, gains, router_grad, mixed_rows, residual, qkv_parts, grad_up, which):
    size, split, chips, experts_local = sizes
    f32, half = jnp.float32, jnp.bfloat16
    tok_rows, model_width = residual.shape
    hidden_width = grad_up.shape[1]
    part, slice_width = model_width // split, model_width // size
    rows = 8 + router_grad.shape[0]
    vmem = pl.BlockSpec(memory_space=pltpu.VMEM)
    anywhere = pl.BlockSpec(memory_space=pl.ANY)
    kind = pltpu.SemaphoreType.DMA
    shape = jax.ShapeDtypeStruct
    seq, fsdp = kind((size,)), kind((split,))
    share = qkv_parts.shape[2:]
    return pl.pallas_call(
        functools.partial(close_kernel, sizes),
        out_shape=(
            shape((tok_rows, model_width), half),
            shape((4, model_width), f32),
            shape(router_grad.shape, f32),
            shape(share, f32),
            shape(share, f32),
            shape(share, f32),
            shape((split, part, hidden_width), half),
        ),
        in_specs=[vmem] * 3 + [anywhere] * 4,
        out_specs=tuple([vmem] * 6 + [anywhere]),
        scratch_shapes=[
            pltpu.VMEM(mixed_rows.shape, half),
            pltpu.VMEM(residual.shape, f32),
            pltpu.VMEM(qkv_parts.shape, half),
            pltpu.VMEM((6, 3, share[0] // 2, share[1]) if split == 4 else qkv_parts.shape, half),
            pltpu.VMEM((2, 3, share[0] // 2, share[1]), half),
            kind((3,)),
            kind((max(6, split),)),
            kind((max(6, split),)),
            pltpu.VMEM((tok_rows, model_width), f32),
            pltpu.VMEM((rows, model_width), f32),
            pltpu.VMEM((size, rows, slice_width), f32),
            pltpu.VMEM((split, rows, slice_width), f32),
            pltpu.VMEM((size, rows, slice_width), f32),
            kind,
            fsdp,
            fsdp,
            seq,
            seq,
            fsdp,
            fsdp,
            seq,
            seq,
            *ChainReduce.scratch(chips, tok_rows, model_width),
        ],
        compiler_params=pltpu.CompilerParams(
            collective_id=which, has_side_effects=True, vmem_limit_bytes=56 * 2**20
        ),
    )(onehot, gains, router_grad, mixed_rows, residual, qkv_parts, grad_up)


def finish_kernel(count, *refs):
    sources, targets = refs[: len(refs) // 2], refs[len(refs) // 2 :]
    for source, target in zip(sources[:count], targets[:count]):
        target[...] = source[...]
    for source, target in zip(sources[count:], targets[count:]):
        total = source[0].astype(target.dtype)
        for index in range(1, source.shape[0]):
            total += source[index].astype(target.dtype)
        target[...] = total


def finish(results, landings, experts_local):
    halves = 1
    steps = experts_local * halves
    in_specs, out_specs, shapes = [], [], []
    for one in results:
        rows = one.shape[0] // steps
        spec = pl.BlockSpec((rows, one.shape[1]), lambda step: (step, 0))
        if one.shape[0] % (steps * 16):
            spec = pl.BlockSpec(one.shape, lambda step: (0, 0))
        in_specs.append(spec)
        out_specs.append(spec)
        shapes.append(jax.ShapeDtypeStruct(one.shape, one.dtype))
    grouped = []
    for one in landings:
        groups = one.shape[0] // experts_local
        grouped.append(one.reshape(groups, experts_local, *one.shape[1:]))
        block = (one.shape[1] // halves, one.shape[2])
        in_specs.append(
            pl.BlockSpec(
                (groups, 1, *block), lambda step: (0, step // halves, step % halves, 0)
            )
        )
        out_specs.append(
            pl.BlockSpec((1, *block), lambda step: (step // halves, step % halves, 0))
        )
        shapes.append(jax.ShapeDtypeStruct((experts_local, *one.shape[1:]), jnp.float32))
    return pl.pallas_call(
        functools.partial(finish_kernel, len(results)),
        grid=(steps,),
        in_specs=in_specs,
        out_specs=out_specs,
        out_shape=shapes,
        compiler_params=pltpu.CompilerParams(vmem_limit_bytes=63 * 2**20),
    )(*results, *grouped)


def shards(
    tokens,
    norm_gains,
    w_query,
    w_key,
    w_value,
    w_out,
    w_router,
    w_gate,
    w_up,
    w_down,
    segment_ids,
    expert_ids,
    expert_slots,
    cotangent,
):
    half_type = jnp.bfloat16
    model_width = tokens.shape[1]
    experts_local = w_gate.shape[0]
    seq_size = lax.axis_size("seq")
    split = lax.axis_size("fsdp")
    length = seq_size * tokens.shape[0]
    sizes = (seq_size, split, seq_size // 2, experts_local)
    cosine_wide, sine_wide = rope_tables(length, HEAD_DIM)
    segment_row = segment_ids.reshape(1, -1)
    (
        normed_seq,
        qkv_stack,
        out_stack,
        query_heads,
        key_heads,
        value_heads,
        unit_pair,
        log_wide,
        attended_heads,
        square_sums,
        residual,
        gain_rows,
        segment_cols,
        routed_seq,
        routed_cross,
        placed,
        gate_full,
        up_full,
        down_full,
        choices,
        onehot,
        mate_onehot,
    ) = front(
        sizes,
        tokens,
        norm_gains,
        cosine_wide,
        sine_wide,
        segment_row,
        expert_ids.T,
        expert_slots.T,
        cotangent,
        (w_query, w_key, w_value, w_out, w_gate, w_up, w_down),
        0,
    )
    router_rows = jnp.zeros((seq_size, 8, model_width), half_type)
    router_rows = router_rows.at[:, :experts_local].set(
        w_router.T.reshape(seq_size, experts_local, model_width)
    )
    router_rows = router_rows.reshape(seq_size * 8, model_width)
    (
        residual_grad,
        out_grad,
        gain_second_grad,
        router_grad,
        hidden,
        grad_gate_full,
        grad_up_full,
        down_landing,
        _,
    ) = experts(
        sizes,
        routed_seq,
        routed_cross,
        choices,
        onehot,
        mate_onehot,
        placed,
        router_rows,
        gain_rows,
        residual,
        cotangent,
        (gate_full, up_full, down_full),
        1,
    )
    input_grad, gain_grads, out_owned, mixed_rows, gate_landing, qkv_parts = back(
        sizes,
        out_grad,
        (gain_rows, gain_second_grad, segment_row, square_sums),
        (
            out_stack,
            attended_heads,
            query_heads,
            key_heads,
            value_heads,
            segment_cols,
            log_wide,
            cosine_wide,
            sine_wide,
            unit_pair,
            qkv_stack,
            tokens,
            residual_grad,
        ),
        (normed_seq, hidden, down_full, grad_gate_full),
        2,
    )
    output, gain_sums, router_sums, query_owned, key_owned, value_owned, up_landing = close(
        sizes, onehot, gain_grads, router_grad, mixed_rows, residual, qkv_parts, grad_up_full, 3
    )
    (
        output,
        input_grad,
        gain_sums,
        query_owned,
        key_owned,
        value_owned,
        out_owned,
        router_sums,
        gate_owned,
        up_owned,
        down_owned,
    ) = finish(
        (
            output,
            input_grad,
            gain_sums,
            query_owned,
            key_owned,
            value_owned,
            out_owned,
            router_sums,
        ),
        (gate_landing, up_landing, down_landing),
        experts_local,
    )
    return (
        output,
        input_grad,
        gain_sums,
        query_owned,
        key_owned,
        value_owned,
        out_owned,
        router_sums.T,
        gate_owned,
        up_owned,
        down_owned,
    )


def solution(mesh):
    in_specs = (
        P(("fsdp", "seq"), None),
        P(),
        P("fsdp", "seq"),
        P("fsdp", "seq"),
        P("fsdp", "seq"),
        P("seq", "fsdp"),
        P(),
        P("seq", "fsdp", None),
        P("seq", "fsdp", None),
        P("seq", None, "fsdp"),
        P("fsdp"),
        P(("fsdp", "seq"), None),
        P(("fsdp", "seq"), None),
        P(("fsdp", "seq"), None),
    )
    out_specs = (
        P(("fsdp", "seq"), None),
        P(("fsdp", "seq"), None),
        P(),
        P("fsdp", "seq"),
        P("fsdp", "seq"),
        P("fsdp", "seq"),
        P("seq", "fsdp"),
        P(),
        P("seq", "fsdp", None),
        P("seq", "fsdp", None),
        P("seq", None, "fsdp"),
    )
    return jax.shard_map(shards, mesh=mesh, in_specs=in_specs, out_specs=out_specs, check_vma=False)
```
